32 devices in a mesh: seq: 8 (over z, y), head: 4 (over x, core).
Axes of the slice: x: 2, y: 2, z: 4, core: 2. Of those that a mesh axis runs over, the one named last changes fastest.
Arguments:
- x_input: bfloat16 [8192, 8192], P('seq', 'head'), may hold values from -6 to 6
- z_input: bfloat16 [8192, 8192], P('seq', 'head'), may hold values from -6 to 6
- bc_input: bfloat16 [8192, 8, 256], P('seq', 'head'), may hold values from -6 to 6
- conv_weight_x: float32 [4, 8192], P(None, 'head'), may hold values from -3 to 3
- conv_weight_bc: float32 [4, 8, 256], P(None, 'head'), may hold values from -3 to 3
- step_size: float32 [8192, 128], P('seq', 'head'), may hold values from 0 to 1
- log_decay: float32 [8192, 128], P('seq', 'head'), may hold values from -1 to 0
- skip_gain: float32 [128], P('head'), may hold values from 0.5 to 2
- norm_gain: float32 [8192], P('head'), may hold values from 0.1 to 1.9
- out_weight: bfloat16 [8192, 4096], P('head'), may hold values from -0.0625 to 0.0625
Outputs:
- layer_out: bfloat16 [8192, 4096], P(('seq', 'head'))
The draws below stay inside these ranges and needn't reach their ends.
All inputs are finite; a program needn't handle non-finite values.
Results may differ from the reference program's by a relative error of at most 0.012.
Values may be sent and summed in bfloat16 or wider, within the bound.
No kernel may reach another device: no remote copies, remote signals or barrier semaphores. Data moves between devices by JAX's collectives and lax.ppermute only.
A program may use at most 256 MiB of HBM per device.

```python
import math
import jax
import jax.numpy as jnp
from jax import lax

D = 4096
H = 128
P_SIZE = 64
N = 128
G = 8
KCONV = 4
BLOCK_LEN = 256
TOK_DEV = 1024
DI = 8192
TEXT_ITEMS = 8192


def head_rates(key):
    seq_devices = TEXT_ITEMS // TOK_DEV
    stochastic_seeds = jax.random.split(jax.random.fold_in(key, 11), 3)
    fast_share = 0.15
    spectrum_top = 3.0
    spectrum_low = 0.03 / seq_devices
    fast_heads = jax.random.uniform(stochastic_seeds[0], (H,), jnp.float32) < fast_share
    fast_low = math.log(max(TOK_DEV / 50.0, 3.0))
    fast_high = math.log(max(TOK_DEV / 30.0, 5.0))
    fast_device = jnp.exp(jax.random.uniform(stochastic_seeds[1], (H,), jnp.float32, fast_low, fast_high))
    spread_device = jnp.exp(jax.random.uniform(stochastic_seeds[2], (H,), jnp.float32, math.log(spectrum_low), math.log(spectrum_top)))
    return jnp.where(fast_heads, fast_device, spread_device) / TOK_DEV


def device_blocks(key):
    seq_devices = TEXT_ITEMS // TOK_DEV
    factor = jnp.exp(jax.random.uniform(key, (seq_devices, 1, H), jnp.float32, math.log(0.5), math.log(2.0)))
    return jnp.broadcast_to(factor, (seq_devices, TOK_DEV, H)).reshape(TEXT_ITEMS, H)


def draw_log_decay(key, part):
    forgetting_speeds = head_rates(key)
    stochastic_seeds = jax.random.split(jax.random.fold_in(key, 21), 4)
    seed_shift_amount = jax.random.uniform(stochastic_seeds[0], (TEXT_ITEMS, H), jnp.float32, 0.5, 1.5)
    processor_factor = device_blocks(stochastic_seeds[1])
    segment_entries = jax.random.randint(stochastic_seeds[2], (2,), 0, TEXT_ITEMS)
    segment_span = jax.random.uniform(stochastic_seeds[3], (2,), jnp.float32, 0.22, 0.45)
    symbol_indices = jnp.arange(TEXT_ITEMS)
    symbol_segment = jnp.sum(jnp.where(symbol_indices[:, None] == segment_entries[None, :], segment_span[None, :], 0.0), axis=1)
    return -jnp.minimum(forgetting_speeds[None, :] * seed_shift_amount * processor_factor + symbol_segment[:, None], 1.0)


def draw_step_size(key, part):
    forgetting_speeds = head_rates(key)
    stochastic_seeds = jax.random.split(jax.random.fold_in(key, 31), 2)
    seed_shift_amount = jnp.exp(jax.random.uniform(stochastic_seeds[0], (TEXT_ITEMS, H), jnp.float32, math.log(0.5), math.log(2.0)))
    processor_factor = device_blocks(stochastic_seeds[1])
    floor_rate = jnp.maximum(forgetting_speeds, 1.0 / TEXT_ITEMS)
    return jnp.minimum(2.0 * floor_rate[None, :] * seed_shift_amount * processor_factor, 1.0)


def levels(own_key, dims, shards, smallest, largest):
    gain = 1.0
    for dim, blocks in shards:
        draws = jax.random.uniform(jax.random.fold_in(jax.random.fold_in(own_key, 6), dim), (blocks,), jnp.float32, smallest / len(shards), largest / len(shards))
        gain = gain * jnp.repeat(jnp.exp(draws), dims[dim] // blocks).reshape((-1,) + (1,) * (len(dims) - 1 - dim))
    return gain


def centred(own_key, shape, width, reach, shards=(), kind=jnp.bfloat16):
    result = width * jax.random.normal(own_key, shape, jnp.float32)
    if shards:
        result = result * levels(own_key, shape, shards, -0.22, 0.18)
    return jnp.clip(result, -reach, reach).astype(kind)


def setup_inputs(seed: int = 0) -> dict:
    arg_keys = jax.random.split(jax.random.key(seed), 11)
    return {
        "x_input": centred(arg_keys[0], (TEXT_ITEMS, DI), 1.0, 6.0, ((0, 8), (1, 4))),
        "z_input": centred(arg_keys[1], (TEXT_ITEMS, DI), 1.0, 6.0, ((0, 8), (1, 4))),
        "bc_input": centred(arg_keys[2], (TEXT_ITEMS, G, 2 * N), 1.0, 6.0, ((0, 8), (1, 4))),
        "conv_weight_x": centred(arg_keys[3], (KCONV, DI), 0.5, 3.0, ((1, 4),), jnp.float32),
        "conv_weight_bc": centred(arg_keys[4], (KCONV, G, 2 * N), 0.5, 3.0, ((1, 4),), jnp.float32),
        "step_size": draw_step_size(jax.random.fold_in(arg_keys[10], 71), 0),
        "log_decay": draw_log_decay(jax.random.fold_in(arg_keys[10], 71), 0),
        "skip_gain": jnp.clip(jnp.exp(math.log(2.0) - 1.3862944 * jax.random.uniform(arg_keys[7], (H,), jnp.float32) ** levels(arg_keys[7], (H,), ((0, 4),), -0.2, 0.2)), 0.5, 2.0),
        "norm_gain": jnp.clip(1.0 + 0.18 * jax.random.normal(arg_keys[8], (DI,), jnp.float32), 0.1, 1.9),
        "out_weight": centred(arg_keys[9], (DI, D), DI ** -0.5, 0.0625, ((0, 4),)),
    }


EPS = 1e-05

def conv_silu(padded, weight, length):
    summed = jnp.zeros((length,) + padded.shape[1:], jnp.float32)
    for offset in range(weight.shape[0]):
        summed = summed + weight[offset] * padded[offset:offset + length].astype(jnp.float32)
    return jax.nn.silu(summed).astype(jnp.bfloat16)

def reference(x_input, z_input, bc_input, conv_weight_x, conv_weight_bc, step_size, log_decay, skip_gain, norm_gain, out_weight):
    lead_rows = KCONV - 1
    x_conv = conv_silu(jnp.concatenate([jnp.zeros((lead_rows, DI), jnp.bfloat16), x_input], 0), conv_weight_x, TEXT_ITEMS)
    bc_conv = conv_silu(jnp.concatenate([jnp.zeros((lead_rows, G, 2 * N), jnp.bfloat16), bc_input], 0), conv_weight_bc, TEXT_ITEMS)
    per_group = H // G
    blocks = TEXT_ITEMS // BLOCK_LEN
    highest = lax.Precision.HIGHEST
    lower_mask = jnp.tril(jnp.ones((BLOCK_LEN, BLOCK_LEN), bool))[:, :, None, None]
    skip_table = skip_gain.reshape(G, per_group)

    def advance(carry_state, block_data):
        x_block, bc_block, step_block, decay_block, z_block = block_data
        x_float = x_block.astype(jnp.float32).reshape(BLOCK_LEN, G, per_group, P_SIZE)
        bc_float = bc_block.astype(jnp.float32)
        b_mat = bc_float[..., :N]
        c_mat = bc_float[..., N:]
        driven = step_block.reshape(BLOCK_LEN, G, per_group)[..., None] * x_float
        cumulative = jnp.cumsum(decay_block.reshape(BLOCK_LEN, G, per_group), axis=0)
        log_gap = cumulative[:, None] - cumulative[None, :]
        decay_table = jnp.where(lower_mask, jnp.exp(jnp.where(lower_mask, log_gap, 0.0)), 0.0)
        scores = jnp.einsum('tgn,sgn->tsg', c_mat, b_mat, precision=highest)
        within = jnp.einsum('tsgh,sghp->tghp', scores[..., None] * decay_table, driven, precision=highest)
        carried = jnp.exp(cumulative)[..., None] * jnp.einsum('tgn,ghnp->tghp', c_mat, carry_state, precision=highest)
        mixed = within + carried + skip_table[..., None] * x_float
        last_log = cumulative[-1]
        fading = jnp.exp(last_log[None] - cumulative)[..., None] * driven
        carry_state = jnp.exp(last_log)[..., None, None] * carry_state + jnp.einsum('sgn,sghp->ghnp', b_mat, fading, precision=highest)
        gated_out = mixed.reshape(BLOCK_LEN, DI) * jax.nn.silu(z_block.astype(jnp.float32))
        grouped = gated_out.reshape(BLOCK_LEN, G, DI // G)
        normed = grouped * lax.rsqrt(lax.optimization_barrier(jnp.mean(grouped * grouped, axis=-1, keepdims=True)) + EPS)
        normed = (normed.reshape(BLOCK_LEN, DI) * norm_gain).astype(jnp.bfloat16)
        return (carry_state, jnp.dot(normed, out_weight, preferred_element_type=jnp.float32).astype(jnp.bfloat16))
    inputs = (x_conv.reshape(blocks, BLOCK_LEN, DI), bc_conv.reshape(blocks, BLOCK_LEN, G, 2 * N), step_size.reshape(blocks, BLOCK_LEN, H), log_decay.reshape(blocks, BLOCK_LEN, H), z_input.reshape(blocks, BLOCK_LEN, DI))
    initial = jnp.zeros((G, per_group, N, P_SIZE), jnp.float32)
    _, outputs = lax.scan(advance, initial, inputs)
    return outputs.reshape(TEXT_ITEMS, D)
```

```python
import functools

import jax
import jax.numpy as jnp
import numpy as np
from jax import lax
from jax.experimental import pallas as pl
from jax.experimental.pallas import tpu as pltpu
from jax.sharding import PartitionSpec as P

P_SIZE = 64
N = 128
KCONV = 4
EPS = 1e-05
LOG2E = 1.4426950408889634

TOK_A = 256
TOK_B = 128
SLAB = 256
LEAD = 16
B_PARTS = 4
VMEM_LIMIT = 50 * 1024 * 1024
HIGHEST = lax.Precision.HIGHEST
F32 = jnp.float32
BF16 = jnp.bfloat16


def params(limit=VMEM_LIMIT):
    return pltpu.CompilerParams(vmem_limit_bytes=limit)


def dot(a, b, dims=((1,), (0,)), precision=None):
    return lax.dot_general(a, b, (dims, ((), ())), precision=precision, preferred_element_type=F32)


def half_silu(half):
    return half + half * jnp.tanh(half)


def whole(shape):
    return pl.BlockSpec(shape, lambda *_: (0,) * len(shape))


def decay_kernel(ld, ld_t, step, ones, cum, cum_t, f_dev, st, f_blk, e_blk, e_dev, blk_x, dev_total):
    length, heads = ld.shape
    blocks = length // TOK_B
    row = lax.broadcasted_iota(jnp.int32, (TOK_B, TOK_B), 0)
    col = lax.broadcasted_iota(jnp.int32, (TOK_B, TOK_B), 1)
    lower = (row >= col).astype(F32)
    upper = (row <= col).astype(F32)

    def put(ref, rows, value):
        high = value.astype(BF16)
        ref[rows, 0:heads] = high
        ref[rows, heads : 2 * heads] = (value - high.astype(F32)).astype(BF16)

    cums, totals = [], []
    for b in range(blocks):
        rows = slice(b * TOK_B, (b + 1) * TOK_B)
        c = dot(lower, ld[rows, :] * LOG2E, precision=HIGHEST)
        cum[rows, :] = c
        cum_t[:, rows] = dot(ld_t[:, rows] * LOG2E, upper, precision=HIGHEST)
        cums.append(c)
        totals.append(c[TOK_B - 1 : TOK_B, :])
    before = [jnp.zeros_like(totals[0])]
    for b in range(blocks):
        before.append(before[-1] + totals[b])
    total = before[-1]
    dev_total[...] = total
    blk_x[...] = dot(jnp.exp2(jnp.concatenate(totals, 0)), ones[0:heads, :].astype(F32), precision=HIGHEST)
    for b in range(blocks):
        rows = slice(b * TOK_B, (b + 1) * TOK_B)
        s = step[rows, :]
        dev = cums[b] + before[b]
        put(f_dev, rows, jnp.exp2(total - dev) * s)
        put(st, rows, s)
        put(f_blk, rows, jnp.exp2(totals[b] - cums[b]) * s)
        put(e_blk, rows, jnp.exp2(cums[b]))
        put(e_dev, rows, jnp.exp2(dev))


def decays(log_decay, step, ones):
    length, heads = log_decay.shape
    blocks = length // TOK_B
    width = ones.shape[1]
    pair = jax.ShapeDtypeStruct((length, 2 * heads), BF16)
    return pl.pallas_call(
        decay_kernel,
        out_shape=(
            jax.ShapeDtypeStruct((length, heads), F32),
            jax.ShapeDtypeStruct((heads, length), F32),
            pair,
            pair,
            pair,
            pair,
            pair,
            jax.ShapeDtypeStruct((blocks, width), F32),
            jax.ShapeDtypeStruct((1, heads), F32),
        ),
        compiler_params=params(),
        name="decays",
    )(log_decay, log_decay.T, step, ones)


def conv_kernel(odd, x, x_lead, bc, bc_lead, halo, wx, wbc, f_dev, ones, x_out, bc_out, keep, send, buf, xf, state):
    i = pl.program_id(0)
    rows, width = x.shape
    bc_width = bc.shape[1]
    groups = bc_width // (2 * N)
    per = width // groups
    half = width // 2
    part = 64

    @pl.when(i == 0)
    def _():
        buf[0:LEAD, 0:width] = halo[:, 0:width].astype(F32)
        buf[0:LEAD, width:] = halo[:, width:].astype(F32)
        state[...] = jnp.zeros_like(state)

    @pl.when(i > 0)
    def _():
        buf[0:LEAD, 0:width] = x_lead[...].astype(F32)
        buf[0:LEAD, width:] = bc_lead[...].astype(F32)

    def conv(offset, lanes, weights, r):
        total = None
        for k in range(KCONV):
            first = LEAD - (KCONV - 1) + k + r
            term = weights[k : k + 1, :] * buf[first : first + part, pl.ds(offset + lanes, SLAB)]
            total = term if total is None else total + term
        return half_silu(total)

    for c in range(bc_width // SLAB):
        lanes = c * SLAB
        buf[LEAD:, width + lanes : width + lanes + SLAB] = bc[:, lanes : lanes + SLAB].astype(F32)
        w = wbc[:, lanes : lanes + SLAB] * 0.5
        for r in range(0, rows, part):
            bc_out[r : r + part, lanes : lanes + SLAB] = conv(width, lanes, w, r).astype(BF16)

    def slab(c, _):
        lanes = pl.multiple_of(c * SLAB, SLAB)
        ds = pl.ds(lanes, SLAB)
        buf[LEAD:, ds] = x[:, ds].astype(F32)
        w = wx[:, ds] * 0.5
        scale = dot(f_dev[...], ones[:, ds])
        for r in range(0, rows, part):
            value = conv(0, lanes, w, r).astype(BF16)
            x_out[r : r + part, ds] = value
            xf[r : r + part, ds] = (value.astype(F32) * scale[r : r + part]).astype(BF16)
        return 0

    lax.fori_loop(0, width // SLAB, slab, 0)
    for g in range(groups):
        b_mat = bc_out[:, 2 * N * g : 2 * N * g + N]
        lanes = slice(g * per, (g + 1) * per)
        state[:, lanes] += dot(b_mat, xf[:, lanes], ((0,), (0,)))

    @pl.when(i == pl.num_programs(0) - 1)
    def _():
        is_odd = odd[0] == 1
        low, high = state[:, 0:half], state[:, half:]
        keep[...] = jnp.where(is_odd, high, low)
        send[...] = jnp.where(is_odd, low, high).astype(BF16)


def conv_states(odd, x, bc, halo, wx, wbc, f_dev, ones):
    length, width = x.shape
    bc_width = bc.shape[1]
    half = width // 2
    lead = lambda i, _: (jnp.maximum(i * (TOK_A // LEAD) - 1, 0), 0)
    block = lambda i, _: (i, 0)
    return pl.pallas_call(
        conv_kernel,
        grid_spec=pltpu.PrefetchScalarGridSpec(
            num_scalar_prefetch=1,
            grid=(length // TOK_A,),
            in_specs=[
                pl.BlockSpec((TOK_A, width), block),
                pl.BlockSpec((LEAD, width), lead),
                pl.BlockSpec((TOK_A, bc_width), block),
                pl.BlockSpec((LEAD, bc_width), lead),
                whole(halo.shape),
                whole(wx.shape),
                whole(wbc.shape),
                pl.BlockSpec((TOK_A, f_dev.shape[1]), block),
                whole(ones.shape),
            ],
            out_specs=[
                pl.BlockSpec((TOK_A, width), block),
                pl.BlockSpec((TOK_A, bc_width), block),
                whole((N, half)),
                whole((N, half)),
            ],
            scratch_shapes=[
                pltpu.VMEM((LEAD + TOK_A, width + bc_width), F32),
                pltpu.VMEM((TOK_A, width), BF16),
                pltpu.VMEM((N, width), F32),
            ],
        ),
        out_shape=(
            jax.ShapeDtypeStruct((length, width), BF16),
            jax.ShapeDtypeStruct((length, bc_width), BF16),
            jax.ShapeDtypeStruct((N, half), F32),
            jax.ShapeDtypeStruct((N, half), BF16),
        ),
        compiler_params=params(),
        name="conv_states",
    )(odd, x, x, bc, bc, halo, wx, wbc, f_dev, ones)


def scan_kernel(head0, x, bc, z, cum, cum_t, st, f_blk, e_blk, e_dev, blk_x, skip, ones, u_out, v_out, state):
    i = pl.program_id(0)
    rows, width = x.shape
    per_slab = SLAB // P_SIZE

    @pl.when(i == 0)
    def _():
        state[...] = jnp.zeros_like(state)

    row = lax.broadcasted_iota(jnp.int32, (rows, rows), 0)
    col = lax.broadcasted_iota(jnp.int32, (rows, rows), 1)
    b_mat = bc[:, 0:N]
    c_mat = bc[:, N : 2 * N]
    scores = jnp.where(row >= col, dot(c_mat, b_mat, ((1,), (1,))), 0.0)
    lane = lax.broadcasted_iota(jnp.int32, (rows, 2 * P_SIZE), 1)
    first = lane < P_SIZE
    zero = jnp.zeros((rows, 2 * P_SIZE), BF16)
    fade_rows = blk_x[pl.ds(i, 1), :]
    for s in range(width // SLAB):
        lanes = slice(s * SLAB, (s + 1) * SLAB)
        xs = x[:, lanes].astype(F32)
        sel = ones[:, lanes]
        xd = (xs * dot(st[...], sel)).astype(BF16)
        old = state[:, lanes]
        carried = dot(c_mat, old.astype(BF16)) * dot(e_blk[...], sel)
        within = []
        for q in range(per_slab // 2):
            tables = []
            for h in (2 * q, 2 * q + 1):
                head = head0 + s * per_slab + h
                gap = jnp.minimum(cum[:, head : head + 1] - cum_t[head : head + 1, :], 0.0)
                tables.append((scores * jnp.exp2(gap)).astype(BF16))
            xp = xd[:, q * 2 * P_SIZE : (q + 1) * 2 * P_SIZE]
            stacked = jnp.concatenate([jnp.where(first, xp, zero), jnp.where(first, zero, xp)], 0)
            within.append(dot(jnp.concatenate(tables, 1), stacked))
        y = jnp.concatenate(within, 1) + carried + skip[:, lanes] * xs
        gate = half_silu(z[:, lanes].astype(F32) * 0.5)
        u_out[:, lanes] = (y * gate).astype(BF16)
        v_out[:, lanes] = (gate * dot(e_dev[...], sel)).astype(BF16)
        xf = (xs * dot(f_blk[...], sel)).astype(BF16)
        state[:, lanes] = old * fade_rows[:, lanes] + dot(b_mat, xf, ((0,), (0,)))


def scan_part(part, x, bc, z, cum, cum_t, st, f_blk, e_blk, e_dev, blk_x, skip, ones):
    length, full = x.shape
    width = full // B_PARTS
    groups = bc.shape[1] // (2 * N)
    group = part * groups // B_PARTS
    heads = cum.shape[1]
    blocks = length // TOK_B
    out = jax.ShapeDtypeStruct((length, width), BF16)
    cols = lambda i: (i, part)
    narrow = pl.BlockSpec((TOK_B, 2 * heads), lambda i: (i, 0))
    return pl.pallas_call(
        functools.partial(scan_kernel, part * heads // B_PARTS),
        grid=(blocks,),
        in_specs=[
            pl.BlockSpec((TOK_B, width), cols),
            pl.BlockSpec((TOK_B, 2 * N), lambda i: (i, group)),
            pl.BlockSpec((TOK_B, width), cols),
            pl.BlockSpec((TOK_B, heads), lambda i: (i, 0)),
            pl.BlockSpec((heads, TOK_B), lambda i: (0, i)),
            narrow,
            narrow,
            narrow,
            narrow,
            pl.BlockSpec((blocks, width), lambda i: (0, part)),
            pl.BlockSpec((1, width), lambda i: (0, part)),
            pl.BlockSpec((2 * heads, width), lambda i: (0, part)),
        ],
        out_specs=[pl.BlockSpec((TOK_B, width), lambda i: (i, 0))] * 2,
        out_shape=(out, out),
        scratch_shapes=[pltpu.VMEM((N, width), F32)],
        compiler_params=params(),
        cost_estimate=pl.CostEstimate(
            flops=length * width * 4000, bytes_accessed=length * width * 10, transcendentals=length * width * 4
        ),
        name="scan_part",
    )(x, bc, z, cum, cum_t, st, f_blk, e_blk, e_dev, blk_x, skip, ones)


def norm_kernel(info, bc, keep, recv, gain, *refs):
    uv, out = refs[:-1], refs[-1]
    us, vs = uv[:B_PARTS], uv[B_PARTS:]
    width = out.shape[1]
    groups = bc.shape[1] // (2 * N)
    per = width // groups
    half = width // 2
    part = width // B_PARTS
    is_odd = info[1] == 1
    for g in range(groups):
        c_mat = bc[:, 2 * N * g + N : 2 * N * (g + 1)]
        pieces = []
        squares = None
        for p in range(g * per // part, (g + 1) * per // part):
            start = p * part
            side = start // half
            lanes = slice(start - side * half, start - side * half + part)
            mine, other = keep[:, lanes], recv[:, lanes]
            inc = jnp.where(is_odd, other, mine) if side == 0 else jnp.where(is_odd, mine, other)
            gated = us[p][...].astype(F32) + vs[p][...].astype(F32) * dot(c_mat, inc)
            square = jnp.sum(gated * gated, axis=-1, keepdims=True)
            squares = square if squares is None else squares + square
            pieces.append((start, gated))
        scale = lax.rsqrt(squares * (1.0 / per) + EPS)
        for start, gated in pieces:
            out[:, start : start + part] = (gated * scale * gain[:, start : start + part]).astype(BF16)


def norm_rows(info, count, bc, keep, recv, gain, us, vs):
    rows = 128
    steps = count // rows
    width = gain.shape[1]
    take = lambda i, info: (info[0] * steps + i, 0)
    return pl.pallas_call(
        norm_kernel,
        grid_spec=pltpu.PrefetchScalarGridSpec(
            num_scalar_prefetch=1,
            grid=(steps,),
            in_specs=[
                pl.BlockSpec((rows, bc.shape[1]), take),
                whole(keep.shape),
                whole(recv.shape),
                whole(gain.shape),
            ]
            + [pl.BlockSpec((rows, u.shape[1]), take) for u in us + vs],
            out_specs=pl.BlockSpec((rows, width), lambda i, info: (i, 0)),
        ),
        out_shape=jax.ShapeDtypeStruct((count, width), BF16),
        compiler_params=params(),
        cost_estimate=pl.CostEstimate(
            flops=count * width * 256, bytes_accessed=count * width * 6, transcendentals=0
        ),
        name="norm_rows",
    )(info, bc, keep, recv, gain, *us, *vs)


def project_kernel(a0, a1, w0, w1, out):
    out[...] = (dot(a0[...], w0[...]) + dot(a1[...], w1[...])).astype(out.dtype)


def project(a0, a1, w0, w1, first, count, kind):
    rows, depth = a0.shape
    tile = min(512, count)
    base = first // tile
    return pl.pallas_call(
        project_kernel,
        grid=(count // tile,),
        in_specs=[
            whole(a0.shape),
            whole(a1.shape),
            pl.BlockSpec((depth, tile), lambda j: (0, base + j)),
            pl.BlockSpec((depth, tile), lambda j: (0, base + j)),
        ],
        out_specs=pl.BlockSpec((rows, tile), lambda j: (0, j)),
        out_shape=jax.ShapeDtypeStruct((rows, count), kind),
        compiler_params=params(),
        cost_estimate=pl.CostEstimate(
            flops=4 * rows * depth * count, bytes_accessed=4 * depth * count, transcendentals=0
        ),
        name="project",
    )(a0, a1, w0, w1)


def shift(block, distance):
    size = lax.axis_size("seq")
    return lax.ppermute(block, "seq", [(i, i + distance) for i in range(size - distance)])


def swap(block, axis, bit):
    return lax.ppermute(block, axis, [(i, i ^ bit) for i in range(lax.axis_size(axis))])


def after(value, *others):
    return lax.optimization_barrier((value,) + others)[0]


def local(
    x_input,
    z_input,
    bc_input,
    conv_weight_x,
    conv_weight_bc,
    step_size,
    log_decay,
    skip_gain,
    norm_gain,
    out_weight,
):
    length, width = x_input.shape
    heads = step_size.shape[1]
    seq = lax.axis_size("seq")
    ways = lax.axis_size("head")
    me = lax.axis_index("seq")
    mine = lax.axis_index("head")
    half = width // 2
    odd = me % 2
    is_odd = odd == 1

    bc = bc_input.reshape(length, -1)
    halo = shift(jnp.concatenate([x_input[length - LEAD :], bc[length - LEAD :]], 1), 1)
    weight_mate = swap(out_weight, "head", 1)

    ones = jnp.asarray(np.tile(np.repeat(np.eye(heads), P_SIZE, axis=1), (2, 1)), BF16)
    cum, cum_t, f_dev, st, f_blk, e_blk, e_dev, blk_x, dev_total = decays(log_decay, step_size, ones)
    x_conv, bc_conv, keep, send = conv_states(
        odd.reshape(1).astype(jnp.int32),
        x_input,
        bc,
        halo,
        conv_weight_x,
        conv_weight_bc.reshape(KCONV, -1),
        f_dev,
        ones,
    )

    logs = lax.all_gather(dev_total[0], "seq")
    side = jnp.where(is_odd, logs[:, heads // 2 :], logs[:, : heads // 2])
    spread = lambda v: jnp.repeat(jnp.exp2(v), P_SIZE)[None, :]
    pair = me // 2
    even_log = lax.dynamic_index_in_dim(side, 2 * pair, 0, keepdims=False)
    odd_log = lax.dynamic_index_in_dim(side, 2 * pair + 1, 0, keepdims=False)
    index = jnp.arange(seq)[:, None] // 2

    def window(count):
        inside = (index >= pair - count) & (index < pair)
        return spread(jnp.sum(jnp.where(inside, side, 0.0), axis=0))

    skip = jnp.repeat(skip_gain, P_SIZE)[None, :]
    us, vs = [], []

    def scan_next(x):
        k = len(us)
        u, v = scan_part(k, x, bc_conv, z_input, cum, cum_t, st, f_blk, e_blk, e_dev, blk_x, skip, ones)
        us.append(u)
        vs.append(v)

    got = swap(send, "seq", 1)
    scan_next(x_conv)
    received = got.astype(F32)
    first = jnp.where(is_odd, received, keep)
    second = jnp.where(is_odd, keep, received)
    own = spread(odd_log) * first + second
    behind = jnp.zeros_like(own)
    covered = 0
    pairs = seq // 2
    while covered < pairs - 1:
        if covered == 0:
            wave = own
        else:
            wave = own + spread(even_log + odd_log) * behind
        arrived = shift(wave.astype(BF16), 2 * (covered + 1))
        if len(us) < B_PARTS - 1:
            scan_next(after(x_conv, got))
        got = arrived
        behind = behind + window(covered) * arrived.astype(F32)
        covered = 2 * covered + 1
    entering_odd = spread(even_log) * behind + first
    back = swap(jnp.where(is_odd, behind, entering_odd).astype(BF16), "seq", 1)
    while len(us) < B_PARTS:
        scan_next(after(x_conv, got))
    held = jnp.where(is_odd, entering_odd, behind).astype(BF16)

    count = length // ways
    gain = norm_gain[None, :]

    def rows_for(target):
        info = jnp.stack([target, odd]).astype(jnp.int32)
        return norm_rows(info, count, bc_conv, held, back, gain, us, vs)

    far_mate = swap(rows_for(mine ^ 3), "head", 1)
    far = rows_for(mine ^ 2)
    columns = out_weight.shape[1]
    chunk = columns // 4
    arrivals = []
    for c in range(0, columns, chunk):
        sent = project(far, far_mate, out_weight, weight_mate, c, chunk, BF16)
        arrivals.append(swap(sent, "head", 2))
    near_mate = swap(rows_for(mine ^ 1), "head", 1)
    near = rows_for(mine)
    total = project(near, near_mate, out_weight, weight_mate, 0, columns, F32)
    return (total + jnp.concatenate(arrivals, 1).astype(F32)).astype(BF16)


def solution(mesh):
    in_specs = (
        P("seq", "head"),
        P("seq", "head"),
        P("seq", "head", None),
        P(None, "head"),
        P(None, "head", None),
        P("seq", "head"),
        P("seq", "head"),
        P("head"),
        P("head"),
        P("head", None),
    )
    out_specs = P(("seq", "head"), None)
    return jax.shard_map(local, mesh=mesh, in_specs=in_specs, out_specs=out_specs, check_vma=False)
```

```python
import functools

import jax
import jax.numpy as jnp
import numpy as np
from jax import lax
from jax.experimental import pallas as pl
from jax.experimental.pallas import tpu as pltpu
from jax.sharding import PartitionSpec as P

P_SIZE = 64
N = 128
KCONV = 4
EPS = 1e-05
LOG2E = 1.4426950408889634

TOK_A = 256
ROWS_A = 32
TOK_B = 128
STEP_B = 512
EXTRA = 16
SLAB = 256
LEAD = 16
B_PARTS = 4
MIB = 1024 * 1024
HIGHEST = lax.Precision.HIGHEST
F32 = jnp.float32
BF16 = jnp.bfloat16


def params(mib):
    return pltpu.CompilerParams(vmem_limit_bytes=mib * MIB)


def dot(a, b, dims=((1,), (0,)), precision=None):
    return lax.dot_general(a, b, (dims, ((), ())), precision=precision, preferred_element_type=F32)


def half_silu(half):
    return half + half * jnp.tanh(half)


def whole(shape):
    return pl.BlockSpec(shape, lambda *_: (0,) * len(shape))


def decay_kernel(ld_t, step_t, ones, cum, cum_s, log_s, f_dev, f_blk, e_blk, rates):
    heads, length = ld_t.shape
    blocks = length // TOK_B
    row = lax.broadcasted_iota(jnp.int32, (TOK_B, TOK_B), 0)
    col = lax.broadcasted_iota(jnp.int32, (TOK_B, TOK_B), 1)
    lower = (row >= col).astype(F32)
    upper = (row <= col).astype(F32)
    eye = (row == col).astype(BF16)

    def put(ref, rows, value):
        high = value.astype(BF16)
        low = (value - high.astype(F32)).astype(BF16)
        ref[rows, :] = dot(eye, jnp.concatenate([high, low], 0), ((1,), (1,))).astype(BF16)

    cums, totals, row_totals = [], [], []
    for b in range(blocks):
        rows = slice(b * TOK_B, (b + 1) * TOK_B)
        logs = ld_t[:, rows] * LOG2E
        c = dot(lower, logs, ((1,), (1,)), HIGHEST)
        cum[rows, :] = c
        row_totals.append(c[TOK_B - 1 : TOK_B, :])
        c = dot(logs, upper, precision=HIGHEST)
        cums.append(c)
        totals.append(c[:, TOK_B - 1 : TOK_B])
    before, row_before = [jnp.zeros_like(totals[0])], [jnp.zeros_like(row_totals[0])]
    for b in range(blocks):
        before.append(before[-1] + totals[b])
        row_before.append(row_before[-1] + row_totals[b])
    total = before[-1]
    logs = jnp.concatenate(row_totals + row_before[:-1] + row_before[-1:] * 8, 0)
    rates[...] = dot(jnp.exp2(logs), ones[0:heads, :].astype(F32), precision=HIGHEST)
    for b in range(blocks):
        rows = slice(b * TOK_B, (b + 1) * TOK_B)
        s = step_t[:, rows]
        log_step = jnp.log2(s)
        log_s[:, rows] = log_step
        cum_s[:, rows] = cums[b] - log_step
        put(f_dev, rows, jnp.exp2(total - (cums[b] + before[b])) * s)
        put(f_blk, rows, jnp.exp2(totals[b] - cums[b]) * s)
        put(e_blk, rows, jnp.exp2(cums[b]))


def decays(log_decay, step, ones):
    length, heads = log_decay.shape
    blocks = length // TOK_B
    width = ones.shape[1]
    wide = jax.ShapeDtypeStruct((heads, length), F32)
    pair = jax.ShapeDtypeStruct((length, 2 * heads), BF16)
    return pl.pallas_call(
        decay_kernel,
        out_shape=(
            jax.ShapeDtypeStruct((length, heads), F32),
            wide,
            wide,
            pair,
            pair,
            pair,
            jax.ShapeDtypeStruct((2 * blocks + 8, width), F32),
        ),
        compiler_params=params(16),
        name="decays",
    )(log_decay.T, step.T, ones)


def put_message(ref, state, decay):
    high = decay.astype(BF16)
    low = (decay - high.astype(F32)).astype(BF16)
    rest = jnp.zeros((EXTRA - 2, state.shape[1]), BF16)
    ref[0:N, :] = state.astype(BF16)
    ref[N:, :] = jnp.concatenate([high, low, rest], 0)


def take_message(ref):
    extra = ref[N:, :].astype(F32)
    return ref[0:N, :].astype(F32), extra[0:1] + extra[1:2]


def conv_kernel(odd, x, x_lead, bc, bc_lead, halo, wx, wbc, f_dev, ones, rates, x_out, bc_out, keep, send, xf, state):
    i = pl.program_id(0)
    rows, width = x.shape
    bc_width = bc.shape[1]
    groups = bc_width // (2 * N)
    per = width // groups
    half = width // 2

    @pl.when(i == 0)
    def _():
        state[...] = jnp.zeros_like(state)

    def conv(src, lead, weights, emit):
        w0, w1, w2, w3 = [w * 0.5 for w in weights]
        back = LEAD - 8
        r1 = pltpu.roll(lead, 1, 0)
        last_x, last_p = lead[back:], (w1 * lead + w0 * r1)[back:]
        for r in range(0, rows, ROWS_A):
            cur = src(r).astype(F32)
            r1 = pltpu.roll(jnp.concatenate([last_x, cur], 0), 1, 0)[8:]
            p = w1 * cur + w0 * r1
            p2 = pltpu.roll(jnp.concatenate([last_p, p], 0), 2, 0)[8:]
            emit(r, half_silu((w3 * cur + w2 * r1) + p2))
            last_x, last_p = cur[ROWS_A - 8 :], p[ROWS_A - 8 :]

    start = i == 0
    for c in range(groups):
        for lanes in range(c * 2 * N, (c + 1) * 2 * N, N):
            ds = slice(lanes, lanes + N)

            def emit_bc(r, value):
                bc_out[r : r + ROWS_A, ds] = value.astype(BF16)

            lead = jnp.where(start, halo[:, width + lanes : width + lanes + N], bc_lead[:, ds]).astype(F32)
            inner = slice(lanes - c * 2 * N, lanes - c * 2 * N + N)
            conv(lambda r: bc[r : r + ROWS_A, ds], lead, [wbc[k, c : c + 1, inner] for k in range(KCONV)], emit_bc)

    def slab(c, _):
        ds = pl.ds(pl.multiple_of(c * SLAB, SLAB), SLAB)
        scale = dot(f_dev[...], ones[:, ds])

        def emit(r, value):
            value = value.astype(BF16)
            x_out[r : r + ROWS_A, ds] = value
            xf[r : r + ROWS_A, ds] = (value.astype(F32) * scale[r : r + ROWS_A]).astype(BF16)

        lead = jnp.where(start, halo[:, ds], x_lead[:, ds]).astype(F32)
        conv(lambda r: x[r : r + ROWS_A, ds], lead, [wx[k : k + 1, ds] for k in range(KCONV)], emit)
        return 0

    lax.fori_loop(0, width // SLAB, slab, 0)
    for g in range(groups):
        b_mat = bc_out[:, 2 * N * g : 2 * N * g + N]
        lanes = slice(g * per, (g + 1) * per)
        state[:, lanes] += dot(b_mat, xf[:, lanes], ((0,), (0,)))

    @pl.when(i == pl.num_programs(0) - 1)
    def _():
        is_odd = odd[0] == 1
        low, high = state[:, 0:half], state[:, half:]
        keep[...] = jnp.where(is_odd, high, low)
        row = rates.shape[0] - 1
        decay = jnp.where(is_odd, rates[row : row + 1, 0:half], rates[row : row + 1, half:])
        put_message(send, jnp.where(is_odd, low, high), decay)


def conv_states(odd, x, bc, halo, wx, wbc, f_dev, ones, rates):
    length, width = x.shape
    bc_width = bc.shape[1]
    half = width // 2
    lead = lambda i, _: (jnp.maximum(i * (TOK_A // LEAD) - 1, 0), 0)
    block = lambda i, _: (i, 0)
    return pl.pallas_call(
        conv_kernel,
        grid_spec=pltpu.PrefetchScalarGridSpec(
            num_scalar_prefetch=1,
            grid=(length // TOK_A,),
            in_specs=[
                pl.BlockSpec((TOK_A, width), block),
                pl.BlockSpec((LEAD, width), lead),
                pl.BlockSpec((TOK_A, bc_width), block),
                pl.BlockSpec((LEAD, bc_width), lead),
                whole(halo.shape),
                whole(wx.shape),
                whole(wbc.shape),
                pl.BlockSpec((TOK_A, f_dev.shape[1]), block),
                whole(ones.shape),
                whole(rates.shape),
            ],
            out_specs=[
                pl.BlockSpec((TOK_A, width), block),
                pl.BlockSpec((TOK_A, bc_width), block),
                whole((N, half)),
                whole((N + EXTRA, half)),
            ],
            scratch_shapes=[
                pltpu.VMEM((TOK_A, width), BF16),
                pltpu.VMEM((N, width), F32),
            ],
        ),
        out_shape=(
            jax.ShapeDtypeStruct((length, width), BF16),
            jax.ShapeDtypeStruct((length, bc_width), BF16),
            jax.ShapeDtypeStruct((N, half), F32),
            jax.ShapeDtypeStruct((N + EXTRA, half), BF16),
        ),
        compiler_params=params(20),
        name="conv_states",
    )(odd, x, x, bc, bc, halo, wx, wbc, f_dev, ones, rates)


def pair_kernel(odd, got, keep, rates, _, msg, own, first, aux):
    half = keep.shape[1]
    is_odd = odd[0] == 1
    arrived, their = take_message(got)
    row = rates.shape[0] - 1
    mine = jnp.where(is_odd, rates[row : row + 1, half:], rates[row : row + 1, 0:half])
    early = jnp.where(is_odd, arrived, keep[...])
    late = jnp.where(is_odd, keep[...], arrived)
    even_decay = jnp.where(is_odd, their, mine)
    odd_decay = jnp.where(is_odd, mine, their)
    state = odd_decay * early + late
    own[...] = state
    first[...] = early
    aux[0:8, :] = jnp.broadcast_to(even_decay, (8, half))
    aux[8:16, :] = jnp.broadcast_to(even_decay * odd_decay, (8, half))
    put_message(msg, state, even_decay * odd_decay)


def wave_kernel(got, own, aux, behind_in, _, msg, behind):
    before, decay = take_message(got)
    if behind_in is not None:
        before_decay = behind_in[N : N + 1, :]
        before = behind_in[0:N, :] + before_decay * before
        decay = before_decay * decay
    pair_decay = aux[8:9, :]
    behind[0:N, :] = before
    behind[N:, :] = jnp.broadcast_to(decay, (8, before.shape[1]))
    put_message(msg, own[...] + pair_decay * before, pair_decay * decay)


def last_kernel(odd, got, behind_in, first, aux, _, back, held):
    is_odd = odd[0] == 1
    before, _unused = take_message(got)
    if behind_in is not None:
        before = behind_in[0:N, :] + behind_in[N : N + 1, :] * before
    entering_odd = aux[0:1, :] * before + first[...]
    back[...] = jnp.where(is_odd, before, entering_odd).astype(BF16)
    held[...] = jnp.where(is_odd, entering_odd, before).astype(BF16)


SCALAR = pl.BlockSpec(memory_space=pltpu.SMEM)
FULL = pl.BlockSpec(memory_space=pltpu.VMEM)
ANY = pl.BlockSpec(memory_space=pl.ANY)


def combine(kernel, operands, specs, outs, name):
    return pl.pallas_call(
        kernel,
        in_specs=specs,
        out_specs=[FULL] * len(outs),
        out_shape=[jax.ShapeDtypeStruct(s, t) for s, t in outs],
        compiler_params=params(12),
        name=name,
    )(*operands)


def scan_kernel(head0, x, bc, z, cum, cum_s, log_s, f_blk, e_blk, rates, skip, ones, _, uv_out, state):
    i = pl.program_id(0)
    rows, width = x.shape
    per_slab = SLAB // P_SIZE
    inner = rows // TOK_B
    blocks = (rates.shape[0] - 8) // 2

    @pl.when(i == 0)
    def _():
        state[...] = jnp.zeros_like(state)

    row = lax.broadcasted_iota(jnp.int32, (TOK_B, TOK_B), 0)
    col = lax.broadcasted_iota(jnp.int32, (TOK_B, TOK_B), 1)
    keep = row >= col
    first = lax.broadcasted_iota(jnp.int32, (TOK_B, 2 * P_SIZE), 1) < P_SIZE
    zero = jnp.zeros((TOK_B, 2 * P_SIZE), BF16)

    def block(b, _):
        at = pl.ds(pl.multiple_of(b * TOK_B, TOK_B), TOK_B)
        b_mat = bc[at, 0:N]
        c_mat = bc[at, N : 2 * N]
        scores = jnp.where(keep, dot(c_mat, b_mat, ((1,), (1,))), 0.0)
        fade_rows = rates[pl.ds(i * inner + b, 1), :]
        lead_rows = rates[pl.ds(blocks + i * inner + b, 1), :]
        for s in range(width // SLAB):
            lanes = slice(s * SLAB, (s + 1) * SLAB)
            xb = x[at, lanes]
            sel = ones[:, lanes]
            old = state[:, lanes]
            rise = dot(e_blk[at, :], sel)
            carried = dot(c_mat, old.astype(BF16)) * rise
            within = []
            for q in range(per_slab // 2):
                tables = []
                for h in (2 * q, 2 * q + 1):
                    head = head0 + s * per_slab + h
                    column = cum[at, head : head + 1]
                    gap = jnp.minimum(column - cum_s[head : head + 1, at], log_s[head : head + 1, at])
                    tables.append((scores * jnp.exp2(gap)).astype(BF16))
                xp = xb[:, q * 2 * P_SIZE : (q + 1) * 2 * P_SIZE]
                stacked = jnp.concatenate([jnp.where(first, xp, zero), jnp.where(first, zero, xp)], 0)
                within.append(dot(jnp.concatenate(tables, 1), stacked))
            xs = xb.astype(F32)
            y = jnp.concatenate(within, 1) + carried + skip[:, lanes] * xs
            gate = half_silu((z[at, lanes] * 0.5).astype(F32))
            uv_out[at, lanes] = (y * gate).astype(BF16)
            uv_out[at, width + s * SLAB : width + (s + 1) * SLAB] = (gate * rise * lead_rows[:, lanes]).astype(BF16)
            xf = (xs * dot(f_blk[at, :], sel)).astype(BF16)
            state[:, lanes] = old * fade_rows[:, lanes] + dot(b_mat, xf, ((0,), (0,)))
        return 0

    lax.fori_loop(0, inner, block, 0)


def scan_part(part, token, x, bc, z, cum, cum_s, log_s, f_blk, e_blk, rates, skip, ones):
    length, full = x.shape
    width = full // B_PARTS
    groups = bc.shape[1] // (2 * N)
    group = part * groups // B_PARTS
    heads = cum.shape[1]
    cols = lambda i: (i, part)
    narrow = pl.BlockSpec((STEP_B, 2 * heads), lambda i: (i, 0))
    across = pl.BlockSpec((heads, STEP_B), lambda i: (0, i))
    return pl.pallas_call(
        functools.partial(scan_kernel, part * heads // B_PARTS),
        grid=(length // STEP_B,),
        in_specs=[
            pl.BlockSpec((STEP_B, width), cols),
            pl.BlockSpec((STEP_B, 2 * N), lambda i: (i, group)),
            pl.BlockSpec((STEP_B, width), cols),
            pl.BlockSpec((STEP_B, heads), lambda i: (i, 0)),
            across,
            across,
            narrow,
            narrow,
            pl.BlockSpec((rates.shape[0], width), lambda i: (0, part)),
            pl.BlockSpec((1, width), lambda i: (0, part)),
            pl.BlockSpec((2 * heads, width), lambda i: (0, part)),
            ANY,
        ],
        out_specs=pl.BlockSpec((STEP_B, 2 * width), lambda i: (i, 0)),
        out_shape=jax.ShapeDtypeStruct((length, 2 * width), BF16),
        scratch_shapes=[pltpu.VMEM((N, width), F32)],
        compiler_params=params(16),
        cost_estimate=pl.CostEstimate(
            flops=length * width * 4000, bytes_accessed=length * width * 10, transcendentals=length * width * 4
        ),
        name="scan_part",
    )(x, bc, z, cum, cum_s, log_s, f_blk, e_blk, rates, skip, ones, token)


def norm_kernel(info, bc, keep, recv, gain, _, *refs):
    uvs, out = refs[:-1], refs[-1]
    width = out.shape[1]
    groups = bc.shape[1] // (2 * N)
    per = width // groups
    half = width // 2
    part = width // B_PARTS
    is_odd = info[1] == 1
    for g in range(groups):
        c_mat = bc[:, 2 * N * g + N : 2 * N * (g + 1)]
        pieces = []
        squares = None
        for p in range(g * per // part, (g + 1) * per // part):
            start = p * part
            side = start // half
            lanes = slice(start - side * half, start - side * half + part)
            mine, other = keep[:, lanes], recv[:, lanes]
            inc = jnp.where(is_odd, other, mine) if side == 0 else jnp.where(is_odd, mine, other)
            gated = uvs[p][:, 0:part].astype(F32) + uvs[p][:, part:].astype(F32) * dot(c_mat, inc)
            square = jnp.sum(gated * gated, axis=-1, keepdims=True)
            squares = square if squares is None else squares + square
            pieces.append((start, gated))
        scale = lax.rsqrt(squares * (1.0 / per) + EPS)
        for start, gated in pieces:
            out[:, start : start + part] = (gated * scale * gain[:, start : start + part]).astype(BF16)


def norm_rows(info, count, token, bc, keep, recv, gain, uvs):
    rows = 128
    steps = count // rows
    width = gain.shape[1]
    take = lambda i, info: (info[0] * steps + i, 0)
    return pl.pallas_call(
        norm_kernel,
        grid_spec=pltpu.PrefetchScalarGridSpec(
            num_scalar_prefetch=1,
            grid=(steps,),
            in_specs=[
                pl.BlockSpec((rows, bc.shape[1]), take),
                whole(keep.shape),
                whole(recv.shape),
                whole(gain.shape),
                ANY,
            ]
            + [pl.BlockSpec((rows, uv.shape[1]), take) for uv in uvs],
            out_specs=pl.BlockSpec((rows, width), lambda i, info: (i, 0)),
        ),
        out_shape=jax.ShapeDtypeStruct((count, width), BF16),
        compiler_params=params(16),
        cost_estimate=pl.CostEstimate(
            flops=count * width * 256, bytes_accessed=count * width * 6, transcendentals=0
        ),
        name="norm_rows",
    )(info, bc, keep, recv, gain, token, *uvs)


def project_kernel(a0, a1, w0, w1, out):
    out[...] = (dot(a0[...], w0[...]) + dot(a1[...], w1[...])).astype(out.dtype)


def project(a0, a1, w0, w1, first, count, kind):
    rows, depth = a0.shape
    tile = min(512, count)
    base = first // tile
    return pl.pallas_call(
        project_kernel,
        grid=(count // tile,),
        in_specs=[
            whole(a0.shape),
            whole(a1.shape),
            pl.BlockSpec((depth, tile), lambda j: (0, base + j)),
            pl.BlockSpec((depth, tile), lambda j: (0, base + j)),
        ],
        out_specs=pl.BlockSpec((rows, tile), lambda j: (0, j)),
        out_shape=jax.ShapeDtypeStruct((rows, count), kind),
        compiler_params=params(24),
        cost_estimate=pl.CostEstimate(
            flops=4 * rows * depth * count, bytes_accessed=4 * depth * count, transcendentals=0
        ),
        name="project",
    )(a0, a1, w0, w1)


def add_kernel(part, arrived, *refs):
    refs[-1][...] = (part[...] + arrived[...].astype(F32)).astype(BF16)


def add_chunk(total, arrived, out, first):
    rows, count = arrived.shape
    tile = min(512, count)
    base = first // tile
    placed = pl.BlockSpec((rows, tile), lambda j: (0, base + j))
    return pl.pallas_call(
        add_kernel,
        grid=(count // tile,),
        in_specs=[placed, pl.BlockSpec((rows, tile), lambda j: (0, j))] + ([] if out is None else [ANY]),
        out_specs=placed,
        out_shape=jax.ShapeDtypeStruct(total.shape, BF16),
        input_output_aliases={} if out is None else {2: 0},
        compiler_params=params(8),
        name="add_chunk",
    )(*((total, arrived) if out is None else (total, arrived, out)))


def shift(block, distance):
    size = lax.axis_size("seq")
    return lax.ppermute(block, "seq", [(i, i + distance) for i in range(size - distance)])


def swap(block, axis, bit):
    return lax.ppermute(block, axis, [(i, i ^ bit) for i in range(lax.axis_size(axis))])


def local(
    x_input,
    z_input,
    bc_input,
    conv_weight_x,
    conv_weight_bc,
    step_size,
    log_decay,
    skip_gain,
    norm_gain,
    out_weight,
):
    length, width = x_input.shape
    heads = step_size.shape[1]
    ways = lax.axis_size("head")
    pairs = lax.axis_size("seq") // 2
    mine = lax.axis_index("head")
    half = width // 2
    odd = (lax.axis_index("seq") & 1).reshape(1).astype(jnp.int32)

    bc = bc_input.reshape(length, -1)
    halo = shift(jnp.concatenate([x_input[length - LEAD :], bc[length - LEAD :]], 1), 1)
    weight_mate = swap(out_weight, "head", 1)

    ones = jnp.asarray(np.tile(np.repeat(np.eye(heads), P_SIZE, axis=1), (2, 1)), BF16)
    cum, cum_s, log_s, f_dev, f_blk, e_blk, rates = decays(log_decay, step_size, ones)
    x_conv, bc_conv, keep, send = conv_states(
        odd, x_input, bc, halo, conv_weight_x, conv_weight_bc, f_dev, ones, rates
    )

    skip = jnp.repeat(skip_gain, P_SIZE)[None, :]
    uvs = []

    def scan_next(token):
        if len(uvs) < B_PARTS:
            uvs.append(
                scan_part(len(uvs), token, x_conv, bc_conv, z_input, cum, cum_s, log_s, f_blk, e_blk, rates, skip, ones)
            )
        return uvs[-1]

    message = ((N + EXTRA, half), BF16)
    full = ((N, half), F32)
    got = swap(send, "seq", 1)
    done = scan_next(send)
    msg, own, first, aux = combine(
        pair_kernel,
        (odd, got, keep, rates, done),
        [SCALAR, FULL, FULL, FULL, ANY],
        [message, full, full, ((16, half), F32)],
        "pair",
    )
    behind = None
    covered = 0
    while True:
        got = shift(msg, 2 * (covered + 1))
        done = scan_next(msg)
        covered = 2 * covered + 1
        if covered >= pairs - 1:
            break
        operands, specs = [got, own, aux], [FULL, FULL, FULL]
        if behind is None:
            kernel = lambda g, o, a, t, m, b: wave_kernel(g, o, a, None, t, m, b)
        else:
            kernel = wave_kernel
            operands.append(behind)
            specs.append(FULL)
        msg, behind = combine(kernel, operands + [done], specs + [ANY], [message, ((N + 8, half), F32)], "wave")
    operands, specs = [odd, got], [SCALAR, FULL]
    if behind is None:
        kernel = lambda o, g, f, a, t, b, h: last_kernel(o, g, None, f, a, t, b, h)
    else:
        kernel = last_kernel
        operands.append(behind)
        specs.append(FULL)
    out = ((N, half), BF16)
    back, held = combine(kernel, operands + [first, aux, done], specs + [FULL, FULL, ANY], [out, out], "last")
    other = swap(back, "seq", 1)
    while len(uvs) < B_PARTS:
        scan_next(back)

    count = length // ways
    gain = norm_gain[None, :]

    def rows_for(target, token):
        info = jnp.concatenate([target.reshape(1).astype(jnp.int32), odd])
        return norm_rows(info, count, token, bc_conv, held, other, gain, uvs)

    far_mate = rows_for(mine ^ 3, held)
    far = rows_for(mine ^ 2, far_mate)
    far_mate = swap(far_mate, "head", 1)
    columns = out_weight.shape[1]
    eighth = columns // 8
    cuts = [0, eighth, 3 * eighth, 5 * eighth, 7 * eighth, columns]
    arrivals = []
    for lo, hi in zip(cuts[:-1], cuts[1:]):
        sent = project(far, far_mate, out_weight, weight_mate, lo, hi - lo, BF16)
        arrivals.append(swap(sent, "head", 2))
    near_mate = rows_for(mine ^ 1, sent)
    near = rows_for(mine, near_mate)
    near_mate = swap(near_mate, "head", 1)
    total = project(near, near_mate, out_weight, weight_mate, 0, columns, F32)
    result = None
    for arrived, lo in zip(arrivals, cuts):
        result = add_chunk(total, arrived, result, lo)
    return result


def solution(mesh):
    in_specs = (
        P("seq", "head"),
        P("seq", "head"),
        P("seq", "head", None),
        P(None, "head"),
        P(None, "head", None),
        P("seq", "head"),
        P("seq", "head"),
        P("head"),
        P("head"),
        P("head", None),
    )
    out_specs = P(("seq", "head"), None)
    return jax.shard_map(local, mesh=mesh, in_specs=in_specs, out_specs=out_specs, check_vma=False)
```

```python
import functools

import jax
import jax.numpy as jnp
import numpy as np
from jax import lax
from jax.experimental import pallas as pl
from jax.experimental.pallas import tpu as pltpu
from jax.sharding import PartitionSpec as P

P_SIZE = 64
N = 128
KCONV = 4
EPS = 1e-05
LOG2E = 1.4426950408889634

TOK_A = 256
ROWS_A = 32
TOK_B = 128
STEP_B = 512
EXTRA = 16
SLAB = 256
LEAD = 16
B_PARTS = 4
HIGHEST = lax.Precision.HIGHEST
F32 = jnp.float32
BF16 = jnp.bfloat16


PARAMS = pltpu.CompilerParams(vmem_limit_bytes=64 * 1024 * 1024)


def dot(a, b, dims=((1,), (0,)), precision=None):
    return lax.dot_general(a, b, (dims, ((), ())), precision=precision, preferred_element_type=F32)


def half_silu(half):
    return half + half * jnp.tanh(half)


def whole(shape):
    return pl.BlockSpec(shape, lambda *_: (0,) * len(shape))


def decay_kernel(ld_t, step_t, ones, cum, cum_s, log_s, f_dev, f_blk, e_blk, rates):
    heads, length = ld_t.shape
    blocks = length // TOK_B
    row = lax.broadcasted_iota(jnp.int32, (TOK_B, TOK_B), 0)
    col = lax.broadcasted_iota(jnp.int32, (TOK_B, TOK_B), 1)
    lower = (row >= col).astype(F32)
    upper = (row <= col).astype(F32)
    eye = (row == col).astype(BF16)

    def put(ref, rows, value):
        high = value.astype(BF16)
        low = (value - high.astype(F32)).astype(BF16)
        ref[rows, :] = dot(eye, jnp.concatenate([high, low], 0), ((1,), (1,))).astype(BF16)

    cums, totals, row_totals = [], [], []
    for b in range(blocks):
        rows = slice(b * TOK_B, (b + 1) * TOK_B)
        logs = ld_t[:, rows] * LOG2E
        c = dot(lower, logs, ((1,), (1,)), HIGHEST)
        cum[rows, :] = c
        row_totals.append(c[TOK_B - 1 : TOK_B, :])
        c = dot(logs, upper, precision=HIGHEST)
        cums.append(c)
        totals.append(c[:, TOK_B - 1 : TOK_B])
    before, row_before = [jnp.zeros_like(totals[0])], [jnp.zeros_like(row_totals[0])]
    for b in range(blocks):
        before.append(before[-1] + totals[b])
        row_before.append(row_before[-1] + row_totals[b])
    total = before[-1]
    logs = jnp.concatenate(row_totals + row_before[:-1] + row_before[-1:] * 8, 0)
    rates[...] = dot(jnp.exp2(logs), ones[0:heads, :].astype(F32), precision=HIGHEST)
    for b in range(blocks):
        rows = slice(b * TOK_B, (b + 1) * TOK_B)
        s = step_t[:, rows]
        log_step = jnp.log2(s)
        log_s[:, rows] = log_step
        cum_s[:, rows] = cums[b] - log_step
        put(f_dev, rows, jnp.exp2(total - (cums[b] + before[b])) * s)
        put(f_blk, rows, jnp.exp2(totals[b] - cums[b]) * s)
        put(e_blk, rows, jnp.exp2(cums[b]))


def decays(log_decay, step, ones):
    length, heads = log_decay.shape
    blocks = length // TOK_B
    width = ones.shape[1]
    wide = jax.ShapeDtypeStruct((heads, length), F32)
    pair = jax.ShapeDtypeStruct((length, 2 * heads), BF16)
    return pl.pallas_call(
        decay_kernel,
        out_shape=(
            jax.ShapeDtypeStruct((length, heads), F32),
            wide,
            wide,
            pair,
            pair,
            pair,
            jax.ShapeDtypeStruct((2 * blocks + 8, width), F32),
        ),
        compiler_params=PARAMS,
        name="decays",
    )(log_decay.T, step.T, ones)


def put_message(ref, state, decay):
    high = decay.astype(BF16)
    low = (decay - high.astype(F32)).astype(BF16)
    rest = jnp.zeros((EXTRA - 2, state.shape[1]), BF16)
    ref[0:N, :] = state.astype(BF16)
    ref[N:, :] = jnp.concatenate([high, low, rest], 0)


def take_message(ref):
    extra = ref[N:, :].astype(F32)
    return ref[0:N, :].astype(F32), extra[0:1] + extra[1:2]


def conv_kernel(odd, x, x_lead, bc, bc_lead, halo, wx, wbc, f_dev, ones, rates, x_out, bc_out, keep, send, xf, state):
    i = pl.program_id(0)
    rows, width = x.shape
    bc_width = bc.shape[1]
    groups = bc_width // (2 * N)
    per = width // groups
    half = width // 2

    @pl.when(i == 0)
    def _():
        state[...] = jnp.zeros_like(state)

    def conv(src, lead, weights, emit):
        w0, w1, w2, w3 = [w * 0.5 for w in weights]
        back = LEAD - 8
        r1 = pltpu.roll(lead, 1, 0)
        last_x, last_p = lead[back:], (w1 * lead + w0 * r1)[back:]
        for r in range(0, rows, ROWS_A):
            cur = src(r).astype(F32)
            r1 = pltpu.roll(jnp.concatenate([last_x, cur], 0), 1, 0)[8:]
            p = w1 * cur + w0 * r1
            p2 = pltpu.roll(jnp.concatenate([last_p, p], 0), 2, 0)[8:]
            emit(r, half_silu((w3 * cur + w2 * r1) + p2))
            last_x, last_p = cur[ROWS_A - 8 :], p[ROWS_A - 8 :]

    start = i == 0
    for c in range(groups):
        for lanes in range(c * 2 * N, (c + 1) * 2 * N, N):
            ds = slice(lanes, lanes + N)

            def emit_bc(r, value):
                bc_out[r : r + ROWS_A, ds] = value.astype(BF16)

            lead = jnp.where(start, halo[:, width + lanes : width + lanes + N], bc_lead[:, ds]).astype(F32)
            inner = slice(lanes - c * 2 * N, lanes - c * 2 * N + N)
            conv(lambda r: bc[r : r + ROWS_A, ds], lead, [wbc[k, c : c + 1, inner] for k in range(KCONV)], emit_bc)

    def slab(c, _):
        ds = pl.ds(pl.multiple_of(c * SLAB, SLAB), SLAB)
        scale = dot(f_dev[...], ones[:, ds])

        def emit(r, value):
            value = value.astype(BF16)
            x_out[r : r + ROWS_A, ds] = value
            xf[r : r + ROWS_A, ds] = (value.astype(F32) * scale[r : r + ROWS_A]).astype(BF16)

        lead = jnp.where(start, halo[:, ds], x_lead[:, ds]).astype(F32)
        conv(lambda r: x[r : r + ROWS_A, ds], lead, [wx[k : k + 1, ds] for k in range(KCONV)], emit)
        return 0

    lax.fori_loop(0, width // SLAB, slab, 0)
    for g in range(groups):
        b_mat = bc_out[:, 2 * N * g : 2 * N * g + N]
        lanes = slice(g * per, (g + 1) * per)
        state[:, lanes] += dot(b_mat, xf[:, lanes], ((0,), (0,)))

    @pl.when(i == pl.num_programs(0) - 1)
    def _():
        is_odd = odd[0] == 1
        low, high = state[:, 0:half], state[:, half:]
        keep[...] = jnp.where(is_odd, high, low)
        row = rates.shape[0] - 1
        decay = jnp.where(is_odd, rates[row : row + 1, 0:half], rates[row : row + 1, half:])
        put_message(send, jnp.where(is_odd, low, high), decay)


def conv_states(odd, x, bc, halo, wx, wbc, f_dev, ones, rates):
    length, width = x.shape
    bc_width = bc.shape[1]
    half = width // 2
    lead = lambda i, _: (jnp.maximum(i * (TOK_A // LEAD) - 1, 0), 0)
    block = lambda i, _: (i, 0)
    return pl.pallas_call(
        conv_kernel,
        grid_spec=pltpu.PrefetchScalarGridSpec(
            num_scalar_prefetch=1,
            grid=(length // TOK_A,),
            in_specs=[
                pl.BlockSpec((TOK_A, width), block),
                pl.BlockSpec((LEAD, width), lead),
                pl.BlockSpec((TOK_A, bc_width), block),
                pl.BlockSpec((LEAD, bc_width), lead),
                whole(halo.shape),
                whole(wx.shape),
                whole(wbc.shape),
                pl.BlockSpec((TOK_A, f_dev.shape[1]), block),
                whole(ones.shape),
                whole(rates.shape),
            ],
            out_specs=[
                pl.BlockSpec((TOK_A, width), block),
                pl.BlockSpec((TOK_A, bc_width), block),
                whole((N, half)),
                whole((N + EXTRA, half)),
            ],
            scratch_shapes=[
                pltpu.VMEM((TOK_A, width), BF16),
                pltpu.VMEM((N, width), F32),
            ],
        ),
        out_shape=(
            jax.ShapeDtypeStruct((length, width), BF16),
            jax.ShapeDtypeStruct((length, bc_width), BF16),
            jax.ShapeDtypeStruct((N, half), F32),
            jax.ShapeDtypeStruct((N + EXTRA, half), BF16),
        ),
        compiler_params=PARAMS,
        name="conv_states",
    )(odd, x, x, bc, bc, halo, wx, wbc, f_dev, ones, rates)


def pair_kernel(odd, got, keep, rates, _, msg, own, first, aux):
    half = keep.shape[1]
    is_odd = odd[0] == 1
    arrived, their = take_message(got)
    row = rates.shape[0] - 1
    mine = jnp.where(is_odd, rates[row : row + 1, half:], rates[row : row + 1, 0:half])
    early = jnp.where(is_odd, arrived, keep[...])
    late = jnp.where(is_odd, keep[...], arrived)
    even_decay = jnp.where(is_odd, their, mine)
    odd_decay = jnp.where(is_odd, mine, their)
    state = odd_decay * early + late
    own[...] = state
    first[...] = early
    aux[0:8, :] = jnp.broadcast_to(even_decay, (8, half))
    aux[8:16, :] = jnp.broadcast_to(even_decay * odd_decay, (8, half))
    put_message(msg, state, even_decay * odd_decay)


def wave_kernel(got, own, aux, behind_in, _, msg, behind):
    before, decay = take_message(got)
    if behind_in is not None:
        before_decay = behind_in[N : N + 1, :]
        before = behind_in[0:N, :] + before_decay * before
        decay = before_decay * decay
    pair_decay = aux[8:9, :]
    behind[0:N, :] = before
    behind[N:, :] = jnp.broadcast_to(decay, (8, before.shape[1]))
    put_message(msg, own[...] + pair_decay * before, pair_decay * decay)


def last_kernel(odd, got, behind_in, first, aux, _, back, held):
    is_odd = odd[0] == 1
    before, _unused = take_message(got)
    if behind_in is not None:
        before = behind_in[0:N, :] + behind_in[N : N + 1, :] * before
    entering_odd = aux[0:1, :] * before + first[...]
    back[...] = jnp.where(is_odd, before, entering_odd).astype(BF16)
    held[...] = jnp.where(is_odd, entering_odd, before).astype(BF16)


SCALAR = pl.BlockSpec(memory_space=pltpu.SMEM)
FULL = pl.BlockSpec(memory_space=pltpu.VMEM)
ANY = pl.BlockSpec(memory_space=pl.ANY)


def combine(kernel, operands, specs, outs, name):
    return pl.pallas_call(
        kernel,
        in_specs=specs,
        out_specs=[FULL] * len(outs),
        out_shape=[jax.ShapeDtypeStruct(s, t) for s, t in outs],
        compiler_params=PARAMS,
        name=name,
    )(*operands)


def scan_kernel(head0, x, bc, z, cum, cum_s, log_s, f_blk, e_blk, rates, skip, ones, _, uv_out, state):
    i = pl.program_id(0)
    rows, width = x.shape
    per_slab = SLAB // P_SIZE
    inner = rows // TOK_B
    blocks = (rates.shape[0] - 8) // 2

    @pl.when(i == 0)
    def _():
        state[...] = jnp.zeros_like(state)

    row = lax.broadcasted_iota(jnp.int32, (TOK_B, TOK_B), 0)
    col = lax.broadcasted_iota(jnp.int32, (TOK_B, TOK_B), 1)
    keep = row >= col
    first = lax.broadcasted_iota(jnp.int32, (TOK_B, 2 * P_SIZE), 1) < P_SIZE
    zero = jnp.zeros((TOK_B, 2 * P_SIZE), BF16)

    def block(b, _):
        at = pl.ds(pl.multiple_of(b * TOK_B, TOK_B), TOK_B)
        b_mat = bc[at, 0:N]
        c_mat = bc[at, N : 2 * N]
        scores = jnp.where(keep, dot(c_mat, b_mat, ((1,), (1,))), 0.0)
        fade_rows = rates[pl.ds(i * inner + b, 1), :]
        lead_rows = rates[pl.ds(blocks + i * inner + b, 1), :]
        for s in range(width // SLAB):
            lanes = slice(s * SLAB, (s + 1) * SLAB)
            xb = x[at, lanes]
            sel = ones[:, lanes]
            old = state[:, lanes]
            rise = dot(e_blk[at, :], sel)
            carried = dot(c_mat, old.astype(BF16)) * rise
            within = []
            for q in range(per_slab // 2):
                tables = []
                for h in (2 * q, 2 * q + 1):
                    head = head0 + s * per_slab + h
                    column = cum[at, head : head + 1]
                    gap = jnp.minimum(column - cum_s[head : head + 1, at], log_s[head : head + 1, at])
                    tables.append((scores * jnp.exp2(gap)).astype(BF16))
                xp = xb[:, q * 2 * P_SIZE : (q + 1) * 2 * P_SIZE]
                stacked = jnp.concatenate([jnp.where(first, xp, zero), jnp.where(first, zero, xp)], 0)
                within.append(dot(jnp.concatenate(tables, 1), stacked))
            xs = xb.astype(F32)
            y = jnp.concatenate(within, 1) + carried + skip[:, lanes] * xs
            gate = half_silu((z[at, lanes] * 0.5).astype(F32))
            uv_out[at, lanes] = (y * gate).astype(BF16)
            uv_out[at, width + s * SLAB : width + (s + 1) * SLAB] = (gate * rise * lead_rows[:, lanes]).astype(BF16)
            xf = (xs * dot(f_blk[at, :], sel)).astype(BF16)
            state[:, lanes] = old * fade_rows[:, lanes] + dot(b_mat, xf, ((0,), (0,)))
        return 0

    lax.fori_loop(0, inner, block, 0)


def scan_part(part, token, x, bc, z, cum, cum_s, log_s, f_blk, e_blk, rates, skip, ones):
    length, full = x.shape
    width = full // B_PARTS
    groups = bc.shape[1] // (2 * N)
    group = part * groups // B_PARTS
    heads = cum.shape[1]
    cols = lambda i: (i, part)
    narrow = pl.BlockSpec((STEP_B, 2 * heads), lambda i: (i, 0))
    across = pl.BlockSpec((heads, STEP_B), lambda i: (0, i))
    return pl.pallas_call(
        functools.partial(scan_kernel, part * heads // B_PARTS),
        grid=(length // STEP_B,),
        in_specs=[
            pl.BlockSpec((STEP_B, width), cols),
            pl.BlockSpec((STEP_B, 2 * N), lambda i: (i, group)),
            pl.BlockSpec((STEP_B, width), cols),
            pl.BlockSpec((STEP_B, heads), lambda i: (i, 0)),
            across,
            across,
            narrow,
            narrow,
            pl.BlockSpec((rates.shape[0], width), lambda i: (0, part)),
            pl.BlockSpec((1, width), lambda i: (0, part)),
            pl.BlockSpec((2 * heads, width), lambda i: (0, part)),
            ANY,
        ],
        out_specs=pl.BlockSpec((STEP_B, 2 * width), lambda i: (i, 0)),
        out_shape=jax.ShapeDtypeStruct((length, 2 * width), BF16),
        scratch_shapes=[pltpu.VMEM((N, width), F32)],
        compiler_params=PARAMS,
        cost_estimate=pl.CostEstimate(
            flops=length * width * 4000, bytes_accessed=length * width * 10, transcendentals=length * width * 4
        ),
        name="scan_part",
    )(x, bc, z, cum, cum_s, log_s, f_blk, e_blk, rates, skip, ones, token)


def norm_kernel(info, bc, keep, recv, gain, _, *refs):
    uvs, out = refs[:-1], refs[-1]
    width = out.shape[1]
    groups = bc.shape[1] // (2 * N)
    per = width // groups
    half = width // 2
    part = width // B_PARTS
    is_odd = info[1] == 1
    for g in range(groups):
        c_mat = bc[:, 2 * N * g + N : 2 * N * (g + 1)]
        pieces = []
        squares = None
        for p in range(g * per // part, (g + 1) * per // part):
            start = p * part
            side = start // half
            lanes = slice(start - side * half, start - side * half + part)
            mine, other = keep[:, lanes], recv[:, lanes]
            inc = jnp.where(is_odd, other, mine) if side == 0 else jnp.where(is_odd, mine, other)
            gated = uvs[p][:, 0:part].astype(F32) + uvs[p][:, part:].astype(F32) * dot(c_mat, inc)
            square = jnp.sum(gated * gated, axis=-1, keepdims=True)
            squares = square if squares is None else squares + square
            pieces.append((start, gated))
        scale = lax.rsqrt(squares * (1.0 / per) + EPS)
        for start, gated in pieces:
            out[:, start : start + part] = (gated * scale * gain[:, start : start + part]).astype(BF16)


def norm_rows(info, count, token, bc, keep, recv, gain, uvs):
    rows = 128
    steps = count // rows
    width = gain.shape[1]
    take = lambda i, info: (info[0] * steps + i, 0)
    return pl.pallas_call(
        norm_kernel,
        grid_spec=pltpu.PrefetchScalarGridSpec(
            num_scalar_prefetch=1,
            grid=(steps,),
            in_specs=[
                pl.BlockSpec((rows, bc.shape[1]), take),
                whole(keep.shape),
                whole(recv.shape),
                whole(gain.shape),
                ANY,
            ]
            + [pl.BlockSpec((rows, uv.shape[1]), take) for uv in uvs],
            out_specs=pl.BlockSpec((rows, width), lambda i, info: (i, 0)),
        ),
        out_shape=jax.ShapeDtypeStruct((count, width), BF16),
        compiler_params=PARAMS,
        cost_estimate=pl.CostEstimate(
            flops=count * width * 256, bytes_accessed=count * width * 6, transcendentals=0
        ),
        name="norm_rows",
    )(info, bc, keep, recv, gain, token, *uvs)


def project_kernel(a0, a1, w0, w1, _, out):
    out[...] = (dot(a0[...], w0[...]) + dot(a1[...], w1[...])).astype(out.dtype)


def project(token, a0, a1, w0, w1, first, count, kind):
    rows, depth = a0.shape
    tile = min(512, count)
    base = first // tile
    return pl.pallas_call(
        project_kernel,
        grid=(count // tile,),
        in_specs=[
            whole(a0.shape),
            whole(a1.shape),
            pl.BlockSpec((depth, tile), lambda j: (0, base + j)),
            pl.BlockSpec((depth, tile), lambda j: (0, base + j)),
            ANY,
        ],
        out_specs=pl.BlockSpec((rows, tile), lambda j: (0, j)),
        out_shape=jax.ShapeDtypeStruct((rows, count), kind),
        compiler_params=PARAMS,
        cost_estimate=pl.CostEstimate(
            flops=4 * rows * depth * count, bytes_accessed=4 * depth * count, transcendentals=0
        ),
        name="project",
    )(a0, a1, w0, w1, token)


def add_kernel(part, arrived, *refs):
    refs[-1][...] = (part[...] + arrived[...].astype(F32)).astype(BF16)


def add_chunk(total, arrived, out, first):
    rows, count = arrived.shape
    tile = min(512, count)
    base = first // tile
    placed = pl.BlockSpec((rows, tile), lambda j: (0, base + j))
    return pl.pallas_call(
        add_kernel,
        grid=(count // tile,),
        in_specs=[placed, pl.BlockSpec((rows, tile), lambda j: (0, j))] + ([] if out is None else [ANY]),
        out_specs=placed,
        out_shape=jax.ShapeDtypeStruct(total.shape, BF16),
        input_output_aliases={} if out is None else {2: 0},
        compiler_params=PARAMS,
        name="add_chunk",
    )(*((total, arrived) if out is None else (total, arrived, out)))


def shift(block, distance):
    size = lax.axis_size("seq")
    return lax.ppermute(block, "seq", [(i, i + distance) for i in range(size - distance)])


def swap(block, axis, bit):
    return lax.ppermute(block, axis, [(i, i ^ bit) for i in range(lax.axis_size(axis))])


def local(
    x_input,
    z_input,
    bc_input,
    conv_weight_x,
    conv_weight_bc,
    step_size,
    log_decay,
    skip_gain,
    norm_gain,
    out_weight,
):
    length, width = x_input.shape
    heads = step_size.shape[1]
    ways = lax.axis_size("head")
    pairs = lax.axis_size("seq") // 2
    mine = lax.axis_index("head")
    half = width // 2
    odd = (lax.axis_index("seq") & 1).reshape(1).astype(jnp.int32)

    bc = bc_input.reshape(length, -1)
    halo = shift(jnp.concatenate([x_input[length - LEAD :], bc[length - LEAD :]], 1), 1)
    weight_mate = swap(out_weight, "head", 1)

    ones = jnp.asarray(np.tile(np.repeat(np.eye(heads), P_SIZE, axis=1), (2, 1)), BF16)
    cum, cum_s, log_s, f_dev, f_blk, e_blk, rates = decays(log_decay, step_size, ones)
    x_conv, bc_conv, keep, send = conv_states(
        odd, x_input, bc, halo, conv_weight_x, conv_weight_bc, f_dev, ones, rates
    )

    skip = jnp.repeat(skip_gain, P_SIZE)[None, :]
    uvs = []

    def scan_next(token):
        if len(uvs) < B_PARTS:
            uvs.append(
                scan_part(len(uvs), token, x_conv, bc_conv, z_input, cum, cum_s, log_s, f_blk, e_blk, rates, skip, ones)
            )
        return uvs[-1]

    message = ((N + EXTRA, half), BF16)
    full = ((N, half), F32)
    got = swap(send, "seq", 1)
    done = scan_next(send)
    msg, own, first, aux = combine(
        pair_kernel,
        (odd, got, keep, rates, done),
        [SCALAR, FULL, FULL, FULL, ANY],
        [message, full, full, ((16, half), F32)],
        "pair",
    )
    behind = None
    covered = 0
    while True:
        got = shift(msg, 2 * (covered + 1))
        done = scan_next(msg)
        covered = 2 * covered + 1
        if covered >= pairs - 1:
            break
        operands, specs = [got, own, aux], [FULL, FULL, FULL]
        if behind is None:
            kernel = lambda g, o, a, t, m, b: wave_kernel(g, o, a, None, t, m, b)
        else:
            kernel = wave_kernel
            operands.append(behind)
            specs.append(FULL)
        msg, behind = combine(kernel, operands + [done], specs + [ANY], [message, ((N + 8, half), F32)], "wave")
    operands, specs = [odd, got], [SCALAR, FULL]
    if behind is None:
        kernel = lambda o, g, f, a, t, b, h: last_kernel(o, g, None, f, a, t, b, h)
    else:
        kernel = last_kernel
        operands.append(behind)
        specs.append(FULL)
    out = ((N, half), BF16)
    back, held = combine(kernel, operands + [first, aux, done], specs + [FULL, FULL, ANY], [out, out], "last")
    other = swap(back, "seq", 1)
    while len(uvs) < B_PARTS:
        scan_next(back)

    count = length // ways
    gain = norm_gain[None, :]

    def rows_for(target, token):
        info = jnp.concatenate([target.reshape(1).astype(jnp.int32), odd])
        return norm_rows(info, count, token, bc_conv, held, other, gain, uvs)

    far_mate = rows_for(mine ^ 3, held)
    far = rows_for(mine ^ 2, far_mate)
    far_mate = swap(far_mate, "head", 1)
    columns = out_weight.shape[1]
    eighth = columns // 8
    cuts = [0, eighth, 3 * eighth, 5 * eighth, 7 * eighth, columns]
    arrivals = []
    sent = far
    for lo, hi in zip(cuts[:-1], cuts[1:]):
        sent = project(sent, far, far_mate, out_weight, weight_mate, lo, hi - lo, BF16)
        arrivals.append(swap(sent, "head", 2))
    near_mate = rows_for(mine ^ 1, sent)
    near = rows_for(mine, near_mate)
    near_mate = swap(near_mate, "head", 1)
    total = project(near, near, near_mate, out_weight, weight_mate, 0, columns, F32)
    result = None
    for arrived, lo in zip(arrivals, cuts):
        result = add_chunk(total, arrived, result, lo)
    return result


def solution(mesh):
    in_specs = (
        P("seq", "head"),
        P("seq", "head"),
        P("seq", "head", None),
        P(None, "head"),
        P(None, "head", None),
        P("seq", "head"),
        P("seq", "head"),
        P("head"),
        P("head"),
        P("head", None),
    )
    out_specs = P(("seq", "head"), None)
    return jax.shard_map(local, mesh=mesh, in_specs=in_specs, out_specs=out_specs, check_vma=False)
```

```python
import functools

import jax
import jax.numpy as jnp
import numpy as np
from jax import lax
from jax.experimental import pallas as pl
from jax.experimental.pallas import tpu as pltpu
from jax.sharding import PartitionSpec as P

P_SIZE = 64
N = 128
KCONV = 4
EPS = 1e-05
LOG2E = 1.4426950408889634

TOK_A = 256
ROWS_A = 32
TOK_B = 128
STEP_B = 256
EXTRA = 16
SLAB = 256
ROWS_C = 128
TILE = 256
SLOTS = 4
LEAD = 16
B_PARTS = 4
HIGHEST = lax.Precision.HIGHEST
F32 = jnp.float32
BF16 = jnp.bfloat16


def params(mib):
    return pltpu.CompilerParams(vmem_limit_bytes=mib * 1024 * 1024)


CHEAP = pl.CostEstimate(flops=1, bytes_accessed=1, transcendentals=0)
SCALAR = pl.BlockSpec(memory_space=pltpu.SMEM)
FULL = pl.BlockSpec(memory_space=pltpu.VMEM)
FAR = pl.BlockSpec(memory_space=pltpu.HBM)
ANY = pl.BlockSpec(memory_space=pl.ANY)


def dot(a, b, dims=((1,), (0,)), precision=None):
    return lax.dot_general(a, b, (dims, ((), ())), precision=precision, preferred_element_type=F32)


def half_silu(half):
    return half + half * jnp.tanh(half)


def whole(shape):
    return pl.BlockSpec(shape, lambda *_: (0,) * len(shape))


def decay_kernel(ld_t, step_t, skip, ones, cum, cum_s, log_s, f_dev, f_blk, e_blk, rates):
    heads, length = ld_t.shape
    blocks = length // TOK_B
    row = lax.broadcasted_iota(jnp.int32, (TOK_B, TOK_B), 0)
    col = lax.broadcasted_iota(jnp.int32, (TOK_B, TOK_B), 1)
    lower = (row >= col).astype(F32)
    upper = (row <= col).astype(F32)
    eye = (row == col).astype(BF16)

    def put(ref, rows, value):
        high = value.astype(BF16)
        low = (value - high.astype(F32)).astype(BF16)
        ref[rows, :] = dot(eye, jnp.concatenate([high, low], 0), ((1,), (1,))).astype(BF16)

    cums, totals, row_totals = [], [], []
    for b in range(blocks):
        rows = slice(b * TOK_B, (b + 1) * TOK_B)
        logs = ld_t[:, rows] * LOG2E
        c = dot(lower, logs, ((1,), (1,)), HIGHEST)
        cum[rows, :] = c
        row_totals.append(c[TOK_B - 1 : TOK_B, :])
        c = dot(logs, upper, precision=HIGHEST)
        cums.append(c)
        totals.append(c[:, TOK_B - 1 : TOK_B])
    before, row_before = [jnp.zeros_like(totals[0])], [jnp.zeros_like(row_totals[0])]
    for b in range(blocks):
        before.append(before[-1] + totals[b])
        row_before.append(row_before[-1] + row_totals[b])
    total = before[-1]
    logs = jnp.concatenate(row_totals + row_before[:-1] + row_before[-1:] * 8, 0)
    values = jnp.concatenate([jnp.exp2(logs), jnp.broadcast_to(skip[...], (8, heads))], 0)
    rates[...] = dot(values, ones[0:heads, :].astype(F32), precision=HIGHEST)
    for b in range(blocks):
        rows = slice(b * TOK_B, (b + 1) * TOK_B)
        s = step_t[:, rows]
        log_step = jnp.log2(s)
        log_s[:, rows] = log_step
        cum_s[:, rows] = cums[b] - log_step
        put(f_dev, rows, jnp.exp2(total - (cums[b] + before[b])) * s)
        put(f_blk, rows, jnp.exp2(totals[b] - cums[b]) * s)
        put(e_blk, rows, jnp.exp2(cums[b]))


def decays(log_decay, step, skip, ones):
    length, heads = log_decay.shape
    blocks = length // TOK_B
    width = ones.shape[1]
    wide = jax.ShapeDtypeStruct((heads, length), F32)
    pair = jax.ShapeDtypeStruct((length, 2 * heads), BF16)
    return pl.pallas_call(
        decay_kernel,
        out_shape=(
            jax.ShapeDtypeStruct((length, heads), F32),
            wide,
            wide,
            pair,
            pair,
            pair,
            jax.ShapeDtypeStruct((2 * blocks + 16, width), F32),
        ),
        compiler_params=params(16),
        name="decays",
    )(log_decay.T, step.T, skip[None, :], ones)


def put_message(ref, state, decay):
    high = decay.astype(BF16)
    low = (decay - high.astype(F32)).astype(BF16)
    rest = jnp.zeros((EXTRA - 2, state.shape[1]), BF16)
    ref[0:N, :] = state.astype(BF16)
    ref[N:, :] = jnp.concatenate([high, low, rest], 0)


def take_message(ref):
    extra = ref[N:, :].astype(F32)
    return ref[0:N, :].astype(F32), extra[0:1] + extra[1:2]


def conv_kernel(info, x_far, bc, halo, wx, wbc, f_dev, ones, rates, x_out, bc_out, keep, send, x, sem, xf, state):
    i = pl.program_id(0)
    rows, width = x_out.shape
    bc_width = bc.shape[1]
    groups = bc_width // (2 * N)
    per = width // groups
    half = width // 2

    def fetch(step):
        piece = pl.ds(pl.multiple_of(step * rows, rows), rows)
        return pltpu.make_async_copy(x_far.at[piece], x.at[piece], sem.at[step])

    @pl.when(i == 0)
    def _():
        for step in range(x.shape[0] // rows):
            fetch(step).start()
        state[...] = jnp.zeros_like(state)

    fetch(i).wait()
    base = pl.multiple_of(i * rows, rows)
    before = pl.ds(pl.multiple_of(jnp.maximum(base - LEAD, 0), LEAD), LEAD)

    def at(r):
        return pl.ds(pl.multiple_of(base + r, ROWS_A), ROWS_A)

    def conv(src, lead, weights, emit):
        w0, w1, w2, w3 = [w * 0.5 for w in weights]
        back = LEAD - 8
        r1 = pltpu.roll(lead, 1, 0)
        last_x, last_p = lead[back:], (w1 * lead + w0 * r1)[back:]
        for r in range(0, rows, ROWS_A):
            cur = src(r).astype(F32)
            r1 = pltpu.roll(jnp.concatenate([last_x, cur], 0), 1, 0)[8:]
            p = w1 * cur + w0 * r1
            p2 = pltpu.roll(jnp.concatenate([last_p, p], 0), 2, 0)[8:]
            emit(r, half_silu((w3 * cur + w2 * r1) + p2))
            last_x, last_p = cur[ROWS_A - 8 :], p[ROWS_A - 8 :]

    start = i == 0
    for c in range(groups):
        for lanes in range(c * 2 * N, (c + 1) * 2 * N, N):
            ds = slice(lanes, lanes + N)

            def emit_bc(r, value):
                bc_out[r : r + ROWS_A, ds] = value.astype(BF16)

            lead = jnp.where(start, halo[:, width + lanes : width + lanes + N], bc[before, ds]).astype(F32)
            inner = slice(lanes - c * 2 * N, lanes - c * 2 * N + N)
            conv(lambda r: bc[at(r), ds], lead, [wbc[k, c : c + 1, inner] for k in range(KCONV)], emit_bc)

    def slab(c, _):
        ds = pl.ds(pl.multiple_of(c * SLAB, SLAB), SLAB)
        scale = dot(f_dev[pl.ds(base, rows), :], ones[:, ds])

        def emit(r, value):
            value = value.astype(BF16)
            x_out[r : r + ROWS_A, ds] = value
            xf[r : r + ROWS_A, ds] = (value.astype(F32) * scale[r : r + ROWS_A]).astype(BF16)

        lead = jnp.where(start, halo[:, ds], x[before, ds]).astype(F32)
        conv(lambda r: x[at(r), ds], lead, [wx[k : k + 1, ds] for k in range(KCONV)], emit)
        return 0

    lax.fori_loop(0, width // SLAB, slab, 0)
    for g in range(groups):
        b_mat = bc_out[:, 2 * N * g : 2 * N * g + N]
        lanes = slice(g * per, (g + 1) * per)
        state[:, lanes] += dot(b_mat, xf[:, lanes], ((0,), (0,)))

    @pl.when(i == pl.num_programs(0) - 1)
    def _():
        is_odd = info[0] == 1
        low, high = state[:, 0:half], state[:, half:]
        keep[...] = jnp.where(is_odd, high, low)
        row = rates.shape[0] - 16
        decay = jnp.where(is_odd, rates[row : row + 1, 0:half], rates[row : row + 1, half:])
        put_message(send, jnp.where(is_odd, low, high), decay)


def conv_states(info, x, bc, halo, wx, wbc, f_dev, ones, rates):
    length, width = x.shape
    bc_width = bc.shape[1]
    half = width // 2
    return pl.pallas_call(
        conv_kernel,
        grid=(length // TOK_A,),
        in_specs=[SCALAR, FAR] + [FULL] * 7,
        out_specs=[
            pl.BlockSpec((TOK_A, width), lambda i: (i, 0)),
            pl.BlockSpec((TOK_A, bc_width), lambda i: (i, 0)),
            whole((N, half)),
            whole((N + EXTRA, half)),
        ],
        scratch_shapes=[
            pltpu.VMEM((length, width), BF16),
            pltpu.SemaphoreType.DMA((length // TOK_A,)),
            pltpu.VMEM((TOK_A, width), BF16),
            pltpu.VMEM((N, width), F32),
        ],
        out_shape=(
            pltpu.HBM((length, width), BF16),
            jax.ShapeDtypeStruct((length, bc_width), BF16),
            jax.ShapeDtypeStruct((N, half), F32),
            jax.ShapeDtypeStruct((N + EXTRA, half), BF16),
        ),
        compiler_params=params(20),
        cost_estimate=CHEAP,
        name="conv_states",
    )(info, x, bc, halo, wx, wbc, f_dev, ones, rates)


def pair_kernel(info, got, keep, rates, _, msg, own, first, aux):
    half = keep.shape[1]
    is_odd = info[0] == 1
    arrived, their = take_message(got)
    row = rates.shape[0] - 16
    mine = jnp.where(is_odd, rates[row : row + 1, half:], rates[row : row + 1, 0:half])
    early = jnp.where(is_odd, arrived, keep[...])
    late = jnp.where(is_odd, keep[...], arrived)
    even_decay = jnp.where(is_odd, their, mine)
    odd_decay = jnp.where(is_odd, mine, their)
    state = odd_decay * early + late
    own[...] = state
    first[...] = early
    aux[0:8, :] = jnp.broadcast_to(even_decay, (8, half))
    aux[8:16, :] = jnp.broadcast_to(even_decay * odd_decay, (8, half))
    put_message(msg, state, even_decay * odd_decay)


def wave_kernel(got, own, aux, behind_in, _, msg, behind):
    before, decay = take_message(got)
    if behind_in is not None:
        before_decay = behind_in[N : N + 1, :]
        before = behind_in[0:N, :] + before_decay * before
        decay = before_decay * decay
    pair_decay = aux[8:9, :]
    behind[0:N, :] = before
    behind[N:, :] = jnp.broadcast_to(decay, (8, before.shape[1]))
    put_message(msg, own[...] + pair_decay * before, pair_decay * decay)


def last_kernel(info, got, behind_in, first, aux, _, back, held):
    is_odd = info[0] == 1
    before, _unused = take_message(got)
    if behind_in is not None:
        before = behind_in[0:N, :] + behind_in[N : N + 1, :] * before
    entering_odd = aux[0:1, :] * before + first[...]
    back[...] = jnp.where(is_odd, before, entering_odd).astype(BF16)
    held[...] = jnp.where(is_odd, entering_odd, before).astype(BF16)


def combine(kernel, operands, specs, outs, name):
    return pl.pallas_call(
        kernel,
        in_specs=specs,
        out_specs=[FULL] * len(outs),
        out_shape=[jax.ShapeDtypeStruct(s, t) for s, t in outs],
        compiler_params=params(16),
        name=name,
    )(*operands)


def scan_kernel(part, x_far, z_far, bc_all, cum, cum_s, log_s, f_blk, e_blk, rates, ones, _, uv_out, x, z, sem, state):
    length, width = x.shape
    per_slab = SLAB // P_SIZE
    head0 = part * width // P_SIZE
    first_lane = part * width
    inner = STEP_B // TOK_B
    blocks = length // TOK_B
    group = first_lane * (bc_all.shape[1] // (2 * N)) // (width * B_PARTS)
    b_lanes = slice(2 * N * group, 2 * N * group + N)
    c_lanes = slice(2 * N * group + N, 2 * N * (group + 1))

    def fetch(step):
        piece = pl.ds(pl.multiple_of(step * STEP_B, STEP_B), STEP_B)
        lanes = pl.ds(first_lane, width)
        return (
            pltpu.make_async_copy(x_far.at[piece, lanes], x.at[piece], sem.at[0, step]),
            pltpu.make_async_copy(z_far.at[piece, lanes], z.at[piece], sem.at[1, step]),
        )

    for step in range(length // STEP_B):
        for copy in fetch(step):
            copy.start()
    state[...] = jnp.zeros_like(state)

    row = lax.broadcasted_iota(jnp.int32, (TOK_B, TOK_B), 0)
    col = lax.broadcasted_iota(jnp.int32, (TOK_B, TOK_B), 1)
    keep = row >= col
    first = lax.broadcasted_iota(jnp.int32, (TOK_B, 2 * P_SIZE), 1) < P_SIZE
    zero = jnp.zeros((TOK_B, 2 * P_SIZE), BF16)

    def block(b, _):
        @pl.when(lax.rem(b, inner) == 0)
        def _():
            for copy in fetch(lax.div(b, inner)):
                copy.wait()

        at = pl.ds(pl.multiple_of(b * TOK_B, TOK_B), TOK_B)
        b_mat = bc_all[at, b_lanes]
        c_mat = bc_all[at, c_lanes]
        scores = jnp.where(keep, dot(c_mat, b_mat, ((1,), (1,))), 0.0)
        wide = pl.ds(first_lane, width)
        fade_rows = rates[pl.ds(b, 1), wide]
        lead_rows = rates[pl.ds(blocks + b, 1), wide]
        skip = rates[2 * blocks + 8 : 2 * blocks + 9, wide]
        for s in range(width // SLAB):
            lanes = slice(s * SLAB, (s + 1) * SLAB)
            xb = x[at, lanes]
            sel = ones[:, first_lane + s * SLAB : first_lane + (s + 1) * SLAB]
            old = state[:, lanes]
            rise = dot(e_blk[at, :], sel)
            carried = dot(c_mat, old.astype(BF16)) * rise
            within = []
            for q in range(per_slab // 2):
                tables = []
                for h in (2 * q, 2 * q + 1):
                    head = head0 + s * per_slab + h
                    column = cum[at, head : head + 1]
                    gap = jnp.minimum(column - cum_s[head : head + 1, at], log_s[head : head + 1, at])
                    tables.append((scores * jnp.exp2(gap)).astype(BF16))
                xp = xb[:, q * 2 * P_SIZE : (q + 1) * 2 * P_SIZE]
                stacked = jnp.concatenate([jnp.where(first, xp, zero), jnp.where(first, zero, xp)], 0)
                within.append(dot(jnp.concatenate(tables, 1), stacked))
            xs = xb.astype(F32)
            y = jnp.concatenate(within, 1) + carried + skip[:, lanes] * xs
            gate = half_silu((z[at, lanes] * 0.5).astype(F32))
            uv_out[at, lanes] = (y * gate).astype(BF16)
            uv_out[at, width + s * SLAB : width + (s + 1) * SLAB] = (gate * rise * lead_rows[:, lanes]).astype(BF16)
            xf = (xs * dot(f_blk[at, :], sel)).astype(BF16)
            state[:, lanes] = old * fade_rows[:, lanes] + dot(b_mat, xf, ((0,), (0,)))
        return 0

    lax.fori_loop(0, blocks, block, 0)


def scan_part(part, token, x, bc, z, cum, cum_s, log_s, f_blk, e_blk, rates, ones):
    length, full = x.shape
    width = full // B_PARTS
    return pl.pallas_call(
        functools.partial(scan_kernel, part),
        in_specs=[FAR, FAR] + [FULL] * 8 + [ANY],
        out_specs=FULL,
        out_shape=jax.ShapeDtypeStruct((length, 2 * width), BF16),
        scratch_shapes=[
            pltpu.VMEM((length, width), BF16),
            pltpu.VMEM((length, width), BF16),
            pltpu.SemaphoreType.DMA((2, length // STEP_B)),
            pltpu.VMEM((N, width), F32),
        ],
        compiler_params=params(16),
        cost_estimate=CHEAP,
        name="scan_part",
    )(x, z, bc, cum, cum_s, log_s, f_blk, e_blk, rates, ones, token)


def norm_kernel(slot, info, bc, keep, recv, gain, _, *refs):
    uvs, out = refs[:-1], refs[-1]
    count, width = out.shape
    groups = bc.shape[1] // (2 * N)
    per = width // groups
    half = width // 2
    part = width // B_PARTS
    is_odd = info[0] == 1
    base = info[slot] * count

    def rows(j, _):
        to = pl.ds(pl.multiple_of(j * ROWS_C, ROWS_C), ROWS_C)
        at = pl.ds(pl.multiple_of(base + j * ROWS_C, ROWS_C), ROWS_C)
        for g in range(groups):
            c_mat = bc[at, 2 * N * g + N : 2 * N * (g + 1)]
            pieces = []
            squares = None
            for p in range(g * per // part, (g + 1) * per // part):
                start = p * part
                side = start // half
                lanes = slice(start - side * half, start - side * half + part)
                mine, other = keep[:, lanes], recv[:, lanes]
                inc = jnp.where(is_odd, other, mine) if side == 0 else jnp.where(is_odd, mine, other)
                gated = uvs[p][at, 0:part].astype(F32) + uvs[p][at, part:].astype(F32) * dot(c_mat, inc)
                square = jnp.sum(gated * gated, axis=-1, keepdims=True)
                squares = square if squares is None else squares + square
                pieces.append((start, gated))
            scale = lax.rsqrt(squares * (1.0 / per) + EPS)
            for start, gated in pieces:
                out[to, start : start + part] = (gated * scale * gain[:, start : start + part]).astype(BF16)
        return 0

    lax.fori_loop(0, count // ROWS_C, rows, 0)


def norm_rows(slot, info, count, token, bc, keep, recv, gain, uvs):
    return pl.pallas_call(
        functools.partial(norm_kernel, slot),
        in_specs=[SCALAR] + [FULL] * 4 + [ANY] + [FULL] * len(uvs),
        out_specs=FULL,
        out_shape=jax.ShapeDtypeStruct((count, gain.shape[1]), BF16),
        compiler_params=params(16),
        cost_estimate=CHEAP,
        name="norm_rows",
    )(info, bc, keep, recv, gain, token, *uvs)


def project_kernel(base, added, a0, a1, w0_far, w1_far, *refs):
    out, w0, w1, sem = refs[-4:]
    j = pl.program_id(0)
    tiles = pl.num_programs(0)

    def fetch(t):
        slot = lax.rem(t, SLOTS)
        lanes = pl.ds(pl.multiple_of((base + t) * TILE, TILE), TILE)
        return (
            pltpu.make_async_copy(w0_far.at[:, lanes], w0.at[slot], sem.at[0, slot]),
            pltpu.make_async_copy(w1_far.at[:, lanes], w1.at[slot], sem.at[1, slot]),
        )

    def start(t):
        @pl.when(t < tiles)
        def _():
            for copy in fetch(t):
                copy.start()

    @pl.when(j == 0)
    def _():
        for t in range(SLOTS - 1):
            start(t)

    start(j + SLOTS - 1)
    for copy in fetch(j):
        copy.wait()
    slot = lax.rem(j, SLOTS)
    total = dot(a0[...], w0[slot]) + dot(a1[...], w1[slot])
    if added:
        total = total + refs[0][...].astype(F32)
    out[...] = total.astype(out.dtype)


def project(a0, a1, w0, w1, first, count, kind, arrived=None, result=None):
    rows, depth = a0.shape
    base = first // TILE
    full = arrived is not None
    operands, specs = [a0, a1, w0, w1], [FULL, FULL, FAR, FAR]
    if full:
        operands.append(arrived)
        specs.append(pl.BlockSpec((rows, TILE), lambda j: (0, j)))
    if result is not None:
        operands.append(result)
        specs.append(ANY)
    return pl.pallas_call(
        functools.partial(project_kernel, base, full),
        grid=(count // TILE,),
        in_specs=specs,
        out_specs=pl.BlockSpec((rows, TILE), lambda j: (0, base + j if full else j)),
        out_shape=jax.ShapeDtypeStruct((rows, w0.shape[1] if full else count), kind),
        scratch_shapes=[
            pltpu.VMEM((SLOTS, depth, TILE), BF16),
            pltpu.VMEM((SLOTS, depth, TILE), BF16),
            pltpu.SemaphoreType.DMA((2, SLOTS)),
        ],
        input_output_aliases={} if result is None else {len(operands) - 1: 0},
        compiler_params=params(20),
        cost_estimate=CHEAP,
        name="project",
    )(*operands)


def add_kernel(part, arrived, _, out):
    out[...] = (part[...] + arrived[...].astype(F32)).astype(BF16)


def add_chunk(part, arrived, result, first):
    rows, count = arrived.shape
    base = first // count
    return pl.pallas_call(
        add_kernel,
        grid=(1,),
        in_specs=[FULL, FULL, ANY],
        out_specs=pl.BlockSpec((rows, count), lambda j: (0, base)),
        out_shape=jax.ShapeDtypeStruct(result.shape, BF16),
        input_output_aliases={2: 0},
        compiler_params=params(8),
        cost_estimate=CHEAP,
        name="add_chunk",
    )(part, arrived, result)


def shift(block, distance):
    size = lax.axis_size("seq")
    return lax.ppermute(block, "seq", [(i, i + distance) for i in range(size - distance)])


def swap(block, axis, bit):
    return lax.ppermute(block, axis, [(i, i ^ bit) for i in range(lax.axis_size(axis))])


def local(
    x_input,
    z_input,
    bc_input,
    conv_weight_x,
    conv_weight_bc,
    step_size,
    log_decay,
    skip_gain,
    norm_gain,
    out_weight,
):
    length, width = x_input.shape
    heads = step_size.shape[1]
    ways = lax.axis_size("head")
    pairs = lax.axis_size("seq") // 2
    mine = lax.axis_index("head")
    half = width // 2
    info = jnp.stack([lax.axis_index("seq") & 1, mine ^ 3, mine ^ 2, mine ^ 1, mine]).astype(jnp.int32)

    x_far, z_far, w_far = [pltpu.with_memory_space_constraint(v, pltpu.HBM) for v in (x_input, z_input, out_weight)]
    bc = bc_input.reshape(length, -1)
    halo = shift(jnp.concatenate([x_input[length - LEAD :], bc[length - LEAD :]], 1), 1)
    weight_mate = swap(out_weight, "head", 1)

    ones = jnp.asarray(np.tile(np.repeat(np.eye(heads), P_SIZE, axis=1), (2, 1)), BF16)
    cum, cum_s, log_s, f_dev, f_blk, e_blk, rates = decays(log_decay, step_size, skip_gain, ones)
    x_conv, bc_conv, keep, send = conv_states(
        info, x_far, bc, halo, conv_weight_x, conv_weight_bc, f_dev, ones, rates
    )

    x_conv = pltpu.with_memory_space_constraint(x_conv, pltpu.HBM)
    uvs = []

    def scan_next(token):
        if len(uvs) < B_PARTS:
            uvs.append(
                scan_part(len(uvs), token, x_conv, bc_conv, z_far, cum, cum_s, log_s, f_blk, e_blk, rates, ones)
            )
        return uvs[-1]

    message = ((N + EXTRA, half), BF16)
    full = ((N, half), F32)
    got = swap(send, "seq", 1)
    done = scan_next(send)
    msg, own, first, aux = combine(
        pair_kernel,
        (info, got, keep, rates, done),
        [SCALAR, FULL, FULL, FULL, ANY],
        [message, full, full, ((16, half), F32)],
        "pair",
    )
    behind = None
    covered = 0
    while True:
        got = shift(msg, 2 * (covered + 1))
        done = scan_next(msg)
        covered = 2 * covered + 1
        if covered >= pairs - 1:
            break
        operands, specs = [got, own, aux], [FULL, FULL, FULL]
        if behind is None:
            kernel = lambda g, o, a, t, m, b: wave_kernel(g, o, a, None, t, m, b)
        else:
            kernel = wave_kernel
            operands.append(behind)
            specs.append(FULL)
        msg, behind = combine(kernel, operands + [done], specs + [ANY], [message, ((N + 8, half), F32)], "wave")
    operands, specs = [info, got], [SCALAR, FULL]
    if behind is None:
        kernel = lambda o, g, f, a, t, b, h: last_kernel(o, g, None, f, a, t, b, h)
    else:
        kernel = last_kernel
        operands.append(behind)
        specs.append(FULL)
    out = ((N, half), BF16)
    back, held = combine(kernel, operands + [first, aux, done], specs + [FULL, FULL, ANY], [out, out], "last")
    other = swap(back, "seq", 1)
    while len(uvs) < B_PARTS:
        scan_next(back)

    count = length // ways
    gain = norm_gain[None, :]

    def rows_for(slot, token):
        return norm_rows(slot, info, count, token, bc_conv, held, other, gain, uvs)

    far_mate = rows_for(1, held)
    far = rows_for(2, far_mate)
    far_mate = swap(far_mate, "head", 1)
    columns = out_weight.shape[1]
    cuts = [columns * c // 16 for c in (0, 3, 6, 9, 12, 14, 16)]
    arrivals = []
    for lo, hi in zip(cuts[:-1], cuts[1:]):
        sent = project(far, far_mate, w_far, weight_mate, lo, hi - lo, BF16)
        arrivals.append(swap(sent, "head", 2))
    near_mate = rows_for(3, far)
    near = rows_for(4, near_mate)
    near_mate = swap(near_mate, "head", 1)
    last = project(near, near_mate, w_far, weight_mate, cuts[-2], columns - cuts[-2], F32)
    result = None
    for arrived, lo, hi in zip(arrivals[:-1], cuts[:-2], cuts[1:-1]):
        result = project(near, near_mate, w_far, weight_mate, lo, hi - lo, BF16, arrived, result)
    return add_chunk(last, arrivals[-1], result, cuts[-2])


def solution(mesh):
    in_specs = (
        P("seq", "head"),
        P("seq", "head"),
        P("seq", "head", None),
        P(None, "head"),
        P(None, "head", None),
        P("seq", "head"),
        P("seq", "head"),
        P("head"),
        P("head"),
        P("head", None),
    )
    out_specs = P(("seq", "head"), None)
    return jax.shard_map(local, mesh=mesh, in_specs=in_specs, out_specs=out_specs, check_vma=False)
```

```python
import functools

import jax
import jax.numpy as jnp
import numpy as np
from jax import lax
from jax.experimental import pallas as pl
from jax.experimental.pallas import tpu as pltpu
from jax.sharding import PartitionSpec as P

P_SIZE = 64
N = 128
KCONV = 4
EPS = 1e-05
LOG2E = 1.4426950408889634

TOK_A = 256
ROWS_A = 64
TOK_B = 128
STEP_B = 256
EXTRA = 16
SLAB = 256
ROWS_C = 128
TILE = 256
SLOTS = 4
LEAD = 16
B_PARTS = 4
HIGHEST = lax.Precision.HIGHEST
F32 = jnp.float32
BF16 = jnp.bfloat16


def params(mib):
    return pltpu.CompilerParams(vmem_limit_bytes=mib * 1024 * 1024)


CHEAP = pl.CostEstimate(flops=1, bytes_accessed=1, transcendentals=0)
SCALAR = pl.BlockSpec(memory_space=pltpu.SMEM)
FULL = pl.BlockSpec(memory_space=pltpu.VMEM)
FAR = pl.BlockSpec(memory_space=pltpu.HBM)
ANY = pl.BlockSpec(memory_space=pl.ANY)


def dot(a, b, dims=((1,), (0,)), precision=None):
    return lax.dot_general(a, b, (dims, ((), ())), precision=precision, preferred_element_type=F32)


def half_silu(half):
    return half + half * jnp.tanh(half)


def whole(shape):
    return pl.BlockSpec(shape, lambda *_: (0,) * len(shape))


def decay_kernel(ld_t, step_t, skip, ones, cum, cum_s, log_s, f_dev, f_blk, e_blk, rates):
    heads, length = ld_t.shape
    blocks = length // TOK_B
    row = lax.broadcasted_iota(jnp.int32, (TOK_B, TOK_B), 0)
    col = lax.broadcasted_iota(jnp.int32, (TOK_B, TOK_B), 1)
    lower = (row >= col).astype(F32)
    upper = (row <= col).astype(F32)
    eye = (row == col).astype(BF16)

    def put(ref, rows, value):
        high = value.astype(BF16)
        low = (value - high.astype(F32)).astype(BF16)
        ref[rows, :] = dot(eye, jnp.concatenate([high, low], 0), ((1,), (1,))).astype(BF16)

    cums, totals, row_totals = [], [], []
    for b in range(blocks):
        rows = slice(b * TOK_B, (b + 1) * TOK_B)
        logs = ld_t[:, rows] * LOG2E
        c = dot(lower, logs, ((1,), (1,)), HIGHEST)
        cum[rows, :] = c
        row_totals.append(c[TOK_B - 1 : TOK_B, :])
        c = dot(logs, upper, precision=HIGHEST)
        cums.append(c)
        totals.append(c[:, TOK_B - 1 : TOK_B])
    before, row_before = [jnp.zeros_like(totals[0])], [jnp.zeros_like(row_totals[0])]
    for b in range(blocks):
        before.append(before[-1] + totals[b])
        row_before.append(row_before[-1] + row_totals[b])
    total = before[-1]
    logs = jnp.concatenate(row_totals + row_before[:-1] + row_before[-1:] * 8, 0)
    values = jnp.concatenate([jnp.exp2(logs), jnp.broadcast_to(skip[...], (8, heads))], 0)
    rates[...] = dot(values, ones[0:heads, :].astype(F32), precision=HIGHEST)
    for b in range(blocks):
        rows = slice(b * TOK_B, (b + 1) * TOK_B)
        s = step_t[:, rows]
        log_step = jnp.log2(s)
        log_s[:, rows] = log_step
        cum_s[:, rows] = cums[b] - log_step
        put(f_dev, rows, jnp.exp2(total - (cums[b] + before[b])) * s)
        put(f_blk, rows, jnp.exp2(totals[b] - cums[b]) * s)
        put(e_blk, rows, jnp.exp2(cums[b]))


def decays(log_decay, step, skip, ones):
    length, heads = log_decay.shape
    blocks = length // TOK_B
    width = ones.shape[1]
    wide = jax.ShapeDtypeStruct((heads, length), F32)
    pair = jax.ShapeDtypeStruct((length, 2 * heads), BF16)
    return pl.pallas_call(
        decay_kernel,
        out_shape=(
            jax.ShapeDtypeStruct((length, heads), F32),
            wide,
            wide,
            pair,
            pair,
            pair,
            jax.ShapeDtypeStruct((2 * blocks + 16, width), F32),
        ),
        compiler_params=params(16),
        name="decays",
    )(log_decay.T, step.T, skip[None, :], ones)


def put_message(ref, state, decay):
    high = decay.astype(BF16)
    low = (decay - high.astype(F32)).astype(BF16)
    rest = jnp.zeros((EXTRA - 2, state.shape[1]), BF16)
    ref[0:N, :] = state.astype(BF16)
    ref[N:, :] = jnp.concatenate([high, low, rest], 0)


def take_message(ref):
    extra = ref[N:, :].astype(F32)
    return ref[0:N, :].astype(F32), extra[0:1] + extra[1:2]


def conv_kernel(info, x_far, bc, halo, wx, wbc, f_dev, ones, rates, x_out, bc_out, keep, send, x, sem, xf, state):
    i = pl.program_id(0)
    rows, width = x_out.shape
    bc_width = bc.shape[1]
    groups = bc_width // (2 * N)
    per = width // groups
    half = width // 2

    def fetch(step):
        piece = pl.ds(pl.multiple_of(step * rows, rows), rows)
        return pltpu.make_async_copy(x_far.at[piece], x.at[piece], sem.at[step])

    @pl.when(i == 0)
    def _():
        fetch(0).start()
        state[...] = jnp.zeros_like(state)

    fetch(i).wait()

    @pl.when(i + 1 < pl.num_programs(0))
    def _():
        fetch(i + 1).start()

    base = pl.multiple_of(i * rows, rows)
    before = pl.ds(pl.multiple_of(jnp.maximum(base - LEAD, 0), LEAD), LEAD)

    def at(r):
        return pl.ds(pl.multiple_of(base + r, ROWS_A), ROWS_A)

    def conv(src, lead, weights, emit):
        w0, w1, w2, w3 = [w * 0.5 for w in weights]
        back = LEAD - 8
        r1 = pltpu.roll(lead, 1, 0)
        last_x, last_p = lead[back:], (w1 * lead + w0 * r1)[back:]
        for r in range(0, rows, ROWS_A):
            cur = src(r).astype(F32)
            r1 = pltpu.roll(jnp.concatenate([last_x, cur], 0), 1, 0)[8:]
            p = w1 * cur + w0 * r1
            p2 = pltpu.roll(jnp.concatenate([last_p, p], 0), 2, 0)[8:]
            emit(r, half_silu((w3 * cur + w2 * r1) + p2))
            last_x, last_p = cur[ROWS_A - 8 :], p[ROWS_A - 8 :]

    start = i == 0
    for c in range(groups):
        for lanes in range(c * 2 * N, (c + 1) * 2 * N, N):
            ds = slice(lanes, lanes + N)

            def emit_bc(r, value):
                bc_out[r : r + ROWS_A, ds] = value.astype(BF16)

            lead = jnp.where(start, halo[:, width + lanes : width + lanes + N], bc[before, ds]).astype(F32)
            inner = slice(lanes - c * 2 * N, lanes - c * 2 * N + N)
            conv(lambda r: bc[at(r), ds], lead, [wbc[k, c : c + 1, inner] for k in range(KCONV)], emit_bc)

    def slab(c, _):
        first = pl.multiple_of(c * SLAB, SLAB)
        scale = dot(f_dev[pl.ds(base, rows), :], ones[:, pl.ds(first, SLAB)])
        for sub in range(0, SLAB, N):
            ds = pl.ds(pl.multiple_of(first + sub, N), N)

            def emit(r, value):
                value = value.astype(BF16)
                x_out[r : r + ROWS_A, ds] = value
                xf[r : r + ROWS_A, ds] = (value.astype(F32) * scale[r : r + ROWS_A, sub : sub + N]).astype(BF16)

            lead = jnp.where(start, halo[:, ds], x[before, ds]).astype(F32)
            conv(lambda r: x[at(r), ds], lead, [wx[k : k + 1, ds] for k in range(KCONV)], emit)
        return 0

    lax.fori_loop(0, width // SLAB, slab, 0)
    for g in range(groups):
        b_mat = bc_out[:, 2 * N * g : 2 * N * g + N]
        lanes = slice(g * per, (g + 1) * per)
        state[:, lanes] += dot(b_mat, xf[:, lanes], ((0,), (0,)))

    @pl.when(i == pl.num_programs(0) - 1)
    def _():
        is_odd = info[0] == 1
        low, high = state[:, 0:half], state[:, half:]
        keep[...] = jnp.where(is_odd, high, low)
        row = rates.shape[0] - 16
        decay = jnp.where(is_odd, rates[row : row + 1, 0:half], rates[row : row + 1, half:])
        put_message(send, jnp.where(is_odd, low, high), decay)


def conv_states(info, x, bc, halo, wx, wbc, f_dev, ones, rates):
    length, width = x.shape
    bc_width = bc.shape[1]
    half = width // 2
    return pl.pallas_call(
        conv_kernel,
        grid=(length // TOK_A,),
        in_specs=[SCALAR, FAR] + [FULL] * 7,
        out_specs=[
            pl.BlockSpec((TOK_A, width), lambda i: (i, 0)),
            pl.BlockSpec((TOK_A, bc_width), lambda i: (i, 0)),
            whole((N, half)),
            whole((N + EXTRA, half)),
        ],
        scratch_shapes=[
            pltpu.VMEM((length, width), BF16),
            pltpu.SemaphoreType.DMA((length // TOK_A,)),
            pltpu.VMEM((TOK_A, width), BF16),
            pltpu.VMEM((N, width), F32),
        ],
        out_shape=(
            pltpu.HBM((length, width), BF16),
            jax.ShapeDtypeStruct((length, bc_width), BF16),
            jax.ShapeDtypeStruct((N, half), F32),
            jax.ShapeDtypeStruct((N + EXTRA, half), BF16),
        ),
        compiler_params=params(20),
        cost_estimate=CHEAP,
        name="conv_states",
    )(info, x, bc, halo, wx, wbc, f_dev, ones, rates)


def pair_kernel(info, got, keep, rates, _, msg, own, first, aux):
    half = keep.shape[1]
    is_odd = info[0] == 1
    arrived, their = take_message(got)
    row = rates.shape[0] - 16
    mine = jnp.where(is_odd, rates[row : row + 1, half:], rates[row : row + 1, 0:half])
    early = jnp.where(is_odd, arrived, keep[...])
    late = jnp.where(is_odd, keep[...], arrived)
    even_decay = jnp.where(is_odd, their, mine)
    odd_decay = jnp.where(is_odd, mine, their)
    state = odd_decay * early + late
    own[...] = state
    first[...] = early
    aux[0:8, :] = jnp.broadcast_to(even_decay, (8, half))
    aux[8:16, :] = jnp.broadcast_to(even_decay * odd_decay, (8, half))
    put_message(msg, state, even_decay * odd_decay)


def wave_kernel(got, own, aux, behind_in, _, msg, behind):
    before, decay = take_message(got)
    if behind_in is not None:
        before_decay = behind_in[N : N + 1, :]
        before = behind_in[0:N, :] + before_decay * before
        decay = before_decay * decay
    pair_decay = aux[8:9, :]
    behind[0:N, :] = before
    behind[N:, :] = jnp.broadcast_to(decay, (8, before.shape[1]))
    put_message(msg, own[...] + pair_decay * before, pair_decay * decay)


def last_kernel(info, got, behind_in, first, aux, _, back, held):
    is_odd = info[0] == 1
    before, _unused = take_message(got)
    if behind_in is not None:
        before = behind_in[0:N, :] + behind_in[N : N + 1, :] * before
    entering_odd = aux[0:1, :] * before + first[...]
    back[...] = jnp.where(is_odd, before, entering_odd).astype(BF16)
    held[...] = jnp.where(is_odd, entering_odd, before).astype(BF16)


def pair_split_kernel(info, got, keep, rates, _, first, aux, *refs):
    outs, wide = refs[:-1], refs[-1]
    half = keep.shape[1]
    pairs = len(outs)
    piece = half // pairs
    is_odd = info[0] == 1
    arrived, their = take_message(got)
    row = rates.shape[0] - 16
    mine = jnp.where(is_odd, rates[row : row + 1, half:], rates[row : row + 1, 0:half])
    early = jnp.where(is_odd, arrived, keep[...])
    late = jnp.where(is_odd, keep[...], arrived)
    even_decay = jnp.where(is_odd, their, mine)
    odd_decay = jnp.where(is_odd, mine, their)
    first[...] = early
    aux[...] = jnp.broadcast_to(even_decay, (8, half))
    put_message(wide, odd_decay * early + late, even_decay * odd_decay)
    for r in range(pairs):
        owner = lax.rem(info[5] + r, pairs)
        outs[r][...] = wide[:, pl.ds(pl.multiple_of(owner * piece, piece), piece)]


def owner_kernel(info, *refs):
    pairs = (len(refs) - 3) // 2
    ins, outs = refs[:pairs], refs[pairs + 1 : 2 * pairs + 1]
    states, prefixes = refs[-2:]
    for r in range(pairs):
        states[lax.rem(info[5] + pairs - r, pairs)] = ins[r][...]
    before = jnp.zeros(prefixes.shape[1:], F32)
    for q in range(pairs):
        prefixes[q] = before.astype(BF16)
        if q < pairs - 1:
            state, decay = take_message(states.at[q])
            before = decay * before + state
    for r in range(pairs):
        outs[r][...] = prefixes[lax.rem(info[5] + r, pairs)]


def last_split_kernel(info, first, aux, _, *refs):
    pairs = len(refs) - 3
    back, held, wide = refs[-3:]
    piece = back.shape[1] // pairs
    for r in range(pairs):
        owner = lax.rem(info[5] + pairs - r, pairs)
        wide[:, pl.ds(pl.multiple_of(owner * piece, piece), piece)] = refs[r][...]
    is_odd = info[0] == 1
    before = wide[...].astype(F32)
    entering_odd = aux[0:1, :] * before + first[...]
    back[...] = jnp.where(is_odd, before, entering_odd).astype(BF16)
    held[...] = jnp.where(is_odd, entering_odd, before).astype(BF16)


def combine(kernel, operands, specs, outs, name, scratch=()):
    return pl.pallas_call(
        kernel,
        in_specs=specs,
        out_specs=[FULL] * len(outs),
        out_shape=[jax.ShapeDtypeStruct(s, t) for s, t in outs],
        scratch_shapes=list(scratch),
        compiler_params=params(16),
        cost_estimate=CHEAP,
        name=name,
    )(*operands)


def scan_kernel(part, x_far, z_far, bc_all, cum, cum_s, log_s, f_blk, e_blk, rates, ones, _, uv_out, x, z, sem, state):
    length, width = x.shape
    per_slab = SLAB // P_SIZE
    head0 = part * width // P_SIZE
    first_lane = part * width
    inner = STEP_B // TOK_B
    blocks = length // TOK_B
    group = first_lane * (bc_all.shape[1] // (2 * N)) // (width * B_PARTS)
    b_lanes = slice(2 * N * group, 2 * N * group + N)
    c_lanes = slice(2 * N * group + N, 2 * N * (group + 1))

    def fetch(step):
        piece = pl.ds(pl.multiple_of(step * STEP_B, STEP_B), STEP_B)
        lanes = pl.ds(first_lane, width)
        return (
            pltpu.make_async_copy(x_far.at[piece, lanes], x.at[piece], sem.at[0, step]),
            pltpu.make_async_copy(z_far.at[piece, lanes], z.at[piece], sem.at[1, step]),
        )

    for step in range(length // STEP_B):
        for copy in fetch(step):
            copy.start()
    state[...] = jnp.zeros_like(state)

    row = lax.broadcasted_iota(jnp.int32, (TOK_B, TOK_B), 0)
    col = lax.broadcasted_iota(jnp.int32, (TOK_B, TOK_B), 1)
    keep = row >= col
    first = lax.broadcasted_iota(jnp.int32, (TOK_B, 2 * P_SIZE), 1) < P_SIZE
    zero = jnp.zeros((TOK_B, 2 * P_SIZE), BF16)

    def turn(step, _):
        for copy in fetch(step):
            copy.wait()
        for k in range(inner):
            block(step * inner + k)
        return 0

    def block(b):
        at = pl.ds(pl.multiple_of(b * TOK_B, TOK_B), TOK_B)
        b_mat = bc_all[at, b_lanes]
        c_mat = bc_all[at, c_lanes]
        scores = jnp.where(keep, dot(c_mat, b_mat, ((1,), (1,))), 0.0)
        wide = pl.ds(first_lane, width)
        fade_rows = rates[pl.ds(b, 1), wide]
        lead_rows = rates[pl.ds(blocks + b, 1), wide]
        skip = rates[2 * blocks + 8 : 2 * blocks + 9, wide]
        for s in range(width // SLAB):
            lanes = slice(s * SLAB, (s + 1) * SLAB)
            xb = x[at, lanes]
            sel = ones[:, first_lane + s * SLAB : first_lane + (s + 1) * SLAB]
            old = state[:, lanes]
            rise = dot(e_blk[at, :], sel)
            carried = dot(c_mat, old.astype(BF16)) * rise
            within = []
            for q in range(per_slab // 2):
                tables = []
                for h in (2 * q, 2 * q + 1):
                    head = head0 + s * per_slab + h
                    column = cum[at, head : head + 1]
                    gap = jnp.minimum(column - cum_s[head : head + 1, at], log_s[head : head + 1, at])
                    tables.append((scores * jnp.exp2(gap)).astype(BF16))
                xp = xb[:, q * 2 * P_SIZE : (q + 1) * 2 * P_SIZE]
                stacked = jnp.concatenate([jnp.where(first, xp, zero), jnp.where(first, zero, xp)], 0)
                within.append(dot(jnp.concatenate(tables, 1), stacked))
            xs = xb.astype(F32)
            y = jnp.concatenate(within, 1) + carried + skip[:, lanes] * xs
            gate = half_silu((z[at, lanes] * 0.5).astype(F32))
            uv_out[at, lanes] = (y * gate).astype(BF16)
            uv_out[at, width + s * SLAB : width + (s + 1) * SLAB] = (gate * rise * lead_rows[:, lanes]).astype(BF16)
            xf = (xs * dot(f_blk[at, :], sel)).astype(BF16)
            state[:, lanes] = old * fade_rows[:, lanes] + dot(b_mat, xf, ((0,), (0,)))

    lax.fori_loop(0, length // STEP_B, turn, 0)


def scan_part(part, token, x, bc, z, cum, cum_s, log_s, f_blk, e_blk, rates, ones):
    length, full = x.shape
    width = full // B_PARTS
    return pl.pallas_call(
        functools.partial(scan_kernel, part),
        in_specs=[FAR, FAR] + [FULL] * 8 + [ANY],
        out_specs=FULL,
        out_shape=jax.ShapeDtypeStruct((length, 2 * width), BF16),
        scratch_shapes=[
            pltpu.VMEM((length, width), BF16),
            pltpu.VMEM((length, width), BF16),
            pltpu.SemaphoreType.DMA((2, length // STEP_B)),
            pltpu.VMEM((N, width), F32),
        ],
        compiler_params=params(16),
        cost_estimate=CHEAP,
        name="scan_part",
    )(x, z, bc, cum, cum_s, log_s, f_blk, e_blk, rates, ones, token)


def norm_kernel(slot, info, bc, keep, recv, gain, _, *refs):
    uvs, out = refs[:-1], refs[-1]
    count, width = out.shape
    groups = bc.shape[1] // (2 * N)
    per = width // groups
    half = width // 2
    part = width // B_PARTS
    is_odd = info[0] == 1
    base = info[slot] * count

    def rows(j, _):
        to = pl.ds(pl.multiple_of(j * ROWS_C, ROWS_C), ROWS_C)
        at = pl.ds(pl.multiple_of(base + j * ROWS_C, ROWS_C), ROWS_C)
        for g in range(groups):
            c_mat = bc[at, 2 * N * g + N : 2 * N * (g + 1)]
            pieces = []
            squares = None
            for p in range(g * per // part, (g + 1) * per // part):
                start = p * part
                side = start // half
                lanes = slice(start - side * half, start - side * half + part)
                mine, other = keep[:, lanes], recv[:, lanes]
                inc = jnp.where(is_odd, other, mine) if side == 0 else jnp.where(is_odd, mine, other)
                gated = uvs[p][at, 0:part].astype(F32) + uvs[p][at, part:].astype(F32) * dot(c_mat, inc)
                square = jnp.sum(gated * gated, axis=-1, keepdims=True)
                squares = square if squares is None else squares + square
                pieces.append((start, gated))
            scale = lax.rsqrt(squares * (1.0 / per) + EPS)
            for start, gated in pieces:
                out[to, start : start + part] = (gated * scale * gain[:, start : start + part]).astype(BF16)
        return 0

    lax.fori_loop(0, count // ROWS_C, rows, 0)


def norm_rows(slot, info, count, token, bc, keep, recv, gain, uvs):
    return pl.pallas_call(
        functools.partial(norm_kernel, slot),
        in_specs=[SCALAR] + [FULL] * 4 + [ANY] + [FULL] * len(uvs),
        out_specs=FULL,
        out_shape=jax.ShapeDtypeStruct((count, gain.shape[1]), BF16),
        compiler_params=params(16),
        cost_estimate=CHEAP,
        name="norm_rows",
    )(info, bc, keep, recv, gain, token, *uvs)


def project_kernel(base, added, a0, a1, w0_far, w1_far, *refs):
    out, w0, w1, sem = refs[-4:]
    j = pl.program_id(0)
    tiles = pl.num_programs(0)

    def fetch(t):
        slot = lax.rem(t, SLOTS)
        lanes = pl.ds(pl.multiple_of((base + t) * TILE, TILE), TILE)
        return (
            pltpu.make_async_copy(w0_far.at[:, lanes], w0.at[slot], sem.at[0, slot]),
            pltpu.make_async_copy(w1_far.at[:, lanes], w1.at[slot], sem.at[1, slot]),
        )

    def start(t):
        @pl.when(t < tiles)
        def _():
            for copy in fetch(t):
                copy.start()

    @pl.when(j == 0)
    def _():
        for t in range(SLOTS - 1):
            start(t)

    start(j + SLOTS - 1)
    for copy in fetch(j):
        copy.wait()
    slot = lax.rem(j, SLOTS)
    total = dot(a0[...], w0[slot]) + dot(a1[...], w1[slot])
    if added:
        total = total + refs[0][...].astype(F32)
    out[...] = total.astype(out.dtype)


def project(a0, a1, w0, w1, first, count, kind, arrived=None, result=None):
    rows, depth = a0.shape
    base = first // TILE
    full = arrived is not None
    operands, specs = [a0, a1, w0, w1], [FULL, FULL, FAR, FAR]
    if full:
        operands.append(arrived)
        specs.append(pl.BlockSpec((rows, TILE), lambda j: (0, j)))
    if result is not None:
        operands.append(result)
        specs.append(ANY)
    return pl.pallas_call(
        functools.partial(project_kernel, base, full),
        grid=(count // TILE,),
        in_specs=specs,
        out_specs=pl.BlockSpec((rows, TILE), lambda j: (0, base + j if full else j)),
        out_shape=jax.ShapeDtypeStruct((rows, w0.shape[1] if full else count), kind),
        scratch_shapes=[
            pltpu.VMEM((SLOTS, depth, TILE), BF16),
            pltpu.VMEM((SLOTS, depth, TILE), BF16),
            pltpu.SemaphoreType.DMA((2, SLOTS)),
        ],
        input_output_aliases={} if result is None else {len(operands) - 1: 0},
        compiler_params=params(20),
        cost_estimate=CHEAP,
        name="project",
    )(*operands)


def project_both_kernel(base, a0_far, a1_far, a0_near, a1_near, w0_far, w1_far, far, near, a0, a1, w0, w1, sem):
    j = pl.program_id(0)
    tiles = pl.num_programs(0)
    rows = far.shape[0]

    def fetch(t):
        slot = lax.rem(t, SLOTS)
        lanes = pl.ds(pl.multiple_of((base + t) * TILE, TILE), TILE)
        return (
            pltpu.make_async_copy(w0_far.at[:, lanes], w0.at[slot], sem.at[0, slot]),
            pltpu.make_async_copy(w1_far.at[:, lanes], w1.at[slot], sem.at[1, slot]),
        )

    def start(t):
        @pl.when(t < tiles)
        def _():
            for copy in fetch(t):
                copy.start()

    @pl.when(j == 0)
    def _():
        for t in range(SLOTS - 1):
            start(t)
        a0[0:rows, :] = a0_far[...]
        a0[rows:, :] = a0_near[...]
        a1[0:rows, :] = a1_far[...]
        a1[rows:, :] = a1_near[...]

    start(j + SLOTS - 1)
    for copy in fetch(j):
        copy.wait()
    slot = lax.rem(j, SLOTS)
    total = dot(a0[...], w0[slot]) + dot(a1[...], w1[slot])
    far[...] = total[0:rows].astype(BF16)
    near[...] = total[rows:]


def project_both(far, far_mate, near, near_mate, w0, w1, first, count):
    rows, depth = far.shape
    placed = pl.BlockSpec((rows, TILE), lambda j: (0, j))
    return pl.pallas_call(
        functools.partial(project_both_kernel, first // TILE),
        grid=(count // TILE,),
        in_specs=[FULL] * 4 + [FAR] * 2,
        out_specs=[placed, placed],
        out_shape=[jax.ShapeDtypeStruct((rows, count), BF16), jax.ShapeDtypeStruct((rows, count), F32)],
        scratch_shapes=[
            pltpu.VMEM((2 * rows, depth), BF16),
            pltpu.VMEM((2 * rows, depth), BF16),
            pltpu.VMEM((SLOTS, depth, TILE), BF16),
            pltpu.VMEM((SLOTS, depth, TILE), BF16),
            pltpu.SemaphoreType.DMA((2, SLOTS)),
        ],
        compiler_params=params(24),
        cost_estimate=CHEAP,
        name="project_both",
    )(far, far_mate, near, near_mate, w0, w1)


def add_kernel(part, arrived, _, out):
    out[...] = (part[...] + arrived[...].astype(F32)).astype(BF16)


def add_chunk(part, arrived, result, first):
    rows, count = arrived.shape
    base = first // count
    return pl.pallas_call(
        add_kernel,
        grid=(1,),
        in_specs=[FULL, FULL, ANY],
        out_specs=pl.BlockSpec((rows, count), lambda j: (0, base)),
        out_shape=jax.ShapeDtypeStruct(result.shape, BF16),
        input_output_aliases={2: 0},
        compiler_params=params(8),
        cost_estimate=CHEAP,
        name="add_chunk",
    )(part, arrived, result)


def shift(block, distance):
    size = lax.axis_size("seq")
    return lax.ppermute(block, "seq", [(i, i + distance) for i in range(size - distance)])


def swap(block, axis, bit):
    return lax.ppermute(block, axis, [(i, i ^ bit) for i in range(lax.axis_size(axis))])


def rotate(block, turns, sends):
    pairs = lax.axis_size("seq") // 2
    route = [(2 * q + y, 2 * ((q + turns) % pairs) + y) for q in range(pairs) if sends(q) for y in (0, 1)]
    return lax.ppermute(block, "seq", route)


def log_steps(info, got, keep, rates, done, pairs, scan_next):
    half = keep.shape[1]
    message = ((N + EXTRA, half), BF16)
    full = ((N, half), F32)
    msg, own, first, aux = combine(
        pair_kernel,
        (info, got, keep, rates, done),
        [SCALAR, FULL, FULL, FULL, ANY],
        [message, full, full, ((16, half), F32)],
        "pair",
    )
    behind = None
    covered = 0
    while True:
        got = shift(msg, 2 * (covered + 1))
        done = scan_next(msg)
        covered = 2 * covered + 1
        if covered >= pairs - 1:
            break
        operands, specs = [got, own, aux], [FULL, FULL, FULL]
        if behind is None:
            kernel = lambda g, o, a, t, m, b: wave_kernel(g, o, a, None, t, m, b)
        else:
            kernel = wave_kernel
            operands.append(behind)
            specs.append(FULL)
        msg, behind = combine(kernel, operands + [done], specs + [ANY], [message, ((N + 8, half), F32)], "wave")
    operands, specs = [info, got], [SCALAR, FULL]
    if behind is None:
        kernel = lambda o, g, f, a, t, b, h: last_kernel(o, g, None, f, a, t, b, h)
    else:
        kernel = last_kernel
        operands.append(behind)
        specs.append(FULL)
    out = ((N, half), BF16)
    back, held = combine(kernel, operands + [first, aux, done], specs + [FULL, FULL, ANY], [out, out], "last")
    return back, held


def local(
    x_input,
    z_input,
    bc_input,
    conv_weight_x,
    conv_weight_bc,
    step_size,
    log_decay,
    skip_gain,
    norm_gain,
    out_weight,
):
    length, width = x_input.shape
    heads = step_size.shape[1]
    ways = lax.axis_size("head")
    pairs = lax.axis_size("seq") // 2
    mine = lax.axis_index("head")
    half = width // 2
    seq = lax.axis_index("seq")
    info = jnp.stack([seq & 1, mine ^ 3, mine ^ 2, mine ^ 1, mine, seq >> 1]).astype(jnp.int32)

    x_far, z_far, w_far = [pltpu.with_memory_space_constraint(v, pltpu.HBM) for v in (x_input, z_input, out_weight)]
    bc = bc_input.reshape(length, -1)
    halo = shift(jnp.concatenate([x_input[length - LEAD :], bc[length - LEAD :]], 1), 1)
    weight_mate = swap(out_weight, "head", 1)

    ones = jnp.asarray(np.tile(np.repeat(np.eye(heads), P_SIZE, axis=1), (2, 1)), BF16)
    cum, cum_s, log_s, f_dev, f_blk, e_blk, rates = decays(log_decay, step_size, skip_gain, ones)
    x_conv, bc_conv, keep, send = conv_states(
        info, x_far, bc, halo, conv_weight_x, conv_weight_bc, f_dev, ones, rates
    )

    x_conv = pltpu.with_memory_space_constraint(x_conv, pltpu.HBM)
    uvs = []

    def scan_next(token):
        if len(uvs) < B_PARTS:
            uvs.append(
                scan_part(len(uvs), token, x_conv, bc_conv, z_far, cum, cum_s, log_s, f_blk, e_blk, rates, ones)
            )
        return uvs[-1]

    message = ((N + EXTRA, half), BF16)
    full = ((N, half), F32)
    got = swap(send, "seq", 1)
    done = scan_next(send)
    out = ((N, half), BF16)
    if pairs > 1 and half % (pairs * N) == 0:
        piece = half // pairs
        part = ((N + EXTRA, piece), BF16)
        first, aux, *parts = combine(
            pair_split_kernel,
            (info, got, keep, rates, done),
            [SCALAR, FULL, FULL, FULL, ANY],
            [full, ((8, half), F32)] + [part] * pairs,
            "pair",
            [pltpu.VMEM(*message)],
        )
        parts = list(parts[:1]) + [rotate(parts[r], r, lambda q: q < pairs - 1) for r in range(1, pairs)]
        done = scan_next(parts[0])
        parts = combine(
            owner_kernel,
            [info] + parts + [done],
            [SCALAR] + [FULL] * pairs + [ANY],
            [((N, piece), BF16)] * pairs,
            "owner",
            [pltpu.VMEM((pairs, N + EXTRA, piece), BF16), pltpu.VMEM((pairs, N, piece), BF16)],
        )
        ready = parts[0]
        parts = list(parts[:1]) + [rotate(parts[r], r, lambda q: (q + r) % pairs > 0) for r in range(1, pairs)]
        done = scan_next(ready)
        back, held = combine(
            last_split_kernel,
            [info, first, aux, done] + parts,
            [SCALAR, FULL, FULL, ANY] + [FULL] * pairs,
            [out, out],
            "last",
            [pltpu.VMEM(*out)],
        )
    else:
        back, held = log_steps(info, got, keep, rates, done, pairs, scan_next)
    other = swap(back, "seq", 1)
    while len(uvs) < B_PARTS:
        scan_next(back)

    count = length // ways
    gain = norm_gain[None, :]

    def rows_for(slot, token):
        return norm_rows(slot, info, count, token, bc_conv, held, other, gain, uvs)

    far_mate = rows_for(1, held)
    far = rows_for(2, far_mate)
    far_mate = swap(far_mate, "head", 1)
    columns = out_weight.shape[1]
    quarter = columns // 4
    weights = (w_far, weight_mate)
    sent = project(far, far_mate, *weights, 0, quarter, BF16)
    arrivals = [swap(sent, "head", 2)]
    near_mate = rows_for(3, sent)
    near = rows_for(4, near_mate)
    near_mate = swap(near_mate, "head", 1)
    parts = []
    for c in range(quarter, columns, quarter):
        sent, part = project_both(far, far_mate, near, near_mate, *weights, c, quarter)
        arrivals.append(swap(sent, "head", 2))
        parts.append(part)
    result = project(near, near_mate, *weights, 0, quarter, BF16, arrivals[0])
    for c, part in enumerate(parts, 1):
        result = add_chunk(part, arrivals[c], result, c * quarter)
    return result


def solution(mesh):
    in_specs = (
        P("seq", "head"),
        P("seq", "head"),
        P("seq", "head", None),
        P(None, "head"),
        P(None, "head", None),
        P("seq", "head"),
        P("seq", "head"),
        P("head"),
        P("head"),
        P("head", None),
    )
    out_specs = P(("seq", "head"), None)
    return jax.shard_map(local, mesh=mesh, in_specs=in_specs, out_specs=out_specs, check_vma=False)
```

```python
import functools

import jax
import jax.numpy as jnp
import numpy as np
from jax import lax
from jax.experimental import pallas as pl
from jax.experimental.pallas import tpu as pltpu
from jax.sharding import PartitionSpec as P

P_SIZE = 64
N = 128
KCONV = 4
EPS = 1e-05
LOG2E = 1.4426950408889634

TOK_A = 256
ROWS_A = 32
TOK_B = 128
STEP_B = 256
EXTRA = 16
SLAB = 256
ROWS_C = 128
TILE = 256
SLOTS = 4
LEAD = 16
B_PARTS = 4
HIGHEST = lax.Precision.HIGHEST
F32 = jnp.float32
BF16 = jnp.bfloat16


def params(mib):
    return pltpu.CompilerParams(vmem_limit_bytes=mib * 1024 * 1024)


CHEAP = pl.CostEstimate(flops=1, bytes_accessed=1, transcendentals=0)
SCALAR = pl.BlockSpec(memory_space=pltpu.SMEM)
FULL = pl.BlockSpec(memory_space=pltpu.VMEM)
FAR = pl.BlockSpec(memory_space=pltpu.HBM)
ANY = pl.BlockSpec(memory_space=pl.ANY)


def dot(a, b, dims=((1,), (0,)), precision=None):
    return lax.dot_general(a, b, (dims, ((), ())), precision=precision, preferred_element_type=F32)


def half_silu(half):
    return half + half * jnp.tanh(half)


def whole(shape):
    return pl.BlockSpec(shape, lambda *_: (0,) * len(shape))


def decay_kernel(ld_t, step_t, skip, ones, cum, cum_s, log_s, f_dev, f_blk, e_blk, rates):
    heads, length = ld_t.shape
    blocks = length // TOK_B
    row = lax.broadcasted_iota(jnp.int32, (TOK_B, TOK_B), 0)
    col = lax.broadcasted_iota(jnp.int32, (TOK_B, TOK_B), 1)
    lower = (row >= col).astype(F32)
    upper = (row <= col).astype(F32)
    eye = (row == col).astype(BF16)

    def put(ref, rows, value):
        high = value.astype(BF16)
        low = (value - high.astype(F32)).astype(BF16)
        ref[rows, :] = dot(eye, jnp.concatenate([high, low], 0), ((1,), (1,))).astype(BF16)

    cums, totals, row_totals = [], [], []
    for b in range(blocks):
        rows = slice(b * TOK_B, (b + 1) * TOK_B)
        logs = ld_t[:, rows] * LOG2E
        c = dot(lower, logs, ((1,), (1,)), HIGHEST)
        cum[rows, :] = c
        row_totals.append(c[TOK_B - 1 : TOK_B, :])
        c = dot(logs, upper, precision=HIGHEST)
        cums.append(c)
        totals.append(c[:, TOK_B - 1 : TOK_B])
    before, row_before = [jnp.zeros_like(totals[0])], [jnp.zeros_like(row_totals[0])]
    for b in range(blocks):
        before.append(before[-1] + totals[b])
        row_before.append(row_before[-1] + row_totals[b])
    total = before[-1]
    logs = jnp.concatenate(row_totals + row_before[:-1] + row_before[-1:] * 8, 0)
    values = jnp.concatenate([jnp.exp2(logs), jnp.broadcast_to(skip[...], (8, heads))], 0)
    rates[...] = dot(values, ones[0:heads, :].astype(F32), precision=HIGHEST)
    for b in range(blocks):
        rows = slice(b * TOK_B, (b + 1) * TOK_B)
        s = step_t[:, rows]
        log_step = jnp.log2(s)
        log_s[:, rows] = log_step
        cum_s[:, rows] = cums[b] - log_step
        put(f_dev, rows, jnp.exp2(total - (cums[b] + before[b])) * s)
        put(f_blk, rows, jnp.exp2(totals[b] - cums[b]) * s)
        put(e_blk, rows, jnp.exp2(cums[b]))


def decays(log_decay, step, skip, ones):
    length, heads = log_decay.shape
    blocks = length // TOK_B
    width = ones.shape[1]
    wide = jax.ShapeDtypeStruct((heads, length), F32)
    pair = jax.ShapeDtypeStruct((length, 2 * heads), BF16)
    return pl.pallas_call(
        decay_kernel,
        out_shape=(
            jax.ShapeDtypeStruct((length, heads), F32),
            wide,
            wide,
            pair,
            pair,
            pair,
            jax.ShapeDtypeStruct((2 * blocks + 16, width), F32),
        ),
        compiler_params=params(16),
        name="decays",
    )(log_decay.T, step.T, skip[None, :], ones)


def put_message(ref, state, decay):
    high = decay.astype(BF16)
    low = (decay - high.astype(F32)).astype(BF16)
    rest = jnp.zeros((EXTRA - 2, state.shape[1]), BF16)
    ref[0:N, :] = state.astype(BF16)
    ref[N:, :] = jnp.concatenate([high, low, rest], 0)


def take_message(ref):
    extra = ref[N:, :].astype(F32)
    return ref[0:N, :].astype(F32), extra[0:1] + extra[1:2]


def conv_kernel(info, x_far, bc, halo, wx, wbc, f_dev, ones, rates, x_out, bc_out, send, x, sem, xf, state):
    i = pl.program_id(0)
    rows, width = x_out.shape
    bc_width = bc.shape[1]
    groups = bc_width // (2 * N)
    per = width // groups

    def fetch(step):
        piece = pl.ds(pl.multiple_of(step * rows, rows), rows)
        return pltpu.make_async_copy(x_far.at[piece], x.at[piece], sem.at[step])

    @pl.when(i == 0)
    def _():
        fetch(0).start()
        state[...] = jnp.zeros_like(state)

    base = pl.multiple_of(i * rows, rows)
    before = pl.ds(pl.multiple_of(jnp.maximum(base - LEAD, 0), LEAD), LEAD)

    def at(r):
        return pl.ds(pl.multiple_of(base + r, ROWS_A), ROWS_A)

    def conv(src, lead, weights, emit):
        w0, w1, w2, w3 = [w * 0.5 for w in weights]
        back = LEAD - 8
        r1 = pltpu.roll(lead, 1, 0)
        last_x, last_p = lead[back:], (w1 * lead + w0 * r1)[back:]
        for r in range(0, rows, ROWS_A):
            cur = src(r).astype(F32)
            r1 = pltpu.roll(jnp.concatenate([last_x, cur], 0), 1, 0)[8:]
            p = w1 * cur + w0 * r1
            p2 = pltpu.roll(jnp.concatenate([last_p, p], 0), 2, 0)[8:]
            emit(r, half_silu((w3 * cur + w2 * r1) + p2))
            last_x, last_p = cur[ROWS_A - 8 :], p[ROWS_A - 8 :]

    start = i == 0

    def halo_of(lanes):
        value = halo[:, lanes]
        return jnp.where(info[0] == 0, jnp.zeros_like(value), value)

    for c in range(groups):
        for lanes in range(c * 2 * N, (c + 1) * 2 * N, N):
            ds = slice(lanes, lanes + N)

            def emit_bc(r, value):
                bc_out[r : r + ROWS_A, ds] = value.astype(BF16)

            lead = jnp.where(start, halo_of(slice(width + lanes, width + lanes + N)), bc[before, ds]).astype(F32)
            inner = slice(lanes - c * 2 * N, lanes - c * 2 * N + N)
            conv(lambda r: bc[at(r), ds], lead, [wbc[k, c : c + 1, inner] for k in range(KCONV)], emit_bc)

    fetch(i).wait()

    @pl.when(i + 1 < pl.num_programs(0))
    def _():
        fetch(i + 1).start()

    def slab(c, _):
        first = pl.multiple_of(c * SLAB, SLAB)
        scale = dot(f_dev[pl.ds(base, rows), :], ones[:, pl.ds(first, SLAB)])
        ds = pl.ds(first, SLAB)

        def emit(r, value):
            value = value.astype(BF16)
            x_out[r : r + ROWS_A, ds] = value
            xf[r : r + ROWS_A, ds] = (value.astype(F32) * scale[r : r + ROWS_A]).astype(BF16)

        lead = jnp.where(start, halo_of(ds), x[before, ds]).astype(F32)
        conv(lambda r: x[at(r), ds], lead, [wx[k : k + 1, ds] for k in range(KCONV)], emit)
        return 0

    lax.fori_loop(0, width // SLAB, slab, 0)
    for g in range(groups):
        b_mat = bc_out[:, 2 * N * g : 2 * N * g + N]
        lanes = slice(g * per, (g + 1) * per)
        state[:, lanes] += dot(b_mat, xf[:, lanes], ((0,), (0,)))

    @pl.when(i == pl.num_programs(0) - 1)
    def _():
        row = rates.shape[0] - 16
        piece = send.shape[2]
        for owner in range(send.shape[0]):
            lanes = slice(owner * piece, (owner + 1) * piece)
            put_message(send.at[owner], state[:, lanes], rates[row : row + 1, lanes])


def conv_states(owners, info, x, bc, halo, wx, wbc, f_dev, ones, rates):
    length, width = x.shape
    bc_width = bc.shape[1]
    sent = (owners, N + EXTRA, width // owners)
    return pl.pallas_call(
        conv_kernel,
        grid=(length // TOK_A,),
        in_specs=[SCALAR, FAR] + [FULL] * 7,
        out_specs=[
            pl.BlockSpec((TOK_A, width), lambda i: (i, 0)),
            pl.BlockSpec((TOK_A, bc_width), lambda i: (i, 0)),
            whole(sent),
        ],
        scratch_shapes=[
            pltpu.VMEM((length, width), BF16),
            pltpu.SemaphoreType.DMA((length // TOK_A,)),
            pltpu.VMEM((TOK_A, width), BF16),
            pltpu.VMEM((N, width), F32),
        ],
        out_shape=(
            pltpu.HBM((length, width), BF16),
            jax.ShapeDtypeStruct((length, bc_width), BF16),
            jax.ShapeDtypeStruct(sent, BF16),
        ),
        compiler_params=params(20),
        cost_estimate=CHEAP,
        name="conv_states",
    )(info, x, bc, halo, wx, wbc, f_dev, ones, rates)


def prefix_kernel(states, _, prefixes):
    before = jnp.zeros(prefixes.shape[1:], F32)
    for device in range(states.shape[0]):
        prefixes[device] = before.astype(BF16)
        state, decay = take_message(states.at[device])
        before = decay * before + state


def prefix(states, token):
    devices, rows, piece = states.shape
    return pl.pallas_call(
        prefix_kernel,
        in_specs=[FULL, ANY],
        out_specs=FULL,
        out_shape=jax.ShapeDtypeStruct((devices, rows - EXTRA, piece), BF16),
        compiler_params=params(16),
        cost_estimate=CHEAP,
        name="prefix",
    )(states, token)


def scan_kernel(part, x_far, z_far, bc_all, cum, cum_s, log_s, f_blk, e_blk, rates, ones, _, uv_out, x, z, sem, state):
    length, width = x.shape
    per_slab = SLAB // P_SIZE
    head0 = part * width // P_SIZE
    first_lane = part * width
    inner = STEP_B // TOK_B
    blocks = length // TOK_B
    group = first_lane * (bc_all.shape[1] // (2 * N)) // (width * B_PARTS)
    b_lanes = slice(2 * N * group, 2 * N * group + N)
    c_lanes = slice(2 * N * group + N, 2 * N * (group + 1))

    def fetch(step):
        piece = pl.ds(pl.multiple_of(step * STEP_B, STEP_B), STEP_B)
        lanes = pl.ds(first_lane, width)
        return (
            pltpu.make_async_copy(x_far.at[piece, lanes], x.at[piece], sem.at[0, step]),
            pltpu.make_async_copy(z_far.at[piece, lanes], z.at[piece], sem.at[1, step]),
        )

    for step in range(length // STEP_B):
        for copy in fetch(step):
            copy.start()
    state[...] = jnp.zeros_like(state)

    row = lax.broadcasted_iota(jnp.int32, (TOK_B, TOK_B), 0)
    col = lax.broadcasted_iota(jnp.int32, (TOK_B, TOK_B), 1)
    keep = row >= col
    first = lax.broadcasted_iota(jnp.int32, (TOK_B, 2 * P_SIZE), 1) < P_SIZE
    zero = jnp.zeros((TOK_B, 2 * P_SIZE), BF16)

    def turn(step, _):
        for copy in fetch(step):
            copy.wait()
        for k in range(inner):
            block(step * inner + k)
        return 0

    def block(b):
        at = pl.ds(pl.multiple_of(b * TOK_B, TOK_B), TOK_B)
        b_mat = bc_all[at, b_lanes]
        c_mat = bc_all[at, c_lanes]
        scores = jnp.where(keep, dot(c_mat, b_mat, ((1,), (1,))), 0.0)
        wide = pl.ds(first_lane, width)
        fade_rows = rates[pl.ds(b, 1), wide]
        lead_rows = rates[pl.ds(blocks + b, 1), wide]
        skip = rates[2 * blocks + 8 : 2 * blocks + 9, wide]
        for s in range(width // SLAB):
            lanes = slice(s * SLAB, (s + 1) * SLAB)
            xb = x[at, lanes]
            sel = ones[:, first_lane + s * SLAB : first_lane + (s + 1) * SLAB]
            old = state[:, lanes]
            rise = dot(e_blk[at, :], sel)
            carried = dot(c_mat, old.astype(BF16)) * rise
            within = []
            for q in range(per_slab // 2):
                tables = []
                for h in (2 * q, 2 * q + 1):
                    head = head0 + s * per_slab + h
                    column = cum[at, head : head + 1]
                    gap = jnp.minimum(column - cum_s[head : head + 1, at], log_s[head : head + 1, at])
                    tables.append((scores * jnp.exp2(gap)).astype(BF16))
                xp = xb[:, q * 2 * P_SIZE : (q + 1) * 2 * P_SIZE]
                stacked = jnp.concatenate([jnp.where(first, xp, zero), jnp.where(first, zero, xp)], 0)
                within.append(dot(jnp.concatenate(tables, 1), stacked))
            xs = xb.astype(F32)
            y = jnp.concatenate(within, 1) + carried + skip[:, lanes] * xs
            gate = half_silu((z[at, lanes] * 0.5).astype(F32))
            uv_out[at, lanes] = (y * gate).astype(BF16)
            uv_out[at, width + s * SLAB : width + (s + 1) * SLAB] = (gate * rise * lead_rows[:, lanes]).astype(BF16)
            xf = (xs * dot(f_blk[at, :], sel)).astype(BF16)
            state[:, lanes] = old * fade_rows[:, lanes] + dot(b_mat, xf, ((0,), (0,)))

    lax.fori_loop(0, length // STEP_B, turn, 0)


def scan_part(part, token, x, bc, z, cum, cum_s, log_s, f_blk, e_blk, rates, ones):
    length, full = x.shape
    width = full // B_PARTS
    return pl.pallas_call(
        functools.partial(scan_kernel, part),
        in_specs=[FAR, FAR] + [FULL] * 8 + [ANY],
        out_specs=FULL,
        out_shape=jax.ShapeDtypeStruct((length, 2 * width), BF16),
        scratch_shapes=[
            pltpu.VMEM((length, width), BF16),
            pltpu.VMEM((length, width), BF16),
            pltpu.SemaphoreType.DMA((2, length // STEP_B)),
            pltpu.VMEM((N, width), F32),
        ],
        compiler_params=params(16),
        cost_estimate=CHEAP,
        name="scan_part",
    )(x, z, bc, cum, cum_s, log_s, f_blk, e_blk, rates, ones, token)


def norm_kernel(slot, info, bc, entering, gain, _, *refs):
    uvs, out = refs[:-1], refs[-1]
    count, width = out.shape
    groups = bc.shape[1] // (2 * N)
    per = width // groups
    part = width // B_PARTS
    piece = entering.shape[2]
    base = info[slot] * count

    def rows(j, _):
        to = pl.ds(pl.multiple_of(j * ROWS_C, ROWS_C), ROWS_C)
        at = pl.ds(pl.multiple_of(base + j * ROWS_C, ROWS_C), ROWS_C)
        for g in range(groups):
            c_mat = bc[at, 2 * N * g + N : 2 * N * (g + 1)]
            pieces = []
            squares = None
            for p in range(g * per // part, (g + 1) * per // part):
                start = p * part
                inc = jnp.concatenate([entering[k] for k in range(start // piece, (start + part) // piece)], 1)
                gated = uvs[p][at, 0:part].astype(F32) + uvs[p][at, part:].astype(F32) * dot(c_mat, inc)
                square = jnp.sum(gated * gated, axis=-1, keepdims=True)
                squares = square if squares is None else squares + square
                pieces.append((start, gated))
            scale = lax.rsqrt(squares * (1.0 / per) + EPS)
            for start, gated in pieces:
                out[to, start : start + part] = (gated * scale * gain[:, start : start + part]).astype(BF16)
        return 0

    lax.fori_loop(0, count // ROWS_C, rows, 0)


def norm_rows(slot, info, count, token, bc, entering, gain, uvs):
    return pl.pallas_call(
        functools.partial(norm_kernel, slot),
        in_specs=[SCALAR] + [FULL] * 3 + [ANY] + [FULL] * len(uvs),
        out_specs=FULL,
        out_shape=jax.ShapeDtypeStruct((count, gain.shape[1]), BF16),
        compiler_params=params(16),
        cost_estimate=CHEAP,
        name="norm_rows",
    )(info, bc, entering, gain, token, *uvs)


def project_kernel(base, added, a0, a1, w0_far, w1_far, *refs):
    out, w0, w1, sem = refs[-4:]
    j = pl.program_id(0)
    tiles = pl.num_programs(0)

    def fetch(t):
        slot = lax.rem(t, SLOTS)
        lanes = pl.ds(pl.multiple_of((base + t) * TILE, TILE), TILE)
        return (
            pltpu.make_async_copy(w0_far.at[:, lanes], w0.at[slot], sem.at[0, slot]),
            pltpu.make_async_copy(w1_far.at[:, lanes], w1.at[slot], sem.at[1, slot]),
        )

    def start(t):
        @pl.when(t < tiles)
        def _():
            for copy in fetch(t):
                copy.start()

    @pl.when(j == 0)
    def _():
        for t in range(SLOTS - 1):
            start(t)

    start(j + SLOTS - 1)
    for copy in fetch(j):
        copy.wait()
    slot = lax.rem(j, SLOTS)
    total = dot(a0[...], w0[slot]) + dot(a1[...], w1[slot])
    if added:
        total = total + refs[0][...].astype(F32)
    out[...] = total.astype(out.dtype)


def project(a0, a1, w0, w1, first, count, kind, arrived=None, result=None):
    rows, depth = a0.shape
    base = first // TILE
    full = arrived is not None
    operands, specs = [a0, a1, w0, w1], [FULL, FULL, FAR, FAR]
    if full:
        operands.append(arrived)
        specs.append(pl.BlockSpec((rows, TILE), lambda j: (0, j)))
    if result is not None:
        operands.append(result)
        specs.append(ANY)
    return pl.pallas_call(
        functools.partial(project_kernel, base, full),
        grid=(count // TILE,),
        in_specs=specs,
        out_specs=pl.BlockSpec((rows, TILE), lambda j: (0, base + j if full else j)),
        out_shape=jax.ShapeDtypeStruct((rows, w0.shape[1] if full else count), kind),
        scratch_shapes=[
            pltpu.VMEM((SLOTS, depth, TILE), BF16),
            pltpu.VMEM((SLOTS, depth, TILE), BF16),
            pltpu.SemaphoreType.DMA((2, SLOTS)),
        ],
        input_output_aliases={} if result is None else {len(operands) - 1: 0},
        compiler_params=params(20),
        cost_estimate=CHEAP,
        name="project",
    )(*operands)


def project_both_kernel(base, a0_far, a1_far, a0_near, a1_near, w0_far, w1_far, far, near, a0, a1, w0, w1, sem):
    j = pl.program_id(0)
    tiles = pl.num_programs(0)
    rows = far.shape[0]

    def fetch(t):
        slot = lax.rem(t, SLOTS)
        lanes = pl.ds(pl.multiple_of((base + t) * TILE, TILE), TILE)
        return (
            pltpu.make_async_copy(w0_far.at[:, lanes], w0.at[slot], sem.at[0, slot]),
            pltpu.make_async_copy(w1_far.at[:, lanes], w1.at[slot], sem.at[1, slot]),
        )

    def start(t):
        @pl.when(t < tiles)
        def _():
            for copy in fetch(t):
                copy.start()

    @pl.when(j == 0)
    def _():
        for t in range(SLOTS - 1):
            start(t)
        a0[0:rows, :] = a0_far[...]
        a0[rows:, :] = a0_near[...]
        a1[0:rows, :] = a1_far[...]
        a1[rows:, :] = a1_near[...]

    start(j + SLOTS - 1)
    for copy in fetch(j):
        copy.wait()
    slot = lax.rem(j, SLOTS)
    total = dot(a0[...], w0[slot]) + dot(a1[...], w1[slot])
    far[...] = total[0:rows].astype(BF16)
    near[...] = total[rows:]


def project_both(far, far_mate, near, near_mate, w0, w1, first, count):
    rows, depth = far.shape
    placed = pl.BlockSpec((rows, TILE), lambda j: (0, j))
    return pl.pallas_call(
        functools.partial(project_both_kernel, first // TILE),
        grid=(count // TILE,),
        in_specs=[FULL] * 4 + [FAR] * 2,
        out_specs=[placed, placed],
        out_shape=[jax.ShapeDtypeStruct((rows, count), BF16), jax.ShapeDtypeStruct((rows, count), F32)],
        scratch_shapes=[
            pltpu.VMEM((2 * rows, depth), BF16),
            pltpu.VMEM((2 * rows, depth), BF16),
            pltpu.VMEM((SLOTS, depth, TILE), BF16),
            pltpu.VMEM((SLOTS, depth, TILE), BF16),
            pltpu.SemaphoreType.DMA((2, SLOTS)),
        ],
        compiler_params=params(24),
        cost_estimate=CHEAP,
        name="project_both",
    )(far, far_mate, near, near_mate, w0, w1)


def add_kernel(part, arrived, _, out):
    out[...] = (part[...] + arrived[...].astype(F32)).astype(BF16)


def add_chunk(part, arrived, result, first):
    rows, count = arrived.shape
    base = first // count
    return pl.pallas_call(
        add_kernel,
        grid=(1,),
        in_specs=[FULL, FULL, ANY],
        out_specs=pl.BlockSpec((rows, count), lambda j: (0, base)),
        out_shape=jax.ShapeDtypeStruct(result.shape, BF16),
        input_output_aliases={2: 0},
        compiler_params=params(8),
        cost_estimate=CHEAP,
        name="add_chunk",
    )(part, arrived, result)


def shift(block, axis):
    size = lax.axis_size(axis)
    return lax.ppermute(block, axis, [(i, (i + 1) % size) for i in range(size)])


def swap(block, axis, bit):
    return lax.ppermute(block, axis, [(i, i ^ bit) for i in range(lax.axis_size(axis))])


def local(
    x_input,
    z_input,
    bc_input,
    conv_weight_x,
    conv_weight_bc,
    step_size,
    log_decay,
    skip_gain,
    norm_gain,
    out_weight,
):
    length, width = x_input.shape
    heads = step_size.shape[1]
    ways = lax.axis_size("head")
    devices = lax.axis_size("seq")
    mine = lax.axis_index("head")
    seq = lax.axis_index("seq")
    info = jnp.stack([seq, mine ^ 3, mine ^ 2, mine ^ 1, mine]).astype(jnp.int32)

    x_far, z_far, w_far = [pltpu.with_memory_space_constraint(v, pltpu.HBM) for v in (x_input, z_input, out_weight)]
    bc = bc_input.reshape(length, -1)
    halo = shift(jnp.concatenate([x_input[length - LEAD :], bc[length - LEAD :]], 1), "seq")
    weight_mate = swap(out_weight, "head", 1)

    ones = jnp.asarray(np.tile(np.repeat(np.eye(heads), P_SIZE, axis=1), (2, 1)), BF16)
    cum, cum_s, log_s, f_dev, f_blk, e_blk, rates = decays(log_decay, step_size, skip_gain, ones)
    x_conv, bc_conv, send = conv_states(
        devices, info, x_far, bc, halo, conv_weight_x, conv_weight_bc, f_dev, ones, rates
    )

    x_conv = pltpu.with_memory_space_constraint(x_conv, pltpu.HBM)
    uvs = []

    def scan_next(token):
        uvs.append(
            scan_part(len(uvs), token, x_conv, bc_conv, z_far, cum, cum_s, log_s, f_blk, e_blk, rates, ones)
        )
        return uvs[-1]

    states = lax.all_to_all(send, "seq", 0, 0)
    done = send
    for _ in range(B_PARTS // 2):
        done = scan_next(done)
    prefixes = prefix(states, done)
    entering = lax.all_to_all(prefixes, "seq", 0, 0)
    done = prefixes
    while len(uvs) < B_PARTS:
        done = scan_next(done)

    count = length // ways
    gain = norm_gain[None, :]

    def rows_for(slot, token):
        return norm_rows(slot, info, count, token, bc_conv, entering, gain, uvs)

    far_mate = rows_for(1, done)
    far = rows_for(2, far_mate)
    far_mate = swap(far_mate, "head", 1)
    columns = out_weight.shape[1]
    quarter = columns // 4
    weights = (w_far, weight_mate)
    sent = project(far, far_mate, *weights, 0, quarter, BF16)
    arrivals = [swap(sent, "head", 2)]
    near_mate = rows_for(3, sent)
    near = rows_for(4, near_mate)
    near_mate = swap(near_mate, "head", 1)
    parts = []
    for c in range(quarter, columns, quarter):
        sent, part = project_both(far, far_mate, near, near_mate, *weights, c, quarter)
        arrivals.append(swap(sent, "head", 2))
        parts.append(part)
    result = project(near, near_mate, *weights, 0, quarter, BF16, arrivals[0])
    for c, part in enumerate(parts, 1):
        result = add_chunk(part, arrivals[c], result, c * quarter)
    return result


def solution(mesh):
    in_specs = (
        P("seq", "head"),
        P("seq", "head"),
        P("seq", "head", None),
        P(None, "head"),
        P(None, "head", None),
        P("seq", "head"),
        P("seq", "head"),
        P("head"),
        P("head"),
        P("head", None),
    )
    out_specs = P(("seq", "head"), None)
    return jax.shard_map(local, mesh=mesh, in_specs=in_specs, out_specs=out_specs, check_vma=False)
```

```python
import functools

import jax
import jax.numpy as jnp
import numpy as np
from jax import lax
from jax.experimental import pallas as pl
from jax.experimental.pallas import tpu as pltpu
from jax.sharding import PartitionSpec as P

P_SIZE = 64
N = 128
KCONV = 4
EPS = 1e-05
LOG2E = 1.4426950408889634

TOK_A = 256
ROWS_A = 32
TOK_B = 128
STEP_B = 256
EXTRA = 16
SLAB = 256
ROWS_C = 128
HALF_C = 512
TILE = 256
SLOTS = 4
LEAD = 16
B_PARTS = 2
HIGHEST = lax.Precision.HIGHEST
F32 = jnp.float32
BF16 = jnp.bfloat16


def params(mib):
    return pltpu.CompilerParams(vmem_limit_bytes=mib * 1024 * 1024)


CHEAP = pl.CostEstimate(flops=1, bytes_accessed=1, transcendentals=0)
SCALAR = pl.BlockSpec(memory_space=pltpu.SMEM)
FULL = pl.BlockSpec(memory_space=pltpu.VMEM)
FAR = pl.BlockSpec(memory_space=pltpu.HBM)
ANY = pl.BlockSpec(memory_space=pl.ANY)


def dot(a, b, dims=((1,), (0,)), precision=None):
    return lax.dot_general(a, b, (dims, ((), ())), precision=precision, preferred_element_type=F32)


def half_silu(half):
    return half + half * jnp.tanh(half)


def far(*arrays):
    return [pltpu.with_memory_space_constraint(a, pltpu.HBM) for a in arrays]


def whole(shape):
    return pl.BlockSpec(shape, lambda *_: (0,) * len(shape))


def decay_kernel(ld_t, step_t, skip, ones, cum, cum_s, log_s, f_dev, f_blk, e_blk, rates):
    heads, length = ld_t.shape
    blocks = length // TOK_B
    row = lax.broadcasted_iota(jnp.int32, (TOK_B, TOK_B), 0)
    col = lax.broadcasted_iota(jnp.int32, (TOK_B, TOK_B), 1)
    lower = (row >= col).astype(F32)
    upper = (row <= col).astype(F32)
    eye = (row == col).astype(BF16)

    def put(ref, rows, value):
        high = value.astype(BF16)
        low = (value - high.astype(F32)).astype(BF16)
        ref[rows, :] = dot(eye, jnp.concatenate([high, low], 0), ((1,), (1,))).astype(BF16)

    cums, totals, row_totals = [], [], []
    for b in range(blocks):
        rows = slice(b * TOK_B, (b + 1) * TOK_B)
        logs = ld_t[:, rows] * LOG2E
        c = dot(lower, logs, ((1,), (1,)), HIGHEST)
        cum[rows, :] = c
        row_totals.append(c[TOK_B - 1 : TOK_B, :])
        c = dot(logs, upper, precision=HIGHEST)
        cums.append(c)
        totals.append(c[:, TOK_B - 1 : TOK_B])
    before, row_before = [jnp.zeros_like(totals[0])], [jnp.zeros_like(row_totals[0])]
    for b in range(blocks):
        before.append(before[-1] + totals[b])
        row_before.append(row_before[-1] + row_totals[b])
    total = before[-1]
    logs = jnp.concatenate(row_totals + row_before[:-1] + row_before[-1:] * 8, 0)
    values = jnp.concatenate([jnp.exp2(logs), jnp.broadcast_to(skip[...], (8, heads))], 0)
    rates[...] = dot(values, ones[0:heads, :].astype(F32), precision=HIGHEST)
    for b in range(blocks):
        rows = slice(b * TOK_B, (b + 1) * TOK_B)
        s = step_t[:, rows]
        log_step = jnp.log2(s)
        log_s[:, rows] = log_step
        cum_s[:, rows] = cums[b] - log_step
        put(f_dev, rows, jnp.exp2(total - (cums[b] + before[b])) * s)
        put(f_blk, rows, jnp.exp2(totals[b] - cums[b]) * s)
        put(e_blk, rows, jnp.exp2(cums[b]))


def decays(log_decay, step, skip, ones):
    length, heads = log_decay.shape
    blocks = length // TOK_B
    width = ones.shape[1]
    wide = pltpu.HBM((heads, length), F32)
    pair = pltpu.HBM((length, 2 * heads), BF16)
    return pl.pallas_call(
        decay_kernel,
        out_shape=(
            pltpu.HBM((length, heads), F32),
            wide,
            wide,
            pair,
            pair,
            pair,
            pltpu.HBM((2 * blocks + 16, width), F32),
        ),
        compiler_params=params(16),
        name="decays",
    )(log_decay.T, step.T, skip[None, :], ones)


def put_message(ref, state, decay):
    high = decay.astype(BF16)
    low = (decay - high.astype(F32)).astype(BF16)
    rest = jnp.zeros((EXTRA - 2, state.shape[1]), BF16)
    ref[0:N, :] = state.astype(BF16)
    ref[N:, :] = jnp.concatenate([high, low, rest], 0)


def take_message(ref):
    extra = ref[N:, :].astype(F32)
    return ref[0:N, :].astype(F32), extra[0:1] + extra[1:2]


def conv_kernel(info, x_far, bc, halo, wx, wbc, f_dev, ones, rates, x_out, bc_out, send, x, sem, xf, state):
    i = pl.program_id(0)
    rows, width = x_out.shape
    bc_width = bc.shape[1]
    groups = bc_width // (2 * N)
    per = width // groups

    def fetch(step):
        piece = pl.ds(pl.multiple_of(step * rows, rows), rows)
        return pltpu.make_async_copy(x_far.at[piece], x.at[piece], sem.at[step])

    @pl.when(i == 0)
    def _():
        fetch(0).start()
        state[...] = jnp.zeros_like(state)

    base = pl.multiple_of(i * rows, rows)
    before = pl.ds(pl.multiple_of(jnp.maximum(base - LEAD, 0), LEAD), LEAD)

    def at(r):
        return pl.ds(pl.multiple_of(base + r, ROWS_A), ROWS_A)

    def conv(src, lead, weights, emit):
        w0, w1, w2, w3 = [w * 0.5 for w in weights]
        back = LEAD - 8
        r1 = pltpu.roll(lead, 1, 0)
        last_x, last_p = lead[back:], (w1 * lead + w0 * r1)[back:]
        for r in range(0, rows, ROWS_A):
            cur = src(r).astype(F32)
            r1 = pltpu.roll(jnp.concatenate([last_x, cur], 0), 1, 0)[8:]
            p = w1 * cur + w0 * r1
            p2 = pltpu.roll(jnp.concatenate([last_p, p], 0), 2, 0)[8:]
            emit(r, half_silu((w3 * cur + w2 * r1) + p2))
            last_x, last_p = cur[ROWS_A - 8 :], p[ROWS_A - 8 :]

    start = i == 0

    def halo_of(lanes):
        value = halo[:, lanes]
        return jnp.where(info[0] == 0, jnp.zeros_like(value), value)

    for c in range(groups):
        for lanes in range(c * 2 * N, (c + 1) * 2 * N, N):
            ds = slice(lanes, lanes + N)

            def emit_bc(r, value):
                bc_out[r : r + ROWS_A, ds] = value.astype(BF16)

            lead = jnp.where(start, halo_of(slice(width + lanes, width + lanes + N)), bc[before, ds]).astype(F32)
            inner = slice(lanes - c * 2 * N, lanes - c * 2 * N + N)
            conv(lambda r: bc[at(r), ds], lead, [wbc[k, c : c + 1, inner] for k in range(KCONV)], emit_bc)

    fetch(i).wait()

    @pl.when(i + 1 < pl.num_programs(0))
    def _():
        fetch(i + 1).start()

    def slab(c, _):
        first = pl.multiple_of(c * SLAB, SLAB)
        scale = dot(f_dev[pl.ds(base, rows), :], ones[:, pl.ds(first, SLAB)])
        ds = pl.ds(first, SLAB)

        def emit(r, value):
            value = value.astype(BF16)
            x_out[r : r + ROWS_A, ds] = value
            xf[r : r + ROWS_A, ds] = (value.astype(F32) * scale[r : r + ROWS_A]).astype(BF16)

        lead = jnp.where(start, halo_of(ds), x[before, ds]).astype(F32)
        conv(lambda r: x[at(r), ds], lead, [wx[k : k + 1, ds] for k in range(KCONV)], emit)
        return 0

    lax.fori_loop(0, width // SLAB, slab, 0)
    for g in range(groups):
        b_mat = bc_out[:, 2 * N * g : 2 * N * g + N]
        lanes = slice(g * per, (g + 1) * per)
        state[:, lanes] += dot(b_mat, xf[:, lanes], ((0,), (0,)))

    @pl.when(i == pl.num_programs(0) - 1)
    def _():
        row = rates.shape[0] - 16
        piece = send.shape[2]
        for owner in range(send.shape[0]):
            lanes = slice(owner * piece, (owner + 1) * piece)
            put_message(send.at[owner], state[:, lanes], rates[row : row + 1, lanes])


def conv_states(owners, info, x, bc, halo, wx, wbc, f_dev, ones, rates):
    length, width = x.shape
    bc_width = bc.shape[1]
    sent = (owners, N + EXTRA, width // owners)
    return pl.pallas_call(
        conv_kernel,
        grid=(length // TOK_A,),
        in_specs=[SCALAR, FAR] + [FULL] * 7,
        out_specs=[
            pl.BlockSpec((TOK_A, width), lambda i: (i, 0)),
            pl.BlockSpec((TOK_A, bc_width), lambda i: (i, 0)),
            whole(sent),
        ],
        scratch_shapes=[
            pltpu.VMEM((length, width), BF16),
            pltpu.SemaphoreType.DMA((length // TOK_A,)),
            pltpu.VMEM((TOK_A, width), BF16),
            pltpu.VMEM((N, width), F32),
        ],
        out_shape=(
            pltpu.HBM((length, width), BF16),
            pltpu.HBM((length, bc_width), BF16),
            pltpu.HBM(sent, BF16),
        ),
        compiler_params=params(20),
        cost_estimate=CHEAP,
        name="conv_states",
    )(info, x, bc, halo, wx, wbc, f_dev, ones, rates)


def prefix_kernel(states, _, prefixes):
    before = jnp.zeros(prefixes.shape[1:], F32)
    for device in range(states.shape[0]):
        prefixes[device] = before.astype(BF16)
        state, decay = take_message(states.at[device])
        before = decay * before + state


def prefix(states, token):
    devices, rows, piece = states.shape
    return pl.pallas_call(
        prefix_kernel,
        in_specs=[FULL, ANY],
        out_specs=FULL,
        out_shape=pltpu.HBM((devices, rows - EXTRA, piece), BF16),
        compiler_params=params(16),
        cost_estimate=CHEAP,
        name="prefix",
    )(states, token)


def scan_kernel(part, *refs):
    sources, uv_far = refs[:10], refs[11]
    bc, cum, cum_s, log_s, f_blk, e_blk, rates, ones, x, z, uv, state, small_sem, sem, out_sem = refs[12:]
    length, width = x.shape
    per_slab = SLAB // P_SIZE
    head0 = part * width // P_SIZE
    inner = STEP_B // TOK_B
    blocks = length // TOK_B
    wide = pl.ds(part * width, width)
    x_far, z_far, bc_far = sources[:3]
    group = part * (bc_far.shape[1] // (2 * N)) // B_PARTS
    halves = (bc_far.at[:, pl.ds(2 * N * group, 2 * N)],) + sources[3:8]
    halves += (sources[8].at[:, wide], sources[9].at[:, wide])
    small = [
        pltpu.make_async_copy(source, target, small_sem.at[k])
        for k, (source, target) in enumerate(zip(halves, (bc, cum, cum_s, log_s, f_blk, e_blk, rates, ones)))
    ]

    def rows_of(step):
        return pl.ds(pl.multiple_of(step * STEP_B, STEP_B), STEP_B)

    def fetch(step):
        return (
            pltpu.make_async_copy(x_far.at[rows_of(step), wide], x.at[rows_of(step)], sem.at[0, step]),
            pltpu.make_async_copy(z_far.at[rows_of(step), wide], z.at[rows_of(step)], sem.at[1, step]),
        )

    def store(step):
        return pltpu.make_async_copy(uv.at[rows_of(step)], uv_far.at[rows_of(step)], out_sem.at[step])

    for copy in small:
        copy.start()
    for step in range(length // STEP_B):
        for copy in fetch(step):
            copy.start()
    state[...] = jnp.zeros_like(state)
    for copy in small:
        copy.wait()

    row = lax.broadcasted_iota(jnp.int32, (TOK_B, TOK_B), 0)
    col = lax.broadcasted_iota(jnp.int32, (TOK_B, TOK_B), 1)
    keep = row >= col
    first = lax.broadcasted_iota(jnp.int32, (TOK_B, 2 * P_SIZE), 1) < P_SIZE
    zero = jnp.zeros((TOK_B, 2 * P_SIZE), BF16)

    def turn(step, _):
        for copy in fetch(step):
            copy.wait()
        for k in range(inner):
            block(step * inner + k)
        store(step).start()
        return 0

    def block(b):
        at = pl.ds(pl.multiple_of(b * TOK_B, TOK_B), TOK_B)
        b_mat = bc[at, 0:N]
        c_mat = bc[at, N : 2 * N]
        scores = jnp.where(keep, dot(c_mat, b_mat, ((1,), (1,))), 0.0)
        fade_rows = rates[pl.ds(b, 1), :]
        lead_rows = rates[pl.ds(blocks + b, 1), :]
        skip = rates[2 * blocks + 8 : 2 * blocks + 9, :]
        for s in range(width // SLAB):
            lanes = slice(s * SLAB, (s + 1) * SLAB)
            xb = x[at, lanes]
            sel = ones[:, lanes]
            old = state[:, lanes]
            rise = dot(e_blk[at, :], sel)
            carried = dot(c_mat, old.astype(BF16)) * rise
            within = []
            for q in range(per_slab // 2):
                tables = []
                for h in (2 * q, 2 * q + 1):
                    head = head0 + s * per_slab + h
                    column = cum[at, head : head + 1]
                    gap = jnp.minimum(column - cum_s[head : head + 1, at], log_s[head : head + 1, at])
                    tables.append((scores * jnp.exp2(gap)).astype(BF16))
                xp = xb[:, q * 2 * P_SIZE : (q + 1) * 2 * P_SIZE]
                stacked = jnp.concatenate([jnp.where(first, xp, zero), jnp.where(first, zero, xp)], 0)
                within.append(dot(jnp.concatenate(tables, 1), stacked))
            xs = xb.astype(F32)
            y = jnp.concatenate(within, 1) + carried + skip[:, lanes] * xs
            gate = half_silu((z[at, lanes] * 0.5).astype(F32))
            uv[at, lanes] = (y * gate).astype(BF16)
            uv[at, width + s * SLAB : width + (s + 1) * SLAB] = (gate * rise * lead_rows[:, lanes]).astype(BF16)
            xf = (xs * dot(f_blk[at, :], sel)).astype(BF16)
            state[:, lanes] = old * fade_rows[:, lanes] + dot(b_mat, xf, ((0,), (0,)))

    lax.fori_loop(0, length // STEP_B, turn, 0)
    for step in range(length // STEP_B):
        store(step).wait()


def scan_part(part, token, x, z, bc, cum, cum_s, log_s, f_blk, e_blk, rates, ones):
    length, full = x.shape
    width = full // B_PARTS
    steps = length // STEP_B
    same = [pltpu.VMEM(a.shape, a.dtype) for a in (cum, cum_s, log_s, f_blk, e_blk)]
    return pl.pallas_call(
        functools.partial(scan_kernel, part),
        in_specs=[FAR] * 10 + [ANY],
        out_specs=FAR,
        out_shape=pltpu.HBM((length, 2 * width), BF16),
        scratch_shapes=[pltpu.VMEM((length, 2 * N), BF16)]
        + same
        + [
            pltpu.VMEM((rates.shape[0], width), F32),
            pltpu.VMEM((ones.shape[0], width), BF16),
            pltpu.VMEM((length, width), BF16),
            pltpu.VMEM((length, width), BF16),
            pltpu.VMEM((length, 2 * width), BF16),
            pltpu.VMEM((N, width), F32),
            pltpu.SemaphoreType.DMA((8,)),
            pltpu.SemaphoreType.DMA((2, steps)),
            pltpu.SemaphoreType.DMA((steps,)),
        ],
        compiler_params=params(24),
        cost_estimate=CHEAP,
        name="scan_part",
    )(x, z, bc, cum, cum_s, log_s, f_blk, e_blk, rates, ones, token)


def norm_kernel(slot, info, bc_far, entering, gain, _, *refs):
    uvs_far, out = refs[:B_PARTS], refs[B_PARTS]
    bc, uvs, sem = refs[B_PARTS + 1], refs[B_PARTS + 2 : -1], refs[-1]
    count, width = out.shape
    groups = bc.shape[1] // (2 * N)
    per = width // groups
    part = width // B_PARTS
    piece = entering.shape[2]
    base = info[slot] * count

    def fetch(j):
        to = pl.ds(pl.multiple_of(j * ROWS_C, ROWS_C), ROWS_C)
        at = pl.ds(pl.multiple_of(base + j * ROWS_C, ROWS_C), ROWS_C)
        pairs = zip((bc_far,) + uvs_far, (bc,) + uvs)
        return [pltpu.make_async_copy(a.at[at], b.at[to], sem.at[k, j]) for k, (a, b) in enumerate(pairs)]

    for j in range(count // ROWS_C):
        for copy in fetch(j):
            copy.start()

    def rows(j, _):
        for copy in fetch(j):
            copy.wait()
        to = pl.ds(pl.multiple_of(j * ROWS_C, ROWS_C), ROWS_C)
        for g in range(groups):
            c_mat = bc[to, 2 * N * g + N : 2 * N * (g + 1)]
            pieces = []
            squares = None
            for start in range(g * per, (g + 1) * per, HALF_C):
                p, lane = start // part, start % part
                inc = jnp.concatenate([entering[k] for k in range(start // piece, (start + HALF_C) // piece)], 1)
                u = uvs[p][to, lane : lane + HALF_C].astype(F32)
                v = uvs[p][to, part + lane : part + lane + HALF_C].astype(F32)
                gated = u + v * dot(c_mat, inc)
                square = jnp.sum(gated * gated, axis=-1, keepdims=True)
                squares = square if squares is None else squares + square
                pieces.append((start, gated))
            scale = lax.rsqrt(squares * (1.0 / per) + EPS)
            for start, gated in pieces:
                out[to, start : start + HALF_C] = (gated * scale * gain[:, start : start + HALF_C]).astype(BF16)
        return 0

    lax.fori_loop(0, count // ROWS_C, rows, 0)


def norm_rows(slot, info, count, token, bc, entering, gain, uvs):
    return pl.pallas_call(
        functools.partial(norm_kernel, slot),
        in_specs=[SCALAR, FAR, FULL, FULL, ANY] + [FAR] * len(uvs),
        out_specs=FULL,
        out_shape=jax.ShapeDtypeStruct((count, gain.shape[1]), BF16),
        scratch_shapes=[pltpu.VMEM((count, a.shape[1]), BF16) for a in [bc] + uvs]
        + [pltpu.SemaphoreType.DMA((1 + len(uvs), count // ROWS_C))],
        compiler_params=params(16),
        cost_estimate=CHEAP,
        name="norm_rows",
    )(info, bc, entering, gain, token, *uvs)


def project_kernel(base, added, a0, a1, w0_far, w1_far, *refs):
    out, w0, w1, sem = refs[-4:]
    j = pl.program_id(0)
    tiles = pl.num_programs(0)

    def fetch(t):
        slot = lax.rem(t, SLOTS)
        lanes = pl.ds(pl.multiple_of((base + t) * TILE, TILE), TILE)
        return (
            pltpu.make_async_copy(w0_far.at[:, lanes], w0.at[slot], sem.at[0, slot]),
            pltpu.make_async_copy(w1_far.at[:, lanes], w1.at[slot], sem.at[1, slot]),
        )

    def start(t):
        @pl.when(t < tiles)
        def _():
            for copy in fetch(t):
                copy.start()

    @pl.when(j == 0)
    def _():
        for t in range(SLOTS - 1):
            start(t)

    start(j + SLOTS - 1)
    for copy in fetch(j):
        copy.wait()
    slot = lax.rem(j, SLOTS)
    total = dot(a0[...], w0[slot]) + dot(a1[...], w1[slot])
    if added:
        total = total + refs[0][...].astype(F32)
    out[...] = total.astype(out.dtype)


def project(a0, a1, w0, w1, first, count, kind, arrived=None, result=None):
    rows, depth = a0.shape
    base = first // TILE
    full = arrived is not None
    operands, specs = [a0, a1, w0, w1], [FULL, FULL, FAR, FAR]
    if full:
        operands.append(arrived)
        specs.append(pl.BlockSpec((rows, TILE), lambda j: (0, j)))
    if result is not None:
        operands.append(result)
        specs.append(ANY)
    return pl.pallas_call(
        functools.partial(project_kernel, base, full),
        grid=(count // TILE,),
        in_specs=specs,
        out_specs=pl.BlockSpec((rows, TILE), lambda j: (0, base + j if full else j)),
        out_shape=jax.ShapeDtypeStruct((rows, w0.shape[1] if full else count), kind),
        scratch_shapes=[
            pltpu.VMEM((SLOTS, depth, TILE), BF16),
            pltpu.VMEM((SLOTS, depth, TILE), BF16),
            pltpu.SemaphoreType.DMA((2, SLOTS)),
        ],
        input_output_aliases={} if result is None else {len(operands) - 1: 0},
        compiler_params=params(20),
        cost_estimate=CHEAP,
        name="project",
    )(*operands)


def project_both_kernel(base, a0_far, a1_far, a0_near, a1_near, w0_far, w1_far, far, near, a0, a1, w0, w1, sem):
    j = pl.program_id(0)
    tiles = pl.num_programs(0)
    rows = far.shape[0]

    def fetch(t):
        slot = lax.rem(t, SLOTS)
        lanes = pl.ds(pl.multiple_of((base + t) * TILE, TILE), TILE)
        return (
            pltpu.make_async_copy(w0_far.at[:, lanes], w0.at[slot], sem.at[0, slot]),
            pltpu.make_async_copy(w1_far.at[:, lanes], w1.at[slot], sem.at[1, slot]),
        )

    def start(t):
        @pl.when(t < tiles)
        def _():
            for copy in fetch(t):
                copy.start()

    @pl.when(j == 0)
    def _():
        for t in range(SLOTS - 1):
            start(t)
        a0[0:rows, :] = a0_far[...]
        a0[rows:, :] = a0_near[...]
        a1[0:rows, :] = a1_far[...]
        a1[rows:, :] = a1_near[...]

    start(j + SLOTS - 1)
    for copy in fetch(j):
        copy.wait()
    slot = lax.rem(j, SLOTS)
    total = dot(a0[...], w0[slot]) + dot(a1[...], w1[slot])
    far[...] = total[0:rows].astype(BF16)
    near[...] = total[rows:]


def project_both(far, far_mate, near, near_mate, w0, w1, first, count):
    rows, depth = far.shape
    placed = pl.BlockSpec((rows, TILE), lambda j: (0, j))
    return pl.pallas_call(
        functools.partial(project_both_kernel, first // TILE),
        grid=(count // TILE,),
        in_specs=[FULL] * 4 + [FAR] * 2,
        out_specs=[placed, placed],
        out_shape=[jax.ShapeDtypeStruct((rows, count), BF16), jax.ShapeDtypeStruct((rows, count), F32)],
        scratch_shapes=[
            pltpu.VMEM((2 * rows, depth), BF16),
            pltpu.VMEM((2 * rows, depth), BF16),
            pltpu.VMEM((SLOTS, depth, TILE), BF16),
            pltpu.VMEM((SLOTS, depth, TILE), BF16),
            pltpu.SemaphoreType.DMA((2, SLOTS)),
        ],
        compiler_params=params(24),
        cost_estimate=CHEAP,
        name="project_both",
    )(far, far_mate, near, near_mate, w0, w1)


def add_kernel(part, arrived, _, out):
    out[...] = (part[...] + arrived[...].astype(F32)).astype(BF16)


def add_chunk(part, arrived, result, first):
    rows, count = arrived.shape
    base = first // count
    return pl.pallas_call(
        add_kernel,
        grid=(1,),
        in_specs=[FULL, FULL, ANY],
        out_specs=pl.BlockSpec((rows, count), lambda j: (0, base)),
        out_shape=jax.ShapeDtypeStruct(result.shape, BF16),
        input_output_aliases={2: 0},
        compiler_params=params(8),
        cost_estimate=CHEAP,
        name="add_chunk",
    )(part, arrived, result)


def shift(block, axis):
    size = lax.axis_size(axis)
    return lax.ppermute(block, axis, [(i, (i + 1) % size) for i in range(size)])


def swap(block, axis, bit):
    return lax.ppermute(block, axis, [(i, i ^ bit) for i in range(lax.axis_size(axis))])


def local(
    x_input,
    z_input,
    bc_input,
    conv_weight_x,
    conv_weight_bc,
    step_size,
    log_decay,
    skip_gain,
    norm_gain,
    out_weight,
):
    length, width = x_input.shape
    heads = step_size.shape[1]
    ways = lax.axis_size("head")
    devices = lax.axis_size("seq")
    mine = lax.axis_index("head")
    seq = lax.axis_index("seq")
    info = jnp.stack([seq, mine ^ 3, mine ^ 2, mine ^ 1, mine]).astype(jnp.int32)

    x_far, z_far, w_far = far(x_input, z_input, out_weight)
    bc = bc_input.reshape(length, -1)
    halo = shift(jnp.concatenate([x_input[length - LEAD :], bc[length - LEAD :]], 1), "seq")
    weight_mate = swap(out_weight, "head", 1)

    ones = jnp.asarray(np.tile(np.repeat(np.eye(heads), P_SIZE, axis=1), (2, 1)), BF16)
    cum, cum_s, log_s, f_dev, f_blk, e_blk, rates = decays(log_decay, step_size, skip_gain, ones)
    f_dev, rates = far(f_dev, rates)
    x_conv, bc_conv, send = conv_states(
        devices, info, x_far, bc, halo, conv_weight_x, conv_weight_bc, f_dev, ones, rates
    )

    x_conv, bc_conv = far(x_conv, bc_conv)
    small = far(cum, cum_s, log_s, f_blk, e_blk)
    uvs = []

    def scan_next(token):
        uvs.extend(far(scan_part(len(uvs), token, x_conv, z_far, bc_conv, *small, rates, far(ones)[0])))
        return uvs[-1]

    states = lax.all_to_all(send, "seq", 0, 0)
    done = send
    for _ in range(B_PARTS // 2):
        done = scan_next(done)
    prefixes = prefix(states, done)
    entering = lax.all_to_all(prefixes, "seq", 0, 0)
    done = prefixes
    while len(uvs) < B_PARTS:
        done = scan_next(done)

    count = length // ways
    gain = norm_gain[None, :]

    def rows_for(slot, token):
        return norm_rows(slot, info, count, token, bc_conv, entering, gain, uvs)

    far_mate = rows_for(1, done)
    ahead = rows_for(2, far_mate)
    far_mate = swap(far_mate, "head", 1)
    columns = out_weight.shape[1]
    quarter = columns // 4
    weights = (w_far, weight_mate)
    sent = project(ahead, far_mate, *weights, 0, quarter, BF16)
    arrivals = [swap(sent, "head", 2)]
    near_mate = rows_for(3, sent)
    near = rows_for(4, near_mate)
    near_mate = swap(near_mate, "head", 1)
    parts = []
    for c in range(quarter, columns, quarter):
        sent, part = project_both(ahead, far_mate, near, near_mate, *weights, c, quarter)
        arrivals.append(swap(sent, "head", 2))
        parts.append(part)
    result = project(near, near_mate, *weights, 0, quarter, BF16, arrivals[0])
    for c, part in enumerate(parts, 1):
        result = add_chunk(part, arrivals[c], result, c * quarter)
    return result


def solution(mesh):
    in_specs = (
        P("seq", "head"),
        P("seq", "head"),
        P("seq", "head", None),
        P(None, "head"),
        P(None, "head", None),
        P("seq", "head"),
        P("seq", "head"),
        P("head"),
        P("head"),
        P("head", None),
    )
    out_specs = P(("seq", "head"), None)
    return jax.shard_map(local, mesh=mesh, in_specs=in_specs, out_specs=out_specs, check_vma=False)
```

```python
import functools

import jax
import jax.numpy as jnp
import numpy as np
from jax import lax
from jax.experimental import pallas as pl
from jax.experimental.pallas import tpu as pltpu
from jax.sharding import PartitionSpec as P

P_SIZE = 64
N = 128
KCONV = 4
EPS = 1e-05
LOG2E = 1.4426950408889634

TOK_A = 256
ROWS_A = 32
TOK_B = 128
STEP_B = 256
EXTRA = 16
SLAB = 256
ROWS_C = 128
TILE = 256
SLOTS = 4
LEAD = 16
B_PARTS = 4
HIGHEST = lax.Precision.HIGHEST
F32 = jnp.float32
BF16 = jnp.bfloat16


def params(mib):
    return pltpu.CompilerParams(vmem_limit_bytes=mib * 1024 * 1024)


CHEAP = pl.CostEstimate(flops=1, bytes_accessed=1, transcendentals=0)
SCALAR = pl.BlockSpec(memory_space=pltpu.SMEM)
FULL = pl.BlockSpec(memory_space=pltpu.VMEM)
FAR = pl.BlockSpec(memory_space=pltpu.HBM)
ANY = pl.BlockSpec(memory_space=pl.ANY)


def dot(a, b, dims=((1,), (0,)), precision=None):
    return lax.dot_general(a, b, (dims, ((), ())), precision=precision, preferred_element_type=F32)


def silu(v):
    return v * pl.reciprocal(1.0 + jnp.exp2(v * -LOG2E), approx=True)


def far(*arrays):
    return [pltpu.with_memory_space_constraint(a, pltpu.HBM) for a in arrays]


def whole(shape):
    return pl.BlockSpec(shape, lambda *_: (0,) * len(shape))


def decay_kernel(ld_t, step_t, skip, ones, cum, cum_s, log_s, f_dev, f_blk, e_blk, rates):
    heads, length = ld_t.shape
    blocks = length // TOK_B
    row = lax.broadcasted_iota(jnp.int32, (TOK_B, TOK_B), 0)
    col = lax.broadcasted_iota(jnp.int32, (TOK_B, TOK_B), 1)
    lower = (row >= col).astype(F32)
    upper = (row <= col).astype(F32)
    eye = (row == col).astype(BF16)

    def put(ref, rows, value):
        high = value.astype(BF16)
        low = (value - high.astype(F32)).astype(BF16)
        ref[rows, :] = dot(eye, jnp.concatenate([high, low], 0), ((1,), (1,))).astype(BF16)

    cums, totals, row_totals = [], [], []
    for b in range(blocks):
        rows = slice(b * TOK_B, (b + 1) * TOK_B)
        logs = ld_t[:, rows] * LOG2E
        c = dot(lower, logs, ((1,), (1,)), HIGHEST)
        cum[rows, :] = c
        row_totals.append(c[TOK_B - 1 : TOK_B, :])
        c = dot(logs, upper, precision=HIGHEST)
        cums.append(c)
        totals.append(c[:, TOK_B - 1 : TOK_B])
    before, row_before = [jnp.zeros_like(totals[0])], [jnp.zeros_like(row_totals[0])]
    for b in range(blocks):
        before.append(before[-1] + totals[b])
        row_before.append(row_before[-1] + row_totals[b])
    total = before[-1]
    logs = jnp.concatenate(row_totals + row_before[:-1] + row_before[-1:] * 8, 0)
    values = jnp.concatenate([jnp.exp2(logs), jnp.broadcast_to(skip[...], (8, heads))], 0)
    rates[...] = dot(values, ones[0:heads, :].astype(F32), precision=HIGHEST)
    for b in range(blocks):
        rows = slice(b * TOK_B, (b + 1) * TOK_B)
        s = step_t[:, rows]
        log_step = jnp.log2(s)
        log_s[:, rows] = log_step
        cum_s[:, rows] = cums[b] - log_step
        put(f_dev, rows, jnp.exp2(total - (cums[b] + before[b])) * s)
        put(f_blk, rows, jnp.exp2(totals[b] - cums[b]) * s)
        put(e_blk, rows, jnp.exp2(cums[b]))


def decays(log_decay, step, skip, ones):
    length, heads = log_decay.shape
    blocks = length // TOK_B
    width = ones.shape[1]
    wide = jax.ShapeDtypeStruct((heads, length), F32)
    pair = jax.ShapeDtypeStruct((length, 2 * heads), BF16)
    return pl.pallas_call(
        decay_kernel,
        out_shape=(
            jax.ShapeDtypeStruct((length, heads), F32),
            wide,
            wide,
            pair,
            pair,
            pair,
            jax.ShapeDtypeStruct((2 * blocks + 16, width), F32),
        ),
        compiler_params=params(16),
        name="decays",
    )(log_decay.T, step.T, skip[None, :], ones)


def tail_kernel(x, bc, out):
    width, bc_width = x.shape[1], bc.shape[2]
    out[:, 0:width] = x[...]
    for g in range(bc.shape[1]):
        out[:, width + g * bc_width : width + (g + 1) * bc_width] = bc[:, g, :]


def tail_rows(x, bc):
    length, width = x.shape
    groups, bc_width = bc.shape[1:]
    at = length // LEAD - 1
    shape = (LEAD, width + groups * bc_width)
    return pl.pallas_call(
        tail_kernel,
        grid=(1,),
        in_specs=[
            pl.BlockSpec((LEAD, width), lambda i: (at, 0)),
            pl.BlockSpec((LEAD, groups, bc_width), lambda i: (at, 0, 0)),
        ],
        out_specs=whole(shape),
        out_shape=jax.ShapeDtypeStruct(shape, BF16),
        compiler_params=params(8),
        cost_estimate=CHEAP,
        name="tail_rows",
    )(x, bc)


def put_message(ref, state, decay):
    high = decay.astype(BF16)
    low = (decay - high.astype(F32)).astype(BF16)
    rest = jnp.zeros((EXTRA - 2, state.shape[1]), BF16)
    ref[0:N, :] = state.astype(BF16)
    ref[N:, :] = jnp.concatenate([high, low, rest], 0)


def take_message(ref):
    extra = ref[N:, :].astype(F32)
    return ref[0:N, :].astype(F32), extra[0:1] + extra[1:2]


def conv_kernel(info, x_far, bc, halo, wx, wbc, f_dev, ones, rates, x_out, bc_out, keep, send, x, sem, xf, state):
    i = pl.program_id(0)
    rows, width = x_out.shape
    bc_width = bc.shape[1]
    groups = bc_width // (2 * N)
    per = width // groups
    half = width // 2

    def fetch(step):
        piece = pl.ds(pl.multiple_of(step * rows, rows), rows)
        return pltpu.make_async_copy(x_far.at[piece], x.at[piece], sem.at[step])

    @pl.when(i == 0)
    def _():
        fetch(0).start()
        state[...] = jnp.zeros_like(state)

    base = pl.multiple_of(i * rows, rows)
    before = pl.ds(pl.multiple_of(jnp.maximum(base - LEAD, 0), LEAD), LEAD)

    def at(r):
        return pl.ds(pl.multiple_of(base + r, ROWS_A), ROWS_A)

    def conv(src, lead, weights, emit):
        w0, w1, w2, w3 = weights
        back = LEAD - 8
        r1 = pltpu.roll(lead, 1, 0)
        last_x, last_p = lead[back:], (w1 * lead + w0 * r1)[back:]
        for r in range(0, rows, ROWS_A):
            cur = src(r).astype(F32)
            r1 = pltpu.roll(jnp.concatenate([last_x, cur], 0), 1, 0)[8:]
            p = w1 * cur + w0 * r1
            p2 = pltpu.roll(jnp.concatenate([last_p, p], 0), 2, 0)[8:]
            emit(r, silu((w3 * cur + w2 * r1) + p2))
            last_x, last_p = cur[ROWS_A - 8 :], p[ROWS_A - 8 :]

    start = i == 0

    def halo_of(lanes):
        value = halo[:, lanes]
        return jnp.where(info[6] == 0, jnp.zeros_like(value), value)

    for c in range(groups):
        for lanes in range(c * 2 * N, (c + 1) * 2 * N, N):
            ds = slice(lanes, lanes + N)

            def emit_bc(r, value):
                bc_out[r : r + ROWS_A, ds] = value.astype(BF16)

            lead = jnp.where(start, halo_of(slice(width + lanes, width + lanes + N)), bc[before, ds]).astype(F32)
            inner = slice(lanes - c * 2 * N, lanes - c * 2 * N + N)
            conv(lambda r: bc[at(r), ds], lead, [wbc[k, c : c + 1, inner] for k in range(KCONV)], emit_bc)

    fetch(i).wait()

    @pl.when(i + 1 < pl.num_programs(0))
    def _():
        fetch(i + 1).start()

    def slab(c, _):
        first = pl.multiple_of(c * SLAB, SLAB)
        scale = dot(f_dev[pl.ds(base, rows), :], ones[:, pl.ds(first, SLAB)])
        ds = pl.ds(first, SLAB)

        def emit(r, value):
            value = value.astype(BF16)
            x_out[r : r + ROWS_A, ds] = value
            xf[r : r + ROWS_A, ds] = (value.astype(F32) * scale[r : r + ROWS_A]).astype(BF16)

        lead = jnp.where(start, halo_of(ds), x[before, ds]).astype(F32)
        conv(lambda r: x[at(r), ds], lead, [wx[k : k + 1, ds] for k in range(KCONV)], emit)
        return 0

    lax.fori_loop(0, width // SLAB, slab, 0)
    for g in range(groups):
        b_mat = bc_out[:, 2 * N * g : 2 * N * g + N]
        lanes = slice(g * per, (g + 1) * per)
        state[:, lanes] += dot(b_mat, xf[:, lanes], ((0,), (0,)))

    @pl.when(i == pl.num_programs(0) - 1)
    def _():
        is_odd = info[0] == 1
        low, high = state[:, 0:half], state[:, half:]
        keep[...] = jnp.where(is_odd, high, low)
        row = rates.shape[0] - 16
        decay = jnp.where(is_odd, rates[row : row + 1, 0:half], rates[row : row + 1, half:])
        put_message(send, jnp.where(is_odd, low, high), decay)


def conv_states(info, x, bc, halo, wx, wbc, f_dev, ones, rates):
    length, width = x.shape
    bc_width = bc.shape[1]
    half = width // 2
    return pl.pallas_call(
        conv_kernel,
        grid=(length // TOK_A,),
        in_specs=[SCALAR, FAR] + [FULL] * 7,
        out_specs=[
            pl.BlockSpec((TOK_A, width), lambda i: (i, 0)),
            pl.BlockSpec((TOK_A, bc_width), lambda i: (i, 0)),
            whole((N, half)),
            whole((N + EXTRA, half)),
        ],
        scratch_shapes=[
            pltpu.VMEM((length, width), BF16),
            pltpu.SemaphoreType.DMA((length // TOK_A,)),
            pltpu.VMEM((TOK_A, width), BF16),
            pltpu.VMEM((N, width), F32),
        ],
        out_shape=(
            pltpu.HBM((length, width), BF16),
            jax.ShapeDtypeStruct((length, bc_width), BF16),
            jax.ShapeDtypeStruct((N, half), F32),
            jax.ShapeDtypeStruct((N + EXTRA, half), BF16),
        ),
        compiler_params=params(20),
        cost_estimate=CHEAP,
        name="conv_states",
    )(info, x, bc, halo, wx, wbc, f_dev, ones, rates)


def pair_kernel(info, got, keep, rates, _, msg, own, first, aux):
    half = keep.shape[1]
    is_odd = info[0] == 1
    arrived, their = take_message(got)
    row = rates.shape[0] - 16
    mine = jnp.where(is_odd, rates[row : row + 1, half:], rates[row : row + 1, 0:half])
    early = jnp.where(is_odd, arrived, keep[...])
    late = jnp.where(is_odd, keep[...], arrived)
    even_decay = jnp.where(is_odd, their, mine)
    odd_decay = jnp.where(is_odd, mine, their)
    state = odd_decay * early + late
    own[...] = state
    first[...] = early
    aux[0:8, :] = jnp.broadcast_to(even_decay, (8, half))
    aux[8:16, :] = jnp.broadcast_to(even_decay * odd_decay, (8, half))
    put_message(msg, state, even_decay * odd_decay)


def wave_kernel(got, own, aux, behind_in, _, msg, behind):
    before, decay = take_message(got)
    if behind_in is not None:
        before_decay = behind_in[N : N + 1, :]
        before = behind_in[0:N, :] + before_decay * before
        decay = before_decay * decay
    pair_decay = aux[8:9, :]
    behind[0:N, :] = before
    behind[N:, :] = jnp.broadcast_to(decay, (8, before.shape[1]))
    put_message(msg, own[...] + pair_decay * before, pair_decay * decay)


def last_kernel(info, got, behind_in, first, aux, _, back, held):
    is_odd = info[0] == 1
    before, _unused = take_message(got)
    if behind_in is not None:
        before = behind_in[0:N, :] + behind_in[N : N + 1, :] * before
    entering_odd = aux[0:1, :] * before + first[...]
    back[...] = jnp.where(is_odd, before, entering_odd).astype(BF16)
    held[...] = jnp.where(is_odd, entering_odd, before).astype(BF16)


def pair_split_kernel(info, got, keep, rates, _, first, aux, *refs):
    outs, wide = refs[:-1], refs[-1]
    half = keep.shape[1]
    pairs = len(outs)
    piece = half // pairs
    is_odd = info[0] == 1
    arrived, their = take_message(got)
    row = rates.shape[0] - 16
    mine = jnp.where(is_odd, rates[row : row + 1, half:], rates[row : row + 1, 0:half])
    early = jnp.where(is_odd, arrived, keep[...])
    late = jnp.where(is_odd, keep[...], arrived)
    even_decay = jnp.where(is_odd, their, mine)
    odd_decay = jnp.where(is_odd, mine, their)
    first[...] = early
    aux[...] = jnp.broadcast_to(even_decay, (8, half))
    put_message(wide, odd_decay * early + late, even_decay * odd_decay)
    for r in range(pairs):
        owner = lax.rem(info[5] + r, pairs)
        outs[r][...] = wide[:, pl.ds(pl.multiple_of(owner * piece, piece), piece)]


def owner_kernel(info, *refs):
    pairs = (len(refs) - 3) // 2
    ins, outs = refs[:pairs], refs[pairs + 1 : 2 * pairs + 1]
    states, prefixes = refs[-2:]
    for r in range(pairs):
        states[lax.rem(info[5] + pairs - r, pairs)] = ins[r][...]
    before = jnp.zeros(prefixes.shape[1:], F32)
    for q in range(pairs):
        prefixes[q] = before.astype(BF16)
        if q < pairs - 1:
            state, decay = take_message(states.at[q])
            before = decay * before + state
    for r in range(pairs):
        outs[r][...] = prefixes[lax.rem(info[5] + r, pairs)]


def last_split_kernel(info, first, aux, _, *refs):
    pairs = len(refs) - 3
    back, held, wide = refs[-3:]
    piece = back.shape[1] // pairs
    for r in range(pairs):
        owner = lax.rem(info[5] + pairs - r, pairs)
        wide[:, pl.ds(pl.multiple_of(owner * piece, piece), piece)] = refs[r][...]
    is_odd = info[0] == 1
    before = wide[...].astype(F32)
    entering_odd = aux[0:1, :] * before + first[...]
    back[...] = jnp.where(is_odd, before, entering_odd).astype(BF16)
    held[...] = jnp.where(is_odd, entering_odd, before).astype(BF16)


def combine(kernel, operands, specs, outs, name, scratch=()):
    return pl.pallas_call(
        kernel,
        in_specs=specs,
        out_specs=[FULL] * len(outs),
        out_shape=[jax.ShapeDtypeStruct(s, t) for s, t in outs],
        scratch_shapes=list(scratch),
        compiler_params=params(16),
        cost_estimate=CHEAP,
        name=name,
    )(*operands)


def scan_kernel(part, x_far, z_far, bc_all, cum, cum_s, log_s, f_blk, e_blk, rates, ones, _, uv_out, x, z, sem, state):
    length, width = x.shape
    per_slab = SLAB // P_SIZE
    head0 = part * width // P_SIZE
    first_lane = part * width
    inner = STEP_B // TOK_B
    blocks = length // TOK_B
    group = first_lane * (bc_all.shape[1] // (2 * N)) // (width * B_PARTS)
    b_lanes = slice(2 * N * group, 2 * N * group + N)
    c_lanes = slice(2 * N * group + N, 2 * N * (group + 1))

    def fetch(step):
        piece = pl.ds(pl.multiple_of(step * STEP_B, STEP_B), STEP_B)
        lanes = pl.ds(first_lane, width)
        return (
            pltpu.make_async_copy(x_far.at[piece, lanes], x.at[piece], sem.at[0, step]),
            pltpu.make_async_copy(z_far.at[piece, lanes], z.at[piece], sem.at[1, step]),
        )

    for step in range(length // STEP_B):
        for copy in fetch(step):
            copy.start()
    state[...] = jnp.zeros_like(state)

    row = lax.broadcasted_iota(jnp.int32, (TOK_B, TOK_B), 0)
    col = lax.broadcasted_iota(jnp.int32, (TOK_B, TOK_B), 1)
    keep = row >= col
    first = lax.broadcasted_iota(jnp.int32, (TOK_B, 2 * P_SIZE), 1) < P_SIZE
    zero = jnp.zeros((TOK_B, 2 * P_SIZE), BF16)

    def turn(step, _):
        for copy in fetch(step):
            copy.wait()
        for k in range(inner):
            block(step * inner + k)
        return 0

    def block(b):
        at = pl.ds(pl.multiple_of(b * TOK_B, TOK_B), TOK_B)
        b_mat = bc_all[at, b_lanes]
        c_mat = bc_all[at, c_lanes]
        scores = jnp.where(keep, dot(c_mat, b_mat, ((1,), (1,))), 0.0)
        wide = pl.ds(first_lane, width)
        fade_rows = rates[pl.ds(b, 1), wide]
        lead_rows = rates[pl.ds(blocks + b, 1), wide]
        skip = rates[2 * blocks + 8 : 2 * blocks + 9, wide]
        for s in range(width // SLAB):
            lanes = slice(s * SLAB, (s + 1) * SLAB)
            xb = x[at, lanes]
            sel = ones[:, first_lane + s * SLAB : first_lane + (s + 1) * SLAB]
            old = state[:, lanes]
            rise = dot(e_blk[at, :], sel)
            carried = dot(c_mat, old.astype(BF16)) * rise
            within = []
            for q in range(per_slab // 2):
                tables = []
                for h in (2 * q, 2 * q + 1):
                    head = head0 + s * per_slab + h
                    column = cum[at, head : head + 1]
                    gap = jnp.minimum(column - cum_s[head : head + 1, at], log_s[head : head + 1, at])
                    tables.append((scores * jnp.exp2(gap)).astype(BF16))
                xp = xb[:, q * 2 * P_SIZE : (q + 1) * 2 * P_SIZE]
                stacked = jnp.concatenate([jnp.where(first, xp, zero), jnp.where(first, zero, xp)], 0)
                within.append(dot(jnp.concatenate(tables, 1), stacked))
            xs = xb.astype(F32)
            y = jnp.concatenate(within, 1) + carried + skip[:, lanes] * xs
            gate = silu(z[at, lanes].astype(F32))
            uv_out[at, lanes] = (y * gate).astype(BF16)
            uv_out[at, width + s * SLAB : width + (s + 1) * SLAB] = (gate * rise * lead_rows[:, lanes]).astype(BF16)
            xf = (xs * dot(f_blk[at, :], sel)).astype(BF16)
            state[:, lanes] = old * fade_rows[:, lanes] + dot(b_mat, xf, ((0,), (0,)))

    lax.fori_loop(0, length // STEP_B, turn, 0)


def scan_part(part, token, x, bc, z, cum, cum_s, log_s, f_blk, e_blk, rates, ones):
    length, full = x.shape
    width = full // B_PARTS
    return pl.pallas_call(
        functools.partial(scan_kernel, part),
        in_specs=[FAR, FAR] + [FULL] * 8 + [ANY],
        out_specs=FULL,
        out_shape=jax.ShapeDtypeStruct((length, 2 * width), BF16),
        scratch_shapes=[
            pltpu.VMEM((length, width), BF16),
            pltpu.VMEM((length, width), BF16),
            pltpu.SemaphoreType.DMA((2, length // STEP_B)),
            pltpu.VMEM((N, width), F32),
        ],
        compiler_params=params(16),
        cost_estimate=CHEAP,
        name="scan_part",
    )(x, z, bc, cum, cum_s, log_s, f_blk, e_blk, rates, ones, token)


def norm_kernel(slots, info, bc, keep, recv, gain, _, *refs):
    uvs, out = refs[:-1], refs[-1]
    count, width = out.shape
    groups = bc.shape[1] // (2 * N)
    per = width // groups
    half = width // 2
    part = width // B_PARTS
    is_odd = info[0] == 1
    count = count // len(slots)

    def rows(j, first, base):
        to = pl.ds(pl.multiple_of(first + j * ROWS_C, ROWS_C), ROWS_C)
        at = pl.ds(pl.multiple_of(base + j * ROWS_C, ROWS_C), ROWS_C)
        for g in range(groups):
            c_mat = bc[at, 2 * N * g + N : 2 * N * (g + 1)]
            pieces = []
            squares = None
            for p in range(g * per // part, (g + 1) * per // part):
                start = p * part
                side = start // half
                lanes = slice(start - side * half, start - side * half + part)
                mine, other = keep[:, lanes], recv[:, lanes]
                inc = jnp.where(is_odd, other, mine) if side == 0 else jnp.where(is_odd, mine, other)
                gated = uvs[p][at, 0:part].astype(F32) + uvs[p][at, part:].astype(F32) * dot(c_mat, inc)
                square = jnp.sum(gated * gated, axis=-1, keepdims=True)
                squares = square if squares is None else squares + square
                pieces.append((start, gated))
            scale = lax.rsqrt(squares * (1.0 / per) + EPS)
            for start, gated in pieces:
                out[to, start : start + part] = (gated * scale * gain[:, start : start + part]).astype(BF16)

    for k, slot in enumerate(slots):

        def step(j, _):
            rows(j, k * count, info[slot] * count)
            return 0

        lax.fori_loop(0, count // ROWS_C, step, 0)


def norm_rows(slots, info, count, token, bc, keep, recv, gain, uvs):
    return pl.pallas_call(
        functools.partial(norm_kernel, slots),
        in_specs=[SCALAR] + [FULL] * 4 + [ANY] + [FULL] * len(uvs),
        out_specs=FULL,
        out_shape=jax.ShapeDtypeStruct((len(slots) * count, gain.shape[1]), BF16),
        compiler_params=params(16),
        cost_estimate=CHEAP,
        name="norm_rows",
    )(info, bc, keep, recv, gain, token, *uvs)


def project_kernel(base, mine, added, a0, a1, w0_far, w1_far, *refs):
    out, w0, w1, sem = refs[-4:]
    j = pl.program_id(0)
    tiles = pl.num_programs(0)

    def fetch(t):
        slot = lax.rem(t, SLOTS)
        lanes = pl.ds(pl.multiple_of((base + t) * TILE, TILE), TILE)
        return (
            pltpu.make_async_copy(w0_far.at[:, lanes], w0.at[slot], sem.at[0, slot]),
            pltpu.make_async_copy(w1_far.at[:, lanes], w1.at[slot], sem.at[1, slot]),
        )

    def start(t):
        @pl.when(t < tiles)
        def _():
            for copy in fetch(t):
                copy.start()

    @pl.when(j == 0)
    def _():
        for t in range(SLOTS - 1):
            start(t)

    start(j + SLOTS - 1)
    for copy in fetch(j):
        copy.wait()
    slot = lax.rem(j, SLOTS)
    total = dot(a0[mine, :], w0[slot]) + dot(a1[mine, :], w1[slot])
    if added:
        total = total + refs[0][...].astype(F32)
    out[...] = total.astype(out.dtype)


def project(half, a0, a1, w0, w1, first, count, kind, arrived=None, result=None):
    rows, depth = a0.shape[0] // 2, a0.shape[1]
    base = first // TILE
    full = arrived is not None
    operands, specs = [a0, a1, w0, w1], [FULL, FULL, FAR, FAR]
    if full:
        operands.append(arrived)
        specs.append(pl.BlockSpec((rows, TILE), lambda j: (0, j)))
    if result is not None:
        operands.append(result)
        specs.append(ANY)
    return pl.pallas_call(
        functools.partial(project_kernel, base, slice(half * rows, (half + 1) * rows), full),
        grid=(count // TILE,),
        in_specs=specs,
        out_specs=pl.BlockSpec((rows, TILE), lambda j: (0, base + j if full else j)),
        out_shape=jax.ShapeDtypeStruct((rows, w0.shape[1] if full else count), kind),
        scratch_shapes=[
            pltpu.VMEM((SLOTS, depth, TILE), BF16),
            pltpu.VMEM((SLOTS, depth, TILE), BF16),
            pltpu.SemaphoreType.DMA((2, SLOTS)),
        ],
        input_output_aliases={} if result is None else {len(operands) - 1: 0},
        compiler_params=params(20),
        cost_estimate=CHEAP,
        name="project",
    )(*operands)


def project_both_kernel(base, a0, a1, w0_far, w1_far, far, near, w0, w1, sem):
    j = pl.program_id(0)
    tiles = pl.num_programs(0)
    rows = far.shape[0]

    def fetch(t):
        slot = lax.rem(t, SLOTS)
        lanes = pl.ds(pl.multiple_of((base + t) * TILE, TILE), TILE)
        return (
            pltpu.make_async_copy(w0_far.at[:, lanes], w0.at[slot], sem.at[0, slot]),
            pltpu.make_async_copy(w1_far.at[:, lanes], w1.at[slot], sem.at[1, slot]),
        )

    def start(t):
        @pl.when(t < tiles)
        def _():
            for copy in fetch(t):
                copy.start()

    @pl.when(j == 0)
    def _():
        for t in range(SLOTS - 1):
            start(t)

    start(j + SLOTS - 1)
    for copy in fetch(j):
        copy.wait()
    slot = lax.rem(j, SLOTS)
    total = dot(a0[...], w0[slot]) + dot(a1[...], w1[slot])
    far[...] = total[0:rows].astype(BF16)
    near[...] = total[rows:]


def project_both(a0, a1, w0, w1, first, count):
    rows, depth = a0.shape[0] // 2, a0.shape[1]
    placed = pl.BlockSpec((rows, TILE), lambda j: (0, j))
    return pl.pallas_call(
        functools.partial(project_both_kernel, first // TILE),
        grid=(count // TILE,),
        in_specs=[FULL] * 2 + [FAR] * 2,
        out_specs=[placed, placed],
        out_shape=[jax.ShapeDtypeStruct((rows, count), BF16), jax.ShapeDtypeStruct((rows, count), F32)],
        scratch_shapes=[
            pltpu.VMEM((SLOTS, depth, TILE), BF16),
            pltpu.VMEM((SLOTS, depth, TILE), BF16),
            pltpu.SemaphoreType.DMA((2, SLOTS)),
        ],
        compiler_params=params(24),
        cost_estimate=CHEAP,
        name="project_both",
    )(a0, a1, w0, w1)


def add_kernel(part, arrived, _, out):
    out[...] = (part[...] + arrived[...].astype(F32)).astype(BF16)


def add_chunk(part, arrived, result, first):
    rows, count = arrived.shape
    base = first // count
    return pl.pallas_call(
        add_kernel,
        grid=(1,),
        in_specs=[FULL, FULL, ANY],
        out_specs=pl.BlockSpec((rows, count), lambda j: (0, base)),
        out_shape=jax.ShapeDtypeStruct(result.shape, BF16),
        input_output_aliases={2: 0},
        compiler_params=params(8),
        cost_estimate=CHEAP,
        name="add_chunk",
    )(part, arrived, result)


def shift(block, distance):
    size = lax.axis_size("seq")
    return lax.ppermute(block, "seq", [(i, i + distance) for i in range(size - distance)])


def swap(block, axis, bit):
    return lax.ppermute(block, axis, [(i, i ^ bit) for i in range(lax.axis_size(axis))])


def rotate(block, distance):
    size = lax.axis_size("seq")
    return lax.ppermute(block, "seq", [(i, (i + distance) % size) for i in range(size)])


def log_steps(info, got, keep, rates, done, pairs, scan_next):
    half = keep.shape[1]
    message = ((N + EXTRA, half), BF16)
    full = ((N, half), F32)
    msg, own, first, aux = combine(
        pair_kernel,
        (info, got, keep, rates, done),
        [SCALAR, FULL, FULL, FULL, ANY],
        [message, full, full, ((16, half), F32)],
        "pair",
    )
    behind = None
    covered = 0
    while True:
        got = shift(msg, 2 * (covered + 1))
        done = scan_next(msg)
        covered = 2 * covered + 1
        if covered >= pairs - 1:
            break
        operands, specs = [got, own, aux], [FULL, FULL, FULL]
        if behind is None:
            kernel = lambda g, o, a, t, m, b: wave_kernel(g, o, a, None, t, m, b)
        else:
            kernel = wave_kernel
            operands.append(behind)
            specs.append(FULL)
        msg, behind = combine(kernel, operands + [done], specs + [ANY], [message, ((N + 8, half), F32)], "wave")
    operands, specs = [info, got], [SCALAR, FULL]
    if behind is None:
        kernel = lambda o, g, f, a, t, b, h: last_kernel(o, g, None, f, a, t, b, h)
    else:
        kernel = last_kernel
        operands.append(behind)
        specs.append(FULL)
    out = ((N, half), BF16)
    back, held = combine(kernel, operands + [first, aux, done], specs + [FULL, FULL, ANY], [out, out], "last")
    return back, held


def local(
    x_input,
    z_input,
    bc_input,
    conv_weight_x,
    conv_weight_bc,
    step_size,
    log_decay,
    skip_gain,
    norm_gain,
    out_weight,
):
    length, width = x_input.shape
    heads = step_size.shape[1]
    ways = lax.axis_size("head")
    pairs = lax.axis_size("seq") // 2
    mine = lax.axis_index("head")
    half = width // 2
    seq = lax.axis_index("seq")
    info = jnp.stack([seq & 1, mine ^ 3, mine ^ 2, mine ^ 1, mine, seq >> 1, seq]).astype(jnp.int32)

    x_far, z_far, w_far = far(x_input, z_input, out_weight)
    (bc_far,) = far(bc_input)
    halo = rotate(tail_rows(x_far, bc_far), 1)
    bc = bc_input.reshape(length, -1)
    weight_mate = swap(out_weight, "head", 1)

    ones = jnp.asarray(np.tile(np.repeat(np.eye(heads), P_SIZE, axis=1), (2, 1)), BF16)
    cum, cum_s, log_s, f_dev, f_blk, e_blk, rates = decays(log_decay, step_size, skip_gain, ones)
    x_conv, bc_conv, keep, send = conv_states(
        info, x_far, bc, halo, conv_weight_x, conv_weight_bc, f_dev, ones, rates
    )

    (x_conv,) = far(x_conv)
    uvs = []

    def scan_next(token):
        if len(uvs) < B_PARTS:
            uvs.append(
                scan_part(len(uvs), token, x_conv, bc_conv, z_far, cum, cum_s, log_s, f_blk, e_blk, rates, ones)
            )
        return uvs[-1]

    message = ((N + EXTRA, half), BF16)
    full = ((N, half), F32)
    got = swap(send, "seq", 1)
    done = scan_next(send)
    out = ((N, half), BF16)
    if pairs > 1 and half % (pairs * N) == 0:
        piece = half // pairs
        part = ((N + EXTRA, piece), BF16)
        first, aux, *parts = combine(
            pair_split_kernel,
            (info, got, keep, rates, done),
            [SCALAR, FULL, FULL, FULL, ANY],
            [full, ((8, half), F32)] + [part] * pairs,
            "pair",
            [pltpu.VMEM(*message)],
        )
        parts = list(parts[:1]) + [rotate(parts[r], 2 * r) for r in range(1, pairs)]
        done = scan_next(parts[0])
        parts = combine(
            owner_kernel,
            [info] + parts + [done],
            [SCALAR] + [FULL] * pairs + [ANY],
            [((N, piece), BF16)] * pairs,
            "owner",
            [pltpu.VMEM((pairs, N + EXTRA, piece), BF16), pltpu.VMEM((pairs, N, piece), BF16)],
        )
        ready = parts[0]
        parts = list(parts[:1]) + [rotate(parts[r], 2 * r) for r in range(1, pairs)]
        done = scan_next(ready)
        back, held = combine(
            last_split_kernel,
            [info, first, aux, done] + parts,
            [SCALAR, FULL, FULL, ANY] + [FULL] * pairs,
            [out, out],
            "last",
            [pltpu.VMEM(*out)],
        )
    else:
        back, held = log_steps(info, got, keep, rates, done, pairs, scan_next)
    other = swap(back, "seq", 1)
    while len(uvs) < B_PARTS:
        scan_next(back)

    count = length // ways
    gain = norm_gain[None, :]

    def rows_for(token, *slots):
        return norm_rows(slots, info, count, token, bc_conv, held, other, gain, uvs)

    mates = rows_for(held, 1, 3)
    owns = rows_for(mates, 2, 4)
    operands = (owns, swap(mates, "head", 1), w_far, weight_mate)
    columns = out_weight.shape[1]
    quarter = columns // 4
    sent = project(0, *operands, 0, quarter, BF16)
    arrivals = [swap(sent, "head", 2)]
    parts = []
    for c in range(quarter, columns, quarter):
        sent, part = project_both(*operands, c, quarter)
        arrivals.append(swap(sent, "head", 2))
        parts.append(part)
    result = project(1, *operands, 0, quarter, BF16, arrivals[0])
    for c, part in enumerate(parts, 1):
        result = add_chunk(part, arrivals[c], result, c * quarter)
    return result


def solution(mesh):
    in_specs = (
        P("seq", "head"),
        P("seq", "head"),
        P("seq", "head", None),
        P(None, "head"),
        P(None, "head", None),
        P("seq", "head"),
        P("seq", "head"),
        P("head"),
        P("head"),
        P("head", None),
    )
    out_specs = P(("seq", "head"), None)
    return jax.shard_map(local, mesh=mesh, in_specs=in_specs, out_specs=out_specs, check_vma=False)
```

```python
import functools

import jax
import jax.numpy as jnp
import numpy as np
from jax import lax
from jax.experimental import pallas as pl
from jax.experimental.pallas import tpu as pltpu
from jax.sharding import PartitionSpec as P

P_SIZE = 64
N = 128
KCONV = 4
EPS = 1e-05
LOG2E = 1.4426950408889634

TOK_A = 256
ROWS_A = 32
TOK_B = 128
STEP_B = 256
EXTRA = 16
SLAB = 256
ROWS_C = 128
TILE = 256
SLOTS = 4
LEAD = 16
B_PARTS = 2
HIGHEST = lax.Precision.HIGHEST
F32 = jnp.float32
BF16 = jnp.bfloat16


def params(mib):
    return pltpu.CompilerParams(vmem_limit_bytes=mib * 1024 * 1024)


CHEAP = pl.CostEstimate(flops=1, bytes_accessed=1, transcendentals=0)
SCALAR = pl.BlockSpec(memory_space=pltpu.SMEM)
FULL = pl.BlockSpec(memory_space=pltpu.VMEM)
FAR = pl.BlockSpec(memory_space=pltpu.HBM)
ANY = pl.BlockSpec(memory_space=pl.ANY)

ODD, ROWS, PAIR, SEQ, GROUP = 0, 1, 5, 6, 7


def dot(a, b, dims=((1,), (0,)), precision=None):
    return lax.dot_general(a, b, (dims, ((), ())), precision=precision, preferred_element_type=F32)


def half_silu(half):
    return half + half * jnp.tanh(half)


def far(*arrays):
    return [pltpu.with_memory_space_constraint(a, pltpu.HBM) for a in arrays]


def whole(shape):
    return pl.BlockSpec(shape, lambda *_: (0,) * len(shape))


def decay_kernel(ld_t, step_t, skip, ones, cum, cum_s, log_s, f_dev, f_blk, e_blk, rates, by_row):
    heads, length = ld_t.shape
    blocks = length // TOK_B
    row = lax.broadcasted_iota(jnp.int32, (TOK_B, TOK_B), 0)
    col = lax.broadcasted_iota(jnp.int32, (TOK_B, TOK_B), 1)
    lower = (row >= col).astype(F32)
    upper = (row <= col).astype(F32)
    eye = (row == col).astype(BF16)

    def put(ref, rows, value):
        high = value.astype(BF16)
        low = (value - high.astype(F32)).astype(BF16)
        ref[rows, :] = dot(eye, jnp.concatenate([high, low], 0), ((1,), (1,))).astype(BF16)

    cums, totals, row_totals = [], [], []
    for b in range(blocks):
        rows = slice(b * TOK_B, (b + 1) * TOK_B)
        logs = ld_t[:, rows] * LOG2E
        c = dot(lower, logs, ((1,), (1,)), HIGHEST)
        for g in range(cum.shape[0]):
            cum[g, rows, :] = c[:, g * cum.shape[2] : (g + 1) * cum.shape[2]]
        row_totals.append(c[TOK_B - 1 : TOK_B, :])
        c = dot(logs, upper, precision=HIGHEST)
        cums.append(c)
        totals.append(c[:, TOK_B - 1 : TOK_B])
    before, row_before = [jnp.zeros_like(totals[0])], [jnp.zeros_like(row_totals[0])]
    for b in range(blocks):
        before.append(before[-1] + totals[b])
        row_before.append(row_before[-1] + row_totals[b])
    total = before[-1]
    logs = jnp.concatenate(row_totals + row_before[:-1] + row_before[-1:] * 8, 0)
    values = jnp.concatenate([jnp.exp2(logs), jnp.broadcast_to(skip[...], (8, heads))], 0)
    spread = dot(values, ones[0:heads, :].astype(F32), precision=HIGHEST)
    rates[...] = spread
    for b in range(2 * blocks):
        by_row[b] = spread[b : b + 1, :]
    by_row[2 * blocks] = spread[2 * blocks + 8 : 2 * blocks + 9, :]
    for b in range(blocks):
        rows = slice(b * TOK_B, (b + 1) * TOK_B)
        s = step_t[:, rows]
        log_step = jnp.log2(s)
        shifted = cums[b] - log_step
        for g in range(cum.shape[0]):
            own = slice(g * cum.shape[2], (g + 1) * cum.shape[2])
            log_s[g, :, rows] = log_step[own, :]
            cum_s[g, :, rows] = shifted[own, :]
        put(f_dev, rows, jnp.exp2(total - (cums[b] + before[b])) * s)
        put(f_blk, rows, jnp.exp2(totals[b] - cums[b]) * s)
        put(e_blk, rows, jnp.exp2(cums[b]))


def decays(groups, log_decay, step, skip, ones):
    length, heads = log_decay.shape
    blocks = length // TOK_B
    width = ones.shape[1]
    wide = jax.ShapeDtypeStruct((groups, heads // groups, length), F32)
    pair = jax.ShapeDtypeStruct((length, 2 * heads), BF16)
    return pl.pallas_call(
        decay_kernel,
        out_shape=(
            jax.ShapeDtypeStruct((groups, length, heads // groups), F32),
            wide,
            wide,
            pair,
            pair,
            pair,
            jax.ShapeDtypeStruct((2 * blocks + 16, width), F32),
            jax.ShapeDtypeStruct((2 * blocks + 1, 1, width), F32),
        ),
        compiler_params=params(16),
        name="decays",
    )(log_decay.T, step.T, skip[None, :], ones)


def tail_kernel(x, bc, out):
    width, bc_width = x.shape[1], bc.shape[2]
    out[:, 0:width] = x[...]
    for g in range(bc.shape[1]):
        out[:, width + g * bc_width : width + (g + 1) * bc_width] = bc[:, g, :]


def tail_rows(x, bc):
    length, width = x.shape
    groups, bc_width = bc.shape[1:]
    at = length // LEAD - 1
    shape = (LEAD, width + groups * bc_width)
    return pl.pallas_call(
        tail_kernel,
        grid=(1,),
        in_specs=[
            pl.BlockSpec((LEAD, width), lambda i: (at, 0)),
            pl.BlockSpec((LEAD, groups, bc_width), lambda i: (at, 0, 0)),
        ],
        out_specs=whole(shape),
        out_shape=jax.ShapeDtypeStruct(shape, BF16),
        compiler_params=params(8),
        cost_estimate=CHEAP,
        name="tail_rows",
    )(x, bc)


def put_message(ref, state, decay):
    high = decay.astype(BF16)
    low = (decay - high.astype(F32)).astype(BF16)
    rest = jnp.zeros((EXTRA - 2, state.shape[1]), BF16)
    ref[0:N, :] = state.astype(BF16)
    ref[N:, :] = jnp.concatenate([high, low, rest], 0)


def take_message(ref):
    extra = ref[N:, :].astype(F32)
    return ref[0:N, :].astype(F32), extra[0:1] + extra[1:2]


def conv_kernel(
    order, info, x, x_lead, bc, bc_lead, halo, bc_halo, wx, wbc, f_dev, ones, rates, x_out, bc_out, final, xf, state
):
    i = pl.program_id(0)
    rows, width = x.shape
    group = info[GROUP + order]

    @pl.when(i == 0)
    def _():
        state[...] = jnp.zeros_like(state)

    def conv(src, first, behind, weights, emit):
        at_start = jnp.where(info[SEQ] == 0, jnp.zeros_like(first), first)
        lead = jnp.where(i == 0, at_start, behind).astype(F32)
        w0, w1, w2, w3 = [w * 0.5 for w in weights]
        back = LEAD - 8
        r1 = pltpu.roll(lead, 1, 0)
        last_x, last_p = lead[back:], (w1 * lead + w0 * r1)[back:]
        for r in range(0, rows, ROWS_A):
            cur = src(r).astype(F32)
            r1 = pltpu.roll(jnp.concatenate([last_x, cur], 0), 1, 0)[8:]
            p = w1 * cur + w0 * r1
            p2 = pltpu.roll(jnp.concatenate([last_p, p], 0), 2, 0)[8:]
            emit(r, half_silu((w3 * cur + w2 * r1) + p2))
            last_x, last_p = cur[ROWS_A - 8 :], p[ROWS_A - 8 :]

    for lanes in range(0, 2 * N, N):
        ds = slice(lanes, lanes + N)

        def emit_bc(r, value):
            bc_out[r : r + ROWS_A, ds] = value.astype(BF16)

        weights = [jnp.where(group == 0, wbc[k, 0:1, ds], wbc[k, 1:2, ds]) for k in range(KCONV)]
        conv(lambda r: bc[r : r + ROWS_A, ds], bc_halo[:, ds], bc_lead[:, ds], weights, emit_bc)

    def slab(c, _):
        ds = pl.ds(pl.multiple_of(c * SLAB, SLAB), SLAB)
        scale = dot(f_dev[...], ones[:, ds])

        def emit(r, value):
            x_out[r : r + ROWS_A, ds] = value.astype(BF16)
            xf[r : r + ROWS_A, ds] = (value * scale[r : r + ROWS_A]).astype(BF16)

        weights = [wx[k : k + 1, ds] for k in range(KCONV)]
        conv(lambda r: x[r : r + ROWS_A, ds], halo[:, ds], x_lead[:, ds], weights, emit)
        return 0

    lax.fori_loop(0, width // SLAB, slab, 0)
    state[...] += dot(bc_out[:, 0:N], xf[...], ((0,), (0,)))

    @pl.when(i == pl.num_programs(0) - 1)
    def _():
        if order == 0:
            row = rates.shape[0] - 16
            put_message(final, state[...], rates[row : row + 1, :])
        else:
            final[...] = state[...]


def conv_states(order, info, x, bc, halo, wx, wbc, f_dev, ones, rates):
    length, full = x.shape
    width = full // 2
    lead = lambda i, info: (jnp.maximum(i * (TOK_A // LEAD) - 1, 0), info[GROUP + order])
    block = lambda i, info: (i, info[GROUP + order])
    column = lambda i, info: (0, info[GROUP + order])
    rows = lambda i, info: (i, 0)
    final = ((N + EXTRA, width), BF16) if order == 0 else ((N, width), F32)
    return pl.pallas_call(
        functools.partial(conv_kernel, order),
        grid_spec=pltpu.PrefetchScalarGridSpec(
            num_scalar_prefetch=1,
            grid=(length // TOK_A,),
            in_specs=[
                pl.BlockSpec((TOK_A, width), block),
                pl.BlockSpec((LEAD, width), lead),
                pl.BlockSpec((TOK_A, 2 * N), block),
                pl.BlockSpec((LEAD, 2 * N), lead),
                pl.BlockSpec((LEAD, width), column),
                pl.BlockSpec((LEAD, 2 * N), lambda i, info: (0, full // (2 * N) + info[GROUP + order])),
                pl.BlockSpec((KCONV, width), column),
                whole(wbc.shape),
                pl.BlockSpec((TOK_A, f_dev.shape[1]), rows),
                pl.BlockSpec((ones.shape[0], width), column),
                pl.BlockSpec((rates.shape[0], width), column),
            ],
            out_specs=[
                pl.BlockSpec((TOK_A, width), rows),
                pl.BlockSpec((TOK_A, 2 * N), rows),
                whole(final[0]),
            ],
            scratch_shapes=[pltpu.VMEM((TOK_A, width), BF16), pltpu.VMEM((N, width), F32)],
        ),
        out_shape=(
            pltpu.HBM((length, width), BF16),
            jax.ShapeDtypeStruct((length, 2 * N), BF16),
            jax.ShapeDtypeStruct(*final),
        ),
        compiler_params=params(16),
        cost_estimate=CHEAP,
        name="conv_states",
    )(info, x, x, bc, bc, halo, halo, wx, wbc, f_dev, ones, rates)


def pair_kernel(info, got, keep, rates, _, msg, own, first, aux):
    half = keep.shape[1]
    is_odd = info[ODD] == 1
    arrived, their = take_message(got)
    row = rates.shape[0] - 16
    mine = rates[row : row + 1, pl.ds(pl.multiple_of(info[GROUP + 1] * half, half), half)]
    early = jnp.where(is_odd, arrived, keep[...])
    late = jnp.where(is_odd, keep[...], arrived)
    even_decay = jnp.where(is_odd, their, mine)
    odd_decay = jnp.where(is_odd, mine, their)
    state = odd_decay * early + late
    own[...] = state
    first[...] = early
    aux[0:8, :] = jnp.broadcast_to(even_decay, (8, half))
    aux[8:16, :] = jnp.broadcast_to(even_decay * odd_decay, (8, half))
    put_message(msg, state, even_decay * odd_decay)


def wave_kernel(got, own, aux, behind_in, _, msg, behind):
    before, decay = take_message(got)
    if behind_in is not None:
        before_decay = behind_in[N : N + 1, :]
        before = behind_in[0:N, :] + before_decay * before
        decay = before_decay * decay
    pair_decay = aux[8:9, :]
    behind[0:N, :] = before
    behind[N:, :] = jnp.broadcast_to(decay, (8, before.shape[1]))
    put_message(msg, own[...] + pair_decay * before, pair_decay * decay)


def last_kernel(info, got, behind_in, first, aux, _, back, held):
    is_odd = info[ODD] == 1
    before, _unused = take_message(got)
    if behind_in is not None:
        before = behind_in[0:N, :] + behind_in[N : N + 1, :] * before
    entering_odd = aux[0:1, :] * before + first[...]
    back[...] = jnp.where(is_odd, before, entering_odd).astype(BF16)
    held[...] = jnp.where(is_odd, entering_odd, before).astype(BF16)


def pair_split_kernel(info, got, keep, rates, _, first, aux, *refs):
    outs, wide = refs[:-1], refs[-1]
    half = keep.shape[1]
    pairs = len(outs)
    piece = half // pairs
    is_odd = info[ODD] == 1
    arrived, their = take_message(got)
    row = rates.shape[0] - 16
    mine = rates[row : row + 1, pl.ds(pl.multiple_of(info[GROUP + 1] * half, half), half)]
    early = jnp.where(is_odd, arrived, keep[...])
    late = jnp.where(is_odd, keep[...], arrived)
    even_decay = jnp.where(is_odd, their, mine)
    odd_decay = jnp.where(is_odd, mine, their)
    first[...] = early
    aux[...] = jnp.broadcast_to(even_decay, (8, half))
    put_message(wide, odd_decay * early + late, even_decay * odd_decay)
    for r in range(pairs):
        owner = lax.rem(info[PAIR] + r, pairs)
        outs[r][...] = wide[:, pl.ds(pl.multiple_of(owner * piece, piece), piece)]


def owner_kernel(info, *refs):
    pairs = (len(refs) - 3) // 2
    ins, outs = refs[:pairs], refs[pairs + 1 : 2 * pairs + 1]
    states, prefixes = refs[-2:]
    for r in range(pairs):
        states[lax.rem(info[PAIR] + pairs - r, pairs)] = ins[r][...]
    before = jnp.zeros(prefixes.shape[1:], F32)
    for q in range(pairs):
        prefixes[q] = before.astype(BF16)
        if q < pairs - 1:
            state, decay = take_message(states.at[q])
            before = decay * before + state
    for r in range(pairs):
        outs[r][...] = prefixes[lax.rem(info[PAIR] + r, pairs)]


def last_split_kernel(info, first, aux, _, *refs):
    pairs = len(refs) - 3
    back, held, wide = refs[-3:]
    piece = back.shape[1] // pairs
    for r in range(pairs):
        owner = lax.rem(info[PAIR] + pairs - r, pairs)
        wide[:, pl.ds(pl.multiple_of(owner * piece, piece), piece)] = refs[r][...]
    is_odd = info[ODD] == 1
    before = wide[...].astype(F32)
    entering_odd = aux[0:1, :] * before + first[...]
    back[...] = jnp.where(is_odd, before, entering_odd).astype(BF16)
    held[...] = jnp.where(is_odd, entering_odd, before).astype(BF16)


def combine(kernel, operands, specs, outs, name, scratch=()):
    return pl.pallas_call(
        kernel,
        in_specs=specs,
        out_specs=[FULL] * len(outs),
        out_shape=[jax.ShapeDtypeStruct(s, t) for s, t in outs],
        scratch_shapes=list(scratch),
        compiler_params=params(16),
        cost_estimate=CHEAP,
        name=name,
    )(*operands)


def scan_kernel(order, part, info, x_far, z_far, bc, cum, cum_s, log_s, f_blk, e_blk, by_row, ones, _, uv_out, x, z, sem, state):
    length, width = x.shape
    per_slab = SLAB // P_SIZE
    inner = STEP_B // TOK_B
    blocks = length // TOK_B
    group = info[GROUP + order]
    first_head = part * width // P_SIZE
    first_lane = group * x_far.shape[1] + part * width

    def fetch(step):
        piece = pl.ds(pl.multiple_of(step * STEP_B, STEP_B), STEP_B)
        return (
            pltpu.make_async_copy(x_far.at[piece, pl.ds(part * width, width)], x.at[piece], sem.at[0, step]),
            pltpu.make_async_copy(
                z_far.at[piece, pl.ds(pl.multiple_of(first_lane, width), width)], z.at[piece], sem.at[1, step]
            ),
        )

    for step in range(length // STEP_B):
        for copy in fetch(step):
            copy.start()
    state[...] = jnp.zeros_like(state)

    row = lax.broadcasted_iota(jnp.int32, (TOK_B, TOK_B), 0)
    col = lax.broadcasted_iota(jnp.int32, (TOK_B, TOK_B), 1)
    keep = row >= col
    first = lax.broadcasted_iota(jnp.int32, (TOK_B, 2 * P_SIZE), 1) < P_SIZE
    zero = jnp.zeros((TOK_B, 2 * P_SIZE), BF16)

    def turn(step, _):
        for copy in fetch(step):
            copy.wait()
        for k in range(inner):
            block(step * inner + k)
        return 0

    def block(b):
        at = pl.ds(pl.multiple_of(b * TOK_B, TOK_B), TOK_B)
        b_mat = bc[at, 0:N]
        c_mat = bc[at, N : 2 * N]
        scores = jnp.where(keep, dot(c_mat, b_mat, ((1,), (1,))), 0.0)
        for s in range(width // SLAB):
            lanes = slice(s * SLAB, (s + 1) * SLAB)
            xb = x[at, lanes]
            wide = pl.ds(pl.multiple_of(first_lane + s * SLAB, SLAB), SLAB)
            sel = ones[:, wide]
            fade_row = by_row[b, :, wide]
            lead_row = by_row[blocks + b, :, wide]
            skip = by_row[2 * blocks, :, wide]
            old = state[:, lanes]
            rise = dot(e_blk[at, :], sel)
            carried = dot(c_mat, old.astype(BF16)) * rise
            within = []
            for q in range(per_slab // 2):
                tables = []
                for h in (2 * q, 2 * q + 1):
                    head = first_head + s * per_slab + h
                    column = cum[group, at, head : head + 1]
                    own = slice(head, head + 1)
                    gap = jnp.minimum(column - cum_s[group, own, at], log_s[group, own, at])
                    tables.append((scores * jnp.exp2(gap)).astype(BF16))
                xp = xb[:, q * 2 * P_SIZE : (q + 1) * 2 * P_SIZE]
                stacked = jnp.concatenate([jnp.where(first, xp, zero), jnp.where(first, zero, xp)], 0)
                within.append(dot(jnp.concatenate(tables, 1), stacked))
            xs = xb.astype(F32)
            y = jnp.concatenate(within, 1) + carried + skip * xs
            gate = half_silu(z[at, lanes].astype(F32) * 0.5)
            uv_out[at, lanes] = (y * gate).astype(BF16)
            uv_out[at, width + s * SLAB : width + (s + 1) * SLAB] = (gate * rise * lead_row).astype(BF16)
            xf = (xs * dot(f_blk[at, :], sel)).astype(BF16)
            state[:, lanes] = old * fade_row + dot(b_mat, xf, ((0,), (0,)))

    lax.fori_loop(0, length // STEP_B, turn, 0)


def scan_part(order, part, info, token, x, z, bc, cum, cum_s, log_s, f_blk, e_blk, by_row, ones):
    length, full = x.shape
    width = full // B_PARTS
    return pl.pallas_call(
        functools.partial(scan_kernel, order, part),
        in_specs=[SCALAR, FAR, FAR] + [FULL] * 8 + [ANY],
        out_specs=FULL,
        out_shape=jax.ShapeDtypeStruct((length, 2 * width), BF16),
        scratch_shapes=[
            pltpu.VMEM((length, width), BF16),
            pltpu.VMEM((length, width), BF16),
            pltpu.SemaphoreType.DMA((2, length // STEP_B)),
            pltpu.VMEM((N, width), F32),
        ],
        compiler_params=params(16),
        cost_estimate=CHEAP,
        name="scan_part",
    )(info, x, z, bc, cum, cum_s, log_s, f_blk, e_blk, by_row, ones, token)


def norm_kernel(row, ahead, info, bc0, bc1, state0, state1, gain, *refs):
    uvs, out = refs[:-1][-2 * B_PARTS :], refs[-1]
    skipped = out.shape[0] - ROWS_C * (out.shape[0] // ROWS_C // (2 if ahead else 1))
    count = out.shape[0] - skipped
    per = state0.shape[1]
    part = per // B_PARTS
    if ahead:
        out[0:skipped, :] = refs[0][...]

    def step(j, _):
        to = pl.ds(pl.multiple_of(skipped + j * ROWS_C, ROWS_C), ROWS_C)
        at = pl.ds(pl.multiple_of(info[ROWS + row] * count + j * ROWS_C, ROWS_C), ROWS_C)
        for order, (bc, state) in enumerate(((bc0, state0), (bc1, state1))):
            c_mat = bc[at, N : 2 * N]
            pieces = []
            squares = None
            for p in range(B_PARTS):
                uv = uvs[order * B_PARTS + p]
                inc = state[:, p * part : (p + 1) * part]
                gated = uv[at, 0:part].astype(F32) + uv[at, part:].astype(F32) * dot(c_mat, inc)
                square = jnp.sum(gated * gated, axis=-1, keepdims=True)
                squares = square if squares is None else squares + square
                pieces.append(gated)
            scale = lax.rsqrt(squares * (1.0 / per) + EPS)
            for p, gated in enumerate(pieces):
                lanes = pl.ds(pl.multiple_of(info[GROUP + order] * per + p * part, part), part)
                out[to, lanes] = (gated * scale * gain[:, lanes]).astype(BF16)
        return 0

    lax.fori_loop(0, count // ROWS_C, step, 0)


def norm_rows(row, info, count, tokens, bcs, states, gain, uvs, ahead=None):
    first = [] if ahead is None else [ahead]
    rows = count if ahead is None else 2 * count
    return pl.pallas_call(
        functools.partial(norm_kernel, row, ahead is not None),
        in_specs=[SCALAR] + [FULL] * (5 + len(first)) + [ANY] * len(tokens) + [FULL] * len(uvs),
        out_specs=FULL,
        out_shape=jax.ShapeDtypeStruct((rows, gain.shape[1]), BF16),
        compiler_params=params(16),
        cost_estimate=CHEAP,
        name="norm_rows",
    )(info, *bcs, *states, gain, *first, *tokens, *uvs)


def stream(base, w0_far, w1_far, w0, w1, sem):
    j = pl.program_id(0)
    tiles = pl.num_programs(0)

    def fetch(t):
        slot = lax.rem(t, SLOTS)
        lanes = pl.ds(pl.multiple_of((base + t) * TILE, TILE), TILE)
        return (
            pltpu.make_async_copy(w0_far.at[:, lanes], w0.at[slot], sem.at[0, slot]),
            pltpu.make_async_copy(w1_far.at[:, lanes], w1.at[slot], sem.at[1, slot]),
        )

    def start(t):
        @pl.when(t < tiles)
        def _():
            for copy in fetch(t):
                copy.start()

    @pl.when(j == 0)
    def _():
        for t in range(SLOTS - 1):
            start(t)

    start(j + SLOTS - 1)
    for copy in fetch(j):
        copy.wait()
    return lax.rem(j, SLOTS)


def buffers(depth):
    return [
        pltpu.VMEM((SLOTS, depth, TILE), BF16),
        pltpu.VMEM((SLOTS, depth, TILE), BF16),
        pltpu.SemaphoreType.DMA((2, SLOTS)),
    ]


def ahead_kernel(base, own, mate, w0_far, w1_far, out, w0, w1, sem):
    slot = stream(base, w0_far, w1_far, w0, w1, sem)
    out[...] = (dot(own[...], w0[slot]) + dot(mate[...], w1[slot])).astype(BF16)


def project_ahead(own, mate, w0, w1, first, count):
    rows, depth = own.shape
    return pl.pallas_call(
        functools.partial(ahead_kernel, first // TILE),
        grid=(count // TILE,),
        in_specs=[FULL, FULL, FAR, FAR],
        out_specs=pl.BlockSpec((rows, TILE), lambda j: (0, j)),
        out_shape=jax.ShapeDtypeStruct((rows, count), BF16),
        scratch_shapes=buffers(depth),
        compiler_params=params(20),
        cost_estimate=CHEAP,
        name="project_ahead",
    )(own, mate, w0, w1)


def both_kernel(base, owns, mate0, mate1, w0_far, w1_far, far, near, mates, w0, w1, sem):
    rows = far.shape[0]

    @pl.when(pl.program_id(0) == 0)
    def _():
        mates[0:rows, :] = mate0[...]
        mates[rows:, :] = mate1[...]

    slot = stream(base, w0_far, w1_far, w0, w1, sem)
    total = dot(owns[...], w0[slot]) + dot(mates[...], w1[slot])
    far[...] = total[0:rows].astype(BF16)
    near[...] = total[rows:]


def project_both(owns, mate0, mate1, w0, w1, first, count):
    rows, depth = mate0.shape
    placed = pl.BlockSpec((rows, TILE), lambda j: (0, j))
    return pl.pallas_call(
        functools.partial(both_kernel, first // TILE),
        grid=(count // TILE,),
        in_specs=[FULL] * 3 + [FAR] * 2,
        out_specs=[placed, placed],
        out_shape=[jax.ShapeDtypeStruct((rows, count), BF16), jax.ShapeDtypeStruct((rows, count), F32)],
        scratch_shapes=[pltpu.VMEM((2 * rows, depth), BF16)] + buffers(depth),
        compiler_params=params(24),
        cost_estimate=CHEAP,
        name="project_both",
    )(owns, mate0, mate1, w0, w1)


def near_kernel(split, owns, mate, w0_far, w1_far, arrived0, arrived1, out, w0, w1, sem):
    slot = stream(0, w0_far, w1_far, w0, w1, sem)
    rows = mate.shape[0]
    total = dot(owns[rows:, :], w0[slot]) + dot(mate[...], w1[slot])
    arrived = jnp.where(pl.program_id(0) < split, arrived0[...], arrived1[...])
    out[...] = (total + arrived.astype(F32)).astype(BF16)


def project_near(owns, mate, w0, w1, arrived0, arrived1):
    rows, depth = mate.shape
    split = arrived0.shape[1] // TILE
    tiles = split + arrived1.shape[1] // TILE
    return pl.pallas_call(
        functools.partial(near_kernel, split),
        grid=(tiles,),
        in_specs=[FULL, FULL, FAR, FAR]
        + [
            pl.BlockSpec((rows, TILE), lambda j: (0, jnp.minimum(j, split - 1))),
            pl.BlockSpec((rows, TILE), lambda j: (0, jnp.maximum(j - split, 0))),
        ],
        out_specs=pl.BlockSpec((rows, TILE), lambda j: (0, j)),
        out_shape=jax.ShapeDtypeStruct((rows, w0.shape[1]), BF16),
        scratch_shapes=buffers(depth),
        compiler_params=params(20),
        cost_estimate=CHEAP,
        name="project_near",
    )(owns, mate, w0, w1, arrived0, arrived1)


def add_kernel(part, arrived, _, out):
    out[...] = (part[...] + arrived[...].astype(F32)).astype(BF16)


def add_chunk(part, arrived, result, first):
    rows, count = arrived.shape
    base = first // TILE
    return pl.pallas_call(
        add_kernel,
        grid=(count // TILE,),
        in_specs=[pl.BlockSpec((rows, TILE), lambda j: (0, j))] * 2 + [ANY],
        out_specs=pl.BlockSpec((rows, TILE), lambda j: (0, base + j)),
        out_shape=jax.ShapeDtypeStruct(result.shape, BF16),
        input_output_aliases={2: 0},
        compiler_params=params(8),
        cost_estimate=CHEAP,
        name="add_chunk",
    )(part, arrived, result)


def shift(block, distance):
    size = lax.axis_size("seq")
    return lax.ppermute(block, "seq", [(i, i + distance) for i in range(size - distance)])


def swap(block, axis, bit):
    return lax.ppermute(block, axis, [(i, i ^ bit) for i in range(lax.axis_size(axis))])


def rotate(block, distance):
    size = lax.axis_size("seq")
    return lax.ppermute(block, "seq", [(i, (i + distance) % size) for i in range(size)])


def log_steps(info, got, keep, rates, done, pairs, scan_next):
    half = keep.shape[1]
    message = ((N + EXTRA, half), BF16)
    full = ((N, half), F32)
    msg, own, first, aux = combine(
        pair_kernel,
        (info, got, keep, rates, done),
        [SCALAR, FULL, FULL, FULL, ANY],
        [message, full, full, ((16, half), F32)],
        "pair",
    )
    behind = None
    covered = 0
    while True:
        got = shift(msg, 2 * (covered + 1))
        done = scan_next(msg)
        covered = 2 * covered + 1
        if covered >= pairs - 1:
            break
        operands, specs = [got, own, aux], [FULL, FULL, FULL]
        if behind is None:
            kernel = lambda g, o, a, t, m, b: wave_kernel(g, o, a, None, t, m, b)
        else:
            kernel = wave_kernel
            operands.append(behind)
            specs.append(FULL)
        msg, behind = combine(kernel, operands + [done], specs + [ANY], [message, ((N + 8, half), F32)], "wave")
    operands, specs = [info, got], [SCALAR, FULL]
    if behind is None:
        kernel = lambda o, g, f, a, t, b, h: last_kernel(o, g, None, f, a, t, b, h)
    else:
        kernel = last_kernel
        operands.append(behind)
        specs.append(FULL)
    out = ((N, half), BF16)
    back, held = combine(kernel, operands + [first, aux, done], specs + [FULL, FULL, ANY], [out, out], "last")
    return back, held


def local(
    x_input,
    z_input,
    bc_input,
    conv_weight_x,
    conv_weight_bc,
    step_size,
    log_decay,
    skip_gain,
    norm_gain,
    out_weight,
):
    length, width = x_input.shape
    heads = step_size.shape[1]
    ways = lax.axis_size("head")
    pairs = lax.axis_size("seq") // 2
    mine = lax.axis_index("head")
    half = width // 2
    seq = lax.axis_index("seq")
    info = jnp.stack([seq & 1, mine ^ 3, mine ^ 2, mine ^ 1, mine, seq >> 1, seq, 1 - (seq & 1), seq & 1]).astype(jnp.int32)

    x_far, z_far, w_far = far(x_input, z_input, out_weight)
    (bc_far,) = far(bc_input)
    halo = rotate(tail_rows(x_far, bc_far), 1)
    bc = bc_input.reshape(length, -1)
    weight_mate = swap(out_weight, "head", 1)

    ones = jnp.asarray(np.tile(np.repeat(np.eye(heads), P_SIZE, axis=1), (2, 1)), BF16)
    cum, cum_s, log_s, f_dev, f_blk, e_blk, rates, by_row = decays(2, log_decay, step_size, skip_gain, ones)
    shared = (info, x_far, bc, halo, conv_weight_x, conv_weight_bc, f_dev, ones, rates)
    x0, bc0, send = conv_states(0, *shared)
    got = swap(send, "seq", 1)
    x1, bc1, keep = conv_states(1, *shared)

    uvs = []
    groups = [(x, z_far, y, cum, cum_s, log_s, f_blk, e_blk, by_row, ones) for x, y in zip(far(x0, x1), (bc0, bc1))]

    def scan_next(token):
        if len(uvs) < 2 * B_PARTS:
            order, part = divmod(len(uvs), B_PARTS)
            uvs.append(scan_part(order, part, info, token, *groups[order]))
        return uvs[-1]

    full = ((N, half), F32)
    message = ((N + EXTRA, half), BF16)
    done = keep
    out = ((N, half), BF16)
    if pairs > 1 and half % (pairs * N) == 0:
        piece = half // pairs
        part = ((N + EXTRA, piece), BF16)
        first, aux, *parts = combine(
            pair_split_kernel,
            (info, got, keep, rates, done),
            [SCALAR, FULL, FULL, FULL, ANY],
            [full, ((8, half), F32)] + [part] * pairs,
            "pair",
            [pltpu.VMEM(*message)],
        )
        parts = list(parts[:1]) + [rotate(parts[r], 2 * r) for r in range(1, pairs)]
        done = scan_next(scan_next(parts[0]))
        parts = combine(
            owner_kernel,
            [info] + parts + [done],
            [SCALAR] + [FULL] * pairs + [ANY],
            [((N, piece), BF16)] * pairs,
            "owner",
            [pltpu.VMEM((pairs, N + EXTRA, piece), BF16), pltpu.VMEM((pairs, N, piece), BF16)],
        )
        ready = parts[0]
        parts = list(parts[:1]) + [rotate(parts[r], 2 * r) for r in range(1, pairs)]
        done = scan_next(ready)
        back, held = combine(
            last_split_kernel,
            [info, first, aux, done] + parts,
            [SCALAR, FULL, FULL, ANY] + [FULL] * pairs,
            [out, out],
            "last",
            [pltpu.VMEM(*out)],
        )
    else:
        back, held = log_steps(info, got, keep, rates, done, pairs, scan_next)
    other = swap(back, "seq", 1)
    while len(uvs) < 2 * B_PARTS:
        scan_next(back)

    count = length // ways
    gain = norm_gain[None, :]

    def rows_for(row, *tokens, ahead=None):
        return norm_rows(row, info, count, tokens, (bc0, bc1), (other, held), gain, uvs, ahead)

    weights = (w_far, weight_mate)
    cuts = [out_weight.shape[1] * c // 16 for c in (0, 2, 6, 10, 14, 16)]
    far_mate = rows_for(0)
    far_own = rows_for(1, far_mate)
    far_mate = swap(far_mate, "head", 1)
    arrivals = []
    for lo, hi in zip(cuts[0:2], cuts[1:3]):
        sent = project_ahead(far_own, far_mate, *weights, lo, hi - lo)
        arrivals.append(swap(sent, "head", 2))
    near_mate = rows_for(2, sent)
    owns = rows_for(3, near_mate, arrivals[0], ahead=far_own)
    near_mate = swap(near_mate, "head", 1)
    parts = []
    for lo, hi in zip(cuts[2:-1], cuts[3:]):
        sent, part = project_both(owns, far_mate, near_mate, *weights, lo, hi - lo)
        arrivals.append(swap(sent, "head", 2))
        parts.append(part)
    result = project_near(owns, near_mate, *weights, *arrivals[:2])
    for part, arrived, lo in zip(parts, arrivals[2:], cuts[2:]):
        result = add_chunk(part, arrived, result, lo)
    return result


def solution(mesh):
    in_specs = (
        P("seq", "head"),
        P("seq", "head"),
        P("seq", "head", None),
        P(None, "head"),
        P(None, "head", None),
        P("seq", "head"),
        P("seq", "head"),
        P("head"),
        P("head"),
        P("head", None),
    )
    out_specs = P(("seq", "head"), None)
    return jax.shard_map(local, mesh=mesh, in_specs=in_specs, out_specs=out_specs, check_vma=False)
```

```python
import functools

import jax
import jax.numpy as jnp
from jax import lax
from jax.experimental import pallas as pl
from jax.experimental.pallas import tpu as pltpu
from jax.sharding import PartitionSpec as P

P_SIZE = 64
N = 128
KCONV = 4
EPS = 1e-05
LOG2E = 1.4426950408889634

TOK_A = 256
ROWS_A = 32
TOK_B = 128
STEP_B = 256
EXTRA = 16
SLAB = 256
ROWS_C = 128
TILE = 256
SLOTS = 4
LEAD = 16
B_PARTS = 2
HIGHEST = lax.Precision.HIGHEST
F32 = jnp.float32
BF16 = jnp.bfloat16


def params(mib):
    return pltpu.CompilerParams(vmem_limit_bytes=mib * 1024 * 1024)


CHEAP = pl.CostEstimate(flops=1, bytes_accessed=1, transcendentals=0)
SCALAR = pl.BlockSpec(memory_space=pltpu.SMEM)
FULL = pl.BlockSpec(memory_space=pltpu.VMEM)
FAR = pl.BlockSpec(memory_space=pltpu.HBM)
ANY = pl.BlockSpec(memory_space=pl.ANY)

ODD, ROWS, PAIR, SEQ, GROUP = 0, 1, 5, 6, 7


def dot(a, b, dims=((1,), (0,)), precision=None):
    return lax.dot_general(a, b, (dims, ((), ())), precision=precision, preferred_element_type=F32)


def half_silu(half):
    return half + half * jnp.tanh(half)


def far(*arrays):
    return [pltpu.with_memory_space_constraint(a, pltpu.HBM) for a in arrays]


def whole(shape):
    return pl.BlockSpec(shape, lambda *_: (0,) * len(shape))


def decay_kernel(info, ld_t, step_t, skip, cum, cum_s, log_s, f_dev, f_blk, e_blk, rates, by_row, ones):
    heads, length = ld_t.shape
    blocks = length // TOK_B
    per = heads // 2
    width = rates.shape[2]
    swapped = info[GROUP] == 1
    row = lax.broadcasted_iota(jnp.int32, (TOK_B, TOK_B), 0)
    col = lax.broadcasted_iota(jnp.int32, (TOK_B, TOK_B), 1)
    lower = (row >= col).astype(F32)
    upper = (row <= col).astype(F32)
    eye = (row == col).astype(BF16)

    def ordered(value):
        return jnp.where(swapped, jnp.concatenate([value[per:], value[:per]], 0), value)

    def put(ref, rows, value):
        high = value.astype(BF16)
        low = (value - high.astype(F32)).astype(BF16)
        for g in range(2):
            own = slice(g * per, (g + 1) * per)
            both = jnp.concatenate([high[own], low[own]], 0)
            ref[g, rows, :] = dot(eye, both, ((1,), (1,))).astype(BF16)

    member = lax.broadcasted_iota(jnp.int32, (per, width), 0) == lax.broadcasted_iota(jnp.int32, (per, width), 1) // P_SIZE
    member = member.astype(F32)
    ones[0:per, :] = member.astype(BF16)
    ones[per:, :] = member.astype(BF16)
    cums, totals, row_totals = [], [], []
    for b in range(blocks):
        rows = slice(b * TOK_B, (b + 1) * TOK_B)
        logs = ordered(ld_t[:, rows]) * LOG2E
        c = dot(lower, logs, ((1,), (1,)), HIGHEST)
        for g in range(2):
            cum[g, rows, :] = c[:, g * per : (g + 1) * per]
        row_totals.append(c[TOK_B - 1 : TOK_B, :])
        c = dot(logs, upper, precision=HIGHEST)
        cums.append(c)
        totals.append(c[:, TOK_B - 1 : TOK_B])
    before, row_before = [jnp.zeros_like(totals[0])], [jnp.zeros_like(row_totals[0])]
    for b in range(blocks):
        before.append(before[-1] + totals[b])
        row_before.append(row_before[-1] + row_totals[b])
    total = before[-1]
    logs = jnp.concatenate(row_totals + row_before[:-1] + row_before[-1:] * 8, 0)
    gains = jnp.broadcast_to(skip[...], (8, heads))
    gains = jnp.where(swapped, jnp.concatenate([gains[:, per:], gains[:, :per]], 1), gains)
    values = jnp.concatenate([jnp.exp2(logs), gains], 0)
    for g in range(2):
        spread = dot(values[:, g * per : (g + 1) * per], member, precision=HIGHEST)
        rates[g] = spread
        for b in range(2 * blocks):
            by_row[g, b] = spread[b : b + 1, :]
        by_row[g, 2 * blocks] = spread[2 * blocks + 8 : 2 * blocks + 9, :]
    for b in range(blocks):
        rows = slice(b * TOK_B, (b + 1) * TOK_B)
        s = ordered(step_t[:, rows])
        log_step = jnp.log2(s)
        shifted = cums[b] - log_step
        for g in range(2):
            own = slice(g * per, (g + 1) * per)
            log_s[g, :, rows] = log_step[own, :]
            cum_s[g, :, rows] = shifted[own, :]
        put(f_dev, rows, jnp.exp2(total - (cums[b] + before[b])) * s)
        put(f_blk, rows, jnp.exp2(totals[b] - cums[b]) * s)
        put(e_blk, rows, jnp.exp2(cums[b]))


def decays(info, log_decay, step, skip, width):
    length, heads = log_decay.shape
    blocks = length // TOK_B
    per = heads // 2
    across = jax.ShapeDtypeStruct((2, per, length), F32)
    pair = jax.ShapeDtypeStruct((2, length, 2 * per), BF16)
    shapes = (
        jax.ShapeDtypeStruct((2, length, per), F32),
        across,
        across,
        pair,
        pair,
        pair,
        jax.ShapeDtypeStruct((2, 2 * blocks + 16, width), F32),
        jax.ShapeDtypeStruct((2, 2 * blocks + 1, 1, width), F32),
        jax.ShapeDtypeStruct((2 * per, width), BF16),
    )
    return pl.pallas_call(
        decay_kernel,
        in_specs=[SCALAR] + [FULL] * 3,
        out_specs=[FULL] * len(shapes),
        out_shape=shapes,
        compiler_params=params(16),
        cost_estimate=CHEAP,
        name="decays",
    )(info, *far(log_decay.T, step.T, skip[None, :]))


def tail_kernel(x, bc, out):
    width, bc_width = x.shape[1], bc.shape[2]
    out[:, 0:width] = x[...]
    for g in range(bc.shape[1]):
        out[:, width + g * bc_width : width + (g + 1) * bc_width] = bc[:, g, :]


def tail_rows(x, bc):
    length, width = x.shape
    groups, bc_width = bc.shape[1:]
    at = length // LEAD - 1
    shape = (LEAD, width + groups * bc_width)
    return pl.pallas_call(
        tail_kernel,
        grid=(1,),
        in_specs=[
            pl.BlockSpec((LEAD, width), lambda i: (at, 0)),
            pl.BlockSpec((LEAD, groups, bc_width), lambda i: (at, 0, 0)),
        ],
        out_specs=whole(shape),
        out_shape=jax.ShapeDtypeStruct(shape, BF16),
        compiler_params=params(8),
        cost_estimate=CHEAP,
        name="tail_rows",
    )(x, bc)


def put_message(ref, state, decay):
    high = decay.astype(BF16)
    low = (decay - high.astype(F32)).astype(BF16)
    rest = jnp.zeros((EXTRA - 2, state.shape[1]), BF16)
    ref[0:N, :] = state.astype(BF16)
    ref[N:, :] = jnp.concatenate([high, low, rest], 0)


def take_message(ref):
    extra = ref[N:, :].astype(F32)
    return ref[0:N, :].astype(F32), extra[0:1] + extra[1:2]


def conv_kernel(
    order, info, x, x_lead, bc, bc_lead, halo, bc_halo, wx, wbc, f_dev, ones, rates, x_out, bc_out, final, xf, state, down
):
    i = pl.program_id(0)
    rows, width = x.shape
    group = info[GROUP + order]

    @pl.when(i == 0)
    def _():
        state[...] = jnp.zeros_like(state)
        row = lax.broadcasted_iota(jnp.int32, down.shape, 0)
        col = lax.broadcasted_iota(jnp.int32, down.shape, 1)
        down[...] = (row == col + 1).astype(BF16)

    def conv(src, first, behind, weights, emit):
        at_start = jnp.where(info[SEQ] == 0, jnp.zeros_like(first), first)
        lead = jnp.where(i == 0, at_start, behind).astype(F32)
        w0, w1, w2, w3 = [w * 0.5 for w in weights]
        back = LEAD - 8
        lead_r1 = pltpu.roll(lead, 1, 0)
        last_p = (w1 * lead + w0 * lead_r1)[back:]
        moved = dot(down[...], src)
        top = lax.broadcasted_iota(jnp.int32, (8, lead.shape[1]), 0) == 0
        head = jnp.where(top, jnp.broadcast_to(lead[LEAD - 1 :], top.shape), moved[0:8])
        for r in range(0, rows, ROWS_A):
            cur = src[r : r + ROWS_A].astype(F32)
            r1 = moved[r : r + ROWS_A] if r else jnp.concatenate([head, moved[8:ROWS_A]], 0)
            p = w1 * cur + w0 * r1
            p2 = pltpu.roll(jnp.concatenate([last_p, p], 0), 2, 0)[8:]
            emit(r, half_silu((w3 * cur + w2 * r1) + p2))
            last_p = p[ROWS_A - 8 :]

    for lanes in range(0, 2 * N, SLAB):
        ds = slice(lanes, lanes + SLAB)

        def emit_bc(r, value):
            bc_out[r : r + ROWS_A, ds] = value.astype(BF16)

        weights = [jnp.where(group == 0, wbc[k, 0:1, ds], wbc[k, 1:2, ds]) for k in range(KCONV)]
        conv(bc[:, ds], bc_halo[:, ds], bc_lead[:, ds], weights, emit_bc)

    for lanes in range(0, width, SLAB):
        ds = slice(lanes, lanes + SLAB)
        scale = dot(f_dev[0], ones[:, ds])

        def emit(r, value):
            x_out[r : r + ROWS_A, ds] = value.astype(BF16)
            xf[r : r + ROWS_A, ds] = (value * scale[r : r + ROWS_A]).astype(BF16)

        weights = [wx[k : k + 1, ds] for k in range(KCONV)]
        conv(x[:, ds], halo[:, ds], x_lead[:, ds], weights, emit)

    state[...] += dot(bc_out[:, 0:N], xf[...], ((0,), (0,)))

    @pl.when(i == pl.num_programs(0) - 1)
    def _():
        if order == 0:
            row = rates.shape[1] - 16
            put_message(final, state[...], rates[0, row : row + 1, :])
        else:
            final[...] = state[...]


def conv_states(order, info, x, bc, halo, wx, wbc, f_dev, ones, rates):
    length, full = x.shape
    width = full // 2
    lead = lambda i, info: (jnp.maximum(i * (TOK_A // LEAD) - 1, 0), info[GROUP + order])
    block = lambda i, info: (i, info[GROUP + order])
    column = lambda i, info: (0, info[GROUP + order])
    rows = lambda i, info: (i, 0)
    final = ((N + EXTRA, width), BF16) if order == 0 else ((N, width), F32)
    return pl.pallas_call(
        functools.partial(conv_kernel, order),
        grid_spec=pltpu.PrefetchScalarGridSpec(
            num_scalar_prefetch=1,
            grid=(length // TOK_A,),
            in_specs=[
                pl.BlockSpec((TOK_A, width), block),
                pl.BlockSpec((LEAD, width), lead),
                pl.BlockSpec((TOK_A, 2 * N), block),
                pl.BlockSpec((LEAD, 2 * N), lead),
                pl.BlockSpec((LEAD, width), column),
                pl.BlockSpec((LEAD, 2 * N), lambda i, info: (0, full // (2 * N) + info[GROUP + order])),
                pl.BlockSpec((KCONV, width), column),
                whole(wbc.shape),
                pl.BlockSpec((1, TOK_A, f_dev.shape[2]), lambda i, info: (order, i, 0)),
                whole(ones.shape),
                pl.BlockSpec((1,) + rates.shape[1:], lambda i, info: (order, 0, 0)),
            ],
            out_specs=[
                pl.BlockSpec((TOK_A, width), rows),
                pl.BlockSpec((TOK_A, 2 * N), rows),
                whole(final[0]),
            ],
            scratch_shapes=[
                pltpu.VMEM((TOK_A, width), BF16),
                pltpu.VMEM((N, width), F32),
                pltpu.VMEM((TOK_A, TOK_A), BF16),
            ],
        ),
        out_shape=(
            pltpu.HBM((length, width), BF16),
            jax.ShapeDtypeStruct((length, 2 * N), BF16),
            jax.ShapeDtypeStruct(*final),
        ),
        compiler_params=params(16),
        cost_estimate=CHEAP,
        name="conv_states",
    )(info, x, x, bc, bc, halo, halo, wx, wbc, f_dev, ones, rates)


def pair_kernel(info, got, keep, rates, _, msg, own, first, aux):
    half = keep.shape[1]
    is_odd = info[ODD] == 1
    arrived, their = take_message(got)
    row = rates.shape[1] - 16
    mine = rates[1, row : row + 1, :]
    early = jnp.where(is_odd, arrived, keep[...])
    late = jnp.where(is_odd, keep[...], arrived)
    even_decay = jnp.where(is_odd, their, mine)
    odd_decay = jnp.where(is_odd, mine, their)
    state = odd_decay * early + late
    own[...] = state
    first[...] = early
    aux[0:8, :] = jnp.broadcast_to(even_decay, (8, half))
    aux[8:16, :] = jnp.broadcast_to(even_decay * odd_decay, (8, half))
    put_message(msg, state, even_decay * odd_decay)


def wave_kernel(got, own, aux, behind_in, _, msg, behind):
    before, decay = take_message(got)
    if behind_in is not None:
        before_decay = behind_in[N : N + 1, :]
        before = behind_in[0:N, :] + before_decay * before
        decay = before_decay * decay
    pair_decay = aux[8:9, :]
    behind[0:N, :] = before
    behind[N:, :] = jnp.broadcast_to(decay, (8, before.shape[1]))
    put_message(msg, own[...] + pair_decay * before, pair_decay * decay)


def last_kernel(info, got, behind_in, first, aux, _, back, held):
    is_odd = info[ODD] == 1
    before, _unused = take_message(got)
    if behind_in is not None:
        before = behind_in[0:N, :] + behind_in[N : N + 1, :] * before
    entering_odd = aux[0:1, :] * before + first[...]
    back[...] = jnp.where(is_odd, before, entering_odd).astype(BF16)
    held[...] = jnp.where(is_odd, entering_odd, before).astype(BF16)


def pair_split_kernel(info, got, keep, rates, _, first, aux, *refs):
    outs, wide = refs[:-1], refs[-1]
    half = keep.shape[1]
    pairs = len(outs)
    piece = half // pairs
    is_odd = info[ODD] == 1
    arrived, their = take_message(got)
    row = rates.shape[1] - 16
    mine = rates[1, row : row + 1, :]
    early = jnp.where(is_odd, arrived, keep[...])
    late = jnp.where(is_odd, keep[...], arrived)
    even_decay = jnp.where(is_odd, their, mine)
    odd_decay = jnp.where(is_odd, mine, their)
    first[...] = early
    aux[...] = jnp.broadcast_to(even_decay, (8, half))
    put_message(wide, odd_decay * early + late, even_decay * odd_decay)
    for r in range(pairs):
        owner = lax.rem(info[PAIR] + r, pairs)
        outs[r][...] = wide[:, pl.ds(pl.multiple_of(owner * piece, piece), piece)]


def owner_kernel(info, *refs):
    pairs = (len(refs) - 3) // 2
    ins, outs = refs[:pairs], refs[pairs + 1 : 2 * pairs + 1]
    states, prefixes = refs[-2:]
    for r in range(pairs):
        states[lax.rem(info[PAIR] + pairs - r, pairs)] = ins[r][...]
    before = jnp.zeros(prefixes.shape[1:], F32)
    for q in range(pairs):
        prefixes[q] = before.astype(BF16)
        if q < pairs - 1:
            state, decay = take_message(states.at[q])
            before = decay * before + state
    for r in range(pairs):
        outs[r][...] = prefixes[lax.rem(info[PAIR] + r, pairs)]


def last_split_kernel(info, first, aux, _, *refs):
    pairs = len(refs) - 3
    back, held, wide = refs[-3:]
    piece = back.shape[1] // pairs
    for r in range(pairs):
        owner = lax.rem(info[PAIR] + pairs - r, pairs)
        wide[:, pl.ds(pl.multiple_of(owner * piece, piece), piece)] = refs[r][...]
    is_odd = info[ODD] == 1
    before = wide[...].astype(F32)
    entering_odd = aux[0:1, :] * before + first[...]
    back[...] = jnp.where(is_odd, before, entering_odd).astype(BF16)
    held[...] = jnp.where(is_odd, entering_odd, before).astype(BF16)


def combine(kernel, operands, specs, outs, name, scratch=()):
    return pl.pallas_call(
        kernel,
        in_specs=specs,
        out_specs=[FULL] * len(outs),
        out_shape=[jax.ShapeDtypeStruct(s, t) for s, t in outs],
        scratch_shapes=list(scratch),
        compiler_params=params(16),
        cost_estimate=CHEAP,
        name=name,
    )(*operands)


def scan_kernel(order, part, info, x_far, z_far, bc, cum, cum_s, log_s, f_blk, e_blk, by_row, ones, _, uv_out, x, z, sem, state):
    length, width = x.shape
    per_slab = SLAB // P_SIZE
    inner = STEP_B // TOK_B
    blocks = length // TOK_B
    first_head = part * width // P_SIZE
    first_lane = info[GROUP + order] * x_far.shape[1] + part * width

    def fetch(step):
        piece = pl.ds(pl.multiple_of(step * STEP_B, STEP_B), STEP_B)
        return (
            pltpu.make_async_copy(x_far.at[piece, pl.ds(part * width, width)], x.at[piece], sem.at[0, step]),
            pltpu.make_async_copy(
                z_far.at[piece, pl.ds(pl.multiple_of(first_lane, width), width)], z.at[piece], sem.at[1, step]
            ),
        )

    for step in range(length // STEP_B):
        for copy in fetch(step):
            copy.start()
    state[...] = jnp.zeros_like(state)

    row = lax.broadcasted_iota(jnp.int32, (TOK_B, TOK_B), 0)
    col = lax.broadcasted_iota(jnp.int32, (TOK_B, TOK_B), 1)
    keep = row >= col
    first = lax.broadcasted_iota(jnp.int32, (TOK_B, 2 * P_SIZE), 1) < P_SIZE
    zero = jnp.zeros((TOK_B, 2 * P_SIZE), BF16)

    def turn(step, _):
        for copy in fetch(step):
            copy.wait()
        for k in range(inner):
            block(step * inner + k)
        return 0

    def block(b):
        at = pl.ds(pl.multiple_of(b * TOK_B, TOK_B), TOK_B)
        b_mat = bc[at, 0:N]
        c_mat = bc[at, N : 2 * N]
        b_across = b_mat.T
        scores = jnp.where(keep, dot(c_mat, b_mat, ((1,), (1,))), 0.0)
        for s in range(width // SLAB):
            lanes = slice(s * SLAB, (s + 1) * SLAB)
            xb = x[at, lanes]
            wide = slice(part * width + s * SLAB, part * width + (s + 1) * SLAB)
            sel = ones[:, wide]
            fade_row = by_row[order, b, :, wide]
            lead_row = by_row[order, blocks + b, :, wide]
            skip = by_row[order, 2 * blocks, :, wide]
            old = state[:, lanes]
            rise = dot(e_blk[order, at, :], sel)
            carried = dot(c_mat, old.astype(BF16)) * rise
            within = []
            for q in range(per_slab // 2):
                tables = []
                for h in (2 * q, 2 * q + 1):
                    head = first_head + s * per_slab + h
                    column = cum[order, at, head : head + 1]
                    own = slice(head, head + 1)
                    gap = jnp.minimum(column - cum_s[order, own, at], log_s[order, own, at])
                    tables.append((scores * jnp.exp2(gap)).astype(BF16))
                xp = xb[:, q * 2 * P_SIZE : (q + 1) * 2 * P_SIZE]
                stacked = jnp.concatenate([jnp.where(first, xp, zero), jnp.where(first, zero, xp)], 0)
                within.append(dot(jnp.concatenate(tables, 1), stacked))
            xs = xb.astype(F32)
            y = jnp.concatenate(within, 1) + carried + skip * xs
            gate = half_silu(z[at, lanes].astype(F32) * 0.5)
            uv_out[at, lanes] = (y * gate).astype(BF16)
            uv_out[at, width + s * SLAB : width + (s + 1) * SLAB] = (gate * rise * lead_row).astype(BF16)
            xf = (xs * dot(f_blk[order, at, :], sel)).astype(BF16)
            state[:, lanes] = old * fade_row + dot(b_across, xf)

    lax.fori_loop(0, length // STEP_B, turn, 0)


def scan_part(order, part, info, token, x, z, bc, cum, cum_s, log_s, f_blk, e_blk, by_row, ones):
    length, full = x.shape
    width = full // B_PARTS
    return pl.pallas_call(
        functools.partial(scan_kernel, order, part),
        in_specs=[SCALAR, FAR, FAR] + [FULL] * 8 + [ANY],
        out_specs=FULL,
        out_shape=jax.ShapeDtypeStruct((length, 2 * width), BF16),
        scratch_shapes=[
            pltpu.VMEM((length, width), BF16),
            pltpu.VMEM((length, width), BF16),
            pltpu.SemaphoreType.DMA((2, length // STEP_B)),
            pltpu.VMEM((N, width), F32),
        ],
        compiler_params=params(16),
        cost_estimate=CHEAP,
        name="scan_part",
    )(info, x, z, bc, cum, cum_s, log_s, f_blk, e_blk, by_row, ones, token)


def norm_kernel(places, info, bc0, bc1, state0, state1, gain, _, *refs):
    uvs, out = refs[:-1], refs[-1]
    count = out.shape[0] // len(places)
    per = state0.shape[1]
    part = per // B_PARTS

    def rows(first, base):
        to = pl.ds(pl.multiple_of(first, ROWS_C), ROWS_C)
        at = pl.ds(pl.multiple_of(base, ROWS_C), ROWS_C)
        for order, (bc, state) in enumerate(((bc0, state0), (bc1, state1))):
            c_mat = bc[at, N : 2 * N]
            pieces = []
            squares = None
            for p in range(B_PARTS):
                uv = uvs[order * B_PARTS + p]
                inc = state[:, p * part : (p + 1) * part]
                gated = uv[at, 0:part].astype(F32) + uv[at, part:].astype(F32) * dot(c_mat, inc)
                square = jnp.sum(gated * gated, axis=-1, keepdims=True)
                squares = square if squares is None else squares + square
                pieces.append(gated)
            scale = lax.rsqrt(squares * (1.0 / per) + EPS)
            for p, gated in enumerate(pieces):
                lanes = pl.ds(pl.multiple_of(info[GROUP + order] * per + p * part, part), part)
                out[to, lanes] = (gated * scale * gain[:, lanes]).astype(BF16)

    for k, place in enumerate(places):

        def step(j, _):
            rows(k * count + j * ROWS_C, info[ROWS + place] * count + j * ROWS_C)
            return 0

        lax.fori_loop(0, count // ROWS_C, step, 0)


def norm_rows(places, info, count, token, bcs, states, gain, uvs):
    return pl.pallas_call(
        functools.partial(norm_kernel, places),
        in_specs=[SCALAR] + [FULL] * 5 + [ANY] + [FULL] * len(uvs),
        out_specs=FULL,
        out_shape=jax.ShapeDtypeStruct((len(places) * count, gain.shape[1]), BF16),
        compiler_params=params(16),
        cost_estimate=CHEAP,
        name="norm_rows",
    )(info, *bcs, *states, gain, token, *uvs)


def stream(base, w0_far, w1_far, w0, w1, sem):
    j = pl.program_id(0)
    tiles = pl.num_programs(0)

    def fetch(t):
        slot = lax.rem(t, SLOTS)
        lanes = pl.ds(pl.multiple_of((base + t) * TILE, TILE), TILE)
        return (
            pltpu.make_async_copy(w0_far.at[:, lanes], w0.at[slot], sem.at[0, slot]),
            pltpu.make_async_copy(w1_far.at[:, lanes], w1.at[slot], sem.at[1, slot]),
        )

    def start(t):
        @pl.when(t < tiles)
        def _():
            for copy in fetch(t):
                copy.start()

    @pl.when(j == 0)
    def _():
        for t in range(SLOTS - 1):
            start(t)

    start(j + SLOTS - 1)
    for copy in fetch(j):
        copy.wait()
    return lax.rem(j, SLOTS)


def buffers(depth):
    return [
        pltpu.VMEM((SLOTS, depth, TILE), BF16),
        pltpu.VMEM((SLOTS, depth, TILE), BF16),
        pltpu.SemaphoreType.DMA((2, SLOTS)),
    ]


def ahead_kernel(base, owns, mates, w0_far, w1_far, out, w0, w1, sem):
    slot = stream(base, w0_far, w1_far, w0, w1, sem)
    rows = out.shape[0]
    out[...] = (dot(owns[0:rows, :], w0[slot]) + dot(mates[0:rows, :], w1[slot])).astype(BF16)


def project_ahead(owns, mates, w0, w1, first, count):
    rows, depth = owns.shape[0] // 2, owns.shape[1]
    return pl.pallas_call(
        functools.partial(ahead_kernel, first // TILE),
        grid=(count // TILE,),
        in_specs=[FULL, FULL, FAR, FAR],
        out_specs=pl.BlockSpec((rows, TILE), lambda j: (0, j)),
        out_shape=jax.ShapeDtypeStruct((rows, count), BF16),
        scratch_shapes=buffers(depth),
        compiler_params=params(20),
        cost_estimate=CHEAP,
        name="project_ahead",
    )(owns, mates, w0, w1)


def both_kernel(base, cut, owns, mates, w0_far, w1_far, *refs):
    fars, near, w0, w1, sem = refs[:-4], *refs[-4:]
    rows = near.shape[0]
    slot = stream(base, w0_far, w1_far, w0, w1, sem)
    total = dot(owns[...], w0[slot]) + dot(mates[...], w1[slot])
    near[...] = total[rows:]
    for k, far_out in enumerate(fars):

        @pl.when(pl.program_id(0) // cut == k)
        def _():
            far_out[...] = total[0:rows].astype(BF16)


def project_both(owns, mates, w0, w1, first, count, chunk):
    rows, depth = owns.shape[0] // 2, owns.shape[1]
    cut = chunk // TILE
    chunks = count // chunk

    def placed(k):
        return pl.BlockSpec((rows, TILE), lambda j: (0, jnp.clip(j - k * cut, 0, cut - 1)))

    *fars, near = pl.pallas_call(
        functools.partial(both_kernel, first // TILE, cut),
        grid=(count // TILE,),
        in_specs=[FULL] * 2 + [FAR] * 2,
        out_specs=[placed(k) for k in range(chunks)] + [pl.BlockSpec((rows, TILE), lambda j: (0, j))],
        out_shape=[jax.ShapeDtypeStruct((rows, chunk), BF16)] * chunks + [jax.ShapeDtypeStruct((rows, count), F32)],
        scratch_shapes=buffers(depth),
        compiler_params=params(24),
        cost_estimate=CHEAP,
        name="project_both",
    )(owns, mates, w0, w1)
    return fars, near


def near_kernel(owns, mates, w0_far, w1_far, arrived, out, w0, w1, sem):
    slot = stream(0, w0_far, w1_far, w0, w1, sem)
    rows = out.shape[0]
    total = dot(owns[rows:, :], w0[slot]) + dot(mates[rows:, :], w1[slot])
    out[...] = (total + arrived[...].astype(F32)).astype(BF16)


def project_near(owns, mates, w0, w1, arrived):
    rows, depth = owns.shape[0] // 2, owns.shape[1]
    placed = pl.BlockSpec((rows, TILE), lambda j: (0, j))
    return pl.pallas_call(
        near_kernel,
        grid=(arrived.shape[1] // TILE,),
        in_specs=[FULL, FULL, FAR, FAR, placed],
        out_specs=placed,
        out_shape=jax.ShapeDtypeStruct((rows, w0.shape[1]), BF16),
        scratch_shapes=buffers(depth),
        compiler_params=params(20),
        cost_estimate=CHEAP,
        name="project_near",
    )(owns, mates, w0, w1, arrived)


def add_kernel(near, *refs):
    arrived, out = refs[:-2], refs[-1]
    chunk = arrived[0].shape[1]
    for k, part in enumerate(arrived):
        lanes = slice(k * chunk, (k + 1) * chunk)
        out[:, lanes] = (near[:, lanes] + part[...].astype(F32)).astype(BF16)


def add_chunks(near, first, arrived, result, at):
    rows, chunk = arrived[0].shape
    count = chunk * len(arrived)
    return pl.pallas_call(
        add_kernel,
        grid=(1,),
        in_specs=[pl.BlockSpec((rows, count), lambda j: (0, first // count))] + [FULL] * len(arrived) + [ANY],
        out_specs=pl.BlockSpec((rows, count), lambda j: (0, at // count)),
        out_shape=jax.ShapeDtypeStruct(result.shape, BF16),
        input_output_aliases={1 + len(arrived): 0},
        compiler_params=params(8),
        cost_estimate=CHEAP,
        name="add_chunks",
    )(near, *arrived, result)


def shift(block, distance):
    size = lax.axis_size("seq")
    return lax.ppermute(block, "seq", [(i, i + distance) for i in range(size - distance)])


def swap(block, axis, bit):
    return lax.ppermute(block, axis, [(i, i ^ bit) for i in range(lax.axis_size(axis))])


def rotate(block, distance):
    size = lax.axis_size("seq")
    return lax.ppermute(block, "seq", [(i, (i + distance) % size) for i in range(size)])


def log_steps(info, got, keep, rates, done, pairs, scan_next):
    half = keep.shape[1]
    message = ((N + EXTRA, half), BF16)
    full = ((N, half), F32)
    msg, own, first, aux = combine(
        pair_kernel,
        (info, got, keep, rates, done),
        [SCALAR, FULL, FULL, FULL, ANY],
        [message, full, full, ((16, half), F32)],
        "pair",
    )
    behind = None
    covered = 0
    while True:
        got = shift(msg, 2 * (covered + 1))
        done = scan_next(msg)
        covered = 2 * covered + 1
        if covered >= pairs - 1:
            break
        operands, specs = [got, own, aux], [FULL, FULL, FULL]
        if behind is None:
            kernel = lambda g, o, a, t, m, b: wave_kernel(g, o, a, None, t, m, b)
        else:
            kernel = wave_kernel
            operands.append(behind)
            specs.append(FULL)
        msg, behind = combine(kernel, operands + [done], specs + [ANY], [message, ((N + 8, half), F32)], "wave")
    operands, specs = [info, got], [SCALAR, FULL]
    if behind is None:
        kernel = lambda o, g, f, a, t, b, h: last_kernel(o, g, None, f, a, t, b, h)
    else:
        kernel = last_kernel
        operands.append(behind)
        specs.append(FULL)
    out = ((N, half), BF16)
    back, held = combine(kernel, operands + [first, aux, done], specs + [FULL, FULL, ANY], [out, out], "last")
    return back, held


def local(
    x_input,
    z_input,
    bc_input,
    conv_weight_x,
    conv_weight_bc,
    step_size,
    log_decay,
    skip_gain,
    norm_gain,
    out_weight,
):
    length, width = x_input.shape
    heads = step_size.shape[1]
    ways = lax.axis_size("head")
    pairs = lax.axis_size("seq") // 2
    mine = lax.axis_index("head")
    half = width // 2
    seq = lax.axis_index("seq")
    info = jnp.stack([seq & 1, mine ^ 3, mine ^ 2, mine ^ 1, mine, seq >> 1, seq, 1 - (seq & 1), seq & 1]).astype(jnp.int32)

    x_far, z_far, w_far = far(x_input, z_input, out_weight)
    (bc_far,) = far(bc_input)
    halo = rotate(tail_rows(x_far, bc_far), 1)
    bc = bc_input.reshape(length, -1)
    weight_mate = swap(out_weight, "head", 1)

    cum, cum_s, log_s, f_dev, f_blk, e_blk, rates, by_row, ones = decays(info, log_decay, step_size, skip_gain, half)
    taps = far(conv_weight_x, conv_weight_bc)
    shared = (info, x_far, bc, halo, *taps, f_dev, ones, rates)
    x0, bc0, send = conv_states(0, *shared)
    got = swap(send, "seq", 1)
    x1, bc1, keep = conv_states(1, *shared)

    uvs = []
    groups = [(x, z_far, y, cum, cum_s, log_s, f_blk, e_blk, by_row, ones) for x, y in zip(far(x0, x1), (bc0, bc1))]

    def scan_next(token):
        if len(uvs) < 2 * B_PARTS:
            order, part = divmod(len(uvs), B_PARTS)
            uvs.append(scan_part(order, part, info, token, *groups[order]))
        return uvs[-1]

    full = ((N, half), F32)
    message = ((N + EXTRA, half), BF16)
    done = keep
    out = ((N, half), BF16)
    if pairs > 1 and half % (pairs * N) == 0:
        piece = half // pairs
        part = ((N + EXTRA, piece), BF16)
        first, aux, *parts = combine(
            pair_split_kernel,
            (info, got, keep, rates, done),
            [SCALAR, FULL, FULL, FULL, ANY],
            [full, ((8, half), F32)] + [part] * pairs,
            "pair",
            [pltpu.VMEM(*message)],
        )
        parts = list(parts[:1]) + [rotate(parts[r], 2 * r) for r in range(1, pairs)]
        done = scan_next(scan_next(parts[0]))
        parts = combine(
            owner_kernel,
            [info] + parts + [done],
            [SCALAR] + [FULL] * pairs + [ANY],
            [((N, piece), BF16)] * pairs,
            "owner",
            [pltpu.VMEM((pairs, N + EXTRA, piece), BF16), pltpu.VMEM((pairs, N, piece), BF16)],
        )
        ready = parts[0]
        parts = list(parts[:1]) + [rotate(parts[r], 2 * r) for r in range(1, pairs)]
        done = scan_next(ready)
        back, held = combine(
            last_split_kernel,
            [info, first, aux, done] + parts,
            [SCALAR, FULL, FULL, ANY] + [FULL] * pairs,
            [out, out],
            "last",
            [pltpu.VMEM(*out)],
        )
    else:
        back, held = log_steps(info, got, keep, rates, done, pairs, scan_next)
    other = swap(back, "seq", 1)
    while len(uvs) < 2 * B_PARTS:
        scan_next(back)

    count = length // ways
    gain = norm_gain[None, :]

    def rows_for(token, *places):
        return norm_rows(places, info, count, token, (bc0, bc1), (other, held), gain, uvs)

    mates = rows_for(held, 0, 2)
    owns = rows_for(mates, 1, 3)
    operands = (owns, swap(mates, "head", 1), w_far, weight_mate)
    columns = out_weight.shape[1]
    chunk = columns // 8
    first = swap(project_ahead(*operands, 0, chunk), "head", 2)
    calls = []
    for lo, hi in ((1, 2), (2, 4), (4, 6), (6, 8)):
        sent, near = project_both(*operands, lo * chunk, (hi - lo) * chunk, chunk)
        calls.append((near, lo, [swap(part, "head", 2) for part in sent]))
    result = project_near(*operands, first)
    for near, lo, arrived in calls[:-1]:
        result = add_chunks(near, 0, arrived, result, lo * chunk)
    near, lo, arrived = calls[-1]
    for k, part in enumerate(arrived):
        result = add_chunks(near, k * chunk, [part], result, (lo + k) * chunk)
    return result


def solution(mesh):
    in_specs = (
        P("seq", "head"),
        P("seq", "head"),
        P("seq", "head", None),
        P(None, "head"),
        P(None, "head", None),
        P("seq", "head"),
        P("seq", "head"),
        P("head"),
        P("head"),
        P("head", None),
    )
    out_specs = P(("seq", "head"), None)
    return jax.shard_map(local, mesh=mesh, in_specs=in_specs, out_specs=out_specs, check_vma=False)
```

```python
import functools

import jax
import jax.numpy as jnp
from jax import lax
from jax.experimental import pallas as pl
from jax.experimental.pallas import tpu as pltpu
from jax.sharding import PartitionSpec as P

P_SIZE = 64
N = 128
KCONV = 4
EPS = 1e-05
LOG2E = 1.4426950408889634

TOK_A = 256
ROWS_A = 32
TOK_B = 128
STEP_B = 256
EXTRA = 16
SLAB = 256
ROWS_C = 128
TILE = 256
SLOTS = 4
LEAD = 16
B_PARTS = 2
HIGHEST = lax.Precision.HIGHEST
F32 = jnp.float32
BF16 = jnp.bfloat16


def params(mib):
    return pltpu.CompilerParams(vmem_limit_bytes=mib * 1024 * 1024)


CHEAP = pl.CostEstimate(flops=1, bytes_accessed=1, transcendentals=0)
SCALAR = pl.BlockSpec(memory_space=pltpu.SMEM)
FULL = pl.BlockSpec(memory_space=pltpu.VMEM)
FAR = pl.BlockSpec(memory_space=pltpu.HBM)
ANY = pl.BlockSpec(memory_space=pl.ANY)

ODD, ROWS, PAIR, SEQ, GROUP = 0, 1, 5, 6, 7


def dot(a, b, dims=((1,), (0,)), precision=None):
    return lax.dot_general(a, b, (dims, ((), ())), precision=precision, preferred_element_type=F32)


def half_silu(half):
    return half + half * jnp.tanh(half)


def far(*arrays):
    return [pltpu.with_memory_space_constraint(a, pltpu.HBM) for a in arrays]


def whole(shape):
    return pl.BlockSpec(shape, lambda *_: (0,) * len(shape))


def decay_kernel(info, ld_t, step_t, skip, cum, cum_s, log_s, f_dev, f_blk, e_blk, rates, ones):
    heads, length = ld_t.shape
    blocks = length // TOK_B
    per = heads // 2
    width = rates.shape[2]
    swapped = info[GROUP] == 1
    row = lax.broadcasted_iota(jnp.int32, (TOK_B, TOK_B), 0)
    col = lax.broadcasted_iota(jnp.int32, (TOK_B, TOK_B), 1)
    lower = (row >= col).astype(F32)
    upper = (row <= col).astype(F32)
    eye = (row == col).astype(BF16)

    def ordered(value):
        return jnp.where(swapped, jnp.concatenate([value[per:], value[:per]], 0), value)

    def put(ref, rows, value):
        high = value.astype(BF16)
        low = (value - high.astype(F32)).astype(BF16)
        for g in range(2):
            own = slice(g * per, (g + 1) * per)
            both = jnp.concatenate([high[own], low[own]], 0)
            ref[g, rows, :] = dot(eye, both, ((1,), (1,))).astype(BF16)

    member = lax.broadcasted_iota(jnp.int32, (per, width), 0) == lax.broadcasted_iota(jnp.int32, (per, width), 1) // P_SIZE
    member = member.astype(F32)
    ones[0:per, :] = member.astype(BF16)
    ones[per:, :] = member.astype(BF16)
    cums, totals, row_totals = [], [], []
    for b in range(blocks):
        rows = slice(b * TOK_B, (b + 1) * TOK_B)
        logs = ordered(ld_t[:, rows]) * LOG2E
        c = dot(lower, logs, ((1,), (1,)), HIGHEST)
        for g in range(2):
            cum[g, rows, :] = c[:, g * per : (g + 1) * per]
        row_totals.append(c[TOK_B - 1 : TOK_B, :])
        c = dot(logs, upper, precision=HIGHEST)
        cums.append(c)
        totals.append(c[:, TOK_B - 1 : TOK_B])
    before, row_before = [jnp.zeros_like(totals[0])], [jnp.zeros_like(row_totals[0])]
    for b in range(blocks):
        before.append(before[-1] + totals[b])
        row_before.append(row_before[-1] + row_totals[b])
    total = before[-1]
    logs = jnp.concatenate(row_totals + row_before[:-1] + row_before[-1:] * 8, 0)
    gains = jnp.broadcast_to(skip[...], (8, heads))
    gains = jnp.where(swapped, jnp.concatenate([gains[:, per:], gains[:, :per]], 1), gains)
    values = jnp.concatenate([jnp.exp2(logs), gains], 0)
    for g in range(2):
        rates[g] = dot(values[:, g * per : (g + 1) * per], member, precision=HIGHEST)
    for b in range(blocks):
        rows = slice(b * TOK_B, (b + 1) * TOK_B)
        s = ordered(step_t[:, rows])
        log_step = jnp.log2(s)
        shifted = cums[b] - log_step
        for g in range(2):
            own = slice(g * per, (g + 1) * per)
            log_s[g, :, rows] = log_step[own, :]
            cum_s[g, :, rows] = shifted[own, :]
        put(f_dev, rows, jnp.exp2(total - (cums[b] + before[b])) * s)
        put(f_blk, rows, jnp.exp2(totals[b] - cums[b]) * s)
        put(e_blk, rows, jnp.exp2(cums[b]))


def decays(info, log_decay, step, skip, width):
    length, heads = log_decay.shape
    blocks = length // TOK_B
    per = heads // 2
    across = jax.ShapeDtypeStruct((2, per, length), F32)
    pair = jax.ShapeDtypeStruct((2, length, 2 * per), BF16)
    shapes = (
        jax.ShapeDtypeStruct((2, length, per), F32),
        across,
        across,
        pair,
        pair,
        pair,
        jax.ShapeDtypeStruct((2, 2 * blocks + 16, width), F32),
        jax.ShapeDtypeStruct((2 * per, width), BF16),
    )
    return pl.pallas_call(
        decay_kernel,
        in_specs=[SCALAR] + [FULL] * 3,
        out_specs=[FULL] * len(shapes),
        out_shape=shapes,
        compiler_params=params(16),
        cost_estimate=CHEAP,
        name="decays",
    )(info, *far(log_decay.T, step.T, skip[None, :]))


def tail_kernel(x, bc, out):
    width, bc_width = x.shape[1], bc.shape[2]
    out[:, 0:width] = x[...]
    for g in range(bc.shape[1]):
        out[:, width + g * bc_width : width + (g + 1) * bc_width] = bc[:, g, :]


def tail_rows(x, bc):
    length, width = x.shape
    groups, bc_width = bc.shape[1:]
    at = length // LEAD - 1
    shape = (LEAD, width + groups * bc_width)
    return pl.pallas_call(
        tail_kernel,
        grid=(1,),
        in_specs=[
            pl.BlockSpec((LEAD, width), lambda i: (at, 0)),
            pl.BlockSpec((LEAD, groups, bc_width), lambda i: (at, 0, 0)),
        ],
        out_specs=whole(shape),
        out_shape=jax.ShapeDtypeStruct(shape, BF16),
        compiler_params=params(8),
        cost_estimate=CHEAP,
        name="tail_rows",
    )(x, bc)


def put_message(ref, state, decay):
    high = decay.astype(BF16)
    low = (decay - high.astype(F32)).astype(BF16)
    rest = jnp.zeros((EXTRA - 2, state.shape[1]), BF16)
    ref[0:N, :] = state.astype(BF16)
    ref[N:, :] = jnp.concatenate([high, low, rest], 0)


def take_message(ref):
    extra = ref[N:, :].astype(F32)
    return ref[0:N, :].astype(F32), extra[0:1] + extra[1:2]


def conv_kernel(
    order, info, x, x_lead, bc, bc_lead, halo, bc_halo, wx, wbc, f_dev, ones, rates, x_out, bc_out, final, xf, state, down
):
    i = pl.program_id(0)
    rows, width = x.shape
    group = info[GROUP + order]

    @pl.when(i == 0)
    def _():
        state[...] = jnp.zeros_like(state)
        row = lax.broadcasted_iota(jnp.int32, down.shape, 0)
        col = lax.broadcasted_iota(jnp.int32, down.shape, 1)
        down[...] = (lax.rem(row, rows) == col + 1 + row // rows).astype(BF16)

    def conv(src, first, behind, weights, emit):
        at_start = jnp.where(info[SEQ] == 0, jnp.zeros_like(first), first)
        lead = jnp.where(i == 0, at_start, behind).astype(F32)
        w0, w1, w2, w3 = [w * 0.5 for w in weights]
        moved = dot(down[...], src)
        around = jnp.concatenate([lead[LEAD - 8 :], src[0:8].astype(F32)], 0)
        for r in range(0, rows, ROWS_A):
            total = w3 * src[r : r + ROWS_A].astype(F32)
            for k, weight in ((1, w2), (2, w1), (3, w0)):
                first = (k - 1) * rows + r
                if r:
                    shifted = moved[first : first + ROWS_A]
                else:
                    top = pltpu.roll(around, k, 0)[8:]
                    shifted = jnp.concatenate([top, moved[first + 8 : first + ROWS_A]], 0)
                total = total + weight * shifted
            emit(r, half_silu(total))

    for lanes in range(0, 2 * N, SLAB):
        ds = slice(lanes, lanes + SLAB)

        def emit_bc(r, value):
            bc_out[r : r + ROWS_A, ds] = value.astype(BF16)

        weights = [jnp.where(group == 0, wbc[k, 0:1, ds], wbc[k, 1:2, ds]) for k in range(KCONV)]
        conv(bc[:, ds], bc_halo[:, ds], bc_lead[:, ds], weights, emit_bc)

    for lanes in range(0, width, SLAB):
        ds = slice(lanes, lanes + SLAB)
        scale = dot(f_dev[0], ones[:, ds])

        def emit(r, value):
            x_out[r : r + ROWS_A, ds] = value.astype(BF16)
            xf[r : r + ROWS_A, ds] = (value * scale[r : r + ROWS_A]).astype(BF16)

        weights = [wx[k : k + 1, ds] for k in range(KCONV)]
        conv(x[:, ds], halo[:, ds], x_lead[:, ds], weights, emit)

    state[...] += dot(bc_out[:, 0:N], xf[...], ((0,), (0,)))

    @pl.when(i == pl.num_programs(0) - 1)
    def _():
        if order == 0:
            row = rates.shape[1] - 16
            put_message(final, state[...], rates[0, row : row + 1, :])
        else:
            final[...] = state[...]


def conv_states(order, info, x, bc, halo, wx, wbc, f_dev, ones, rates):
    length, full = x.shape
    width = full // 2
    lead = lambda i, info: (jnp.maximum(i * (TOK_A // LEAD) - 1, 0), info[GROUP + order])
    block = lambda i, info: (i, info[GROUP + order])
    column = lambda i, info: (0, info[GROUP + order])
    rows = lambda i, info: (i, 0)
    final = ((N + EXTRA, width), BF16) if order == 0 else ((N, width), F32)
    return pl.pallas_call(
        functools.partial(conv_kernel, order),
        grid_spec=pltpu.PrefetchScalarGridSpec(
            num_scalar_prefetch=1,
            grid=(length // TOK_A,),
            in_specs=[
                pl.BlockSpec((TOK_A, width), block),
                pl.BlockSpec((LEAD, width), lead),
                pl.BlockSpec((TOK_A, 2 * N), block),
                pl.BlockSpec((LEAD, 2 * N), lead),
                pl.BlockSpec((LEAD, width), column),
                pl.BlockSpec((LEAD, 2 * N), lambda i, info: (0, full // (2 * N) + info[GROUP + order])),
                pl.BlockSpec((KCONV, width), column),
                whole(wbc.shape),
                pl.BlockSpec((1, TOK_A, f_dev.shape[2]), lambda i, info: (order, i, 0)),
                whole(ones.shape),
                pl.BlockSpec((1,) + rates.shape[1:], lambda i, info: (order, 0, 0)),
            ],
            out_specs=[
                pl.BlockSpec((TOK_A, width), rows),
                pl.BlockSpec((TOK_A, 2 * N), rows),
                whole(final[0]),
            ],
            scratch_shapes=[
                pltpu.VMEM((TOK_A, width), BF16),
                pltpu.VMEM((N, width), F32),
                pltpu.VMEM((3 * TOK_A, TOK_A), BF16),
            ],
        ),
        out_shape=(
            pltpu.HBM((length, width), BF16),
            jax.ShapeDtypeStruct((length, 2 * N), BF16),
            jax.ShapeDtypeStruct(*final),
        ),
        compiler_params=params(16),
        cost_estimate=CHEAP,
        name="conv_states",
    )(info, x, x, bc, bc, halo, halo, wx, wbc, f_dev, ones, rates)


def pair_kernel(info, got, keep, rates, _, msg, own, first, aux):
    half = keep.shape[1]
    is_odd = info[ODD] == 1
    arrived, their = take_message(got)
    row = rates.shape[1] - 16
    mine = rates[1, row : row + 1, :]
    early = jnp.where(is_odd, arrived, keep[...])
    late = jnp.where(is_odd, keep[...], arrived)
    even_decay = jnp.where(is_odd, their, mine)
    odd_decay = jnp.where(is_odd, mine, their)
    state = odd_decay * early + late
    own[...] = state
    first[...] = early
    aux[0:8, :] = jnp.broadcast_to(even_decay, (8, half))
    aux[8:16, :] = jnp.broadcast_to(even_decay * odd_decay, (8, half))
    put_message(msg, state, even_decay * odd_decay)


def wave_kernel(got, own, aux, behind_in, _, msg, behind):
    before, decay = take_message(got)
    if behind_in is not None:
        before_decay = behind_in[N : N + 1, :]
        before = behind_in[0:N, :] + before_decay * before
        decay = before_decay * decay
    pair_decay = aux[8:9, :]
    behind[0:N, :] = before
    behind[N:, :] = jnp.broadcast_to(decay, (8, before.shape[1]))
    put_message(msg, own[...] + pair_decay * before, pair_decay * decay)


def last_kernel(info, got, behind_in, first, aux, _, back, held):
    is_odd = info[ODD] == 1
    before, _unused = take_message(got)
    if behind_in is not None:
        before = behind_in[0:N, :] + behind_in[N : N + 1, :] * before
    entering_odd = aux[0:1, :] * before + first[...]
    back[...] = jnp.where(is_odd, before, entering_odd).astype(BF16)
    held[...] = jnp.where(is_odd, entering_odd, before).astype(BF16)


def pair_split_kernel(info, got, keep, rates, _, first, aux, *refs):
    outs, wide = refs[:-1], refs[-1]
    half = keep.shape[1]
    pairs = len(outs)
    piece = half // pairs
    is_odd = info[ODD] == 1
    arrived, their = take_message(got)
    row = rates.shape[1] - 16
    mine = rates[1, row : row + 1, :]
    early = jnp.where(is_odd, arrived, keep[...])
    late = jnp.where(is_odd, keep[...], arrived)
    even_decay = jnp.where(is_odd, their, mine)
    odd_decay = jnp.where(is_odd, mine, their)
    first[...] = early
    aux[...] = jnp.broadcast_to(even_decay, (8, half))
    put_message(wide, odd_decay * early + late, even_decay * odd_decay)
    for r in range(pairs):
        owner = lax.rem(info[PAIR] + r, pairs)
        outs[r][...] = wide[:, pl.ds(pl.multiple_of(owner * piece, piece), piece)]


def owner_kernel(info, *refs):
    pairs = (len(refs) - 3) // 2
    ins, outs = refs[:pairs], refs[pairs + 1 : 2 * pairs + 1]
    states, prefixes = refs[-2:]
    for r in range(pairs):
        states[lax.rem(info[PAIR] + pairs - r, pairs)] = ins[r][...]
    before = jnp.zeros(prefixes.shape[1:], F32)
    for q in range(pairs):
        prefixes[q] = before.astype(BF16)
        if q < pairs - 1:
            state, decay = take_message(states.at[q])
            before = decay * before + state
    for r in range(pairs):
        outs[r][...] = prefixes[lax.rem(info[PAIR] + r, pairs)]


def last_split_kernel(info, first, aux, _, *refs):
    pairs = len(refs) - 3
    back, held, wide = refs[-3:]
    piece = back.shape[1] // pairs
    for r in range(pairs):
        owner = lax.rem(info[PAIR] + pairs - r, pairs)
        wide[:, pl.ds(pl.multiple_of(owner * piece, piece), piece)] = refs[r][...]
    is_odd = info[ODD] == 1
    before = wide[...].astype(F32)
    entering_odd = aux[0:1, :] * before + first[...]
    back[...] = jnp.where(is_odd, before, entering_odd).astype(BF16)
    held[...] = jnp.where(is_odd, entering_odd, before).astype(BF16)


def combine(kernel, operands, specs, outs, name, scratch=()):
    return pl.pallas_call(
        kernel,
        in_specs=specs,
        out_specs=[FULL] * len(outs),
        out_shape=[jax.ShapeDtypeStruct(s, t) for s, t in outs],
        scratch_shapes=list(scratch),
        compiler_params=params(16),
        cost_estimate=CHEAP,
        name=name,
    )(*operands)


def scan_kernel(order, part, info, x_far, z_far, bc, cum, cum_s, log_s, f_blk, e_blk, rates, ones, _, uv_out, x, z, sem, state):
    length, width = x.shape
    per_slab = SLAB // P_SIZE
    inner = STEP_B // TOK_B
    blocks = length // TOK_B
    first_head = part * width // P_SIZE
    first_lane = info[GROUP + order] * x_far.shape[1] + part * width

    def fetch(step):
        piece = pl.ds(pl.multiple_of(step * STEP_B, STEP_B), STEP_B)
        return (
            pltpu.make_async_copy(x_far.at[piece, pl.ds(part * width, width)], x.at[piece], sem.at[0, step]),
            pltpu.make_async_copy(
                z_far.at[piece, pl.ds(pl.multiple_of(first_lane, width), width)], z.at[piece], sem.at[1, step]
            ),
        )

    for step in range(length // STEP_B):
        for copy in fetch(step):
            copy.start()
    state[...] = jnp.zeros_like(state)

    row = lax.broadcasted_iota(jnp.int32, (TOK_B, TOK_B), 0)
    col = lax.broadcasted_iota(jnp.int32, (TOK_B, TOK_B), 1)
    keep = row >= col
    first = lax.broadcasted_iota(jnp.int32, (TOK_B, 2 * P_SIZE), 1) < P_SIZE
    zero = jnp.zeros((TOK_B, 2 * P_SIZE), BF16)

    def turn(step, _):
        for copy in fetch(step):
            copy.wait()
        for k in range(inner):
            block(step * inner + k)
        return 0

    def block(b):
        at = pl.ds(pl.multiple_of(b * TOK_B, TOK_B), TOK_B)
        b_mat = bc[at, 0:N]
        c_mat = bc[at, N : 2 * N]
        b_across = b_mat.T
        scores = jnp.where(keep, dot(c_mat, b_mat, ((1,), (1,))), 0.0)
        for s in range(width // SLAB):
            lanes = slice(s * SLAB, (s + 1) * SLAB)
            xb = x[at, lanes]
            wide = slice(part * width + s * SLAB, part * width + (s + 1) * SLAB)
            sel = ones[:, wide]
            fade_row = rates[order, pl.ds(b, 1), wide]
            lead_row = rates[order, pl.ds(blocks + b, 1), wide]
            skip = rates[order, 2 * blocks + 8 : 2 * blocks + 9, wide]
            old = state[:, lanes]
            rise = dot(e_blk[order, at, :], sel)
            carried = dot(c_mat, old.astype(BF16)) * rise
            within = []
            for q in range(per_slab // 2):
                tables = []
                for h in (2 * q, 2 * q + 1):
                    head = first_head + s * per_slab + h
                    column = cum[order, at, head : head + 1]
                    own = slice(head, head + 1)
                    gap = jnp.minimum(column - cum_s[order, own, at], log_s[order, own, at])
                    tables.append((scores * jnp.exp2(gap)).astype(BF16))
                xp = xb[:, q * 2 * P_SIZE : (q + 1) * 2 * P_SIZE]
                stacked = jnp.concatenate([jnp.where(first, xp, zero), jnp.where(first, zero, xp)], 0)
                within.append(dot(jnp.concatenate(tables, 1), stacked))
            xs = xb.astype(F32)
            y = jnp.concatenate(within, 1) + carried + skip * xs
            gate = half_silu(z[at, lanes].astype(F32) * 0.5)
            uv_out[at, lanes] = (y * gate).astype(BF16)
            uv_out[at, width + s * SLAB : width + (s + 1) * SLAB] = (gate * rise * lead_row).astype(BF16)
            xf = (xs * dot(f_blk[order, at, :], sel)).astype(BF16)
            state[:, lanes] = old * fade_row + dot(b_across, xf)

    lax.fori_loop(0, length // STEP_B, turn, 0)


def scan_part(order, part, info, token, x, z, bc, cum, cum_s, log_s, f_blk, e_blk, rates, ones):
    length, full = x.shape
    width = full // B_PARTS
    return pl.pallas_call(
        functools.partial(scan_kernel, order, part),
        in_specs=[SCALAR, FAR, FAR] + [FULL] * 8 + [ANY],
        out_specs=FULL,
        out_shape=jax.ShapeDtypeStruct((length, 2 * width), BF16),
        scratch_shapes=[
            pltpu.VMEM((length, width), BF16),
            pltpu.VMEM((length, width), BF16),
            pltpu.SemaphoreType.DMA((2, length // STEP_B)),
            pltpu.VMEM((N, width), F32),
        ],
        compiler_params=params(16),
        cost_estimate=CHEAP,
        name="scan_part",
    )(info, x, z, bc, cum, cum_s, log_s, f_blk, e_blk, rates, ones, token)


def norm_kernel(places, info, bc0, bc1, state0, state1, gain, _, *refs):
    uvs, out = refs[:-1], refs[-1]
    count = out.shape[0] // len(places)
    per = state0.shape[1]
    part = per // B_PARTS

    def rows(first, base):
        to = pl.ds(pl.multiple_of(first, ROWS_C), ROWS_C)
        at = pl.ds(pl.multiple_of(base, ROWS_C), ROWS_C)
        for order, (bc, state) in enumerate(((bc0, state0), (bc1, state1))):
            c_mat = bc[at, N : 2 * N]
            pieces = []
            squares = None
            for p in range(B_PARTS):
                uv = uvs[order * B_PARTS + p]
                inc = state[:, p * part : (p + 1) * part]
                gated = uv[at, 0:part].astype(F32) + uv[at, part:].astype(F32) * dot(c_mat, inc)
                square = jnp.sum(gated * gated, axis=-1, keepdims=True)
                squares = square if squares is None else squares + square
                pieces.append(gated)
            scale = lax.rsqrt(squares * (1.0 / per) + EPS)
            for p, gated in enumerate(pieces):
                lanes = pl.ds(pl.multiple_of(info[GROUP + order] * per + p * part, part), part)
                out[to, lanes] = (gated * scale * gain[:, lanes]).astype(BF16)

    for k, place in enumerate(places):

        def step(j, _):
            rows(k * count + j * ROWS_C, info[ROWS + place] * count + j * ROWS_C)
            return 0

        lax.fori_loop(0, count // ROWS_C, step, 0)


def norm_rows(places, info, count, token, bcs, states, gain, uvs):
    return pl.pallas_call(
        functools.partial(norm_kernel, places),
        in_specs=[SCALAR] + [FULL] * 5 + [ANY] + [FULL] * len(uvs),
        out_specs=FULL,
        out_shape=jax.ShapeDtypeStruct((len(places) * count, gain.shape[1]), BF16),
        compiler_params=params(16),
        cost_estimate=CHEAP,
        name="norm_rows",
    )(info, *bcs, *states, gain, token, *uvs)


def stream(base, w0_far, w1_far, w0, w1, sem):
    j = pl.program_id(0)
    tiles = pl.num_programs(0)

    def fetch(t):
        slot = lax.rem(t, SLOTS)
        lanes = pl.ds(pl.multiple_of((base + t) * TILE, TILE), TILE)
        return (
            pltpu.make_async_copy(w0_far.at[:, lanes], w0.at[slot], sem.at[0, slot]),
            pltpu.make_async_copy(w1_far.at[:, lanes], w1.at[slot], sem.at[1, slot]),
        )

    def start(t):
        @pl.when(t < tiles)
        def _():
            for copy in fetch(t):
                copy.start()

    @pl.when(j == 0)
    def _():
        for t in range(SLOTS - 1):
            start(t)

    start(j + SLOTS - 1)
    for copy in fetch(j):
        copy.wait()
    return lax.rem(j, SLOTS)


def buffers(depth):
    return [
        pltpu.VMEM((SLOTS, depth, TILE), BF16),
        pltpu.VMEM((SLOTS, depth, TILE), BF16),
        pltpu.SemaphoreType.DMA((2, SLOTS)),
    ]


def ahead_kernel(base, owns, mates, w0_far, w1_far, out, w0, w1, sem):
    slot = stream(base, w0_far, w1_far, w0, w1, sem)
    rows = out.shape[0]
    out[...] = (dot(owns[0:rows, :], w0[slot]) + dot(mates[0:rows, :], w1[slot])).astype(BF16)


def project_ahead(owns, mates, w0, w1, first, count):
    rows, depth = owns.shape[0] // 2, owns.shape[1]
    return pl.pallas_call(
        functools.partial(ahead_kernel, first // TILE),
        grid=(count // TILE,),
        in_specs=[FULL, FULL, FAR, FAR],
        out_specs=pl.BlockSpec((rows, TILE), lambda j: (0, j)),
        out_shape=jax.ShapeDtypeStruct((rows, count), BF16),
        scratch_shapes=buffers(depth),
        compiler_params=params(20),
        cost_estimate=CHEAP,
        name="project_ahead",
    )(owns, mates, w0, w1)


def both_kernel(base, cut, owns, mates, w0_far, w1_far, *refs):
    fars, near, w0, w1, sem = refs[:-4], *refs[-4:]
    rows = near.shape[0]
    slot = stream(base, w0_far, w1_far, w0, w1, sem)
    total = dot(owns[...], w0[slot]) + dot(mates[...], w1[slot])
    near[...] = total[rows:]
    for k, far_out in enumerate(fars):

        @pl.when(pl.program_id(0) // cut == k)
        def _():
            far_out[...] = total[0:rows].astype(BF16)


def project_both(owns, mates, w0, w1, first, count, chunk):
    rows, depth = owns.shape[0] // 2, owns.shape[1]
    cut = chunk // TILE
    chunks = count // chunk

    def placed(k):
        return pl.BlockSpec((rows, TILE), lambda j: (0, jnp.clip(j - k * cut, 0, cut - 1)))

    *fars, near = pl.pallas_call(
        functools.partial(both_kernel, first // TILE, cut),
        grid=(count // TILE,),
        in_specs=[FULL] * 2 + [FAR] * 2,
        out_specs=[placed(k) for k in range(chunks)] + [pl.BlockSpec((rows, TILE), lambda j: (0, j))],
        out_shape=[jax.ShapeDtypeStruct((rows, chunk), BF16)] * chunks + [jax.ShapeDtypeStruct((rows, count), F32)],
        scratch_shapes=buffers(depth),
        compiler_params=params(24),
        cost_estimate=CHEAP,
        name="project_both",
    )(owns, mates, w0, w1)
    return fars, near


def near_kernel(owns, mates, w0_far, w1_far, arrived, out, w0, w1, sem):
    slot = stream(0, w0_far, w1_far, w0, w1, sem)
    rows = out.shape[0]
    total = dot(owns[rows:, :], w0[slot]) + dot(mates[rows:, :], w1[slot])
    out[...] = (total + arrived[...].astype(F32)).astype(BF16)


def project_near(owns, mates, w0, w1, arrived):
    rows, depth = owns.shape[0] // 2, owns.shape[1]
    placed = pl.BlockSpec((rows, TILE), lambda j: (0, j))
    return pl.pallas_call(
        near_kernel,
        grid=(arrived.shape[1] // TILE,),
        in_specs=[FULL, FULL, FAR, FAR, placed],
        out_specs=placed,
        out_shape=jax.ShapeDtypeStruct((rows, w0.shape[1]), BF16),
        scratch_shapes=buffers(depth),
        compiler_params=params(20),
        cost_estimate=CHEAP,
        name="project_near",
    )(owns, mates, w0, w1, arrived)


def add_kernel(near, *refs):
    arrived, out = refs[:-2], refs[-1]
    chunk = arrived[0].shape[1]
    for k, part in enumerate(arrived):
        lanes = slice(k * chunk, (k + 1) * chunk)
        out[:, lanes] = (near[:, lanes] + part[...].astype(F32)).astype(BF16)


def add_chunks(near, first, arrived, result, at):
    rows, chunk = arrived[0].shape
    count = chunk * len(arrived)
    return pl.pallas_call(
        add_kernel,
        grid=(1,),
        in_specs=[pl.BlockSpec((rows, count), lambda j: (0, first // count))] + [FULL] * len(arrived) + [ANY],
        out_specs=pl.BlockSpec((rows, count), lambda j: (0, at // count)),
        out_shape=jax.ShapeDtypeStruct(result.shape, BF16),
        input_output_aliases={1 + len(arrived): 0},
        compiler_params=params(8),
        cost_estimate=CHEAP,
        name="add_chunks",
    )(near, *arrived, result)


def shift(block, distance):
    size = lax.axis_size("seq")
    return lax.ppermute(block, "seq", [(i, i + distance) for i in range(size - distance)])


def swap(block, axis, bit):
    return lax.ppermute(block, axis, [(i, i ^ bit) for i in range(lax.axis_size(axis))])


def rotate(block, distance):
    size = lax.axis_size("seq")
    return lax.ppermute(block, "seq", [(i, (i + distance) % size) for i in range(size)])


def log_steps(info, got, keep, rates, done, pairs, scan_next):
    half = keep.shape[1]
    message = ((N + EXTRA, half), BF16)
    full = ((N, half), F32)
    msg, own, first, aux = combine(
        pair_kernel,
        (info, got, keep, rates, done),
        [SCALAR, FULL, FULL, FULL, ANY],
        [message, full, full, ((16, half), F32)],
        "pair",
    )
    behind = None
    covered = 0
    while True:
        got = shift(msg, 2 * (covered + 1))
        done = scan_next(msg)
        covered = 2 * covered + 1
        if covered >= pairs - 1:
            break
        operands, specs = [got, own, aux], [FULL, FULL, FULL]
        if behind is None:
            kernel = lambda g, o, a, t, m, b: wave_kernel(g, o, a, None, t, m, b)
        else:
            kernel = wave_kernel
            operands.append(behind)
            specs.append(FULL)
        msg, behind = combine(kernel, operands + [done], specs + [ANY], [message, ((N + 8, half), F32)], "wave")
    operands, specs = [info, got], [SCALAR, FULL]
    if behind is None:
        kernel = lambda o, g, f, a, t, b, h: last_kernel(o, g, None, f, a, t, b, h)
    else:
        kernel = last_kernel
        operands.append(behind)
        specs.append(FULL)
    out = ((N, half), BF16)
    back, held = combine(kernel, operands + [first, aux, done], specs + [FULL, FULL, ANY], [out, out], "last")
    return back, held


def local(
    x_input,
    z_input,
    bc_input,
    conv_weight_x,
    conv_weight_bc,
    step_size,
    log_decay,
    skip_gain,
    norm_gain,
    out_weight,
):
    length, width = x_input.shape
    heads = step_size.shape[1]
    ways = lax.axis_size("head")
    pairs = lax.axis_size("seq") // 2
    mine = lax.axis_index("head")
    half = width // 2
    seq = lax.axis_index("seq")
    info = jnp.stack([seq & 1, mine ^ 3, mine ^ 2, mine ^ 1, mine, seq >> 1, seq, 1 - (seq & 1), seq & 1]).astype(jnp.int32)

    x_far, z_far, w_far = far(x_input, z_input, out_weight)
    (bc_far,) = far(bc_input)
    halo = rotate(tail_rows(x_far, bc_far), 1)
    bc = bc_input.reshape(length, -1)
    weight_mate = swap(out_weight, "head", 1)

    cum, cum_s, log_s, f_dev, f_blk, e_blk, rates, ones = decays(info, log_decay, step_size, skip_gain, half)
    taps = far(conv_weight_x, conv_weight_bc)
    shared = (info, x_far, bc, halo, *taps, f_dev, ones, rates)
    x0, bc0, send = conv_states(0, *shared)
    got = swap(send, "seq", 1)
    x1, bc1, keep = conv_states(1, *shared)

    uvs = []
    groups = [(x, z_far, y, cum, cum_s, log_s, f_blk, e_blk, rates, ones) for x, y in zip(far(x0, x1), (bc0, bc1))]

    def scan_next(token):
        if len(uvs) < 2 * B_PARTS:
            order, part = divmod(len(uvs), B_PARTS)
            uvs.append(scan_part(order, part, info, token, *groups[order]))
        return uvs[-1]

    full = ((N, half), F32)
    message = ((N + EXTRA, half), BF16)
    done = keep
    out = ((N, half), BF16)
    if pairs > 1 and half % (pairs * N) == 0:
        piece = half // pairs
        part = ((N + EXTRA, piece), BF16)
        first, aux, *parts = combine(
            pair_split_kernel,
            (info, got, keep, rates, done),
            [SCALAR, FULL, FULL, FULL, ANY],
            [full, ((8, half), F32)] + [part] * pairs,
            "pair",
            [pltpu.VMEM(*message)],
        )
        parts = list(parts[:1]) + [rotate(parts[r], 2 * r) for r in range(1, pairs)]
        done = scan_next(scan_next(parts[0]))
        parts = combine(
            owner_kernel,
            [info] + parts + [done],
            [SCALAR] + [FULL] * pairs + [ANY],
            [((N, piece), BF16)] * pairs,
            "owner",
            [pltpu.VMEM((pairs, N + EXTRA, piece), BF16), pltpu.VMEM((pairs, N, piece), BF16)],
        )
        ready = parts[0]
        parts = list(parts[:1]) + [rotate(parts[r], 2 * r) for r in range(1, pairs)]
        done = scan_next(ready)
        back, held = combine(
            last_split_kernel,
            [info, first, aux, done] + parts,
            [SCALAR, FULL, FULL, ANY] + [FULL] * pairs,
            [out, out],
            "last",
            [pltpu.VMEM(*out)],
        )
    else:
        back, held = log_steps(info, got, keep, rates, done, pairs, scan_next)
    other = swap(back, "seq", 1)
    while len(uvs) < 2 * B_PARTS:
        scan_next(back)

    count = length // ways
    gain = norm_gain[None, :]

    def rows_for(token, *places):
        return norm_rows(places, info, count, token, (bc0, bc1), (other, held), gain, uvs)

    mates = rows_for(held, 0, 2)
    owns = rows_for(mates, 1, 3)
    operands = (owns, swap(mates, "head", 1), w_far, weight_mate)
    columns = out_weight.shape[1]
    chunk = columns // 8
    first = swap(project_ahead(*operands, 0, chunk), "head", 2)
    calls = []
    for lo, hi in ((1, 2), (2, 4), (4, 6), (6, 8)):
        sent, near = project_both(*operands, lo * chunk, (hi - lo) * chunk, chunk)
        calls.append((near, lo, [swap(part, "head", 2) for part in sent]))
    result = project_near(*operands, first)
    for near, lo, arrived in calls[:-1]:
        result = add_chunks(near, 0, arrived, result, lo * chunk)
    near, lo, arrived = calls[-1]
    for k, part in enumerate(arrived):
        result = add_chunks(near, k * chunk, [part], result, (lo + k) * chunk)
    return result


def solution(mesh):
    in_specs = (
        P("seq", "head"),
        P("seq", "head"),
        P("seq", "head", None),
        P(None, "head"),
        P(None, "head", None),
        P("seq", "head"),
        P("seq", "head"),
        P("head"),
        P("head"),
        P("head", None),
    )
    out_specs = P(("seq", "head"), None)
    return jax.shard_map(local, mesh=mesh, in_specs=in_specs, out_specs=out_specs, check_vma=False)
```

```python
import functools

import jax
import jax.numpy as jnp
from jax import lax
from jax.experimental import pallas as pl
from jax.experimental.pallas import tpu as pltpu
from jax.sharding import PartitionSpec as P

P_SIZE = 64
N = 128
KCONV = 4
EPS = 1e-05
LOG2E = 1.4426950408889634

TOK_A = 256
ROWS_A = 32
TOK_B = 128
STEP_B = 256
EXTRA = 16
SLAB = 256
ROWS_C = 128
TILE = 256
SLOTS = 4
LEAD = 16
B_PARTS = 2
HIGHEST = lax.Precision.HIGHEST
F32 = jnp.float32
BF16 = jnp.bfloat16


def params(mib):
    return pltpu.CompilerParams(vmem_limit_bytes=mib * 1024 * 1024)


CHEAP = pl.CostEstimate(flops=1, bytes_accessed=1, transcendentals=0)
SCALAR = pl.BlockSpec(memory_space=pltpu.SMEM)
FULL = pl.BlockSpec(memory_space=pltpu.VMEM)
FAR = pl.BlockSpec(memory_space=pltpu.HBM)
ANY = pl.BlockSpec(memory_space=pl.ANY)

ODD, ROWS, PAIR, SEQ, GROUP = 0, 1, 5, 6, 7


def dot(a, b, dims=((1,), (0,)), precision=None):
    return lax.dot_general(a, b, (dims, ((), ())), precision=precision, preferred_element_type=F32)


def half_silu(half):
    return half + half * jnp.tanh(half)


def far(*arrays):
    return [pltpu.with_memory_space_constraint(a, pltpu.HBM) for a in arrays]


def whole(shape):
    return pl.BlockSpec(shape, lambda *_: (0,) * len(shape))


def decay_kernel(info, ld_t, step_t, skip, *refs):
    cum, cum_s, log_s, f_dev, f_blk, e_blk, rates = [refs[2 * k : 2 * k + 2] for k in range(7)]
    ones = refs[14]
    heads, length = ld_t.shape
    blocks = length // TOK_B
    per = heads // 2
    width = ones.shape[1]
    swapped = info[GROUP] == 1
    row = lax.broadcasted_iota(jnp.int32, (TOK_B, TOK_B), 0)
    col = lax.broadcasted_iota(jnp.int32, (TOK_B, TOK_B), 1)
    lower = (row >= col).astype(F32)
    upper = (row <= col).astype(F32)
    eye = (row == col).astype(BF16)

    def ordered(value):
        return jnp.where(swapped, jnp.concatenate([value[per:], value[:per]], 0), value)

    def put(ref, rows, value):
        high = value.astype(BF16)
        low = (value - high.astype(F32)).astype(BF16)
        for g in range(2):
            own = slice(g * per, (g + 1) * per)
            both = jnp.concatenate([high[own], low[own]], 0)
            ref[g][rows, :] = dot(eye, both, ((1,), (1,))).astype(BF16)

    member = lax.broadcasted_iota(jnp.int32, (per, width), 0) == lax.broadcasted_iota(jnp.int32, (per, width), 1) // P_SIZE
    member = member.astype(F32)
    ones[0:per, :] = member.astype(BF16)
    ones[per:, :] = member.astype(BF16)
    cums, totals, row_totals = [], [], []
    for b in range(blocks):
        rows = slice(b * TOK_B, (b + 1) * TOK_B)
        logs = ordered(ld_t[:, rows]) * LOG2E
        c = dot(lower, logs, ((1,), (1,)), HIGHEST)
        for g in range(2):
            cum[g][rows, :] = c[:, g * per : (g + 1) * per]
        row_totals.append(c[TOK_B - 1 : TOK_B, :])
        c = dot(logs, upper, precision=HIGHEST)
        cums.append(c)
        totals.append(c[:, TOK_B - 1 : TOK_B])
    before, row_before = [jnp.zeros_like(totals[0])], [jnp.zeros_like(row_totals[0])]
    for b in range(blocks):
        before.append(before[-1] + totals[b])
        row_before.append(row_before[-1] + row_totals[b])
    total = before[-1]
    logs = jnp.concatenate(row_totals + row_before[:-1] + row_before[-1:] * 8, 0)
    gains = jnp.broadcast_to(skip[...], (8, heads))
    gains = jnp.where(swapped, jnp.concatenate([gains[:, per:], gains[:, :per]], 1), gains)
    values = jnp.concatenate([jnp.exp2(logs), gains], 0)
    for g in range(2):
        rates[g][...] = dot(values[:, g * per : (g + 1) * per], member, precision=HIGHEST)
    for b in range(blocks):
        rows = slice(b * TOK_B, (b + 1) * TOK_B)
        s = ordered(step_t[:, rows])
        log_step = jnp.log2(s)
        shifted = cums[b] - log_step
        for g in range(2):
            own = slice(g * per, (g + 1) * per)
            log_s[g][:, rows] = log_step[own, :]
            cum_s[g][:, rows] = shifted[own, :]
        put(f_dev, rows, jnp.exp2(total - (cums[b] + before[b])) * s)
        put(f_blk, rows, jnp.exp2(totals[b] - cums[b]) * s)
        put(e_blk, rows, jnp.exp2(cums[b]))


def decays(info, log_decay, step, skip, width):
    length, heads = log_decay.shape
    blocks = length // TOK_B
    per = heads // 2
    across = jax.ShapeDtypeStruct((per, length), F32)
    pair = jax.ShapeDtypeStruct((length, 2 * per), BF16)
    column = jax.ShapeDtypeStruct((length, per), F32)
    rates = jax.ShapeDtypeStruct((2 * blocks + 16, width), F32)
    shapes = [shape for shape in (column, across, across, pair, pair, pair, rates) for _ in range(2)]
    shapes.append(jax.ShapeDtypeStruct((2 * per, width), BF16))
    *refs, ones = pl.pallas_call(
        decay_kernel,
        in_specs=[SCALAR] + [FULL] * 3,
        out_specs=[FULL] * len(shapes),
        out_shape=shapes,
        compiler_params=params(16),
        cost_estimate=CHEAP,
        name="decays",
    )(info, *far(log_decay.T, step.T, skip[None, :]))
    return [tuple(refs[2 * k : 2 * k + 2]) for k in range(7)], ones


def tail_kernel(x, bc, out):
    width, bc_width = x.shape[1], bc.shape[2]
    out[:, 0:width] = x[...]
    for g in range(bc.shape[1]):
        out[:, width + g * bc_width : width + (g + 1) * bc_width] = bc[:, g, :]


def tail_rows(x, bc):
    length, width = x.shape
    groups, bc_width = bc.shape[1:]
    at = length // LEAD - 1
    shape = (LEAD, width + groups * bc_width)
    return pl.pallas_call(
        tail_kernel,
        grid=(1,),
        in_specs=[
            pl.BlockSpec((LEAD, width), lambda i: (at, 0)),
            pl.BlockSpec((LEAD, groups, bc_width), lambda i: (at, 0, 0)),
        ],
        out_specs=whole(shape),
        out_shape=jax.ShapeDtypeStruct(shape, BF16),
        compiler_params=params(8),
        cost_estimate=CHEAP,
        name="tail_rows",
    )(x, bc)


def put_message(ref, state, decay):
    high = decay.astype(BF16)
    low = (decay - high.astype(F32)).astype(BF16)
    rest = jnp.zeros((EXTRA - 2, state.shape[1]), BF16)
    ref[0:N, :] = state.astype(BF16)
    ref[N:, :] = jnp.concatenate([high, low, rest], 0)


def take_message(ref):
    extra = ref[N:, :].astype(F32)
    return ref[0:N, :].astype(F32), extra[0:1] + extra[1:2]


def conv_kernel(
    order, info, x, x_lead, bc, bc_lead, halo, bc_halo, wx, wbc, f_dev, ones, rates, x_out, bc_out, final, xf, state, down
):
    i = pl.program_id(0)
    rows, width = x.shape
    group = info[GROUP + order]

    @pl.when(i == 0)
    def _():
        state[...] = jnp.zeros_like(state)
        row = lax.broadcasted_iota(jnp.int32, down.shape, 0)
        col = lax.broadcasted_iota(jnp.int32, down.shape, 1)
        down[...] = (row == col + 1).astype(BF16)

    def conv(src, first, behind, weights, emit):
        at_start = jnp.where(info[SEQ] == 0, jnp.zeros_like(first), first)
        lead = jnp.where(i == 0, at_start, behind).astype(F32)
        w0, w1, w2, w3 = [w * 0.5 for w in weights]
        back = LEAD - 8
        lead_r1 = pltpu.roll(lead, 1, 0)
        last_p = (w1 * lead + w0 * lead_r1)[back:]
        moved = dot(down[...], src)
        top = lax.broadcasted_iota(jnp.int32, (8, lead.shape[1]), 0) == 0
        head = jnp.where(top, jnp.broadcast_to(lead[LEAD - 1 :], top.shape), moved[0:8])
        for r in range(0, rows, ROWS_A):
            cur = src[r : r + ROWS_A].astype(F32)
            r1 = moved[r : r + ROWS_A] if r else jnp.concatenate([head, moved[8:ROWS_A]], 0)
            p = w1 * cur + w0 * r1
            p2 = pltpu.roll(jnp.concatenate([last_p, p], 0), 2, 0)[8:]
            emit(r, half_silu((w3 * cur + w2 * r1) + p2))
            last_p = p[ROWS_A - 8 :]

    for lanes in range(0, 2 * N, SLAB):
        ds = slice(lanes, lanes + SLAB)

        def emit_bc(r, value):
            bc_out[r : r + ROWS_A, ds] = value.astype(BF16)

        weights = [jnp.where(group == 0, wbc[k, 0:1, ds], wbc[k, 1:2, ds]) for k in range(KCONV)]
        conv(bc[:, ds], bc_halo[:, ds], bc_lead[:, ds], weights, emit_bc)

    for lanes in range(0, width, SLAB):
        ds = slice(lanes, lanes + SLAB)
        scale = dot(f_dev[...], ones[:, ds])

        def emit(r, value):
            x_out[r : r + ROWS_A, ds] = value.astype(BF16)
            xf[r : r + ROWS_A, ds] = (value * scale[r : r + ROWS_A]).astype(BF16)

        weights = [wx[k : k + 1, ds] for k in range(KCONV)]
        conv(x[:, ds], halo[:, ds], x_lead[:, ds], weights, emit)

    state[...] += dot(bc_out[:, 0:N], xf[...], ((0,), (0,)))

    @pl.when(i == pl.num_programs(0) - 1)
    def _():
        if order == 0:
            row = rates.shape[0] - 16
            put_message(final, state[...], rates[row : row + 1, :])
        else:
            final[...] = state[...]


def conv_states(order, info, x, bc, halo, wx, wbc, f_dev, ones, rates):
    length, full = x.shape
    width = full // 2
    lead = lambda i, info: (jnp.maximum(i * (TOK_A // LEAD) - 1, 0), info[GROUP + order])
    block = lambda i, info: (i, info[GROUP + order])
    column = lambda i, info: (0, info[GROUP + order])
    rows = lambda i, info: (i, 0)
    final = ((N + EXTRA, width), BF16) if order == 0 else ((N, width), F32)
    return pl.pallas_call(
        functools.partial(conv_kernel, order),
        grid_spec=pltpu.PrefetchScalarGridSpec(
            num_scalar_prefetch=1,
            grid=(length // TOK_A,),
            in_specs=[
                pl.BlockSpec((TOK_A, width), block),
                pl.BlockSpec((LEAD, width), lead),
                pl.BlockSpec((TOK_A, 2 * N), block),
                pl.BlockSpec((LEAD, 2 * N), lead),
                pl.BlockSpec((LEAD, width), column),
                pl.BlockSpec((LEAD, 2 * N), lambda i, info: (0, full // (2 * N) + info[GROUP + order])),
                pl.BlockSpec((KCONV, width), column),
                whole(wbc.shape),
                pl.BlockSpec((TOK_A, f_dev.shape[1]), rows),
                whole(ones.shape),
                whole(rates.shape),
            ],
            out_specs=[
                pl.BlockSpec((TOK_A, width), rows),
                pl.BlockSpec((TOK_A, 2 * N), rows),
                whole(final[0]),
            ],
            scratch_shapes=[
                pltpu.VMEM((TOK_A, width), BF16),
                pltpu.VMEM((N, width), F32),
                pltpu.VMEM((TOK_A, TOK_A), BF16),
            ],
        ),
        out_shape=(
            pltpu.HBM((length, width), BF16),
            jax.ShapeDtypeStruct((length, 2 * N), BF16),
            jax.ShapeDtypeStruct(*final),
        ),
        compiler_params=params(16),
        cost_estimate=CHEAP,
        name="conv_states",
    )(info, x, x, bc, bc, halo, halo, wx, wbc, f_dev, ones, rates)


def pair_kernel(info, got, keep, rates, _, msg, own, first, aux):
    half = keep.shape[1]
    is_odd = info[ODD] == 1
    arrived, their = take_message(got)
    row = rates.shape[0] - 16
    mine = rates[row : row + 1, :]
    early = jnp.where(is_odd, arrived, keep[...])
    late = jnp.where(is_odd, keep[...], arrived)
    even_decay = jnp.where(is_odd, their, mine)
    odd_decay = jnp.where(is_odd, mine, their)
    state = odd_decay * early + late
    own[...] = state
    first[...] = early
    aux[0:8, :] = jnp.broadcast_to(even_decay, (8, half))
    aux[8:16, :] = jnp.broadcast_to(even_decay * odd_decay, (8, half))
    put_message(msg, state, even_decay * odd_decay)


def wave_kernel(got, own, aux, behind_in, _, msg, behind):
    before, decay = take_message(got)
    if behind_in is not None:
        before_decay = behind_in[N : N + 1, :]
        before = behind_in[0:N, :] + before_decay * before
        decay = before_decay * decay
    pair_decay = aux[8:9, :]
    behind[0:N, :] = before
    behind[N:, :] = jnp.broadcast_to(decay, (8, before.shape[1]))
    put_message(msg, own[...] + pair_decay * before, pair_decay * decay)


def last_kernel(info, got, behind_in, first, aux, _, back, held):
    is_odd = info[ODD] == 1
    before, _unused = take_message(got)
    if behind_in is not None:
        before = behind_in[0:N, :] + behind_in[N : N + 1, :] * before
    entering_odd = aux[0:1, :] * before + first[...]
    back[...] = jnp.where(is_odd, before, entering_odd).astype(BF16)
    held[...] = jnp.where(is_odd, entering_odd, before).astype(BF16)


def pair_split_kernel(info, got, keep, rates, _, first, aux, *refs):
    outs, wide = refs[:-1], refs[-1]
    half = keep.shape[1]
    pairs = len(outs)
    piece = half // pairs
    is_odd = info[ODD] == 1
    arrived, their = take_message(got)
    row = rates.shape[0] - 16
    mine = rates[row : row + 1, :]
    early = jnp.where(is_odd, arrived, keep[...])
    late = jnp.where(is_odd, keep[...], arrived)
    even_decay = jnp.where(is_odd, their, mine)
    odd_decay = jnp.where(is_odd, mine, their)
    first[...] = early
    aux[...] = jnp.broadcast_to(even_decay, (8, half))
    put_message(wide, odd_decay * early + late, even_decay * odd_decay)
    for r in range(pairs):
        owner = lax.rem(info[PAIR] + r, pairs)
        outs[r][...] = wide[:, pl.ds(pl.multiple_of(owner * piece, piece), piece)]


def owner_kernel(info, *refs):
    pairs = (len(refs) - 3) // 2
    ins, outs = refs[:pairs], refs[pairs + 1 : 2 * pairs + 1]
    states, prefixes = refs[-2:]
    for r in range(pairs):
        states[lax.rem(info[PAIR] + pairs - r, pairs)] = ins[r][...]
    before = jnp.zeros(prefixes.shape[1:], F32)
    for q in range(pairs):
        prefixes[q] = before.astype(BF16)
        if q < pairs - 1:
            state, decay = take_message(states.at[q])
            before = decay * before + state
    for r in range(pairs):
        outs[r][...] = prefixes[lax.rem(info[PAIR] + r, pairs)]


def last_split_kernel(info, first, aux, _, *refs):
    pairs = len(refs) - 3
    back, held, wide = refs[-3:]
    piece = back.shape[1] // pairs
    for r in range(pairs):
        owner = lax.rem(info[PAIR] + pairs - r, pairs)
        wide[:, pl.ds(pl.multiple_of(owner * piece, piece), piece)] = refs[r][...]
    is_odd = info[ODD] == 1
    before = wide[...].astype(F32)
    entering_odd = aux[0:1, :] * before + first[...]
    back[...] = jnp.where(is_odd, before, entering_odd).astype(BF16)
    held[...] = jnp.where(is_odd, entering_odd, before).astype(BF16)


def combine(kernel, operands, specs, outs, name, scratch=()):
    return pl.pallas_call(
        kernel,
        in_specs=specs,
        out_specs=[FULL] * len(outs),
        out_shape=[jax.ShapeDtypeStruct(s, t) for s, t in outs],
        scratch_shapes=list(scratch),
        compiler_params=params(16),
        cost_estimate=CHEAP,
        name=name,
    )(*operands)


def scan_kernel(order, part, info, x_far, z_far, bc, cum, cum_s, log_s, f_blk, e_blk, rates, ones, _, uv_out, x, z, sem, state):
    length, width = x.shape
    per_slab = SLAB // P_SIZE
    inner = STEP_B // TOK_B
    blocks = length // TOK_B
    first_head = part * width // P_SIZE
    first_lane = info[GROUP + order] * x_far.shape[1] + part * width

    def fetch(step):
        piece = pl.ds(pl.multiple_of(step * STEP_B, STEP_B), STEP_B)
        return (
            pltpu.make_async_copy(x_far.at[piece, pl.ds(part * width, width)], x.at[piece], sem.at[0, step]),
            pltpu.make_async_copy(
                z_far.at[piece, pl.ds(pl.multiple_of(first_lane, width), width)], z.at[piece], sem.at[1, step]
            ),
        )

    for step in range(length // STEP_B):
        for copy in fetch(step):
            copy.start()
    state[...] = jnp.zeros_like(state)

    row = lax.broadcasted_iota(jnp.int32, (TOK_B, TOK_B), 0)
    col = lax.broadcasted_iota(jnp.int32, (TOK_B, TOK_B), 1)
    keep = row >= col
    first = lax.broadcasted_iota(jnp.int32, (TOK_B, 2 * P_SIZE), 1) < P_SIZE
    zero = jnp.zeros((TOK_B, 2 * P_SIZE), BF16)

    def turn(step, _):
        for copy in fetch(step):
            copy.wait()
        for k in range(inner):
            block(step * inner + k)
        return 0

    def block(b):
        at = pl.ds(pl.multiple_of(b * TOK_B, TOK_B), TOK_B)
        b_mat = bc[at, 0:N]
        c_mat = bc[at, N : 2 * N]
        b_across = b_mat.T
        scores = jnp.where(keep, dot(c_mat, b_mat, ((1,), (1,))), 0.0)
        for s in range(width // SLAB):
            lanes = slice(s * SLAB, (s + 1) * SLAB)
            xb = x[at, lanes]
            wide = slice(part * width + s * SLAB, part * width + (s + 1) * SLAB)
            sel = ones[:, wide]
            fade_row = rates[pl.ds(b, 1), wide]
            lead_row = rates[pl.ds(blocks + b, 1), wide]
            skip = rates[2 * blocks + 8 : 2 * blocks + 9, wide]
            old = state[:, lanes]
            rise = dot(e_blk[at, :], sel)
            carried = dot(c_mat, old.astype(BF16)) * rise
            within = []
            for q in range(per_slab // 2):
                tables = []
                for h in (2 * q, 2 * q + 1):
                    head = first_head + s * per_slab + h
                    column = cum[at, head : head + 1]
                    own = slice(head, head + 1)
                    gap = jnp.minimum(column - cum_s[own, at], log_s[own, at])
                    tables.append((scores * jnp.exp2(gap)).astype(BF16))
                xp = xb[:, q * 2 * P_SIZE : (q + 1) * 2 * P_SIZE]
                stacked = jnp.concatenate([jnp.where(first, xp, zero), jnp.where(first, zero, xp)], 0)
                within.append(dot(jnp.concatenate(tables, 1), stacked))
            xs = xb.astype(F32)
            y = jnp.concatenate(within, 1) + carried + skip * xs
            gate = half_silu((z[at, lanes] * 0.5).astype(F32))
            uv_out[at, lanes] = (y * gate).astype(BF16)
            uv_out[at, width + s * SLAB : width + (s + 1) * SLAB] = (gate * rise * lead_row).astype(BF16)
            xf = (xs * dot(f_blk[at, :], sel)).astype(BF16)
            state[:, lanes] = old * fade_row + dot(b_across, xf)

    lax.fori_loop(0, length // STEP_B, turn, 0)


def scan_part(order, part, info, token, x, z, bc, cum, cum_s, log_s, f_blk, e_blk, rates, ones):
    length, full = x.shape
    width = full // B_PARTS
    return pl.pallas_call(
        functools.partial(scan_kernel, order, part),
        in_specs=[SCALAR, FAR, FAR] + [FULL] * 8 + [ANY],
        out_specs=FULL,
        out_shape=jax.ShapeDtypeStruct((length, 2 * width), BF16),
        scratch_shapes=[
            pltpu.VMEM((length, width), BF16),
            pltpu.VMEM((length, width), BF16),
            pltpu.SemaphoreType.DMA((2, length // STEP_B)),
            pltpu.VMEM((N, width), F32),
        ],
        compiler_params=params(16),
        cost_estimate=CHEAP,
        name="scan_part",
    )(info, x, z, bc, cum, cum_s, log_s, f_blk, e_blk, rates, ones, token)


def norm_kernel(places, fetched, info, bc0, bc1, state0, state1, gain, _, *refs):
    uvs, refs = refs[: 2 * B_PARTS], refs[2 * B_PARTS :]
    weights, out, tiles, sem = refs[:fetched], refs[fetched], refs[fetched + 1 : 2 * fetched + 1], refs[-1]
    copies = [
        pltpu.make_async_copy(weight.at[:, pl.ds(0, tile.shape[1])], tile, sem.at[k])
        for k, (weight, tile) in enumerate(zip(weights, tiles))
    ]
    for copy in copies:
        copy.start()
    count = out.shape[0] // len(places)
    per = state0.shape[1]
    part = per // B_PARTS

    def rows(first, base):
        to = pl.ds(pl.multiple_of(first, ROWS_C), ROWS_C)
        at = pl.ds(pl.multiple_of(base, ROWS_C), ROWS_C)
        for order, (bc, state) in enumerate(((bc0, state0), (bc1, state1))):
            c_mat = bc[at, N : 2 * N]
            pieces = []
            squares = None
            for p in range(B_PARTS):
                uv = uvs[order * B_PARTS + p]
                inc = state[:, p * part : (p + 1) * part]
                gated = uv[at, 0:part].astype(F32) + uv[at, part:].astype(F32) * dot(c_mat, inc)
                square = jnp.sum(gated * gated, axis=-1, keepdims=True)
                squares = square if squares is None else squares + square
                pieces.append(gated)
            scale = lax.rsqrt(squares * (1.0 / per) + EPS)
            for p, gated in enumerate(pieces):
                lanes = pl.ds(pl.multiple_of(info[GROUP + order] * per + p * part, part), part)
                out[to, lanes] = (gated * scale * gain[:, lanes]).astype(BF16)

    for k, place in enumerate(places):

        def step(j, _):
            rows(k * count + j * ROWS_C, info[ROWS + place] * count + j * ROWS_C)
            return 0

        lax.fori_loop(0, count // ROWS_C, step, 0)
    for copy in copies:
        copy.wait()


def norm_rows(places, info, count, token, bcs, states, gain, uvs, weights=(), columns=0):
    tile = jax.ShapeDtypeStruct((gain.shape[1], columns), BF16)
    return pl.pallas_call(
        functools.partial(norm_kernel, places, len(weights)),
        in_specs=[SCALAR] + [FULL] * 5 + [ANY] + [FULL] * len(uvs) + [FAR] * len(weights),
        out_specs=[FULL] * (1 + len(weights)),
        out_shape=[jax.ShapeDtypeStruct((len(places) * count, gain.shape[1]), BF16)] + [tile] * len(weights),
        scratch_shapes=[pltpu.SemaphoreType.DMA((2,))],
        compiler_params=params(16),
        cost_estimate=CHEAP,
        name="norm_rows",
    )(info, *bcs, *states, gain, token, *uvs, *weights)


def stream(base, w0_far, w1_far, w0, w1, sem):
    j = pl.program_id(0)
    tiles = pl.num_programs(0)

    def fetch(t):
        slot = lax.rem(t, SLOTS)
        lanes = pl.ds(pl.multiple_of((base + t) * TILE, TILE), TILE)
        return (
            pltpu.make_async_copy(w0_far.at[:, lanes], w0.at[slot], sem.at[0, slot]),
            pltpu.make_async_copy(w1_far.at[:, lanes], w1.at[slot], sem.at[1, slot]),
        )

    def start(t):
        @pl.when(t < tiles)
        def _():
            for copy in fetch(t):
                copy.start()

    @pl.when(j == 0)
    def _():
        for t in range(SLOTS - 1):
            start(t)

    start(j + SLOTS - 1)
    for copy in fetch(j):
        copy.wait()
    return lax.rem(j, SLOTS)


def buffers(depth):
    return [
        pltpu.VMEM((SLOTS, depth, TILE), BF16),
        pltpu.VMEM((SLOTS, depth, TILE), BF16),
        pltpu.SemaphoreType.DMA((2, SLOTS)),
    ]


def ahead_kernel(owns, mates, w0, w1, out):
    rows = out.shape[0]
    out[...] = (dot(owns[0:rows, :], w0[...]) + dot(mates[0:rows, :], w1[...])).astype(BF16)


def project_ahead(owns, mates, w0, w1):
    return pl.pallas_call(
        ahead_kernel,
        in_specs=[FULL] * 4,
        out_specs=FULL,
        out_shape=jax.ShapeDtypeStruct((owns.shape[0] // 2, w0.shape[1]), BF16),
        compiler_params=params(16),
        cost_estimate=CHEAP,
        name="project_ahead",
    )(owns, mates, w0, w1)


def both_kernel(base, cut, owns, mates, w0_far, w1_far, *refs):
    fars, near, w0, w1, sem = refs[:-4], *refs[-4:]
    rows = near.shape[0]
    slot = stream(base, w0_far, w1_far, w0, w1, sem)
    total = dot(owns[...], w0[slot]) + dot(mates[...], w1[slot])
    near[...] = total[rows:]
    for k, far_out in enumerate(fars):

        @pl.when(pl.program_id(0) // cut == k)
        def _():
            far_out[...] = total[0:rows].astype(BF16)


def project_both(owns, mates, w0, w1, first, count, chunk):
    rows, depth = owns.shape[0] // 2, owns.shape[1]
    cut = chunk // TILE
    chunks = count // chunk

    def placed(k):
        return pl.BlockSpec((rows, TILE), lambda j: (0, jnp.clip(j - k * cut, 0, cut - 1)))

    *fars, near = pl.pallas_call(
        functools.partial(both_kernel, first // TILE, cut),
        grid=(count // TILE,),
        in_specs=[FULL] * 2 + [FAR] * 2,
        out_specs=[placed(k) for k in range(chunks)] + [pl.BlockSpec((rows, TILE), lambda j: (0, j))],
        out_shape=[jax.ShapeDtypeStruct((rows, chunk), BF16)] * chunks + [jax.ShapeDtypeStruct((rows, count), F32)],
        scratch_shapes=buffers(depth),
        compiler_params=params(24),
        cost_estimate=CHEAP,
        name="project_both",
    )(owns, mates, w0, w1)
    return fars, near


def near_kernel(owns, mates, w0_far, w1_far, arrived, out, w0, w1, sem):
    slot = stream(0, w0_far, w1_far, w0, w1, sem)
    rows = out.shape[0]
    total = dot(owns[rows:, :], w0[slot]) + dot(mates[rows:, :], w1[slot])
    out[...] = (total + arrived[...].astype(F32)).astype(BF16)


def project_near(owns, mates, w0, w1, arrived):
    rows, depth = owns.shape[0] // 2, owns.shape[1]
    placed = pl.BlockSpec((rows, TILE), lambda j: (0, j))
    return pl.pallas_call(
        near_kernel,
        grid=(arrived.shape[1] // TILE,),
        in_specs=[FULL, FULL, FAR, FAR, placed],
        out_specs=placed,
        out_shape=jax.ShapeDtypeStruct((rows, w0.shape[1]), BF16),
        scratch_shapes=buffers(depth),
        compiler_params=params(20),
        cost_estimate=CHEAP,
        name="project_near",
    )(owns, mates, w0, w1, arrived)


def add_kernel(near, *refs):
    arrived, out = refs[:-2], refs[-1]
    chunk = arrived[0].shape[1]
    for k, part in enumerate(arrived):
        lanes = slice(k * chunk, (k + 1) * chunk)
        out[:, lanes] = (near[:, lanes] + part[...].astype(F32)).astype(BF16)


def add_chunks(near, first, arrived, result, at):
    rows, chunk = arrived[0].shape
    count = chunk * len(arrived)
    return pl.pallas_call(
        add_kernel,
        grid=(1,),
        in_specs=[pl.BlockSpec((rows, count), lambda j: (0, first // count))] + [FULL] * len(arrived) + [ANY],
        out_specs=pl.BlockSpec((rows, count), lambda j: (0, at // count)),
        out_shape=jax.ShapeDtypeStruct(result.shape, BF16),
        input_output_aliases={1 + len(arrived): 0},
        compiler_params=params(8),
        cost_estimate=CHEAP,
        name="add_chunks",
    )(near, *arrived, result)


def shift(block, distance):
    size = lax.axis_size("seq")
    return lax.ppermute(block, "seq", [(i, i + distance) for i in range(size - distance)])


def swap(block, axis, bit):
    return lax.ppermute(block, axis, [(i, i ^ bit) for i in range(lax.axis_size(axis))])


def rotate(block, distance):
    size = lax.axis_size("seq")
    return lax.ppermute(block, "seq", [(i, (i + distance) % size) for i in range(size)])


def log_steps(info, got, keep, rates_kept, done, pairs, scan_next):
    half = keep.shape[1]
    message = ((N + EXTRA, half), BF16)
    full = ((N, half), F32)
    msg, own, first, aux = combine(
        pair_kernel,
        (info, got, keep, rates_kept, done),
        [SCALAR, FULL, FULL, FULL, ANY],
        [message, full, full, ((16, half), F32)],
        "pair",
    )
    behind = None
    covered = 0
    while True:
        got = shift(msg, 2 * (covered + 1))
        done = scan_next(msg)
        covered = 2 * covered + 1
        if covered >= pairs - 1:
            break
        operands, specs = [got, own, aux], [FULL, FULL, FULL]
        if behind is None:
            kernel = lambda g, o, a, t, m, b: wave_kernel(g, o, a, None, t, m, b)
        else:
            kernel = wave_kernel
            operands.append(behind)
            specs.append(FULL)
        msg, behind = combine(kernel, operands + [done], specs + [ANY], [message, ((N + 8, half), F32)], "wave")
    operands, specs = [info, got], [SCALAR, FULL]
    if behind is None:
        kernel = lambda o, g, f, a, t, b, h: last_kernel(o, g, None, f, a, t, b, h)
    else:
        kernel = last_kernel
        operands.append(behind)
        specs.append(FULL)
    out = ((N, half), BF16)
    back, held = combine(kernel, operands + [first, aux, done], specs + [FULL, FULL, ANY], [out, out], "last")
    return back, held


def local(
    x_input,
    z_input,
    bc_input,
    conv_weight_x,
    conv_weight_bc,
    step_size,
    log_decay,
    skip_gain,
    norm_gain,
    out_weight,
):
    length, width = x_input.shape
    heads = step_size.shape[1]
    ways = lax.axis_size("head")
    pairs = lax.axis_size("seq") // 2
    mine = lax.axis_index("head")
    half = width // 2
    seq = lax.axis_index("seq")
    info = jnp.stack([seq & 1, mine ^ 3, mine ^ 2, mine ^ 1, mine, seq >> 1, seq, 1 - (seq & 1), seq & 1]).astype(jnp.int32)

    x_far, z_far, w_far = far(x_input, z_input, out_weight)
    (bc_far,) = far(bc_input)
    halo = rotate(tail_rows(x_far, bc_far), 1)
    bc = bc_input.reshape(length, -1)
    (weight_mate,) = far(swap(out_weight, "head", 1))

    (cum, cum_s, log_s, f_dev, f_blk, e_blk, rates), ones = decays(info, log_decay, step_size, skip_gain, half)
    taps = far(conv_weight_x, conv_weight_bc)
    shared = (info, x_far, bc, halo, *taps)
    x0, bc0, send = conv_states(0, *shared, f_dev[0], ones, rates[0])
    got = swap(send, "seq", 1)
    x1, bc1, keep = conv_states(1, *shared, f_dev[1], ones, rates[1])
    rates_kept = rates[1]

    uvs = []
    xs, bcs = far(x0, x1), (bc0, bc1)
    groups = [(x, z_far, *rest, ones) for x, *rest in zip(xs, bcs, cum, cum_s, log_s, f_blk, e_blk, rates)]

    def scan_next(token):
        if len(uvs) < 2 * B_PARTS:
            order, part = divmod(len(uvs), B_PARTS)
            uvs.append(scan_part(order, part, info, token, *groups[order]))
        return uvs[-1]

    full = ((N, half), F32)
    message = ((N + EXTRA, half), BF16)
    done = keep
    out = ((N, half), BF16)
    if pairs > 1 and half % (pairs * N) == 0:
        piece = half // pairs
        part = ((N + EXTRA, piece), BF16)
        first, aux, *parts = combine(
            pair_split_kernel,
            (info, got, keep, rates_kept, done),
            [SCALAR, FULL, FULL, FULL, ANY],
            [full, ((8, half), F32)] + [part] * pairs,
            "pair",
            [pltpu.VMEM(*message)],
        )
        parts = list(parts[:1]) + [rotate(parts[r], 2 * r) for r in range(1, pairs)]
        done = scan_next(scan_next(parts[0]))
        parts = combine(
            owner_kernel,
            [info] + parts + [done],
            [SCALAR] + [FULL] * pairs + [ANY],
            [((N, piece), BF16)] * pairs,
            "owner",
            [pltpu.VMEM((pairs, N + EXTRA, piece), BF16), pltpu.VMEM((pairs, N, piece), BF16)],
        )
        ready = parts[0]
        parts = list(parts[:1]) + [rotate(parts[r], 2 * r) for r in range(1, pairs)]
        done = scan_next(ready)
        back, held = combine(
            last_split_kernel,
            [info, first, aux, done] + parts,
            [SCALAR, FULL, FULL, ANY] + [FULL] * pairs,
            [out, out],
            "last",
            [pltpu.VMEM(*out)],
        )
    else:
        back, held = log_steps(info, got, keep, rates_kept, done, pairs, scan_next)
    other = swap(back, "seq", 1)
    while len(uvs) < 2 * B_PARTS:
        scan_next(back)

    count = length // ways
    gain = norm_gain[None, :]

    columns = out_weight.shape[1]
    chunk = columns // 8
    weights = (w_far, weight_mate)
    shared = ((bc0, bc1), (other, held), gain, uvs)
    (mates,) = norm_rows((0, 2), info, count, held, *shared)
    owns, w0, w1 = norm_rows((1, 3), info, count, mates, *shared, weights, chunk)
    operands = (owns, swap(mates, "head", 1), *weights)
    first = swap(project_ahead(*operands[:2], w0, w1), "head", 2)
    calls = []
    for lo, hi in ((1, 2), (2, 4), (4, 6), (6, 8)):
        sent, near = project_both(*operands, lo * chunk, (hi - lo) * chunk, chunk)
        calls.append((near, lo, [swap(part, "head", 2) for part in sent]))
    result = project_near(*operands, first)
    for near, lo, arrived in calls[:-1]:
        result = add_chunks(near, 0, arrived, result, lo * chunk)
    near, lo, arrived = calls[-1]
    for k, part in enumerate(arrived):
        result = add_chunks(near, k * chunk, [part], result, (lo + k) * chunk)
    return result


def solution(mesh):
    in_specs = (
        P("seq", "head"),
        P("seq", "head"),
        P("seq", "head", None),
        P(None, "head"),
        P(None, "head", None),
        P("seq", "head"),
        P("seq", "head"),
        P("head"),
        P("head"),
        P("head", None),
    )
    out_specs = P(("seq", "head"), None)
    return jax.shard_map(local, mesh=mesh, in_specs=in_specs, out_specs=out_specs, check_vma=False)
```

```python
import functools

import jax
import jax.numpy as jnp
from jax import lax
from jax.experimental import pallas as pl
from jax.experimental.pallas import tpu as pltpu
from jax.sharding import PartitionSpec as P

P_SIZE = 64
N = 128
KCONV = 4
EPS = 1e-05
LOG2E = 1.4426950408889634

TOK_A = 256
ROWS_A = 32
TOK_B = 128
STEP_B = 256
EXTRA = 16
SLAB = 256
ROWS_C = 128
TILE = 256
SLOTS = 4
LEAD = 16
B_PARTS = 2
HIGHEST = lax.Precision.HIGHEST
F32 = jnp.float32
BF16 = jnp.bfloat16


def params(mib):
    return pltpu.CompilerParams(vmem_limit_bytes=mib * 1024 * 1024)


CHEAP = pl.CostEstimate(flops=1, bytes_accessed=1, transcendentals=0)
SCALAR = pl.BlockSpec(memory_space=pltpu.SMEM)
FULL = pl.BlockSpec(memory_space=pltpu.VMEM)
FAR = pl.BlockSpec(memory_space=pltpu.HBM)
ANY = pl.BlockSpec(memory_space=pl.ANY)

ODD, ROWS, PAIR, SEQ, GROUP = 0, 1, 5, 6, 7


def dot(a, b, dims=((1,), (0,)), precision=None):
    return lax.dot_general(a, b, (dims, ((), ())), precision=precision, preferred_element_type=F32)


def half_silu(half):
    return half + half * jnp.tanh(half)


def far(*arrays):
    return [pltpu.with_memory_space_constraint(a, pltpu.HBM) for a in arrays]


def whole(shape):
    return pl.BlockSpec(shape, lambda *_: (0,) * len(shape))


def decay_kernel(info, ld_t, step_t, skip, x_far, *refs):
    cum, cum_s, log_s, f_dev, f_blk, e_blk, rates = [refs[2 * k : 2 * k + 2] for k in range(7)]
    ones, x, sem = refs[14:]
    copy = pltpu.make_async_copy(x_far, x, sem)
    copy.start()
    heads, length = ld_t.shape
    blocks = length // TOK_B
    per = heads // 2
    width = ones.shape[1]
    swapped = info[GROUP] == 1
    row = lax.broadcasted_iota(jnp.int32, (TOK_B, TOK_B), 0)
    col = lax.broadcasted_iota(jnp.int32, (TOK_B, TOK_B), 1)
    lower = (row >= col).astype(F32)
    upper = (row <= col).astype(F32)
    eye = (row == col).astype(BF16)

    def ordered(value):
        return jnp.where(swapped, jnp.concatenate([value[per:], value[:per]], 0), value)

    def put(ref, rows, value):
        high = value.astype(BF16)
        low = (value - high.astype(F32)).astype(BF16)
        for g in range(2):
            own = slice(g * per, (g + 1) * per)
            both = jnp.concatenate([high[own], low[own]], 0)
            ref[g][rows, :] = dot(eye, both, ((1,), (1,))).astype(BF16)

    member = lax.broadcasted_iota(jnp.int32, (per, width), 0) == lax.broadcasted_iota(jnp.int32, (per, width), 1) // P_SIZE
    member = member.astype(F32)
    ones[0:per, :] = member.astype(BF16)
    ones[per:, :] = member.astype(BF16)
    cums, totals, row_totals = [], [], []
    for b in range(blocks):
        rows = slice(b * TOK_B, (b + 1) * TOK_B)
        logs = ordered(ld_t[:, rows]) * LOG2E
        c = dot(lower, logs, ((1,), (1,)), HIGHEST)
        for g in range(2):
            cum[g][rows, :] = c[:, g * per : (g + 1) * per]
        row_totals.append(c[TOK_B - 1 : TOK_B, :])
        c = dot(logs, upper, precision=HIGHEST)
        cums.append(c)
        totals.append(c[:, TOK_B - 1 : TOK_B])
    before, row_before = [jnp.zeros_like(totals[0])], [jnp.zeros_like(row_totals[0])]
    for b in range(blocks):
        before.append(before[-1] + totals[b])
        row_before.append(row_before[-1] + row_totals[b])
    total = before[-1]
    logs = jnp.concatenate(row_totals + row_before[:-1] + row_before[-1:] * 8, 0)
    gains = jnp.broadcast_to(skip[...], (8, heads))
    gains = jnp.where(swapped, jnp.concatenate([gains[:, per:], gains[:, :per]], 1), gains)
    values = jnp.concatenate([jnp.exp2(logs), gains], 0)
    for g in range(2):
        rates[g][...] = dot(values[:, g * per : (g + 1) * per], member, precision=HIGHEST)
    for b in range(blocks):
        rows = slice(b * TOK_B, (b + 1) * TOK_B)
        s = ordered(step_t[:, rows])
        log_step = jnp.log2(s)
        shifted = cums[b] - log_step
        for g in range(2):
            own = slice(g * per, (g + 1) * per)
            log_s[g][:, rows] = log_step[own, :]
            cum_s[g][:, rows] = shifted[own, :]
        put(f_dev, rows, jnp.exp2(total - (cums[b] + before[b])) * s)
        put(f_blk, rows, jnp.exp2(totals[b] - cums[b]) * s)
        put(e_blk, rows, jnp.exp2(cums[b]))
    copy.wait()


def decays(info, log_decay, step, skip, x, width):
    length, heads = log_decay.shape
    blocks = length // TOK_B
    per = heads // 2
    across = jax.ShapeDtypeStruct((per, length), F32)
    pair = jax.ShapeDtypeStruct((length, 2 * per), BF16)
    column = jax.ShapeDtypeStruct((length, per), F32)
    rates = jax.ShapeDtypeStruct((2 * blocks + 16, width), F32)
    shapes = [shape for shape in (column, across, across, pair, pair, pair, rates) for _ in range(2)]
    shapes += [jax.ShapeDtypeStruct((2 * per, width), BF16), pltpu.VMEM(x.shape, BF16)]
    *refs, ones, x_near = pl.pallas_call(
        decay_kernel,
        in_specs=[SCALAR] + [FULL] * 3 + [FAR],
        out_specs=[FULL] * len(shapes),
        out_shape=shapes,
        scratch_shapes=[pltpu.SemaphoreType.DMA],
        compiler_params=params(16),
        cost_estimate=CHEAP,
        name="decays",
    )(info, *far(log_decay.T, step.T, skip[None, :], x))
    return [tuple(refs[2 * k : 2 * k + 2]) for k in range(7)], ones, x_near


def tail_kernel(x, bc, out):
    width, bc_width = x.shape[1], bc.shape[2]
    out[:, 0:width] = x[...]
    for g in range(bc.shape[1]):
        out[:, width + g * bc_width : width + (g + 1) * bc_width] = bc[:, g, :]


def tail_rows(x, bc):
    length, width = x.shape
    groups, bc_width = bc.shape[1:]
    at = length // LEAD - 1
    shape = (LEAD, width + groups * bc_width)
    return pl.pallas_call(
        tail_kernel,
        grid=(1,),
        in_specs=[
            pl.BlockSpec((LEAD, width), lambda i: (at, 0)),
            pl.BlockSpec((LEAD, groups, bc_width), lambda i: (at, 0, 0)),
        ],
        out_specs=whole(shape),
        out_shape=jax.ShapeDtypeStruct(shape, BF16),
        compiler_params=params(8),
        cost_estimate=CHEAP,
        name="tail_rows",
    )(x, bc)


def put_message(ref, state, decay):
    high = decay.astype(BF16)
    low = (decay - high.astype(F32)).astype(BF16)
    rest = jnp.zeros((EXTRA - 2, state.shape[1]), BF16)
    ref[0:N, :] = state.astype(BF16)
    ref[N:, :] = jnp.concatenate([high, low, rest], 0)


def take_message(ref):
    extra = ref[N:, :].astype(F32)
    return ref[0:N, :].astype(F32), extra[0:1] + extra[1:2]


def conv_kernel(order, info, x, bc, halo, wx, wbc, f_dev, ones, rates, *refs):
    z_far, refs = (None, refs) if order == 0 else (refs[0], refs[1:])
    x_out, bc_out, final = refs[:3]
    xf, state, down = refs[-3:]
    length, width = x_out.shape
    rows = TOK_A
    group = info[GROUP + order]
    first_lane = pl.multiple_of(group * width, width)
    first_bc = pl.multiple_of(group * 2 * N, 2 * N)
    if z_far is not None:
        fetch = pltpu.make_async_copy(z_far, refs[3], refs[4])
        fetch.start()
    state[...] = jnp.zeros_like(state)
    row = lax.broadcasted_iota(jnp.int32, down.shape, 0)
    col = lax.broadcasted_iota(jnp.int32, down.shape, 1)
    down[...] = (row == col + 1).astype(BF16)

    def conv(i, src, first, behind, weights, emit):
        at_start = jnp.where(info[SEQ] == 0, jnp.zeros_like(first), first)
        lead = jnp.where(i == 0, at_start, behind).astype(F32)
        w0, w1, w2, w3 = [w * 0.5 for w in weights]
        back = LEAD - 8
        lead_r1 = pltpu.roll(lead, 1, 0)
        last_p = (w1 * lead + w0 * lead_r1)[back:]
        moved = dot(down[...], src)
        top = lax.broadcasted_iota(jnp.int32, (8, lead.shape[1]), 0) == 0
        head = jnp.where(top, jnp.broadcast_to(lead[LEAD - 1 :], top.shape), moved[0:8])
        for r in range(0, rows, ROWS_A):
            cur = src[r : r + ROWS_A].astype(F32)
            r1 = moved[r : r + ROWS_A] if r else jnp.concatenate([head, moved[8:ROWS_A]], 0)
            p = w1 * cur + w0 * r1
            p2 = pltpu.roll(jnp.concatenate([last_p, p], 0), 2, 0)[8:]
            emit(r, half_silu((w3 * cur + w2 * r1) + p2))
            last_p = p[ROWS_A - 8 :]

    def step(i, _):
        at = pl.ds(pl.multiple_of(i * rows, rows), rows)
        behind = pl.ds(pl.multiple_of(jnp.maximum(i * rows - LEAD, 0), LEAD), LEAD)

        def out(r):
            return pl.ds(pl.multiple_of(i * rows + r, ROWS_A), ROWS_A)

        for lanes in range(0, 2 * N, SLAB):
            ds = slice(lanes, lanes + SLAB)
            src = pl.ds(pl.multiple_of(first_bc + lanes, SLAB), SLAB)
            halo_src = pl.ds(pl.multiple_of(x.shape[1] + first_bc + lanes, SLAB), SLAB)

            def emit_bc(r, value):
                bc_out[out(r), ds] = value.astype(BF16)

            weights = [jnp.where(group == 0, wbc[k, 0:1, ds], wbc[k, 1:2, ds]) for k in range(KCONV)]
            conv(i, bc[at, src], halo[:, halo_src], bc[behind, src], weights, emit_bc)

        for lanes in range(0, width, SLAB):
            ds = slice(lanes, lanes + SLAB)
            src = pl.ds(pl.multiple_of(first_lane + lanes, SLAB), SLAB)
            scale = dot(f_dev[at, :], ones[:, ds])

            def emit(r, value):
                x_out[out(r), ds] = value.astype(BF16)
                xf[r : r + ROWS_A, ds] = (value * scale[r : r + ROWS_A]).astype(BF16)

            weights = [wx[k : k + 1, ds] for k in range(KCONV)]
            conv(i, x[at, src], halo[:, src], x[behind, src], weights, emit)

        state[...] += dot(bc_out[at, 0:N], xf[...], ((0,), (0,)))
        return 0

    lax.fori_loop(0, length // rows, step, 0)
    if order == 0:
        row = rates.shape[0] - 16
        put_message(final, state[...], rates[row : row + 1, :])
    else:
        final[...] = state[...]
        fetch.wait()


def conv_states(order, info, x, bc, halo, wx, wbc, f_dev, ones, rates, z=None):
    length, full = x.shape
    width = full // 2
    column = lambda i, info: (0, info[GROUP + order])
    final = ((N + EXTRA, width), BF16) if order == 0 else ((N, width), F32)
    more = [] if z is None else [z]
    return pl.pallas_call(
        functools.partial(conv_kernel, order),
        grid_spec=pltpu.PrefetchScalarGridSpec(
            num_scalar_prefetch=1,
            grid=(1,),
            in_specs=[FULL] * 3 + [pl.BlockSpec((KCONV, width), column)] + [FULL] * 4 + [FAR] * len(more),
            out_specs=[FULL] * (3 + len(more)),
            scratch_shapes=[pltpu.SemaphoreType.DMA] * len(more)
            + [pltpu.VMEM((TOK_A, width), BF16), pltpu.VMEM((N, width), F32), pltpu.VMEM((TOK_A, TOK_A), BF16)],
        ),
        out_shape=[
            pltpu.VMEM((length, width), BF16),
            pltpu.VMEM((length, 2 * N), BF16),
            jax.ShapeDtypeStruct(*final),
        ]
        + [pltpu.VMEM(a.shape, BF16) for a in more],
        compiler_params=params(16),
        cost_estimate=CHEAP,
        name="conv_states",
    )(info, x, bc, halo, wx, wbc, f_dev, ones, rates, *more)


def pair_kernel(info, got, keep, rates, _, msg, own, first, aux):
    half = keep.shape[1]
    is_odd = info[ODD] == 1
    arrived, their = take_message(got)
    row = rates.shape[0] - 16
    mine = rates[row : row + 1, :]
    early = jnp.where(is_odd, arrived, keep[...])
    late = jnp.where(is_odd, keep[...], arrived)
    even_decay = jnp.where(is_odd, their, mine)
    odd_decay = jnp.where(is_odd, mine, their)
    state = odd_decay * early + late
    own[...] = state
    first[...] = early
    aux[0:8, :] = jnp.broadcast_to(even_decay, (8, half))
    aux[8:16, :] = jnp.broadcast_to(even_decay * odd_decay, (8, half))
    put_message(msg, state, even_decay * odd_decay)


def wave_kernel(got, own, aux, behind_in, _, msg, behind):
    before, decay = take_message(got)
    if behind_in is not None:
        before_decay = behind_in[N : N + 1, :]
        before = behind_in[0:N, :] + before_decay * before
        decay = before_decay * decay
    pair_decay = aux[8:9, :]
    behind[0:N, :] = before
    behind[N:, :] = jnp.broadcast_to(decay, (8, before.shape[1]))
    put_message(msg, own[...] + pair_decay * before, pair_decay * decay)


def last_kernel(info, got, behind_in, first, aux, _, back, held):
    is_odd = info[ODD] == 1
    before, _unused = take_message(got)
    if behind_in is not None:
        before = behind_in[0:N, :] + behind_in[N : N + 1, :] * before
    entering_odd = aux[0:1, :] * before + first[...]
    back[...] = jnp.where(is_odd, before, entering_odd).astype(BF16)
    held[...] = jnp.where(is_odd, entering_odd, before).astype(BF16)


def pair_split_kernel(info, got, keep, rates, _, first, aux, *refs):
    outs, wide = refs[:-1], refs[-1]
    half = keep.shape[1]
    pairs = len(outs)
    piece = half // pairs
    is_odd = info[ODD] == 1
    arrived, their = take_message(got)
    row = rates.shape[0] - 16
    mine = rates[row : row + 1, :]
    early = jnp.where(is_odd, arrived, keep[...])
    late = jnp.where(is_odd, keep[...], arrived)
    even_decay = jnp.where(is_odd, their, mine)
    odd_decay = jnp.where(is_odd, mine, their)
    first[...] = early
    aux[...] = jnp.broadcast_to(even_decay, (8, half))
    put_message(wide, odd_decay * early + late, even_decay * odd_decay)
    for r in range(pairs):
        owner = lax.rem(info[PAIR] + r, pairs)
        outs[r][...] = wide[:, pl.ds(pl.multiple_of(owner * piece, piece), piece)]


def owner_kernel(info, *refs):
    pairs = (len(refs) - 3) // 2
    ins, outs = refs[:pairs], refs[pairs + 1 : 2 * pairs + 1]
    states, prefixes = refs[-2:]
    for r in range(pairs):
        states[lax.rem(info[PAIR] + pairs - r, pairs)] = ins[r][...]
    before = jnp.zeros(prefixes.shape[1:], F32)
    for q in range(pairs):
        prefixes[q] = before.astype(BF16)
        if q < pairs - 1:
            state, decay = take_message(states.at[q])
            before = decay * before + state
    for r in range(pairs):
        outs[r][...] = prefixes[lax.rem(info[PAIR] + r, pairs)]


def last_split_kernel(info, first, aux, _, *refs):
    pairs = len(refs) - 3
    back, held, wide = refs[-3:]
    piece = back.shape[1] // pairs
    for r in range(pairs):
        owner = lax.rem(info[PAIR] + pairs - r, pairs)
        wide[:, pl.ds(pl.multiple_of(owner * piece, piece), piece)] = refs[r][...]
    is_odd = info[ODD] == 1
    before = wide[...].astype(F32)
    entering_odd = aux[0:1, :] * before + first[...]
    back[...] = jnp.where(is_odd, before, entering_odd).astype(BF16)
    held[...] = jnp.where(is_odd, entering_odd, before).astype(BF16)


def combine(kernel, operands, specs, outs, name, scratch=()):
    return pl.pallas_call(
        kernel,
        in_specs=specs,
        out_specs=[FULL] * len(outs),
        out_shape=[jax.ShapeDtypeStruct(s, t) for s, t in outs],
        scratch_shapes=list(scratch),
        compiler_params=params(16),
        cost_estimate=CHEAP,
        name=name,
    )(*operands)


def scan_kernel(order, part, info, x, z, bc, cum, cum_s, log_s, f_blk, e_blk, rates, ones, _, uv_out, state):
    length = x.shape[0]
    width = state.shape[1]
    per_slab = SLAB // P_SIZE
    inner = STEP_B // TOK_B
    blocks = length // TOK_B
    first_head = part * width // P_SIZE
    first_lane = info[GROUP + order] * x.shape[1] + part * width
    state[...] = jnp.zeros_like(state)

    row = lax.broadcasted_iota(jnp.int32, (TOK_B, TOK_B), 0)
    col = lax.broadcasted_iota(jnp.int32, (TOK_B, TOK_B), 1)
    keep = row >= col
    first = lax.broadcasted_iota(jnp.int32, (TOK_B, 2 * P_SIZE), 1) < P_SIZE
    zero = jnp.zeros((TOK_B, 2 * P_SIZE), BF16)

    def turn(step, _):
        for k in range(inner):
            block(step * inner + k)
        return 0

    def block(b):
        at = pl.ds(pl.multiple_of(b * TOK_B, TOK_B), TOK_B)
        b_mat = bc[at, 0:N]
        c_mat = bc[at, N : 2 * N]
        b_across = b_mat.T
        scores = jnp.where(keep, dot(c_mat, b_mat, ((1,), (1,))), 0.0)
        for s in range(width // SLAB):
            lanes = slice(s * SLAB, (s + 1) * SLAB)
            xb = x[at, part * width + s * SLAB : part * width + (s + 1) * SLAB]
            wide = slice(part * width + s * SLAB, part * width + (s + 1) * SLAB)
            sel = ones[:, wide]
            fade_row = rates[pl.ds(b, 1), wide]
            lead_row = rates[pl.ds(blocks + b, 1), wide]
            skip = rates[2 * blocks + 8 : 2 * blocks + 9, wide]
            old = state[:, lanes]
            rise = dot(e_blk[at, :], sel)
            carried = dot(c_mat, old.astype(BF16)) * rise
            within = []
            for q in range(per_slab // 2):
                tables = []
                for h in (2 * q, 2 * q + 1):
                    head = first_head + s * per_slab + h
                    column = cum[at, head : head + 1]
                    own = slice(head, head + 1)
                    gap = jnp.minimum(column - cum_s[own, at], log_s[own, at])
                    tables.append((scores * jnp.exp2(gap)).astype(BF16))
                xp = xb[:, q * 2 * P_SIZE : (q + 1) * 2 * P_SIZE]
                stacked = jnp.concatenate([jnp.where(first, xp, zero), jnp.where(first, zero, xp)], 0)
                within.append(dot(jnp.concatenate(tables, 1), stacked))
            xs = xb.astype(F32)
            y = jnp.concatenate(within, 1) + carried + skip * xs
            gate = half_silu((z[at, pl.ds(pl.multiple_of(first_lane + s * SLAB, SLAB), SLAB)] * 0.5).astype(F32))
            uv_out[at, lanes] = (y * gate).astype(BF16)
            uv_out[at, width + s * SLAB : width + (s + 1) * SLAB] = (gate * rise * lead_row).astype(BF16)
            xf = (xs * dot(f_blk[at, :], sel)).astype(BF16)
            state[:, lanes] = old * fade_row + dot(b_across, xf)

    lax.fori_loop(0, length // STEP_B, turn, 0)


def scan_part(order, part, info, token, x, z, bc, cum, cum_s, log_s, f_blk, e_blk, rates, ones):
    length, full = x.shape
    width = full // B_PARTS
    return pl.pallas_call(
        functools.partial(scan_kernel, order, part),
        in_specs=[SCALAR] + [FULL] * 10 + [ANY],
        out_specs=FULL,
        out_shape=pltpu.VMEM((length, 2 * width), BF16),
        scratch_shapes=[pltpu.VMEM((N, width), F32)],
        compiler_params=params(12),
        cost_estimate=CHEAP,
        name="scan_part",
    )(info, x, z, bc, cum, cum_s, log_s, f_blk, e_blk, rates, ones, token)


def norm_kernel(places, fetched, info, bc0, bc1, state0, state1, gain, _, *refs):
    uvs, refs = refs[: 2 * B_PARTS], refs[2 * B_PARTS :]
    weights, out, tiles, sem = refs[:fetched], refs[fetched], refs[fetched + 1 : 2 * fetched + 1], refs[-1]
    copies = [
        pltpu.make_async_copy(weight.at[:, pl.ds(0, tile.shape[1])], tile, sem.at[k])
        for k, (weight, tile) in enumerate(zip(weights, tiles))
    ]
    for copy in copies:
        copy.start()
    count = out.shape[0] // len(places)
    per = state0.shape[1]
    part = per // B_PARTS

    def rows(first, base):
        to = pl.ds(pl.multiple_of(first, ROWS_C), ROWS_C)
        at = pl.ds(pl.multiple_of(base, ROWS_C), ROWS_C)
        for order, (bc, state) in enumerate(((bc0, state0), (bc1, state1))):
            c_mat = bc[at, N : 2 * N]
            pieces = []
            squares = None
            for p in range(B_PARTS):
                uv = uvs[order * B_PARTS + p]
                inc = state[:, p * part : (p + 1) * part]
                gated = uv[at, 0:part].astype(F32) + uv[at, part:].astype(F32) * dot(c_mat, inc)
                square = jnp.sum(gated * gated, axis=-1, keepdims=True)
                squares = square if squares is None else squares + square
                pieces.append(gated)
            scale = lax.rsqrt(squares * (1.0 / per) + EPS)
            for p, gated in enumerate(pieces):
                lanes = pl.ds(pl.multiple_of(info[GROUP + order] * per + p * part, part), part)
                out[to, lanes] = (gated * scale * gain[:, lanes]).astype(BF16)

    for k, place in enumerate(places):

        def step(j, _):
            rows(k * count + j * ROWS_C, info[ROWS + place] * count + j * ROWS_C)
            return 0

        lax.fori_loop(0, count // ROWS_C, step, 0)
    for copy in copies:
        copy.wait()


def norm_rows(places, info, count, token, bcs, states, gain, uvs, weights=(), columns=0):
    tile = jax.ShapeDtypeStruct((gain.shape[1], columns), BF16)
    return pl.pallas_call(
        functools.partial(norm_kernel, places, len(weights)),
        in_specs=[SCALAR] + [FULL] * 5 + [ANY] + [FULL] * len(uvs) + [FAR] * len(weights),
        out_specs=[FULL] * (1 + len(weights)),
        out_shape=[jax.ShapeDtypeStruct((len(places) * count, gain.shape[1]), BF16)] + [tile] * len(weights),
        scratch_shapes=[pltpu.SemaphoreType.DMA((2,))],
        compiler_params=params(16),
        cost_estimate=CHEAP,
        name="norm_rows",
    )(info, *bcs, *states, gain, token, *uvs, *weights)


def stream(base, w0_far, w1_far, w0, w1, sem):
    j = pl.program_id(0)
    tiles = pl.num_programs(0)

    def fetch(t):
        slot = lax.rem(t, SLOTS)
        lanes = pl.ds(pl.multiple_of((base + t) * TILE, TILE), TILE)
        return (
            pltpu.make_async_copy(w0_far.at[:, lanes], w0.at[slot], sem.at[0, slot]),
            pltpu.make_async_copy(w1_far.at[:, lanes], w1.at[slot], sem.at[1, slot]),
        )

    def start(t):
        @pl.when(t < tiles)
        def _():
            for copy in fetch(t):
                copy.start()

    @pl.when(j == 0)
    def _():
        for t in range(SLOTS - 1):
            start(t)

    start(j + SLOTS - 1)
    for copy in fetch(j):
        copy.wait()
    return lax.rem(j, SLOTS)


def buffers(depth):
    return [
        pltpu.VMEM((SLOTS, depth, TILE), BF16),
        pltpu.VMEM((SLOTS, depth, TILE), BF16),
        pltpu.SemaphoreType.DMA((2, SLOTS)),
    ]


def ahead_kernel(owns, mates, w0, w1, out):
    rows = out.shape[0]
    out[...] = (dot(owns[0:rows, :], w0[...]) + dot(mates[0:rows, :], w1[...])).astype(BF16)


def project_ahead(owns, mates, w0, w1):
    return pl.pallas_call(
        ahead_kernel,
        in_specs=[FULL] * 4,
        out_specs=FULL,
        out_shape=jax.ShapeDtypeStruct((owns.shape[0] // 2, w0.shape[1]), BF16),
        compiler_params=params(16),
        cost_estimate=CHEAP,
        name="project_ahead",
    )(owns, mates, w0, w1)


def both_kernel(base, cut, owns, mates, w0_far, w1_far, *refs):
    fars, near, w0, w1, sem = refs[:-4], *refs[-4:]
    rows = near.shape[0]
    slot = stream(base, w0_far, w1_far, w0, w1, sem)
    total = dot(owns[...], w0[slot]) + dot(mates[...], w1[slot])
    near[...] = total[rows:]
    for k, far_out in enumerate(fars):

        @pl.when(pl.program_id(0) // cut == k)
        def _():
            far_out[...] = total[0:rows].astype(BF16)


def project_both(owns, mates, w0, w1, first, count, chunk):
    rows, depth = owns.shape[0] // 2, owns.shape[1]
    cut = chunk // TILE
    chunks = count // chunk

    def placed(k):
        return pl.BlockSpec((rows, TILE), lambda j: (0, jnp.clip(j - k * cut, 0, cut - 1)))

    *fars, near = pl.pallas_call(
        functools.partial(both_kernel, first // TILE, cut),
        grid=(count // TILE,),
        in_specs=[FULL] * 2 + [FAR] * 2,
        out_specs=[placed(k) for k in range(chunks)] + [pl.BlockSpec((rows, TILE), lambda j: (0, j))],
        out_shape=[jax.ShapeDtypeStruct((rows, chunk), BF16)] * chunks + [jax.ShapeDtypeStruct((rows, count), F32)],
        scratch_shapes=buffers(depth),
        compiler_params=params(24),
        cost_estimate=CHEAP,
        name="project_both",
    )(owns, mates, w0, w1)
    return fars, near


def near_kernel(owns, mates, w0_far, w1_far, arrived, out, w0, w1, sem):
    slot = stream(0, w0_far, w1_far, w0, w1, sem)
    rows = out.shape[0]
    total = dot(owns[rows:, :], w0[slot]) + dot(mates[rows:, :], w1[slot])
    out[...] = (total + arrived[...].astype(F32)).astype(BF16)


def project_near(owns, mates, w0, w1, arrived):
    rows, depth = owns.shape[0] // 2, owns.shape[1]
    placed = pl.BlockSpec((rows, TILE), lambda j: (0, j))
    return pl.pallas_call(
        near_kernel,
        grid=(arrived.shape[1] // TILE,),
        in_specs=[FULL, FULL, FAR, FAR, placed],
        out_specs=placed,
        out_shape=jax.ShapeDtypeStruct((rows, w0.shape[1]), BF16),
        scratch_shapes=buffers(depth),
        compiler_params=params(20),
        cost_estimate=CHEAP,
        name="project_near",
    )(owns, mates, w0, w1, arrived)


def add_kernel(near, *refs):
    arrived, out = refs[:-2], refs[-1]
    chunk = arrived[0].shape[1]
    for k, part in enumerate(arrived):
        lanes = slice(k * chunk, (k + 1) * chunk)
        out[:, lanes] = (near[:, lanes] + part[...].astype(F32)).astype(BF16)


def add_chunks(near, first, arrived, result, at):
    rows, chunk = arrived[0].shape
    count = chunk * len(arrived)
    return pl.pallas_call(
        add_kernel,
        grid=(1,),
        in_specs=[pl.BlockSpec((rows, count), lambda j: (0, first // count))] + [FULL] * len(arrived) + [ANY],
        out_specs=pl.BlockSpec((rows, count), lambda j: (0, at // count)),
        out_shape=jax.ShapeDtypeStruct(result.shape, BF16),
        input_output_aliases={1 + len(arrived): 0},
        compiler_params=params(8),
        cost_estimate=CHEAP,
        name="add_chunks",
    )(near, *arrived, result)


def shift(block, distance):
    size = lax.axis_size("seq")
    return lax.ppermute(block, "seq", [(i, i + distance) for i in range(size - distance)])


def swap(block, axis, bit):
    return lax.ppermute(block, axis, [(i, i ^ bit) for i in range(lax.axis_size(axis))])


def rotate(block, distance):
    size = lax.axis_size("seq")
    return lax.ppermute(block, "seq", [(i, (i + distance) % size) for i in range(size)])


def log_steps(info, got, keep, rates_kept, done, pairs, scan_next):
    half = keep.shape[1]
    message = ((N + EXTRA, half), BF16)
    full = ((N, half), F32)
    msg, own, first, aux = combine(
        pair_kernel,
        (info, got, keep, rates_kept, done),
        [SCALAR, FULL, FULL, FULL, ANY],
        [message, full, full, ((16, half), F32)],
        "pair",
    )
    behind = None
    covered = 0
    while True:
        got = shift(msg, 2 * (covered + 1))
        done = scan_next(msg)
        covered = 2 * covered + 1
        if covered >= pairs - 1:
            break
        operands, specs = [got, own, aux], [FULL, FULL, FULL]
        if behind is None:
            kernel = lambda g, o, a, t, m, b: wave_kernel(g, o, a, None, t, m, b)
        else:
            kernel = wave_kernel
            operands.append(behind)
            specs.append(FULL)
        msg, behind = combine(kernel, operands + [done], specs + [ANY], [message, ((N + 8, half), F32)], "wave")
    operands, specs = [info, got], [SCALAR, FULL]
    if behind is None:
        kernel = lambda o, g, f, a, t, b, h: last_kernel(o, g, None, f, a, t, b, h)
    else:
        kernel = last_kernel
        operands.append(behind)
        specs.append(FULL)
    out = ((N, half), BF16)
    back, held = combine(kernel, operands + [first, aux, done], specs + [FULL, FULL, ANY], [out, out], "last")
    return back, held


def local(
    x_input,
    z_input,
    bc_input,
    conv_weight_x,
    conv_weight_bc,
    step_size,
    log_decay,
    skip_gain,
    norm_gain,
    out_weight,
):
    length, width = x_input.shape
    heads = step_size.shape[1]
    ways = lax.axis_size("head")
    pairs = lax.axis_size("seq") // 2
    mine = lax.axis_index("head")
    half = width // 2
    seq = lax.axis_index("seq")
    info = jnp.stack([seq & 1, mine ^ 3, mine ^ 2, mine ^ 1, mine, seq >> 1, seq, 1 - (seq & 1), seq & 1]).astype(jnp.int32)

    x_far, z_far, w_far = far(x_input, z_input, out_weight)
    (bc_far,) = far(bc_input)
    halo = rotate(tail_rows(x_far, bc_far), 1)
    bc = bc_input.reshape(length, -1)
    (weight_mate,) = far(swap(out_weight, "head", 1))

    (cum, cum_s, log_s, f_dev, f_blk, e_blk, rates), ones, x_near = decays(
        info, log_decay, step_size, skip_gain, x_input, half
    )
    taps = far(conv_weight_x, conv_weight_bc)
    shared = (info, x_near, bc, halo, *taps)
    x0, bc0, send = conv_states(0, *shared, f_dev[0], ones, rates[0])
    got = swap(send, "seq", 1)
    x1, bc1, keep, z_near = conv_states(1, *shared, f_dev[1], ones, rates[1], z_far)
    rates_kept = rates[1]

    uvs = []
    groups = [(x, z_near, *rest, ones) for x, *rest in zip((x0, x1), (bc0, bc1), cum, cum_s, log_s, f_blk, e_blk, rates)]

    def scan_next(token):
        if len(uvs) < 2 * B_PARTS:
            order, part = divmod(len(uvs), B_PARTS)
            uvs.append(scan_part(order, part, info, token, *groups[order]))
        return uvs[-1]

    full = ((N, half), F32)
    message = ((N + EXTRA, half), BF16)
    done = keep
    out = ((N, half), BF16)
    if pairs > 1 and half % (pairs * N) == 0:
        piece = half // pairs
        part = ((N + EXTRA, piece), BF16)
        first, aux, *parts = combine(
            pair_split_kernel,
            (info, got, keep, rates_kept, done),
            [SCALAR, FULL, FULL, FULL, ANY],
            [full, ((8, half), F32)] + [part] * pairs,
            "pair",
            [pltpu.VMEM(*message)],
        )
        parts = list(parts[:1]) + [rotate(parts[r], 2 * r) for r in range(1, pairs)]
        done = scan_next(scan_next(parts[0]))
        parts = combine(
            owner_kernel,
            [info] + parts + [done],
            [SCALAR] + [FULL] * pairs + [ANY],
            [((N, piece), BF16)] * pairs,
            "owner",
            [pltpu.VMEM((pairs, N + EXTRA, piece), BF16), pltpu.VMEM((pairs, N, piece), BF16)],
        )
        ready = parts[0]
        parts = list(parts[:1]) + [rotate(parts[r], 2 * r) for r in range(1, pairs)]
        done = scan_next(ready)
        back, held = combine(
            last_split_kernel,
            [info, first, aux, done] + parts,
            [SCALAR, FULL, FULL, ANY] + [FULL] * pairs,
            [out, out],
            "last",
            [pltpu.VMEM(*out)],
        )
    else:
        back, held = log_steps(info, got, keep, rates_kept, done, pairs, scan_next)
    other = swap(back, "seq", 1)
    while len(uvs) < 2 * B_PARTS:
        scan_next(back)

    count = length // ways
    gain = norm_gain[None, :]

    columns = out_weight.shape[1]
    chunk = columns // 8
    weights = (w_far, weight_mate)
    shared = ((bc0, bc1), (other, held), gain, uvs)
    (mates,) = norm_rows((0, 2), info, count, held, *shared)
    owns, w0, w1 = norm_rows((1, 3), info, count, mates, *shared, weights, chunk)
    operands = (owns, swap(mates, "head", 1), *weights)
    first = swap(project_ahead(*operands[:2], w0, w1), "head", 2)
    calls = []
    for lo, hi in ((1, 2), (2, 4), (4, 6), (6, 8)):
        sent, near = project_both(*operands, lo * chunk, (hi - lo) * chunk, chunk)
        calls.append((near, lo, [swap(part, "head", 2) for part in sent]))
    result = project_near(*operands, first)
    for near, lo, arrived in calls[:-1]:
        result = add_chunks(near, 0, arrived, result, lo * chunk)
    near, lo, arrived = calls[-1]
    for k, part in enumerate(arrived):
        result = add_chunks(near, k * chunk, [part], result, (lo + k) * chunk)
    return result


def solution(mesh):
    in_specs = (
        P("seq", "head"),
        P("seq", "head"),
        P("seq", "head", None),
        P(None, "head"),
        P(None, "head", None),
        P("seq", "head"),
        P("seq", "head"),
        P("head"),
        P("head"),
        P("head", None),
    )
    out_specs = P(("seq", "head"), None)
    return jax.shard_map(local, mesh=mesh, in_specs=in_specs, out_specs=out_specs, check_vma=False)
```

```python
import functools

import jax
import jax.numpy as jnp
from jax import lax
from jax.experimental import pallas as pl
from jax.experimental.pallas import tpu as pltpu
from jax.sharding import PartitionSpec as P

P_SIZE = 64
N = 128
KCONV = 4
EPS = 1e-05
LOG2E = 1.4426950408889634

TOK_A = 256
ROWS_A = 32
TOK_B = 128
STEP_B = 256
EXTRA = 16
SLAB = 256
ROWS_C = 128
TILE = 256
SLOTS = 4
LEAD = 16
B_PARTS = 2
HIGHEST = lax.Precision.HIGHEST
F32 = jnp.float32
BF16 = jnp.bfloat16


def params(mib):
    return pltpu.CompilerParams(vmem_limit_bytes=mib * 1024 * 1024)


CHEAP = pl.CostEstimate(flops=1, bytes_accessed=1, transcendentals=0)
SCALAR = pl.BlockSpec(memory_space=pltpu.SMEM)
FULL = pl.BlockSpec(memory_space=pltpu.VMEM)
FAR = pl.BlockSpec(memory_space=pltpu.HBM)
ANY = pl.BlockSpec(memory_space=pl.ANY)

ODD, ROWS, PAIR, SEQ, GROUP = 0, 1, 5, 6, 7


def dot(a, b, dims=((1,), (0,)), precision=None):
    return lax.dot_general(a, b, (dims, ((), ())), precision=precision, preferred_element_type=F32)


def half_silu(half):
    return half + half * jnp.tanh(half)


def far(*arrays):
    return [pltpu.with_memory_space_constraint(a, pltpu.HBM) for a in arrays]


def whole(shape):
    return pl.BlockSpec(shape, lambda *_: (0,) * len(shape))


def group_copies(x_far, x, group, sems):
    length, width = x.shape
    rows = length // 4
    lanes = pl.ds(pl.multiple_of(group * width, width), width)
    pieces = [pl.ds(k * rows, rows) for k in range(4)]
    return [pltpu.make_async_copy(x_far.at[at, lanes], x.at[at], sems.at[k]) for k, at in enumerate(pieces)]


def decay_kernel(info, ld_t, step_t, skip, x_far, *refs):
    cum, cum_s, log_s, f_dev, f_blk, e_blk, rates = [refs[2 * k : 2 * k + 2] for k in range(7)]
    ones, wide_ones, x, sem = refs[14:]
    copies = group_copies(x_far, x, info[GROUP], sem)
    for copy in copies:
        copy.start()
    heads, length = ld_t.shape
    blocks = length // TOK_B
    per = heads // 2
    width = ones.shape[1]
    swapped = info[GROUP] == 1
    row = lax.broadcasted_iota(jnp.int32, (TOK_B, TOK_B), 0)
    col = lax.broadcasted_iota(jnp.int32, (TOK_B, TOK_B), 1)
    lower = (row >= col).astype(F32)
    upper = (row <= col).astype(F32)
    eye = (row == col).astype(BF16)

    def ordered(value):
        return jnp.where(swapped, jnp.concatenate([value[per:], value[:per]], 0), value)

    def put(ref, rows, value):
        high = value.astype(BF16)
        low = (value - high.astype(F32)).astype(BF16)
        for g in range(2):
            own = slice(g * per, (g + 1) * per)
            both = jnp.concatenate([high[own], low[own]], 0)
            ref[g][rows, :] = dot(eye, both, ((1,), (1,))).astype(BF16)

    member = lax.broadcasted_iota(jnp.int32, (per, width), 0) == lax.broadcasted_iota(jnp.int32, (per, width), 1) // P_SIZE
    member = member.astype(F32)
    ones[0:per, :] = member.astype(BF16)
    ones[per:, :] = member.astype(BF16)
    shape = (per, per * TOK_B)
    spread = lax.broadcasted_iota(jnp.int32, shape, 0) == lax.broadcasted_iota(jnp.int32, shape, 1) // TOK_B
    for k in range(3):
        wide_ones[k * per : (k + 1) * per, :] = spread.astype(F32).astype(BF16)
    cums, totals, row_totals = [], [], []
    for b in range(blocks):
        rows = slice(b * TOK_B, (b + 1) * TOK_B)
        logs = ordered(ld_t[:, rows]) * LOG2E
        c = dot(lower, logs, ((1,), (1,)), HIGHEST)
        for g in range(2):
            rest = c[:, g * per : (g + 1) * per]
            for k in range(3):
                kept = rest.astype(BF16)
                cum[g][rows, k * per : (k + 1) * per] = kept
                rest = rest - kept.astype(F32)
        row_totals.append(c[TOK_B - 1 : TOK_B, :])
        c = dot(logs, upper, precision=HIGHEST)
        cums.append(c)
        totals.append(c[:, TOK_B - 1 : TOK_B])
    before, row_before = [jnp.zeros_like(totals[0])], [jnp.zeros_like(row_totals[0])]
    for b in range(blocks):
        before.append(before[-1] + totals[b])
        row_before.append(row_before[-1] + row_totals[b])
    total = before[-1]
    logs = jnp.concatenate(row_totals + row_before[:-1] + row_before[-1:] * 8, 0)
    gains = jnp.broadcast_to(skip[...], (8, heads))
    gains = jnp.where(swapped, jnp.concatenate([gains[:, per:], gains[:, :per]], 1), gains)
    values = jnp.concatenate([jnp.exp2(logs), gains], 0)
    for g in range(2):
        rates[g][...] = dot(values[:, g * per : (g + 1) * per], member, precision=HIGHEST)
    for b in range(blocks):
        rows = slice(b * TOK_B, (b + 1) * TOK_B)
        s = ordered(step_t[:, rows])
        log_step = jnp.log2(s)
        shifted = cums[b] - log_step
        for g in range(2):
            own = slice(g * per, (g + 1) * per)
            log_s[g][:, rows] = log_step[own, :]
            cum_s[g][:, rows] = shifted[own, :]
        put(f_dev, rows, jnp.exp2(total - (cums[b] + before[b])) * s)
        put(f_blk, rows, jnp.exp2(totals[b] - cums[b]) * s)
        put(e_blk, rows, jnp.exp2(cums[b]))
    for copy in copies:
        copy.wait()


def decays(info, log_decay, step, skip, x, width):
    length, heads = log_decay.shape
    blocks = length // TOK_B
    per = heads // 2
    across = jax.ShapeDtypeStruct((per, length), F32)
    pair = jax.ShapeDtypeStruct((length, 2 * per), BF16)
    column = jax.ShapeDtypeStruct((length, 3 * per), BF16)
    rates = jax.ShapeDtypeStruct((2 * blocks + 16, width), F32)
    shapes = [shape for shape in (column, across, across, pair, pair, pair, rates) for _ in range(2)]
    shapes += [
        jax.ShapeDtypeStruct((2 * per, width), BF16),
        jax.ShapeDtypeStruct((3 * per, per * TOK_B), BF16),
        pltpu.VMEM((length, width), BF16),
    ]
    *refs, ones, wide_ones, x_near = pl.pallas_call(
        decay_kernel,
        in_specs=[SCALAR] + [FULL] * 3 + [FAR],
        out_specs=[FULL] * len(shapes),
        out_shape=shapes,
        scratch_shapes=[pltpu.SemaphoreType.DMA((4,))],
        compiler_params=params(16),
        cost_estimate=CHEAP,
        name="decays",
    )(info, *far(log_decay.T, step.T, skip[None, :], x))
    return [tuple(refs[2 * k : 2 * k + 2]) for k in range(7)], ones, wide_ones, x_near


def tail_kernel(x, bc, out):
    width, bc_width = x.shape[1], bc.shape[2]
    out[:, 0:width] = x[...]
    for g in range(bc.shape[1]):
        out[:, width + g * bc_width : width + (g + 1) * bc_width] = bc[:, g, :]


def tail_rows(x, bc):
    length, width = x.shape
    groups, bc_width = bc.shape[1:]
    at = length // LEAD - 1
    shape = (LEAD, width + groups * bc_width)
    return pl.pallas_call(
        tail_kernel,
        grid=(1,),
        in_specs=[
            pl.BlockSpec((LEAD, width), lambda i: (at, 0)),
            pl.BlockSpec((LEAD, groups, bc_width), lambda i: (at, 0, 0)),
        ],
        out_specs=whole(shape),
        out_shape=jax.ShapeDtypeStruct(shape, BF16),
        compiler_params=params(8),
        cost_estimate=CHEAP,
        name="tail_rows",
    )(x, bc)


def put_message(ref, state, decay):
    high = decay.astype(BF16)
    low = (decay - high.astype(F32)).astype(BF16)
    rest = jnp.zeros((EXTRA - 2, state.shape[1]), BF16)
    ref[0:N, :] = state.astype(BF16)
    ref[N:, :] = jnp.concatenate([high, low, rest], 0)


def take_message(ref):
    extra = ref[N:, :].astype(F32)
    return ref[0:N, :].astype(F32), extra[0:1] + extra[1:2]


def conv_kernel(order, info, x, bc, halo, wx, wbc, f_dev, ones, rates, *refs):
    next_far, refs = refs[0], refs[1:]
    x_out, bc_out, final = refs[:3]
    xf, state, down = refs[-3:]
    length, width = x_out.shape
    rows = TOK_A
    group = info[GROUP + order]
    first_lane = pl.multiple_of(group * width, width)
    taken, sem = refs[3:5]
    first_bc = pl.multiple_of(group * 2 * N, 2 * N)
    if order == 0:
        copies = group_copies(next_far, taken, info[GROUP + 1], sem)
    else:
        part = length // 4
        pieces = [pl.ds(k * part, part) for k in range(4)]
        copies = [pltpu.make_async_copy(next_far.at[at], taken.at[at], sem.at[k]) for k, at in enumerate(pieces)]
    for copy in copies:
        copy.start()
    state[...] = jnp.zeros_like(state)
    row = lax.broadcasted_iota(jnp.int32, down.shape, 0)
    col = lax.broadcasted_iota(jnp.int32, down.shape, 1)
    down[...] = (row == col + 1).astype(BF16)

    def conv(i, src, first, behind, weights, emit):
        at_start = jnp.where(info[SEQ] == 0, jnp.zeros_like(first), first)
        lead = jnp.where(i == 0, at_start, behind).astype(F32)
        w0, w1, w2, w3 = [w * 0.5 for w in weights]
        back = LEAD - 8
        lead_r1 = pltpu.roll(lead, 1, 0)
        last_p = (w1 * lead + w0 * lead_r1)[back:]
        moved = dot(down[...], src)
        top = lax.broadcasted_iota(jnp.int32, (8, lead.shape[1]), 0) == 0
        head = jnp.where(top, jnp.broadcast_to(lead[LEAD - 1 :], top.shape), moved[0:8])
        for r in range(0, rows, ROWS_A):
            cur = src[r : r + ROWS_A].astype(F32)
            r1 = moved[r : r + ROWS_A] if r else jnp.concatenate([head, moved[8:ROWS_A]], 0)
            p = w1 * cur + w0 * r1
            p2 = pltpu.roll(jnp.concatenate([last_p, p], 0), 2, 0)[8:]
            emit(r, half_silu((w3 * cur + w2 * r1) + p2))
            last_p = p[ROWS_A - 8 :]

    def step(i, _):
        at = pl.ds(pl.multiple_of(i * rows, rows), rows)
        behind = pl.ds(pl.multiple_of(jnp.maximum(i * rows - LEAD, 0), LEAD), LEAD)

        def out(r):
            return pl.ds(pl.multiple_of(i * rows + r, ROWS_A), ROWS_A)

        for lanes in range(0, 2 * N, SLAB):
            ds = slice(lanes, lanes + SLAB)
            src = pl.ds(pl.multiple_of(first_bc + lanes, SLAB), SLAB)
            halo_src = pl.ds(pl.multiple_of(2 * width + first_bc + lanes, SLAB), SLAB)

            def emit_bc(r, value):
                bc_out[out(r), ds] = value.astype(BF16)

            weights = [jnp.where(group == 0, wbc[k, 0:1, ds], wbc[k, 1:2, ds]) for k in range(KCONV)]
            conv(i, bc[at, src], halo[:, halo_src], bc[behind, src], weights, emit_bc)

        for lanes in range(0, width, SLAB):
            ds = slice(lanes, lanes + SLAB)
            src = pl.ds(pl.multiple_of(first_lane + lanes, SLAB), SLAB)
            scale = dot(f_dev[at, :], ones[:, ds])

            def emit(r, value):
                x_out[out(r), ds] = value.astype(BF16)
                xf[r : r + ROWS_A, ds] = (value * scale[r : r + ROWS_A]).astype(BF16)

            weights = [wx[k : k + 1, ds] for k in range(KCONV)]
            conv(i, x[at, ds], halo[:, src], x[behind, ds], weights, emit)

        state[...] += dot(bc_out[at, 0:N], xf[...], ((0,), (0,)))
        return 0

    lax.fori_loop(0, length // rows, step, 0)
    if order == 0:
        row = rates.shape[0] - 16
        put_message(final, state[...], rates[row : row + 1, :])
    else:
        final[...] = state[...]
    for copy in copies:
        copy.wait()


def conv_states(order, info, x, bc, halo, wx, wbc, f_dev, ones, rates, ahead):
    length, width = x.shape
    column = lambda i, info: (0, info[GROUP + order])
    final = ((N + EXTRA, width), BF16) if order == 0 else ((N, width), F32)
    taken = (length, width) if order == 0 else ahead.shape
    return pl.pallas_call(
        functools.partial(conv_kernel, order),
        grid_spec=pltpu.PrefetchScalarGridSpec(
            num_scalar_prefetch=1,
            grid=(1,),
            in_specs=[FULL] * 3 + [pl.BlockSpec((KCONV, width), column)] + [FULL] * 4 + [FAR],
            out_specs=[FULL] * 4,
            scratch_shapes=[
                pltpu.SemaphoreType.DMA((4,)),
                pltpu.VMEM((TOK_A, width), BF16),
                pltpu.VMEM((N, width), F32),
                pltpu.VMEM((TOK_A, TOK_A), BF16),
            ],
        ),
        out_shape=[
            pltpu.VMEM((length, width), BF16),
            pltpu.VMEM((length, 2 * N), BF16),
            jax.ShapeDtypeStruct(*final),
            pltpu.VMEM(taken, BF16),
        ],
        compiler_params=params(16),
        cost_estimate=CHEAP,
        name="conv_states",
    )(info, x, bc, halo, wx, wbc, f_dev, ones, rates, ahead)


def pair_kernel(info, got, keep, rates, _, msg, own, first, aux):
    half = keep.shape[1]
    is_odd = info[ODD] == 1
    arrived, their = take_message(got)
    row = rates.shape[0] - 16
    mine = rates[row : row + 1, :]
    early = jnp.where(is_odd, arrived, keep[...])
    late = jnp.where(is_odd, keep[...], arrived)
    even_decay = jnp.where(is_odd, their, mine)
    odd_decay = jnp.where(is_odd, mine, their)
    state = odd_decay * early + late
    own[...] = state
    first[...] = early
    aux[0:8, :] = jnp.broadcast_to(even_decay, (8, half))
    aux[8:16, :] = jnp.broadcast_to(even_decay * odd_decay, (8, half))
    put_message(msg, state, even_decay * odd_decay)


def wave_kernel(got, own, aux, behind_in, _, msg, behind):
    before, decay = take_message(got)
    if behind_in is not None:
        before_decay = behind_in[N : N + 1, :]
        before = behind_in[0:N, :] + before_decay * before
        decay = before_decay * decay
    pair_decay = aux[8:9, :]
    behind[0:N, :] = before
    behind[N:, :] = jnp.broadcast_to(decay, (8, before.shape[1]))
    put_message(msg, own[...] + pair_decay * before, pair_decay * decay)


def last_kernel(info, got, behind_in, first, aux, _, back, held):
    is_odd = info[ODD] == 1
    before, _unused = take_message(got)
    if behind_in is not None:
        before = behind_in[0:N, :] + behind_in[N : N + 1, :] * before
    entering_odd = aux[0:1, :] * before + first[...]
    back[...] = jnp.where(is_odd, before, entering_odd).astype(BF16)
    held[...] = jnp.where(is_odd, entering_odd, before).astype(BF16)


def pair_split_kernel(info, got, keep, rates, _, first, aux, *refs):
    outs, wide = refs[:-1], refs[-1]
    half = keep.shape[1]
    pairs = len(outs)
    piece = half // pairs
    is_odd = info[ODD] == 1
    arrived, their = take_message(got)
    row = rates.shape[0] - 16
    mine = rates[row : row + 1, :]
    early = jnp.where(is_odd, arrived, keep[...])
    late = jnp.where(is_odd, keep[...], arrived)
    even_decay = jnp.where(is_odd, their, mine)
    odd_decay = jnp.where(is_odd, mine, their)
    first[...] = early
    aux[...] = jnp.broadcast_to(even_decay, (8, half))
    put_message(wide, odd_decay * early + late, even_decay * odd_decay)
    for r in range(pairs):
        owner = lax.rem(info[PAIR] + r, pairs)
        outs[r][...] = wide[:, pl.ds(pl.multiple_of(owner * piece, piece), piece)]


def owner_kernel(info, *refs):
    pairs = (len(refs) - 3) // 2
    ins, outs = refs[:pairs], refs[pairs + 1 : 2 * pairs + 1]
    states, prefixes = refs[-2:]
    for r in range(pairs):
        states[lax.rem(info[PAIR] + pairs - r, pairs)] = ins[r][...]
    before = jnp.zeros(prefixes.shape[1:], F32)
    for q in range(pairs):
        prefixes[q] = before.astype(BF16)
        if q < pairs - 1:
            state, decay = take_message(states.at[q])
            before = decay * before + state
    for r in range(pairs):
        outs[r][...] = prefixes[lax.rem(info[PAIR] + r, pairs)]


def last_split_kernel(info, first, aux, _, *refs):
    pairs = len(refs) - 3
    back, held, wide = refs[-3:]
    piece = back.shape[1] // pairs
    for r in range(pairs):
        owner = lax.rem(info[PAIR] + pairs - r, pairs)
        wide[:, pl.ds(pl.multiple_of(owner * piece, piece), piece)] = refs[r][...]
    is_odd = info[ODD] == 1
    before = wide[...].astype(F32)
    entering_odd = aux[0:1, :] * before + first[...]
    back[...] = jnp.where(is_odd, before, entering_odd).astype(BF16)
    held[...] = jnp.where(is_odd, entering_odd, before).astype(BF16)


def combine(kernel, operands, specs, outs, name, scratch=()):
    return pl.pallas_call(
        kernel,
        in_specs=specs,
        out_specs=[FULL] * len(outs),
        out_shape=[jax.ShapeDtypeStruct(s, t) for s, t in outs],
        scratch_shapes=list(scratch),
        compiler_params=params(16),
        cost_estimate=CHEAP,
        name=name,
    )(*operands)


def scan_kernel(order, part, info, x, z, bc, cum, cum_s, log_s, f_blk, e_blk, rates, ones, wide_ones, _, uv_out, state):
    length = x.shape[0]
    width = state.shape[1]
    per_slab = SLAB // P_SIZE
    inner = STEP_B // TOK_B
    blocks = length // TOK_B
    first_head = part * width // P_SIZE
    first_lane = info[GROUP + order] * x.shape[1] + part * width
    state[...] = jnp.zeros_like(state)

    row = lax.broadcasted_iota(jnp.int32, (TOK_B, TOK_B), 0)
    col = lax.broadcasted_iota(jnp.int32, (TOK_B, TOK_B), 1)
    keep = row >= col
    first = lax.broadcasted_iota(jnp.int32, (TOK_B, 2 * P_SIZE), 1) < P_SIZE
    zero = jnp.zeros((TOK_B, 2 * P_SIZE), BF16)

    def turn(step, _):
        for k in range(inner):
            block(step * inner + k)
        return 0

    def block(b):
        at = pl.ds(pl.multiple_of(b * TOK_B, TOK_B), TOK_B)
        b_mat = bc[at, 0:N]
        c_mat = bc[at, N : 2 * N]
        b_across = b_mat.T
        scores = jnp.where(keep, dot(c_mat, b_mat, ((1,), (1,))), 0.0)
        for s in range(width // SLAB):
            lanes = slice(s * SLAB, (s + 1) * SLAB)
            xb = x[at, part * width + s * SLAB : part * width + (s + 1) * SLAB]
            wide = slice(part * width + s * SLAB, part * width + (s + 1) * SLAB)
            sel = ones[:, wide]
            fade_row = rates[pl.ds(b, 1), wide]
            lead_row = rates[pl.ds(blocks + b, 1), wide]
            skip = rates[2 * blocks + 8 : 2 * blocks + 9, wide]
            old = state[:, lanes]
            rise = dot(e_blk[at, :], sel)
            carried = dot(c_mat, old.astype(BF16)) * rise
            first_column = (first_head + s * per_slab) * TOK_B
            columns = dot(cum[at, :], wide_ones[:, first_column : first_column + per_slab * TOK_B])
            within = []
            for q in range(per_slab // 2):
                tables = []
                for h in (2 * q, 2 * q + 1):
                    head = first_head + s * per_slab + h
                    column = columns[:, h * TOK_B : (h + 1) * TOK_B]
                    own = slice(head, head + 1)
                    gap = jnp.minimum(column - cum_s[own, at], log_s[own, at])
                    tables.append((scores * jnp.exp2(gap)).astype(BF16))
                xp = xb[:, q * 2 * P_SIZE : (q + 1) * 2 * P_SIZE]
                stacked = jnp.concatenate([jnp.where(first, xp, zero), jnp.where(first, zero, xp)], 0)
                within.append(dot(jnp.concatenate(tables, 1), stacked))
            xs = xb.astype(F32)
            y = jnp.concatenate(within, 1) + carried + skip * xs
            gate = half_silu((z[at, pl.ds(pl.multiple_of(first_lane + s * SLAB, SLAB), SLAB)] * 0.5).astype(F32))
            uv_out[at, lanes] = (y * gate).astype(BF16)
            uv_out[at, width + s * SLAB : width + (s + 1) * SLAB] = (gate * rise * lead_row).astype(BF16)
            xf = (xs * dot(f_blk[at, :], sel)).astype(BF16)
            state[:, lanes] = old * fade_row + dot(b_across, xf)

    lax.fori_loop(0, length // STEP_B, turn, 0)


def scan_part(order, part, info, token, x, z, bc, cum, cum_s, log_s, f_blk, e_blk, rates, ones, wide_ones):
    length, full = x.shape
    width = full // B_PARTS
    return pl.pallas_call(
        functools.partial(scan_kernel, order, part),
        in_specs=[SCALAR] + [FULL] * 11 + [ANY],
        out_specs=FULL,
        out_shape=pltpu.VMEM((length, 2 * width), BF16),
        scratch_shapes=[pltpu.VMEM((N, width), F32)],
        compiler_params=params(12),
        cost_estimate=CHEAP,
        name="scan_part",
    )(info, x, z, bc, cum, cum_s, log_s, f_blk, e_blk, rates, ones, wide_ones, token)


def norm_kernel(places, fetched, info, bc0, bc1, state0, state1, gain, _, *refs):
    uvs, refs = refs[: 2 * B_PARTS], refs[2 * B_PARTS :]
    weights, outs, tiles, sem = refs[:fetched], refs[fetched : -1 - fetched], refs[len(refs) - 1 - fetched : -1], refs[-1]
    copies = [
        pltpu.make_async_copy(weight.at[:, pl.ds(0, tile.shape[1])], tile, sem.at[k])
        for k, (weight, tile) in enumerate(zip(weights, tiles))
    ]
    for copy in copies:
        copy.start()
    count = outs[0].shape[0] * len(outs) // len(places)
    per = state0.shape[1]
    part = per // B_PARTS

    def rows(out, first, base):
        to = pl.ds(pl.multiple_of(first, ROWS_C), ROWS_C)
        at = pl.ds(pl.multiple_of(base, ROWS_C), ROWS_C)
        for order, (bc, state) in enumerate(((bc0, state0), (bc1, state1))):
            c_mat = bc[at, N : 2 * N]
            pieces = []
            squares = None
            for p in range(B_PARTS):
                uv = uvs[order * B_PARTS + p]
                inc = state[:, p * part : (p + 1) * part]
                gated = uv[at, 0:part].astype(F32) + uv[at, part:].astype(F32) * dot(c_mat, inc)
                square = jnp.sum(gated * gated, axis=-1, keepdims=True)
                squares = square if squares is None else squares + square
                pieces.append(gated)
            scale = lax.rsqrt(squares * (1.0 / per) + EPS)
            for p, gated in enumerate(pieces):
                lanes = pl.ds(pl.multiple_of(info[GROUP + order] * per + p * part, part), part)
                out[to, lanes] = (gated * scale * gain[:, lanes]).astype(BF16)

    for k, place in enumerate(places):

        def step(j, _):
            out, first = (outs[k], 0) if len(outs) > 1 else (outs[0], k * count)
            rows(out, first + j * ROWS_C, info[ROWS + place] * count + j * ROWS_C)
            return 0

        lax.fori_loop(0, count // ROWS_C, step, 0)
    for copy in copies:
        copy.wait()


def norm_rows(places, apart, info, count, token, bcs, states, gain, uvs, weights=(), columns=0):
    tile = jax.ShapeDtypeStruct((gain.shape[1], columns), BF16)
    arrays = len(places) if apart else 1
    rows = jax.ShapeDtypeStruct((len(places) * count // arrays, gain.shape[1]), BF16)
    return pl.pallas_call(
        functools.partial(norm_kernel, places, len(weights)),
        in_specs=[SCALAR] + [FULL] * 5 + [ANY] + [FULL] * len(uvs) + [FAR] * len(weights),
        out_specs=[FULL] * (arrays + len(weights)),
        out_shape=[rows] * arrays + [tile] * len(weights),
        scratch_shapes=[pltpu.SemaphoreType.DMA((2,))],
        compiler_params=params(16),
        cost_estimate=CHEAP,
        name="norm_rows",
    )(info, *bcs, *states, gain, token, *uvs, *weights)


def stream(base, w0_far, w1_far, w0, w1, sem):
    j = pl.program_id(0)
    tiles = pl.num_programs(0)

    def fetch(t):
        slot = lax.rem(t, SLOTS)
        lanes = pl.ds(pl.multiple_of((base + t) * TILE, TILE), TILE)
        return (
            pltpu.make_async_copy(w0_far.at[:, lanes], w0.at[slot], sem.at[0, slot]),
            pltpu.make_async_copy(w1_far.at[:, lanes], w1.at[slot], sem.at[1, slot]),
        )

    def start(t):
        @pl.when(t < tiles)
        def _():
            for copy in fetch(t):
                copy.start()

    @pl.when(j == 0)
    def _():
        for t in range(SLOTS - 1):
            start(t)

    start(j + SLOTS - 1)
    for copy in fetch(j):
        copy.wait()
    return lax.rem(j, SLOTS)


def buffers(depth):
    return [
        pltpu.VMEM((SLOTS, depth, TILE), BF16),
        pltpu.VMEM((SLOTS, depth, TILE), BF16),
        pltpu.SemaphoreType.DMA((2, SLOTS)),
    ]


def ahead_kernel(owns, mate, w0, w1, out):
    out[...] = (dot(owns[0 : out.shape[0], :], w0[...]) + dot(mate[...], w1[...])).astype(BF16)


def project_ahead(owns, mate, w0, w1):
    return pl.pallas_call(
        ahead_kernel,
        in_specs=[FULL] * 4,
        out_specs=FULL,
        out_shape=jax.ShapeDtypeStruct((owns.shape[0] // 2, w0.shape[1]), BF16),
        compiler_params=params(16),
        cost_estimate=CHEAP,
        name="project_ahead",
    )(owns, mate, w0, w1)


def join_kernel(first, second, _, out):
    rows = first.shape[0]
    out[0:rows, :] = first[...]
    out[rows:, :] = second[...]


def join(first, second, token):
    rows, depth = first.shape
    return pl.pallas_call(
        join_kernel,
        in_specs=[FULL, FULL, ANY],
        out_specs=FULL,
        out_shape=jax.ShapeDtypeStruct((2 * rows, depth), BF16),
        compiler_params=params(8),
        cost_estimate=CHEAP,
        name="join",
    )(first, second, token)


def both_kernel(base, cut, owns, mates, w0_far, w1_far, *refs):
    fars, near, w0, w1, sem = refs[:-4], *refs[-4:]
    rows = near.shape[0]
    slot = stream(base, w0_far, w1_far, w0, w1, sem)
    total = dot(owns[...], w0[slot]) + dot(mates[...], w1[slot])
    near[...] = total[rows:]
    for k, far_out in enumerate(fars):

        @pl.when(pl.program_id(0) // cut == k)
        def _():
            far_out[...] = total[0:rows].astype(BF16)


def project_both(owns, mates, w0, w1, first, count, chunk):
    rows, depth = owns.shape[0] // 2, owns.shape[1]
    cut = chunk // TILE
    chunks = count // chunk

    def placed(k):
        return pl.BlockSpec((rows, TILE), lambda j: (0, jnp.clip(j - k * cut, 0, cut - 1)))

    *fars, near = pl.pallas_call(
        functools.partial(both_kernel, first // TILE, cut),
        grid=(count // TILE,),
        in_specs=[FULL] * 2 + [FAR] * 2,
        out_specs=[placed(k) for k in range(chunks)] + [pl.BlockSpec((rows, TILE), lambda j: (0, j))],
        out_shape=[jax.ShapeDtypeStruct((rows, chunk), BF16)] * chunks + [jax.ShapeDtypeStruct((rows, count), F32)],
        scratch_shapes=buffers(depth),
        compiler_params=params(24),
        cost_estimate=CHEAP,
        name="project_both",
    )(owns, mates, w0, w1)
    return fars, near


def near_kernel(owns, mates, w0_far, w1_far, arrived, out, w0, w1, sem):
    slot = stream(0, w0_far, w1_far, w0, w1, sem)
    rows = out.shape[0]
    total = dot(owns[rows:, :], w0[slot]) + dot(mates[rows:, :], w1[slot])
    out[...] = (total + arrived[...].astype(F32)).astype(BF16)


def project_near(owns, mates, w0, w1, arrived):
    rows, depth = owns.shape[0] // 2, owns.shape[1]
    placed = pl.BlockSpec((rows, TILE), lambda j: (0, j))
    return pl.pallas_call(
        near_kernel,
        grid=(arrived.shape[1] // TILE,),
        in_specs=[FULL, FULL, FAR, FAR, placed],
        out_specs=placed,
        out_shape=jax.ShapeDtypeStruct((rows, w0.shape[1]), BF16),
        scratch_shapes=buffers(depth),
        compiler_params=params(20),
        cost_estimate=CHEAP,
        name="project_near",
    )(owns, mates, w0, w1, arrived)


def add_kernel(near, *refs):
    arrived, out = refs[:-2], refs[-1]
    chunk = arrived[0].shape[1]
    for k, part in enumerate(arrived):
        lanes = slice(k * chunk, (k + 1) * chunk)
        out[:, lanes] = (near[:, lanes] + part[...].astype(F32)).astype(BF16)


def add_chunks(near, first, arrived, result, at):
    rows, chunk = arrived[0].shape
    count = chunk * len(arrived)
    return pl.pallas_call(
        add_kernel,
        grid=(1,),
        in_specs=[pl.BlockSpec((rows, count), lambda j: (0, first // count))] + [FULL] * len(arrived) + [ANY],
        out_specs=pl.BlockSpec((rows, count), lambda j: (0, at // count)),
        out_shape=jax.ShapeDtypeStruct(result.shape, BF16),
        input_output_aliases={1 + len(arrived): 0},
        compiler_params=params(8),
        cost_estimate=CHEAP,
        name="add_chunks",
    )(near, *arrived, result)


def shift(block, distance):
    size = lax.axis_size("seq")
    return lax.ppermute(block, "seq", [(i, i + distance) for i in range(size - distance)])


def swap(block, axis, bit):
    return lax.ppermute(block, axis, [(i, i ^ bit) for i in range(lax.axis_size(axis))])


def rotate(block, distance):
    size = lax.axis_size("seq")
    return lax.ppermute(block, "seq", [(i, (i + distance) % size) for i in range(size)])


def log_steps(info, got, keep, rates_kept, done, pairs, scan_next):
    half = keep.shape[1]
    message = ((N + EXTRA, half), BF16)
    full = ((N, half), F32)
    msg, own, first, aux = combine(
        pair_kernel,
        (info, got, keep, rates_kept, done),
        [SCALAR, FULL, FULL, FULL, ANY],
        [message, full, full, ((16, half), F32)],
        "pair",
    )
    behind = None
    covered = 0
    while True:
        got = shift(msg, 2 * (covered + 1))
        done = scan_next(msg)
        covered = 2 * covered + 1
        if covered >= pairs - 1:
            break
        operands, specs = [got, own, aux], [FULL, FULL, FULL]
        if behind is None:
            kernel = lambda g, o, a, t, m, b: wave_kernel(g, o, a, None, t, m, b)
        else:
            kernel = wave_kernel
            operands.append(behind)
            specs.append(FULL)
        msg, behind = combine(kernel, operands + [done], specs + [ANY], [message, ((N + 8, half), F32)], "wave")
    operands, specs = [info, got], [SCALAR, FULL]
    if behind is None:
        kernel = lambda o, g, f, a, t, b, h: last_kernel(o, g, None, f, a, t, b, h)
    else:
        kernel = last_kernel
        operands.append(behind)
        specs.append(FULL)
    out = ((N, half), BF16)
    back, held = combine(kernel, operands + [first, aux, done], specs + [FULL, FULL, ANY], [out, out], "last")
    return back, held


def local(
    x_input,
    z_input,
    bc_input,
    conv_weight_x,
    conv_weight_bc,
    step_size,
    log_decay,
    skip_gain,
    norm_gain,
    out_weight,
):
    length, width = x_input.shape
    heads = step_size.shape[1]
    ways = lax.axis_size("head")
    pairs = lax.axis_size("seq") // 2
    mine = lax.axis_index("head")
    half = width // 2
    seq = lax.axis_index("seq")
    info = jnp.stack([seq & 1, mine ^ 3, mine ^ 2, mine ^ 1, mine, seq >> 1, seq, 1 - (seq & 1), seq & 1]).astype(jnp.int32)

    x_far, z_far, w_far = far(x_input, z_input, out_weight)
    (bc_far,) = far(bc_input)
    halo = rotate(tail_rows(x_far, bc_far), 1)
    bc = bc_input.reshape(length, -1)
    (weight_mate,) = far(swap(out_weight, "head", 1))

    (cum, cum_s, log_s, f_dev, f_blk, e_blk, rates), ones, wide_ones, x_sent = decays(
        info, log_decay, step_size, skip_gain, x_input, half
    )
    taps = far(conv_weight_x, conv_weight_bc)
    shared = (bc, halo, *taps)
    x0, bc0, send, x_kept = conv_states(0, info, x_sent, *shared, f_dev[0], ones, rates[0], x_far)
    got = swap(send, "seq", 1)
    x1, bc1, keep, z_near = conv_states(1, info, x_kept, *shared, f_dev[1], ones, rates[1], z_far)
    rates_kept = rates[1]

    uvs = []
    groups = [(x, z_near, *rest, ones, wide_ones) for x, *rest in zip((x0, x1), (bc0, bc1), cum, cum_s, log_s, f_blk, e_blk, rates)]

    def scan_next(token):
        if len(uvs) < 2 * B_PARTS:
            order, part = divmod(len(uvs), B_PARTS)
            uvs.append(scan_part(order, part, info, token, *groups[order]))
        return uvs[-1]

    full = ((N, half), F32)
    message = ((N + EXTRA, half), BF16)
    done = scan_next(keep)
    out = ((N, half), BF16)
    if pairs > 1 and half % (pairs * N) == 0:
        piece = half // pairs
        part = ((N + EXTRA, piece), BF16)
        first, aux, *parts = combine(
            pair_split_kernel,
            (info, got, keep, rates_kept, done),
            [SCALAR, FULL, FULL, FULL, ANY],
            [full, ((8, half), F32)] + [part] * pairs,
            "pair",
            [pltpu.VMEM(*message)],
        )
        parts = list(parts[:1]) + [rotate(parts[r], 2 * r) for r in range(1, pairs)]
        done = scan_next(parts[0])
        parts = combine(
            owner_kernel,
            [info] + parts + [done],
            [SCALAR] + [FULL] * pairs + [ANY],
            [((N, piece), BF16)] * pairs,
            "owner",
            [pltpu.VMEM((pairs, N + EXTRA, piece), BF16), pltpu.VMEM((pairs, N, piece), BF16)],
        )
        ready = parts[0]
        parts = list(parts[:1]) + [rotate(parts[r], 2 * r) for r in range(1, pairs)]
        done = scan_next(ready)
        back, held = combine(
            last_split_kernel,
            [info, first, aux, done] + parts,
            [SCALAR, FULL, FULL, ANY] + [FULL] * pairs,
            [out, out],
            "last",
            [pltpu.VMEM(*out)],
        )
    else:
        back, held = log_steps(info, got, keep, rates_kept, done, pairs, scan_next)
    other = swap(back, "seq", 1)
    while len(uvs) < 2 * B_PARTS:
        scan_next(back)

    count = length // ways
    gain = norm_gain[None, :]

    columns = out_weight.shape[1]
    chunk = columns // 8
    weights = (w_far, weight_mate)
    shared = ((bc0, bc1), (other, held), gain, uvs)
    far_mate, near_mate = norm_rows((0, 2), True, info, count, held, *shared)
    owns, w0, w1 = norm_rows((1, 3), False, info, count, far_mate, *shared, weights, chunk)
    far_mate = swap(far_mate, "head", 1)
    sent = project_ahead(owns, far_mate, w0, w1)
    first = swap(sent, "head", 2)
    operands = (owns, join(far_mate, swap(near_mate, "head", 1), sent), *weights)
    calls = []
    for lo, hi in ((1, 2), (2, 4), (4, 6), (6, 8)):
        sent, near = project_both(*operands, lo * chunk, (hi - lo) * chunk, chunk)
        calls.append((near, lo, [swap(part, "head", 2) for part in sent]))
    result = project_near(*operands, first)
    for near, lo, arrived in calls[:-1]:
        result = add_chunks(near, 0, arrived, result, lo * chunk)
    near, lo, arrived = calls[-1]
    for k, part in enumerate(arrived):
        result = add_chunks(near, k * chunk, [part], result, (lo + k) * chunk)
    return result


def solution(mesh):
    in_specs = (
        P("seq", "head"),
        P("seq", "head"),
        P("seq", "head", None),
        P(None, "head"),
        P(None, "head", None),
        P("seq", "head"),
        P("seq", "head"),
        P("head"),
        P("head"),
        P("head", None),
    )
    out_specs = P(("seq", "head"), None)
    return jax.shard_map(local, mesh=mesh, in_specs=in_specs, out_specs=out_specs, check_vma=False)
```

```python
import functools

import jax
import jax.numpy as jnp
from jax import lax
from jax.experimental import pallas as pl
from jax.experimental.pallas import tpu as pltpu
from jax.sharding import PartitionSpec as P

P_SIZE = 64
N = 128
KCONV = 4
EPS = 1e-05
LOG2E = 1.4426950408889634

TOK_A = 256
ROWS_A = 32
TOK_B = 128
STEP_B = 256
EXTRA = 16
SLAB = 256
ROWS_C = 128
TILE = 256
SLOTS = 4
LEAD = 16
B_PARTS = 2
HIGHEST = lax.Precision.HIGHEST
F32 = jnp.float32
BF16 = jnp.bfloat16


def params(mib):
    return pltpu.CompilerParams(vmem_limit_bytes=mib * 1024 * 1024)


CHEAP = pl.CostEstimate(flops=1, bytes_accessed=1, transcendentals=0)
SCALAR = pl.BlockSpec(memory_space=pltpu.SMEM)
FULL = pl.BlockSpec(memory_space=pltpu.VMEM)
FAR = pl.BlockSpec(memory_space=pltpu.HBM)
ANY = pl.BlockSpec(memory_space=pl.ANY)

ODD, ROWS, PAIR, SEQ, GROUP = 0, 1, 5, 6, 7


def dot(a, b, dims=((1,), (0,)), precision=None):
    return lax.dot_general(a, b, (dims, ((), ())), precision=precision, preferred_element_type=F32)


def half_silu(half):
    return half + half * jnp.tanh(half)


def far(*arrays):
    return [pltpu.with_memory_space_constraint(a, pltpu.HBM) for a in arrays]


def whole(shape):
    return pl.BlockSpec(shape, lambda *_: (0,) * len(shape))


def group_copies(x_far, x, group, sems):
    length, width = x.shape
    rows = length // 4
    lanes = pl.ds(pl.multiple_of(group * width, width), width)
    pieces = [pl.ds(k * rows, rows) for k in range(4)]
    return [pltpu.make_async_copy(x_far.at[at, lanes], x.at[at], sems.at[k]) for k, at in enumerate(pieces)]


def decay_kernel(info, ld_t, step_t, skip, x_far, *refs):
    cum, cum_s, log_s, f_dev, f_blk, rates = [refs[2 * k : 2 * k + 2] for k in range(6)]
    ones, x, sem = refs[12:]
    copies = group_copies(x_far, x, info[GROUP], sem)
    for copy in copies:
        copy.start()
    heads, length = ld_t.shape
    blocks = length // TOK_B
    per = heads // 2
    width = ones.shape[1]
    swapped = info[GROUP] == 1
    row = lax.broadcasted_iota(jnp.int32, (TOK_B, TOK_B), 0)
    col = lax.broadcasted_iota(jnp.int32, (TOK_B, TOK_B), 1)
    lower = (row >= col).astype(F32)
    upper = (row <= col).astype(F32)
    eye = (row == col).astype(BF16)

    def ordered(value):
        return jnp.where(swapped, jnp.concatenate([value[per:], value[:per]], 0), value)

    def put(ref, rows, value):
        high = value.astype(BF16)
        low = (value - high.astype(F32)).astype(BF16)
        for g in range(2):
            own = slice(g * per, (g + 1) * per)
            both = jnp.concatenate([high[own], low[own]], 0)
            ref[g][rows, :] = dot(eye, both, ((1,), (1,))).astype(BF16)

    first = lax.broadcasted_iota(jnp.int32, (per, width), 0) * P_SIZE
    lane = lax.broadcasted_iota(jnp.int32, (per, width), 1)
    member = ((lane >= first) & (lane < first + P_SIZE)).astype(F32)
    ones[0:per, :] = member.astype(BF16)
    ones[per:, :] = member.astype(BF16)
    cums, totals, row_totals = [], [], []
    for b in range(blocks):
        rows = slice(b * TOK_B, (b + 1) * TOK_B)
        logs = ordered(ld_t[:, rows]) * LOG2E
        c = dot(lower, logs, ((1,), (1,)), HIGHEST)
        for g in range(2):
            cum[g][rows, :] = c[:, g * per : (g + 1) * per]
        row_totals.append(c[TOK_B - 1 : TOK_B, :])
        c = dot(logs, upper, precision=HIGHEST)
        cums.append(c)
        totals.append(c[:, TOK_B - 1 : TOK_B])
    before, row_before = [jnp.zeros_like(totals[0])], [jnp.zeros_like(row_totals[0])]
    for b in range(blocks):
        before.append(before[-1] + totals[b])
        row_before.append(row_before[-1] + row_totals[b])
    total = before[-1]
    logs = jnp.concatenate(row_totals + row_before[:-1] + row_before[-1:] * 8, 0)
    gains = jnp.broadcast_to(skip[...], (8, heads))
    gains = jnp.where(swapped, jnp.concatenate([gains[:, per:], gains[:, :per]], 1), gains)
    values = jnp.concatenate([jnp.exp2(logs), gains], 0)
    for g in range(2):
        rates[g][...] = dot(values[:, g * per : (g + 1) * per], member, precision=HIGHEST)
    for b in range(blocks):
        rows = slice(b * TOK_B, (b + 1) * TOK_B)
        s = ordered(step_t[:, rows])
        log_step = jnp.log2(s)
        shifted = cums[b] - log_step
        fade = jnp.exp2(totals[b] - cums[b]) * s
        for g in range(2):
            own = slice(g * per, (g + 1) * per)
            log_s[g][:, rows] = log_step[own, :]
            cum_s[g][:, rows] = shifted[own, :]
            f_blk[g][:, rows] = fade[own, :]
        put(f_dev, rows, jnp.exp2(total - (cums[b] + before[b])) * s)
    for copy in copies:
        copy.wait()


def decays(info, log_decay, step, skip, x, width):
    length, heads = log_decay.shape
    blocks = length // TOK_B
    per = heads // 2
    across = jax.ShapeDtypeStruct((per, length), F32)
    pair = jax.ShapeDtypeStruct((length, 2 * per), BF16)
    column = jax.ShapeDtypeStruct((length, per), F32)
    rates = jax.ShapeDtypeStruct((2 * blocks + 16, width), F32)
    shapes = [shape for shape in (column, across, across, pair, across, rates) for _ in range(2)]
    shapes += [
        jax.ShapeDtypeStruct((2 * per, width), BF16),
        pltpu.VMEM((length, width), BF16),
    ]
    *refs, ones, x_near = pl.pallas_call(
        decay_kernel,
        in_specs=[SCALAR] + [FULL] * 3 + [FAR],
        out_specs=[FULL] * len(shapes),
        out_shape=shapes,
        scratch_shapes=[pltpu.SemaphoreType.DMA((4,))],
        compiler_params=params(16),
        cost_estimate=CHEAP,
        name="decays",
    )(info, *far(log_decay.T, step.T, skip[None, :], x))
    return [tuple(refs[2 * k : 2 * k + 2]) for k in range(6)], ones, x_near


def tail_kernel(x, bc, out):
    width, bc_width = x.shape[1], bc.shape[2]
    out[:, 0:width] = x[...]
    for g in range(bc.shape[1]):
        out[:, width + g * bc_width : width + (g + 1) * bc_width] = bc[:, g, :]


def tail_rows(x, bc):
    length, width = x.shape
    groups, bc_width = bc.shape[1:]
    at = length // LEAD - 1
    shape = (LEAD, width + groups * bc_width)
    return pl.pallas_call(
        tail_kernel,
        grid=(1,),
        in_specs=[
            pl.BlockSpec((LEAD, width), lambda i: (at, 0)),
            pl.BlockSpec((LEAD, groups, bc_width), lambda i: (at, 0, 0)),
        ],
        out_specs=whole(shape),
        out_shape=jax.ShapeDtypeStruct(shape, BF16),
        compiler_params=params(8),
        cost_estimate=CHEAP,
        name="tail_rows",
    )(x, bc)


def put_message(ref, state, decay):
    high = decay.astype(BF16)
    low = (decay - high.astype(F32)).astype(BF16)
    rest = jnp.zeros((EXTRA - 2, state.shape[1]), BF16)
    ref[0:N, :] = state.astype(BF16)
    ref[N:, :] = jnp.concatenate([high, low, rest], 0)


def take_message(ref):
    extra = ref[N:, :].astype(F32)
    return ref[0:N, :].astype(F32), extra[0:1] + extra[1:2]


def conv_kernel(order, info, x, bc, halo, wx, wbc, f_dev, ones, rates, *refs):
    next_far, refs = refs[0], refs[1:]
    x_out, bc_out, final = refs[:3]
    xf, state, down = refs[-3:]
    length, width = x_out.shape
    rows = TOK_A
    group = info[GROUP + order]
    first_lane = pl.multiple_of(group * width, width)
    taken, sem = refs[3:5]
    first_bc = pl.multiple_of(group * 2 * N, 2 * N)
    if order == 0:
        copies = group_copies(next_far, taken, info[GROUP + 1], sem)
    else:
        part = length // 4
        pieces = [pl.ds(k * part, part) for k in range(4)]
        copies = [pltpu.make_async_copy(next_far.at[at], taken.at[at], sem.at[k]) for k, at in enumerate(pieces)]
    for copy in copies:
        copy.start()
    state[...] = jnp.zeros_like(state)
    row = lax.broadcasted_iota(jnp.int32, down.shape, 0)
    col = lax.broadcasted_iota(jnp.int32, down.shape, 1)
    down[...] = (row == col + 1).astype(BF16)

    def conv(i, src, moved, first, behind, weights, emit):
        at_start = jnp.where(info[SEQ] == 0, jnp.zeros_like(first), first)
        lead = jnp.where(i == 0, at_start, behind).astype(F32)
        w0, w1, w2, w3 = [w * 0.5 for w in weights]
        back = LEAD - 8
        lead_r1 = pltpu.roll(lead, 1, 0)
        last_p = (w1 * lead + w0 * lead_r1)[back:]
        top = lax.broadcasted_iota(jnp.int32, (8, lead.shape[1]), 0) == 0
        head = jnp.where(top, jnp.broadcast_to(lead[LEAD - 1 :], top.shape), moved[0:8])
        for r in range(0, rows, ROWS_A):
            cur = src[r : r + ROWS_A].astype(F32)
            r1 = moved[r : r + ROWS_A] if r else jnp.concatenate([head, moved[8:ROWS_A]], 0)
            p = w1 * cur + w0 * r1
            p2 = pltpu.roll(jnp.concatenate([last_p, p], 0), 2, 0)[8:]
            emit(r, half_silu((w3 * cur + w2 * r1) + p2))
            last_p = p[ROWS_A - 8 :]

    def step(i, _):
        at = pl.ds(pl.multiple_of(i * rows, rows), rows)
        behind = pl.ds(pl.multiple_of(jnp.maximum(i * rows - LEAD, 0), LEAD), LEAD)

        def out(r):
            return pl.ds(pl.multiple_of(i * rows + r, ROWS_A), ROWS_A)

        for lanes in range(0, 2 * N, SLAB):
            ds = slice(lanes, lanes + SLAB)
            src = pl.ds(pl.multiple_of(first_bc + lanes, SLAB), SLAB)
            halo_src = pl.ds(pl.multiple_of(2 * width + first_bc + lanes, SLAB), SLAB)

            def emit_bc(r, value):
                bc_out[out(r), ds] = value.astype(BF16)

            weights = [jnp.where(group == 0, wbc[k, 0:1, ds], wbc[k, 1:2, ds]) for k in range(KCONV)]
            conv(i, bc[at, src], dot(down[...], bc[at, src]), halo[:, halo_src], bc[behind, src], weights, emit_bc)

        all_moved = dot(down[...], x[at, :])
        all_scale = dot(f_dev[at, :], ones[...])
        for lanes in range(0, width, SLAB):
            ds = slice(lanes, lanes + SLAB)
            src = pl.ds(pl.multiple_of(first_lane + lanes, SLAB), SLAB)
            scale = all_scale[:, ds]

            def emit(r, value):
                x_out[out(r), ds] = value.astype(BF16)
                xf[r : r + ROWS_A, ds] = (value * scale[r : r + ROWS_A]).astype(BF16)

            weights = [wx[k : k + 1, ds] for k in range(KCONV)]
            conv(i, x[at, ds], all_moved[:, ds], halo[:, src], x[behind, ds], weights, emit)

        state[...] += dot(bc_out[at, 0:N], xf[...], ((0,), (0,)))
        return 0

    lax.fori_loop(0, length // rows, step, 0)
    if order == 0:
        row = rates.shape[0] - 16
        put_message(final, state[...], rates[row : row + 1, :])
    else:
        final[...] = state[...]
    for copy in copies:
        copy.wait()


def conv_states(order, info, x, bc, halo, wx, wbc, f_dev, ones, rates, ahead):
    length, width = x.shape
    column = lambda i, info: (0, info[GROUP + order])
    final = ((N + EXTRA, width), BF16) if order == 0 else ((N, width), F32)
    taken = (length, width) if order == 0 else ahead.shape
    return pl.pallas_call(
        functools.partial(conv_kernel, order),
        grid_spec=pltpu.PrefetchScalarGridSpec(
            num_scalar_prefetch=1,
            grid=(1,),
            in_specs=[FULL] * 3 + [pl.BlockSpec((KCONV, width), column)] + [FULL] * 4 + [FAR],
            out_specs=[FULL] * 4,
            scratch_shapes=[
                pltpu.SemaphoreType.DMA((4,)),
                pltpu.VMEM((TOK_A, width), BF16),
                pltpu.VMEM((N, width), F32),
                pltpu.VMEM((TOK_A, TOK_A), BF16),
            ],
        ),
        out_shape=[
            pltpu.VMEM((length, width), BF16),
            pltpu.VMEM((length, 2 * N), BF16),
            jax.ShapeDtypeStruct(*final),
            pltpu.VMEM(taken, BF16),
        ],
        compiler_params=params(16),
        cost_estimate=CHEAP,
        name="conv_states",
    )(info, x, bc, halo, wx, wbc, f_dev, ones, rates, ahead)


def pair_kernel(info, got, keep, rates, _, msg, own, first, aux):
    half = keep.shape[1]
    is_odd = info[ODD] == 1
    arrived, their = take_message(got)
    row = rates.shape[0] - 16
    mine = rates[row : row + 1, :]
    early = jnp.where(is_odd, arrived, keep[...])
    late = jnp.where(is_odd, keep[...], arrived)
    even_decay = jnp.where(is_odd, their, mine)
    odd_decay = jnp.where(is_odd, mine, their)
    state = odd_decay * early + late
    own[...] = state
    first[...] = early
    aux[0:8, :] = jnp.broadcast_to(even_decay, (8, half))
    aux[8:16, :] = jnp.broadcast_to(even_decay * odd_decay, (8, half))
    put_message(msg, state, even_decay * odd_decay)


def wave_kernel(got, own, aux, behind_in, _, msg, behind):
    before, decay = take_message(got)
    if behind_in is not None:
        before_decay = behind_in[N : N + 1, :]
        before = behind_in[0:N, :] + before_decay * before
        decay = before_decay * decay
    pair_decay = aux[8:9, :]
    behind[0:N, :] = before
    behind[N:, :] = jnp.broadcast_to(decay, (8, before.shape[1]))
    put_message(msg, own[...] + pair_decay * before, pair_decay * decay)


def last_kernel(info, got, behind_in, first, aux, _, back, held):
    is_odd = info[ODD] == 1
    before, _unused = take_message(got)
    if behind_in is not None:
        before = behind_in[0:N, :] + behind_in[N : N + 1, :] * before
    entering_odd = aux[0:1, :] * before + first[...]
    back[...] = jnp.where(is_odd, before, entering_odd).astype(BF16)
    held[...] = jnp.where(is_odd, entering_odd, before).astype(BF16)


def pair_split_kernel(info, got, keep, rates, _, first, aux, *refs):
    outs, wide = refs[:-1], refs[-1]
    half = keep.shape[1]
    pairs = len(outs)
    piece = half // pairs
    is_odd = info[ODD] == 1
    arrived, their = take_message(got)
    row = rates.shape[0] - 16
    mine = rates[row : row + 1, :]
    early = jnp.where(is_odd, arrived, keep[...])
    late = jnp.where(is_odd, keep[...], arrived)
    even_decay = jnp.where(is_odd, their, mine)
    odd_decay = jnp.where(is_odd, mine, their)
    first[...] = early
    aux[...] = jnp.broadcast_to(even_decay, (8, half))
    put_message(wide, odd_decay * early + late, even_decay * odd_decay)
    for r in range(pairs):
        owner = lax.rem(info[PAIR] + r, pairs)
        outs[r][...] = wide[:, pl.ds(pl.multiple_of(owner * piece, piece), piece)]


def owner_kernel(info, *refs):
    pairs = (len(refs) - 3) // 2
    ins, outs = refs[:pairs], refs[pairs + 1 : 2 * pairs + 1]
    states, prefixes = refs[-2:]
    for r in range(pairs):
        states[lax.rem(info[PAIR] + pairs - r, pairs)] = ins[r][...]
    before = jnp.zeros(prefixes.shape[1:], F32)
    for q in range(pairs):
        prefixes[q] = before.astype(BF16)
        if q < pairs - 1:
            state, decay = take_message(states.at[q])
            before = decay * before + state
    for r in range(pairs):
        outs[r][...] = prefixes[lax.rem(info[PAIR] + r, pairs)]


def last_split_kernel(info, first, aux, _, *refs):
    pairs = len(refs) - 3
    back, held, wide = refs[-3:]
    piece = back.shape[1] // pairs
    for r in range(pairs):
        owner = lax.rem(info[PAIR] + pairs - r, pairs)
        wide[:, pl.ds(pl.multiple_of(owner * piece, piece), piece)] = refs[r][...]
    is_odd = info[ODD] == 1
    before = wide[...].astype(F32)
    entering_odd = aux[0:1, :] * before + first[...]
    back[...] = jnp.where(is_odd, before, entering_odd).astype(BF16)
    held[...] = jnp.where(is_odd, entering_odd, before).astype(BF16)


def combine(kernel, operands, specs, outs, name, scratch=()):
    return pl.pallas_call(
        kernel,
        in_specs=specs,
        out_specs=[FULL] * len(outs),
        out_shape=[jax.ShapeDtypeStruct(s, t) for s, t in outs],
        scratch_shapes=list(scratch),
        compiler_params=params(16),
        cost_estimate=CHEAP,
        name=name,
    )(*operands)


def scan_kernel(order, part, info, x, z, bc, cum, cum_s, log_s, f_blk, rates, _, uv_out, state):
    length = x.shape[0]
    width = state.shape[1]
    per_slab = SLAB // P_SIZE
    inner = STEP_B // TOK_B
    blocks = length // TOK_B
    first_head = part * width // P_SIZE
    first_lane = info[GROUP + order] * x.shape[1] + part * width
    state[...] = jnp.zeros_like(state)

    row = lax.broadcasted_iota(jnp.int32, (TOK_B, TOK_B), 0)
    col = lax.broadcasted_iota(jnp.int32, (TOK_B, TOK_B), 1)
    keep = row >= col
    first = lax.broadcasted_iota(jnp.int32, (TOK_B, 2 * P_SIZE), 1) < P_SIZE
    zero = jnp.zeros((TOK_B, 2 * P_SIZE), BF16)

    def turn(step, _):
        for k in range(inner):
            block(step * inner + k)
        return 0

    def block(b):
        at = pl.ds(pl.multiple_of(b * TOK_B, TOK_B), TOK_B)
        b_mat = bc[at, 0:N]
        c_mat = bc[at, N : 2 * N]
        b_across = b_mat.T
        scores = jnp.where(keep, dot(c_mat, b_mat, ((1,), (1,))), 0.0)
        for s in range(width // SLAB):
            lanes = slice(s * SLAB, (s + 1) * SLAB)
            xb = x[at, part * width + s * SLAB : part * width + (s + 1) * SLAB]
            wide = slice(part * width + s * SLAB, part * width + (s + 1) * SLAB)
            fade_row = rates[pl.ds(b, 1), wide]
            lead_row = rates[pl.ds(blocks + b, 1), wide]
            skip = rates[2 * blocks + 8 : 2 * blocks + 9, wide]
            old = state[:, lanes]
            carried = dot(c_mat, old.astype(BF16))
            within, grown, rises = [], [], []
            for q in range(per_slab // 2):
                tables, fades, columns = [], [], []
                for h in (2 * q, 2 * q + 1):
                    head = first_head + s * per_slab + h
                    own = slice(head, head + 1)
                    column = jnp.broadcast_to(cum[at, own], (TOK_B, TOK_B))
                    gap = jnp.minimum(column - cum_s[own, at], log_s[own, at])
                    tables.append((scores * jnp.exp2(gap)).astype(BF16))
                    fades.append(b_across * f_blk[own, at].astype(BF16))
                    columns.append(column)
                xp = xb[:, q * 2 * P_SIZE : (q + 1) * 2 * P_SIZE]
                stacked = jnp.concatenate([jnp.where(first, xp, zero), jnp.where(first, zero, xp)], 0)
                both = jnp.concatenate([jnp.concatenate(tables, 1), jnp.concatenate(fades, 1)], 0)
                product = dot(both, stacked)
                within.append(product[0:TOK_B])
                grown.append(product[TOK_B:])
                rises.append(jnp.exp2(jnp.where(first, columns[0], columns[1])))
            rise = jnp.concatenate(rises, 1)
            xs = xb.astype(F32)
            y = jnp.concatenate(within, 1) + carried * rise + skip * xs
            gate = half_silu((z[at, pl.ds(pl.multiple_of(first_lane + s * SLAB, SLAB), SLAB)] * 0.5).astype(F32))
            uv_out[at, lanes] = (y * gate).astype(BF16)
            uv_out[at, width + s * SLAB : width + (s + 1) * SLAB] = (gate * rise * lead_row).astype(BF16)
            state[:, lanes] = old * fade_row + jnp.concatenate(grown, 1)

    lax.fori_loop(0, length // STEP_B, turn, 0)


def scan_part(order, part, info, token, x, z, bc, cum, cum_s, log_s, f_blk, rates):
    length, full = x.shape
    width = full // B_PARTS
    return pl.pallas_call(
        functools.partial(scan_kernel, order, part),
        in_specs=[SCALAR] + [FULL] * 8 + [ANY],
        out_specs=FULL,
        out_shape=pltpu.VMEM((length, 2 * width), BF16),
        scratch_shapes=[pltpu.VMEM((N, width), F32)],
        compiler_params=params(12),
        cost_estimate=CHEAP,
        name="scan_part",
    )(info, x, z, bc, cum, cum_s, log_s, f_blk, rates, token)


def norm_kernel(places, fetched, info, bc0, bc1, state0, state1, gain, _, *refs):
    uvs, refs = refs[: 2 * B_PARTS], refs[2 * B_PARTS :]
    weights, outs, tiles, sem = refs[:fetched], refs[fetched : -1 - fetched], refs[len(refs) - 1 - fetched : -1], refs[-1]
    copies = [
        pltpu.make_async_copy(weight.at[:, pl.ds(0, tile.shape[1])], tile, sem.at[k])
        for k, (weight, tile) in enumerate(zip(weights, tiles))
    ]
    for copy in copies:
        copy.start()
    count = outs[0].shape[0] * len(outs) // len(places)
    per = state0.shape[1]
    part = per // B_PARTS

    def rows(out, first, base):
        to = pl.ds(pl.multiple_of(first, ROWS_C), ROWS_C)
        at = pl.ds(pl.multiple_of(base, ROWS_C), ROWS_C)
        for order, (bc, state) in enumerate(((bc0, state0), (bc1, state1))):
            c_mat = bc[at, N : 2 * N]
            pieces = []
            squares = None
            for p in range(B_PARTS):
                uv = uvs[order * B_PARTS + p]
                inc = state[:, p * part : (p + 1) * part]
                gated = uv[at, 0:part].astype(F32) + uv[at, part:].astype(F32) * dot(c_mat, inc)
                square = jnp.sum(gated * gated, axis=-1, keepdims=True)
                squares = square if squares is None else squares + square
                pieces.append(gated)
            scale = lax.rsqrt(squares * (1.0 / per) + EPS)
            for p, gated in enumerate(pieces):
                lanes = pl.ds(pl.multiple_of(info[GROUP + order] * per + p * part, part), part)
                out[to, lanes] = (gated * scale * gain[:, lanes]).astype(BF16)

    for k, place in enumerate(places):

        def step(j, _):
            out, first = (outs[k], 0) if len(outs) > 1 else (outs[0], k * count)
            rows(out, first + j * ROWS_C, info[ROWS + place] * count + j * ROWS_C)
            return 0

        lax.fori_loop(0, count // ROWS_C, step, 0)
    for copy in copies:
        copy.wait()


def norm_rows(places, apart, info, count, token, bcs, states, gain, uvs, weights=(), columns=0):
    tile = jax.ShapeDtypeStruct((gain.shape[1], columns), BF16)
    arrays = len(places) if apart else 1
    rows = jax.ShapeDtypeStruct((len(places) * count // arrays, gain.shape[1]), BF16)
    return pl.pallas_call(
        functools.partial(norm_kernel, places, len(weights)),
        in_specs=[SCALAR] + [FULL] * 5 + [ANY] + [FULL] * len(uvs) + [FAR] * len(weights),
        out_specs=[FULL] * (arrays + len(weights)),
        out_shape=[rows] * arrays + [tile] * len(weights),
        scratch_shapes=[pltpu.SemaphoreType.DMA((2,))],
        compiler_params=params(16),
        cost_estimate=CHEAP,
        name="norm_rows",
    )(info, *bcs, *states, gain, token, *uvs, *weights)


def stream(base, w0_far, w1_far, w0, w1, sem):
    j = pl.program_id(0)
    tiles = pl.num_programs(0)

    def fetch(t):
        slot = lax.rem(t, SLOTS)
        lanes = pl.ds(pl.multiple_of((base + t) * TILE, TILE), TILE)
        return (
            pltpu.make_async_copy(w0_far.at[:, lanes], w0.at[slot], sem.at[0, slot]),
            pltpu.make_async_copy(w1_far.at[:, lanes], w1.at[slot], sem.at[1, slot]),
        )

    def start(t):
        @pl.when(t < tiles)
        def _():
            for copy in fetch(t):
                copy.start()

    @pl.when(j == 0)
    def _():
        for t in range(SLOTS - 1):
            start(t)

    start(j + SLOTS - 1)
    for copy in fetch(j):
        copy.wait()
    return lax.rem(j, SLOTS)


def buffers(depth):
    return [
        pltpu.VMEM((SLOTS, depth, TILE), BF16),
        pltpu.VMEM((SLOTS, depth, TILE), BF16),
        pltpu.SemaphoreType.DMA((2, SLOTS)),
    ]


def ahead_kernel(owns, mate, w0, w1, out):
    out[...] = (dot(owns[0 : out.shape[0], :], w0[...]) + dot(mate[...], w1[...])).astype(BF16)


def project_ahead(owns, mate, w0, w1):
    return pl.pallas_call(
        ahead_kernel,
        in_specs=[FULL] * 4,
        out_specs=FULL,
        out_shape=jax.ShapeDtypeStruct((owns.shape[0] // 2, w0.shape[1]), BF16),
        compiler_params=params(16),
        cost_estimate=CHEAP,
        name="project_ahead",
    )(owns, mate, w0, w1)


def join_kernel(first, second, _, out):
    rows = first.shape[0]
    out[0:rows, :] = first[...]
    out[rows:, :] = second[...]


def join(first, second, token):
    rows, depth = first.shape
    return pl.pallas_call(
        join_kernel,
        in_specs=[FULL, FULL, ANY],
        out_specs=FULL,
        out_shape=jax.ShapeDtypeStruct((2 * rows, depth), BF16),
        compiler_params=params(8),
        cost_estimate=CHEAP,
        name="join",
    )(first, second, token)


def both_kernel(base, cut, owns, mates, w0_far, w1_far, *refs):
    fars, near, w0, w1, sem = refs[:-4], *refs[-4:]
    rows = near.shape[0]
    slot = stream(base, w0_far, w1_far, w0, w1, sem)
    total = dot(owns[...], w0[slot]) + dot(mates[...], w1[slot])
    near[...] = total[rows:]
    for k, far_out in enumerate(fars):

        @pl.when(pl.program_id(0) // cut == k)
        def _():
            far_out[...] = total[0:rows].astype(BF16)


def project_both(owns, mates, w0, w1, first, count, chunk):
    rows, depth = owns.shape[0] // 2, owns.shape[1]
    cut = chunk // TILE
    chunks = count // chunk

    def placed(k):
        return pl.BlockSpec((rows, TILE), lambda j: (0, jnp.clip(j - k * cut, 0, cut - 1)))

    *fars, near = pl.pallas_call(
        functools.partial(both_kernel, first // TILE, cut),
        grid=(count // TILE,),
        in_specs=[FULL] * 2 + [FAR] * 2,
        out_specs=[placed(k) for k in range(chunks)] + [pl.BlockSpec((rows, TILE), lambda j: (0, j))],
        out_shape=[jax.ShapeDtypeStruct((rows, chunk), BF16)] * chunks + [jax.ShapeDtypeStruct((rows, count), F32)],
        scratch_shapes=buffers(depth),
        compiler_params=params(24),
        cost_estimate=CHEAP,
        name="project_both",
    )(owns, mates, w0, w1)
    return fars, near


def near_kernel(owns, mates, w0_far, w1_far, arrived, out, w0, w1, sem):
    slot = stream(0, w0_far, w1_far, w0, w1, sem)
    rows = out.shape[0]
    total = dot(owns[rows:, :], w0[slot]) + dot(mates[rows:, :], w1[slot])
    out[...] = (total + arrived[...].astype(F32)).astype(BF16)


def project_near(owns, mates, w0, w1, arrived):
    rows, depth = owns.shape[0] // 2, owns.shape[1]
    placed = pl.BlockSpec((rows, TILE), lambda j: (0, j))
    return pl.pallas_call(
        near_kernel,
        grid=(arrived.shape[1] // TILE,),
        in_specs=[FULL, FULL, FAR, FAR, placed],
        out_specs=placed,
        out_shape=jax.ShapeDtypeStruct((rows, w0.shape[1]), BF16),
        scratch_shapes=buffers(depth),
        compiler_params=params(20),
        cost_estimate=CHEAP,
        name="project_near",
    )(owns, mates, w0, w1, arrived)


def add_kernel(near, *refs):
    arrived, out = refs[:-2], refs[-1]
    chunk = arrived[0].shape[1]
    for k, part in enumerate(arrived):
        lanes = slice(k * chunk, (k + 1) * chunk)
        out[:, lanes] = (near[:, lanes] + part[...].astype(F32)).astype(BF16)


def add_chunks(near, first, arrived, result, at):
    rows, chunk = arrived[0].shape
    count = chunk * len(arrived)
    return pl.pallas_call(
        add_kernel,
        grid=(1,),
        in_specs=[pl.BlockSpec((rows, count), lambda j: (0, first // count))] + [FULL] * len(arrived) + [ANY],
        out_specs=pl.BlockSpec((rows, count), lambda j: (0, at // count)),
        out_shape=jax.ShapeDtypeStruct(result.shape, BF16),
        input_output_aliases={1 + len(arrived): 0},
        compiler_params=params(8),
        cost_estimate=CHEAP,
        name="add_chunks",
    )(near, *arrived, result)


def shift(block, distance):
    size = lax.axis_size("seq")
    return lax.ppermute(block, "seq", [(i, i + distance) for i in range(size - distance)])


def swap(block, axis, bit):
    return lax.ppermute(block, axis, [(i, i ^ bit) for i in range(lax.axis_size(axis))])


def rotate(block, distance):
    size = lax.axis_size("seq")
    return lax.ppermute(block, "seq", [(i, (i + distance) % size) for i in range(size)])


def log_steps(info, got, keep, rates_kept, done, pairs, scan_next):
    half = keep.shape[1]
    message = ((N + EXTRA, half), BF16)
    full = ((N, half), F32)
    msg, own, first, aux = combine(
        pair_kernel,
        (info, got, keep, rates_kept, done),
        [SCALAR, FULL, FULL, FULL, ANY],
        [message, full, full, ((16, half), F32)],
        "pair",
    )
    behind = None
    covered = 0
    while True:
        got = shift(msg, 2 * (covered + 1))
        done = scan_next(msg)
        covered = 2 * covered + 1
        if covered >= pairs - 1:
            break
        operands, specs = [got, own, aux], [FULL, FULL, FULL]
        if behind is None:
            kernel = lambda g, o, a, t, m, b: wave_kernel(g, o, a, None, t, m, b)
        else:
            kernel = wave_kernel
            operands.append(behind)
            specs.append(FULL)
        msg, behind = combine(kernel, operands + [done], specs + [ANY], [message, ((N + 8, half), F32)], "wave")
    operands, specs = [info, got], [SCALAR, FULL]
    if behind is None:
        kernel = lambda o, g, f, a, t, b, h: last_kernel(o, g, None, f, a, t, b, h)
    else:
        kernel = last_kernel
        operands.append(behind)
        specs.append(FULL)
    out = ((N, half), BF16)
    back, held = combine(kernel, operands + [first, aux, done], specs + [FULL, FULL, ANY], [out, out], "last")
    return back, held


def local(
    x_input,
    z_input,
    bc_input,
    conv_weight_x,
    conv_weight_bc,
    step_size,
    log_decay,
    skip_gain,
    norm_gain,
    out_weight,
):
    length, width = x_input.shape
    heads = step_size.shape[1]
    ways = lax.axis_size("head")
    pairs = lax.axis_size("seq") // 2
    mine = lax.axis_index("head")
    half = width // 2
    seq = lax.axis_index("seq")
    info = jnp.stack([seq & 1, mine ^ 3, mine ^ 2, mine ^ 1, mine, seq >> 1, seq, 1 - (seq & 1), seq & 1]).astype(jnp.int32)

    x_far, z_far, w_far = far(x_input, z_input, out_weight)
    (bc_far,) = far(bc_input)
    halo = rotate(tail_rows(x_far, bc_far), 1)
    bc = bc_input.reshape(length, -1)
    (weight_mate,) = far(swap(out_weight, "head", 1))

    (cum, cum_s, log_s, f_dev, f_blk, rates), ones, x_sent = decays(
        info, log_decay, step_size, skip_gain, x_input, half
    )
    taps = far(conv_weight_x, conv_weight_bc)
    shared = (bc, halo, *taps)
    x0, bc0, send, x_kept = conv_states(0, info, x_sent, *shared, f_dev[0], ones, rates[0], x_far)
    got = swap(send, "seq", 1)
    x1, bc1, keep, z_near = conv_states(1, info, x_kept, *shared, f_dev[1], ones, rates[1], z_far)
    rates_kept = rates[1]

    uvs = []
    groups = list(zip((x0, x1), (z_near, z_near), (bc0, bc1), cum, cum_s, log_s, f_blk, rates))

    def scan_next(token):
        if len(uvs) < 2 * B_PARTS:
            order, part = divmod(len(uvs), B_PARTS)
            uvs.append(scan_part(order, part, info, token, *groups[order]))
        return uvs[-1]

    full = ((N, half), F32)
    message = ((N + EXTRA, half), BF16)
    done = scan_next(keep)
    out = ((N, half), BF16)
    if pairs > 1 and half % (pairs * N) == 0:
        piece = half // pairs
        part = ((N + EXTRA, piece), BF16)
        first, aux, *parts = combine(
            pair_split_kernel,
            (info, got, keep, rates_kept, done),
            [SCALAR, FULL, FULL, FULL, ANY],
            [full, ((8, half), F32)] + [part] * pairs,
            "pair",
            [pltpu.VMEM(*message)],
        )
        parts = list(parts[:1]) + [rotate(parts[r], 2 * r) for r in range(1, pairs)]
        done = scan_next(parts[0])
        parts = combine(
            owner_kernel,
            [info] + parts + [done],
            [SCALAR] + [FULL] * pairs + [ANY],
            [((N, piece), BF16)] * pairs,
            "owner",
            [pltpu.VMEM((pairs, N + EXTRA, piece), BF16), pltpu.VMEM((pairs, N, piece), BF16)],
        )
        ready = parts[0]
        parts = list(parts[:1]) + [rotate(parts[r], 2 * r) for r in range(1, pairs)]
        done = scan_next(ready)
        back, held = combine(
            last_split_kernel,
            [info, first, aux, done] + parts,
            [SCALAR, FULL, FULL, ANY] + [FULL] * pairs,
            [out, out],
            "last",
            [pltpu.VMEM(*out)],
        )
    else:
        back, held = log_steps(info, got, keep, rates_kept, done, pairs, scan_next)
    other = swap(back, "seq", 1)
    while len(uvs) < 2 * B_PARTS:
        scan_next(back)

    count = length // ways
    gain = norm_gain[None, :]

    columns = out_weight.shape[1]
    chunk = columns // 8
    weights = (w_far, weight_mate)
    shared = ((bc0, bc1), (other, held), gain, uvs)
    far_mate, near_mate = norm_rows((0, 2), True, info, count, held, *shared)
    owns, w0, w1 = norm_rows((1, 3), False, info, count, far_mate, *shared, weights, chunk)
    far_mate = swap(far_mate, "head", 1)
    sent = project_ahead(owns, far_mate, w0, w1)
    first = swap(sent, "head", 2)
    operands = (owns, join(far_mate, swap(near_mate, "head", 1), sent), *weights)
    calls = []
    for lo, hi in ((1, 2), (2, 4), (4, 6), (6, 8)):
        sent, near = project_both(*operands, lo * chunk, (hi - lo) * chunk, chunk)
        calls.append((near, lo, [swap(part, "head", 2) for part in sent]))
    result = project_near(*operands, first)
    for near, lo, arrived in calls[:-1]:
        result = add_chunks(near, 0, arrived, result, lo * chunk)
    near, lo, arrived = calls[-1]
    for k, part in enumerate(arrived):
        result = add_chunks(near, k * chunk, [part], result, (lo + k) * chunk)
    return result


def solution(mesh):
    in_specs = (
        P("seq", "head"),
        P("seq", "head"),
        P("seq", "head", None),
        P(None, "head"),
        P(None, "head", None),
        P("seq", "head"),
        P("seq", "head"),
        P("head"),
        P("head"),
        P("head", None),
    )
    out_specs = P(("seq", "head"), None)
    return jax.shard_map(local, mesh=mesh, in_specs=in_specs, out_specs=out_specs, check_vma=False)
```

```python
import functools

import jax
import jax.numpy as jnp
from jax import lax
from jax.experimental import pallas as pl
from jax.experimental.pallas import tpu as pltpu
from jax.sharding import PartitionSpec as P

P_SIZE = 64
N = 128
KCONV = 4
EPS = 1e-05
LOG2E = 1.4426950408889634

TOK_A = 256
ROWS_A = 32
TOK_B = 128
STEP_B = 256
EXTRA = 16
SLAB = 256
ROWS_C = 128
TILE = 256
SLOTS = 4
LEAD = 16
B_PARTS = 2
HIGHEST = lax.Precision.HIGHEST
F32 = jnp.float32
BF16 = jnp.bfloat16


def params(mib):
    return pltpu.CompilerParams(vmem_limit_bytes=mib * 1024 * 1024)


CHEAP = pl.CostEstimate(flops=1, bytes_accessed=1, transcendentals=0)
SCALAR = pl.BlockSpec(memory_space=pltpu.SMEM)
FULL = pl.BlockSpec(memory_space=pltpu.VMEM)
FAR = pl.BlockSpec(memory_space=pltpu.HBM)
ANY = pl.BlockSpec(memory_space=pl.ANY)

ODD, ROWS, PAIR, SEQ, GROUP = 0, 1, 5, 6, 7


def dot(a, b, dims=((1,), (0,)), precision=None):
    return lax.dot_general(a, b, (dims, ((), ())), precision=precision, preferred_element_type=F32)


def half_silu(half):
    return half + half * jnp.tanh(half)


def far(*arrays):
    return [pltpu.with_memory_space_constraint(a, pltpu.HBM) for a in arrays]


def whole(shape):
    return pl.BlockSpec(shape, lambda *_: (0,) * len(shape))


def group_copies(x_far, x, group, sems):
    length, width = x.shape
    rows = length // 4
    lanes = pl.ds(pl.multiple_of(group * width, width), width)
    pieces = [pl.ds(k * rows, rows) for k in range(4)]
    return [pltpu.make_async_copy(x_far.at[at, lanes], x.at[at], sems.at[k]) for k, at in enumerate(pieces)]


def decay_kernel(info, ld_t, step_t, skip, x_far, *refs):
    cum, cum_s, log_s, f_dev, f_blk, rates = [refs[2 * k : 2 * k + 2] for k in range(6)]
    ones, x, sem = refs[12:]
    copies = group_copies(x_far, x, info[GROUP], sem)
    for copy in copies:
        copy.start()
    heads, length = ld_t.shape
    blocks = length // TOK_B
    per = heads // 2
    width = ones.shape[1]
    swapped = info[GROUP] == 1
    row = lax.broadcasted_iota(jnp.int32, (TOK_B, TOK_B), 0)
    col = lax.broadcasted_iota(jnp.int32, (TOK_B, TOK_B), 1)
    lower = (row >= col).astype(F32)
    upper = (row <= col).astype(F32)
    eye = (row == col).astype(BF16)

    def ordered(value):
        return jnp.where(swapped, jnp.concatenate([value[per:], value[:per]], 0), value)

    def put(ref, rows, value):
        high = value.astype(BF16)
        low = (value - high.astype(F32)).astype(BF16)
        for g in range(2):
            own = slice(g * per, (g + 1) * per)
            both = jnp.concatenate([high[own], low[own]], 0)
            ref[g][rows, :] = dot(eye, both, ((1,), (1,))).astype(BF16)

    first = lax.broadcasted_iota(jnp.int32, (per, width), 0) * P_SIZE
    lane = lax.broadcasted_iota(jnp.int32, (per, width), 1)
    member = ((lane >= first) & (lane < first + P_SIZE)).astype(F32)
    ones[0:per, :] = member.astype(BF16)
    ones[per:, :] = member.astype(BF16)
    cums, totals, row_totals = [], [], []
    for b in range(blocks):
        rows = slice(b * TOK_B, (b + 1) * TOK_B)
        logs = ordered(ld_t[:, rows]) * LOG2E
        c = dot(lower, logs, ((1,), (1,)), HIGHEST)
        for g in range(2):
            cum[g][rows, :] = c[:, g * per : (g + 1) * per]
        row_totals.append(c[TOK_B - 1 : TOK_B, :])
        c = dot(logs, upper, precision=HIGHEST)
        cums.append(c)
        totals.append(c[:, TOK_B - 1 : TOK_B])
    before, row_before = [jnp.zeros_like(totals[0])], [jnp.zeros_like(row_totals[0])]
    for b in range(blocks):
        before.append(before[-1] + totals[b])
        row_before.append(row_before[-1] + row_totals[b])
    total = before[-1]
    logs = jnp.concatenate(row_totals + row_before[:-1] + row_before[-1:] * 8, 0)
    gains = jnp.broadcast_to(skip[...], (8, heads))
    gains = jnp.where(swapped, jnp.concatenate([gains[:, per:], gains[:, :per]], 1), gains)
    values = jnp.concatenate([jnp.exp2(logs), gains], 0)
    for g in range(2):
        rates[g][...] = dot(values[:, g * per : (g + 1) * per], member, precision=HIGHEST)
    for b in range(blocks):
        rows = slice(b * TOK_B, (b + 1) * TOK_B)
        s = ordered(step_t[:, rows])
        log_step = jnp.log2(s)
        shifted = cums[b] - log_step
        fade = jnp.exp2(totals[b] - cums[b]) * s
        for g in range(2):
            own = slice(g * per, (g + 1) * per)
            log_s[g][:, rows] = log_step[own, :]
            cum_s[g][:, rows] = shifted[own, :]
            f_blk[g][:, rows] = fade[own, :]
        put(f_dev, rows, jnp.exp2(total - (cums[b] + before[b])) * s)
    for copy in copies:
        copy.wait()


def decays(info, log_decay, step, skip, x, width):
    length, heads = log_decay.shape
    blocks = length // TOK_B
    per = heads // 2
    across = jax.ShapeDtypeStruct((per, length), F32)
    pair = jax.ShapeDtypeStruct((length, 2 * per), BF16)
    column = jax.ShapeDtypeStruct((length, per), F32)
    rates = jax.ShapeDtypeStruct((2 * blocks + 16, width), F32)
    shapes = [shape for shape in (column, across, across, pair, across, rates) for _ in range(2)]
    shapes += [
        jax.ShapeDtypeStruct((2 * per, width), BF16),
        pltpu.VMEM((length, width), BF16),
    ]
    *refs, ones, x_near = pl.pallas_call(
        decay_kernel,
        in_specs=[SCALAR] + [FULL] * 3 + [FAR],
        out_specs=[FULL] * len(shapes),
        out_shape=shapes,
        scratch_shapes=[pltpu.SemaphoreType.DMA((4,))],
        compiler_params=params(16),
        cost_estimate=CHEAP,
        name="decays",
    )(info, *far(log_decay.T, step.T, skip[None, :], x))
    return [tuple(refs[2 * k : 2 * k + 2]) for k in range(6)], ones, x_near


def tail_kernel(x, bc, out):
    width, bc_width = x.shape[1], bc.shape[2]
    out[:, 0:width] = x[...]
    for g in range(bc.shape[1]):
        out[:, width + g * bc_width : width + (g + 1) * bc_width] = bc[:, g, :]


def tail_rows(x, bc):
    length, width = x.shape
    groups, bc_width = bc.shape[1:]
    at = length // LEAD - 1
    shape = (LEAD, width + groups * bc_width)
    return pl.pallas_call(
        tail_kernel,
        grid=(1,),
        in_specs=[
            pl.BlockSpec((LEAD, width), lambda i: (at, 0)),
            pl.BlockSpec((LEAD, groups, bc_width), lambda i: (at, 0, 0)),
        ],
        out_specs=whole(shape),
        out_shape=jax.ShapeDtypeStruct(shape, BF16),
        compiler_params=params(8),
        cost_estimate=CHEAP,
        name="tail_rows",
    )(x, bc)


def put_message(ref, state, decay):
    high = decay.astype(BF16)
    low = (decay - high.astype(F32)).astype(BF16)
    rest = jnp.zeros((EXTRA - 2, state.shape[1]), BF16)
    ref[0:N, :] = state.astype(BF16)
    ref[N:, :] = jnp.concatenate([high, low, rest], 0)


def take_message(ref):
    extra = ref[N:, :].astype(F32)
    return ref[0:N, :].astype(F32), extra[0:1] + extra[1:2]


def conv_kernel(order, info, x, bc, halo, wx, wbc, f_dev, ones, rates, *refs):
    next_far, refs = refs[0], refs[1:]
    x_out, bc_out, final = refs[:3]
    xf, state, down = refs[-3:]
    length, width = x_out.shape
    rows = TOK_A
    group = info[GROUP + order]
    first_lane = pl.multiple_of(group * width, width)
    taken, sem = refs[3:5]
    first_bc = pl.multiple_of(group * 2 * N, 2 * N)
    if order == 0:
        copies = group_copies(next_far, taken, info[GROUP + 1], sem)
    else:
        part = length // 4
        pieces = [pl.ds(k * part, part) for k in range(4)]
        copies = [pltpu.make_async_copy(next_far.at[at], taken.at[at], sem.at[k]) for k, at in enumerate(pieces)]
    for copy in copies:
        copy.start()
    state[...] = jnp.zeros_like(state)
    row = lax.broadcasted_iota(jnp.int32, down.shape, 0)
    col = lax.broadcasted_iota(jnp.int32, down.shape, 1)
    down[...] = (row == col + 1).astype(BF16)

    def conv(i, src, moved, first, behind, weights, emit):
        at_start = jnp.where(info[SEQ] == 0, jnp.zeros_like(first), first)
        lead = jnp.where(i == 0, at_start, behind).astype(F32)
        w0, w1, w2, w3 = [w * 0.5 for w in weights]
        back = LEAD - 8
        lead_r1 = pltpu.roll(lead, 1, 0)
        last_p = (w1 * lead + w0 * lead_r1)[back:]
        top = lax.broadcasted_iota(jnp.int32, (8, lead.shape[1]), 0) == 0
        head = jnp.where(top, jnp.broadcast_to(lead[LEAD - 1 :], top.shape), moved[0:8])
        for r in range(0, rows, ROWS_A):
            cur = src[r : r + ROWS_A].astype(F32)
            r1 = moved[r : r + ROWS_A] if r else jnp.concatenate([head, moved[8:ROWS_A]], 0)
            p = w1 * cur + w0 * r1
            p2 = pltpu.roll(jnp.concatenate([last_p, p], 0), 2, 0)[8:]
            emit(r, half_silu((w3 * cur + w2 * r1) + p2))
            last_p = p[ROWS_A - 8 :]

    def step(i, _):
        at = pl.ds(pl.multiple_of(i * rows, rows), rows)
        behind = pl.ds(pl.multiple_of(jnp.maximum(i * rows - LEAD, 0), LEAD), LEAD)

        def out(r):
            return pl.ds(pl.multiple_of(i * rows + r, ROWS_A), ROWS_A)

        for lanes in range(0, 2 * N, SLAB):
            ds = slice(lanes, lanes + SLAB)
            src = pl.ds(pl.multiple_of(first_bc + lanes, SLAB), SLAB)
            halo_src = pl.ds(pl.multiple_of(2 * width + first_bc + lanes, SLAB), SLAB)

            def emit_bc(r, value):
                bc_out[out(r), ds] = value.astype(BF16)

            weights = [jnp.where(group == 0, wbc[k, 0:1, ds], wbc[k, 1:2, ds]) for k in range(KCONV)]
            conv(i, bc[at, src], dot(down[...], bc[at, src]), halo[:, halo_src], bc[behind, src], weights, emit_bc)

        for lanes in range(0, width, SLAB):
            ds = slice(lanes, lanes + SLAB)
            src = pl.ds(pl.multiple_of(first_lane + lanes, SLAB), SLAB)
            scale = dot(f_dev[at, :], ones[:, ds])

            def emit(r, value):
                x_out[out(r), ds] = value.astype(BF16)
                xf[r : r + ROWS_A, ds] = (value * scale[r : r + ROWS_A]).astype(BF16)

            weights = [wx[k : k + 1, ds] for k in range(KCONV)]
            conv(i, x[at, ds], dot(down[...], x[at, ds]), halo[:, src], x[behind, ds], weights, emit)

        state[...] += dot(bc_out[at, 0:N], xf[...], ((0,), (0,)))
        return 0

    lax.fori_loop(0, length // rows, step, 0)
    if order == 0:
        row = rates.shape[0] - 16
        put_message(final, state[...], rates[row : row + 1, :])
    else:
        final[...] = state[...]
    for copy in copies:
        copy.wait()


def conv_states(order, info, x, bc, halo, wx, wbc, f_dev, ones, rates, ahead):
    length, width = x.shape
    column = lambda i, info: (0, info[GROUP + order])
    final = ((N + EXTRA, width), BF16) if order == 0 else ((N, width), F32)
    taken = (length, width) if order == 0 else ahead.shape
    return pl.pallas_call(
        functools.partial(conv_kernel, order),
        grid_spec=pltpu.PrefetchScalarGridSpec(
            num_scalar_prefetch=1,
            grid=(1,),
            in_specs=[FULL] * 3 + [pl.BlockSpec((KCONV, width), column)] + [FULL] * 4 + [FAR],
            out_specs=[FULL] * 4,
            scratch_shapes=[
                pltpu.SemaphoreType.DMA((4,)),
                pltpu.VMEM((TOK_A, width), BF16),
                pltpu.VMEM((N, width), F32),
                pltpu.VMEM((TOK_A, TOK_A), BF16),
            ],
        ),
        out_shape=[
            pltpu.VMEM((length, width), BF16),
            pltpu.VMEM((length, 2 * N), BF16),
            jax.ShapeDtypeStruct(*final),
            pltpu.VMEM(taken, BF16),
        ],
        compiler_params=params(16),
        cost_estimate=CHEAP,
        name="conv_states",
    )(info, x, bc, halo, wx, wbc, f_dev, ones, rates, ahead)


def pair_kernel(info, got, keep, rates, _, msg, own, first, aux):
    half = keep.shape[1]
    is_odd = info[ODD] == 1
    arrived, their = take_message(got)
    row = rates.shape[0] - 16
    mine = rates[row : row + 1, :]
    early = jnp.where(is_odd, arrived, keep[...])
    late = jnp.where(is_odd, keep[...], arrived)
    even_decay = jnp.where(is_odd, their, mine)
    odd_decay = jnp.where(is_odd, mine, their)
    state = odd_decay * early + late
    own[...] = state
    first[...] = early
    aux[0:8, :] = jnp.broadcast_to(even_decay, (8, half))
    aux[8:16, :] = jnp.broadcast_to(even_decay * odd_decay, (8, half))
    put_message(msg, state, even_decay * odd_decay)


def wave_kernel(got, own, aux, behind_in, _, msg, behind):
    before, decay = take_message(got)
    if behind_in is not None:
        before_decay = behind_in[N : N + 1, :]
        before = behind_in[0:N, :] + before_decay * before
        decay = before_decay * decay
    pair_decay = aux[8:9, :]
    behind[0:N, :] = before
    behind[N:, :] = jnp.broadcast_to(decay, (8, before.shape[1]))
    put_message(msg, own[...] + pair_decay * before, pair_decay * decay)


def last_kernel(info, got, behind_in, first, aux, _, back, held):
    is_odd = info[ODD] == 1
    before, _unused = take_message(got)
    if behind_in is not None:
        before = behind_in[0:N, :] + behind_in[N : N + 1, :] * before
    entering_odd = aux[0:1, :] * before + first[...]
    back[...] = jnp.where(is_odd, before, entering_odd).astype(BF16)
    held[...] = jnp.where(is_odd, entering_odd, before).astype(BF16)


def pair_split_kernel(info, got, keep, rates, _, first, aux, *refs):
    outs, wide = refs[:-1], refs[-1]
    half = keep.shape[1]
    pairs = len(outs)
    piece = half // pairs
    is_odd = info[ODD] == 1
    arrived, their = take_message(got)
    row = rates.shape[0] - 16
    mine = rates[row : row + 1, :]
    early = jnp.where(is_odd, arrived, keep[...])
    late = jnp.where(is_odd, keep[...], arrived)
    even_decay = jnp.where(is_odd, their, mine)
    odd_decay = jnp.where(is_odd, mine, their)
    first[...] = early
    aux[...] = jnp.broadcast_to(even_decay, (8, half))
    put_message(wide, odd_decay * early + late, even_decay * odd_decay)
    for r in range(pairs):
        owner = lax.rem(info[PAIR] + r, pairs)
        outs[r][...] = wide[:, pl.ds(pl.multiple_of(owner * piece, piece), piece)]


def owner_kernel(info, *refs):
    pairs = (len(refs) - 3) // 2
    ins, outs = refs[:pairs], refs[pairs + 1 : 2 * pairs + 1]
    states, prefixes = refs[-2:]
    for r in range(pairs):
        states[lax.rem(info[PAIR] + pairs - r, pairs)] = ins[r][...]
    before = jnp.zeros(prefixes.shape[1:], F32)
    for q in range(pairs):
        prefixes[q] = before.astype(BF16)
        if q < pairs - 1:
            state, decay = take_message(states.at[q])
            before = decay * before + state
    for r in range(pairs):
        outs[r][...] = prefixes[lax.rem(info[PAIR] + r, pairs)]


def last_split_kernel(info, first, aux, _, *refs):
    pairs = len(refs) - 3
    back, held, wide = refs[-3:]
    piece = back.shape[1] // pairs
    for r in range(pairs):
        owner = lax.rem(info[PAIR] + pairs - r, pairs)
        wide[:, pl.ds(pl.multiple_of(owner * piece, piece), piece)] = refs[r][...]
    is_odd = info[ODD] == 1
    before = wide[...].astype(F32)
    entering_odd = aux[0:1, :] * before + first[...]
    back[...] = jnp.where(is_odd, before, entering_odd).astype(BF16)
    held[...] = jnp.where(is_odd, entering_odd, before).astype(BF16)


def combine(kernel, operands, specs, outs, name, scratch=()):
    return pl.pallas_call(
        kernel,
        in_specs=specs,
        out_specs=[FULL] * len(outs),
        out_shape=[jax.ShapeDtypeStruct(s, t) for s, t in outs],
        scratch_shapes=list(scratch),
        compiler_params=params(16),
        cost_estimate=CHEAP,
        name=name,
    )(*operands)


def scan_kernel(order, part, info, x, z, bc, cum, cum_s, log_s, f_blk, rates, _, uv_out, state):
    length = x.shape[0]
    width = state.shape[1]
    per_slab = SLAB // P_SIZE
    inner = STEP_B // TOK_B
    blocks = length // TOK_B
    first_head = part * width // P_SIZE
    first_lane = info[GROUP + order] * x.shape[1] + part * width
    state[...] = jnp.zeros_like(state)

    row = lax.broadcasted_iota(jnp.int32, (TOK_B, TOK_B), 0)
    col = lax.broadcasted_iota(jnp.int32, (TOK_B, TOK_B), 1)
    keep = row >= col
    first = lax.broadcasted_iota(jnp.int32, (TOK_B, 2 * P_SIZE), 1) < P_SIZE
    zero = jnp.zeros((TOK_B, 2 * P_SIZE), BF16)

    def turn(step, _):
        for k in range(inner):
            block(step * inner + k)
        return 0

    def block(b):
        at = pl.ds(pl.multiple_of(b * TOK_B, TOK_B), TOK_B)
        b_mat = bc[at, 0:N]
        c_mat = bc[at, N : 2 * N]
        b_across = b_mat.T
        scores = jnp.where(keep, dot(c_mat, b_mat, ((1,), (1,))), 0.0)
        for s in range(width // SLAB):
            lanes = slice(s * SLAB, (s + 1) * SLAB)
            xb = x[at, part * width + s * SLAB : part * width + (s + 1) * SLAB]
            wide = slice(part * width + s * SLAB, part * width + (s + 1) * SLAB)
            fade_row = rates[pl.ds(b, 1), wide]
            lead_row = rates[pl.ds(blocks + b, 1), wide]
            skip = rates[2 * blocks + 8 : 2 * blocks + 9, wide]
            old = state[:, lanes]
            carried = dot(c_mat, old.astype(BF16))
            within, grown, rises = [], [], []
            for q in range(per_slab // 2):
                tables, fades, columns = [], [], []
                for h in (2 * q, 2 * q + 1):
                    head = first_head + s * per_slab + h
                    own = slice(head, head + 1)
                    column = jnp.broadcast_to(cum[at, own], (TOK_B, TOK_B))
                    gap = jnp.minimum(column - cum_s[own, at], log_s[own, at])
                    tables.append((scores * jnp.exp2(gap)).astype(BF16))
                    fades.append(b_across * f_blk[own, at].astype(BF16))
                    columns.append(column)
                xp = xb[:, q * 2 * P_SIZE : (q + 1) * 2 * P_SIZE]
                stacked = jnp.concatenate([jnp.where(first, xp, zero), jnp.where(first, zero, xp)], 0)
                both = jnp.concatenate([jnp.concatenate(tables, 1), jnp.concatenate(fades, 1)], 0)
                product = dot(both, stacked)
                within.append(product[0:TOK_B])
                grown.append(product[TOK_B:])
                rises.append(jnp.exp2(jnp.where(first, columns[0], columns[1])))
            rise = jnp.concatenate(rises, 1)
            xs = xb.astype(F32)
            y = jnp.concatenate(within, 1) + carried * rise + skip * xs
            gate = half_silu((z[at, pl.ds(pl.multiple_of(first_lane + s * SLAB, SLAB), SLAB)] * 0.5).astype(F32))
            uv_out[at, lanes] = (y * gate).astype(BF16)
            uv_out[at, width + s * SLAB : width + (s + 1) * SLAB] = (gate * rise * lead_row).astype(BF16)
            state[:, lanes] = old * fade_row + jnp.concatenate(grown, 1)

    lax.fori_loop(0, length // STEP_B, turn, 0)


def scan_part(order, part, info, token, x, z, bc, cum, cum_s, log_s, f_blk, rates):
    length, full = x.shape
    width = full // B_PARTS
    return pl.pallas_call(
        functools.partial(scan_kernel, order, part),
        in_specs=[SCALAR] + [FULL] * 8 + [ANY],
        out_specs=FULL,
        out_shape=pltpu.VMEM((length, 2 * width), BF16),
        scratch_shapes=[pltpu.VMEM((N, width), F32)],
        compiler_params=params(12),
        cost_estimate=CHEAP,
        name="scan_part",
    )(info, x, z, bc, cum, cum_s, log_s, f_blk, rates, token)


def norm_kernel(order, places, skip, fetched, info, bc, state, gain, _, *refs):
    uvs, refs = refs[:B_PARTS], refs[B_PARTS:]
    if order == 0:
        kept, refs = refs[0], refs[1:]
    weights, outs, tiles, sem = refs[:fetched], refs[fetched : -1 - fetched], refs[len(refs) - 1 - fetched : -1], refs[-1]
    copies = [
        pltpu.make_async_copy(weight.at[:, pl.ds(0, tile.shape[1])], tile, sem.at[k])
        for k, (weight, tile) in enumerate(zip(weights, tiles))
    ]
    for copy in copies:
        copy.start()
    count = outs[0].shape[0] * len(outs) // len(places)
    per = state.shape[1]
    part = per // B_PARTS

    def lanes(group, p=0, size=per):
        return pl.ds(pl.multiple_of(info[GROUP + group] * per + p * part, part), size)

    def rows(out, first, base, source):
        to = pl.ds(pl.multiple_of(first, ROWS_C), ROWS_C)
        at = pl.ds(pl.multiple_of(base, ROWS_C), ROWS_C)
        c_mat = bc[at, N : 2 * N]
        pieces = []
        squares = None
        for p, uv in enumerate(uvs):
            inc = state[:, p * part : (p + 1) * part]
            gated = uv[at, 0:part].astype(F32) + uv[at, part:].astype(F32) * dot(c_mat, inc)
            square = jnp.sum(gated * gated, axis=-1, keepdims=True)
            squares = square if squares is None else squares + square
            pieces.append(gated)
        scale = lax.rsqrt(squares * (1.0 / per) + EPS)
        for p, gated in enumerate(pieces):
            value = (gated * scale * gain[:, lanes(order, p, part)]).astype(BF16)
            if order == 0:
                out[to, lanes(0, p, part)] = value
            else:
                out[to, p * part : (p + 1) * part] = value
        if order == 0:
            out[to, lanes(1)] = kept[pl.ds(pl.multiple_of(source, ROWS_C), ROWS_C), :]

    for k, place in enumerate(places):

        def step(j, _):
            out, first = (outs[k], 0) if len(outs) > 1 else (outs[0], k * count)
            source = skip + k * count + j * ROWS_C
            rows(out, first + j * ROWS_C, info[ROWS + place] * count + j * ROWS_C, source)
            return 0

        lax.fori_loop(0, count // ROWS_C, step, 0)
    for copy in copies:
        copy.wait()


def norm_rows(order, places, info, count, token, bc, state, gain, uvs, kept=None, skip=0, apart=False, weights=(), columns=0):
    width = state.shape[1] if order else gain.shape[1]
    tile = jax.ShapeDtypeStruct((gain.shape[1], columns), BF16)
    arrays = len(places) if apart else 1
    rows = jax.ShapeDtypeStruct((len(places) * count // arrays, width), BF16)
    joined = [] if kept is None else [kept]
    return pl.pallas_call(
        functools.partial(norm_kernel, order, places, skip, len(weights)),
        in_specs=[SCALAR] + [FULL] * 3 + [ANY] + [FULL] * (len(uvs) + len(joined)) + [FAR] * len(weights),
        out_specs=[FULL] * (arrays + len(weights)),
        out_shape=[rows] * arrays + [tile] * len(weights),
        scratch_shapes=[pltpu.SemaphoreType.DMA((2,))],
        compiler_params=params(16),
        cost_estimate=CHEAP,
        name="norm_rows",
    )(info, bc, state, gain, token, *uvs, *joined, *weights)


def stream(base, w0_far, w1_far, w0, w1, sem):
    j = pl.program_id(0)
    tiles = pl.num_programs(0)

    def fetch(t):
        slot = lax.rem(t, SLOTS)
        lanes = pl.ds(pl.multiple_of((base + t) * TILE, TILE), TILE)
        return (
            pltpu.make_async_copy(w0_far.at[:, lanes], w0.at[slot], sem.at[0, slot]),
            pltpu.make_async_copy(w1_far.at[:, lanes], w1.at[slot], sem.at[1, slot]),
        )

    def start(t):
        @pl.when(t < tiles)
        def _():
            for copy in fetch(t):
                copy.start()

    @pl.when(j == 0)
    def _():
        for t in range(SLOTS - 1):
            start(t)

    start(j + SLOTS - 1)
    for copy in fetch(j):
        copy.wait()
    return lax.rem(j, SLOTS)


def buffers(depth):
    return [
        pltpu.VMEM((SLOTS, depth, TILE), BF16),
        pltpu.VMEM((SLOTS, depth, TILE), BF16),
        pltpu.SemaphoreType.DMA((2, SLOTS)),
    ]


def ahead_kernel(owns, mate, w0, w1, out):
    out[...] = (dot(owns[0 : out.shape[0], :], w0[...]) + dot(mate[...], w1[...])).astype(BF16)


def project_ahead(owns, mate, w0, w1):
    return pl.pallas_call(
        ahead_kernel,
        in_specs=[FULL] * 4,
        out_specs=FULL,
        out_shape=jax.ShapeDtypeStruct((owns.shape[0] // 2, w0.shape[1]), BF16),
        compiler_params=params(16),
        cost_estimate=CHEAP,
        name="project_ahead",
    )(owns, mate, w0, w1)


def join_kernel(first, second, _, out):
    rows = first.shape[0]
    out[0:rows, :] = first[...]
    out[rows:, :] = second[...]


def join(first, second, token):
    rows, depth = first.shape
    return pl.pallas_call(
        join_kernel,
        in_specs=[FULL, FULL, ANY],
        out_specs=FULL,
        out_shape=jax.ShapeDtypeStruct((2 * rows, depth), BF16),
        compiler_params=params(8),
        cost_estimate=CHEAP,
        name="join",
    )(first, second, token)


def both_kernel(base, cut, owns, mates, w0_far, w1_far, *refs):
    fars, near, w0, w1, sem = refs[:-4], *refs[-4:]
    rows = near.shape[0]
    slot = stream(base, w0_far, w1_far, w0, w1, sem)
    total = dot(owns[...], w0[slot]) + dot(mates[...], w1[slot])
    near[...] = total[rows:]
    for k, far_out in enumerate(fars):

        @pl.when(pl.program_id(0) // cut == k)
        def _():
            far_out[...] = total[0:rows].astype(BF16)


def project_both(owns, mates, w0, w1, first, count, chunk):
    rows, depth = owns.shape[0] // 2, owns.shape[1]
    cut = chunk // TILE
    chunks = count // chunk

    def placed(k):
        return pl.BlockSpec((rows, TILE), lambda j: (0, jnp.clip(j - k * cut, 0, cut - 1)))

    *fars, near = pl.pallas_call(
        functools.partial(both_kernel, first // TILE, cut),
        grid=(count // TILE,),
        in_specs=[FULL] * 2 + [FAR] * 2,
        out_specs=[placed(k) for k in range(chunks)] + [pl.BlockSpec((rows, TILE), lambda j: (0, j))],
        out_shape=[jax.ShapeDtypeStruct((rows, chunk), BF16)] * chunks + [jax.ShapeDtypeStruct((rows, count), F32)],
        scratch_shapes=buffers(depth),
        compiler_params=params(24),
        cost_estimate=CHEAP,
        name="project_both",
    )(owns, mates, w0, w1)
    return fars, near


def near_kernel(owns, mates, w0_far, w1_far, arrived, out, w0, w1, sem):
    slot = stream(0, w0_far, w1_far, w0, w1, sem)
    rows = out.shape[0]
    total = dot(owns[rows:, :], w0[slot]) + dot(mates[rows:, :], w1[slot])
    out[...] = (total + arrived[...].astype(F32)).astype(BF16)


def project_near(owns, mates, w0, w1, arrived):
    rows, depth = owns.shape[0] // 2, owns.shape[1]
    placed = pl.BlockSpec((rows, TILE), lambda j: (0, j))
    return pl.pallas_call(
        near_kernel,
        grid=(arrived.shape[1] // TILE,),
        in_specs=[FULL, FULL, FAR, FAR, placed],
        out_specs=placed,
        out_shape=jax.ShapeDtypeStruct((rows, w0.shape[1]), BF16),
        scratch_shapes=buffers(depth),
        compiler_params=params(20),
        cost_estimate=CHEAP,
        name="project_near",
    )(owns, mates, w0, w1, arrived)


def add_kernel(near, *refs):
    arrived, out = refs[:-2], refs[-1]
    chunk = arrived[0].shape[1]
    for k, part in enumerate(arrived):
        lanes = slice(k * chunk, (k + 1) * chunk)
        out[:, lanes] = (near[:, lanes] + part[...].astype(F32)).astype(BF16)


def add_chunks(near, first, arrived, result, at):
    rows, chunk = arrived[0].shape
    count = chunk * len(arrived)
    return pl.pallas_call(
        add_kernel,
        grid=(1,),
        in_specs=[pl.BlockSpec((rows, count), lambda j: (0, first // count))] + [FULL] * len(arrived) + [ANY],
        out_specs=pl.BlockSpec((rows, count), lambda j: (0, at // count)),
        out_shape=jax.ShapeDtypeStruct(result.shape, BF16),
        input_output_aliases={1 + len(arrived): 0},
        compiler_params=params(8),
        cost_estimate=CHEAP,
        name="add_chunks",
    )(near, *arrived, result)


def shift(block, distance):
    size = lax.axis_size("seq")
    return lax.ppermute(block, "seq", [(i, i + distance) for i in range(size - distance)])


def swap(block, axis, bit):
    return lax.ppermute(block, axis, [(i, i ^ bit) for i in range(lax.axis_size(axis))])


def rotate(block, distance):
    size = lax.axis_size("seq")
    return lax.ppermute(block, "seq", [(i, (i + distance) % size) for i in range(size)])


def log_steps(info, got, keep, rates_kept, done, pairs, scan_next):
    half = keep.shape[1]
    message = ((N + EXTRA, half), BF16)
    full = ((N, half), F32)
    msg, own, first, aux = combine(
        pair_kernel,
        (info, got, keep, rates_kept, done),
        [SCALAR, FULL, FULL, FULL, ANY],
        [message, full, full, ((16, half), F32)],
        "pair",
    )
    behind = None
    covered = 0
    while True:
        got = shift(msg, 2 * (covered + 1))
        done = scan_next(msg)
        covered = 2 * covered + 1
        if covered >= pairs - 1:
            break
        operands, specs = [got, own, aux], [FULL, FULL, FULL]
        if behind is None:
            kernel = lambda g, o, a, t, m, b: wave_kernel(g, o, a, None, t, m, b)
        else:
            kernel = wave_kernel
            operands.append(behind)
            specs.append(FULL)
        msg, behind = combine(kernel, operands + [done], specs + [ANY], [message, ((N + 8, half), F32)], "wave")
    operands, specs = [info, got], [SCALAR, FULL]
    if behind is None:
        kernel = lambda o, g, f, a, t, b, h: last_kernel(o, g, None, f, a, t, b, h)
    else:
        kernel = last_kernel
        operands.append(behind)
        specs.append(FULL)
    out = ((N, half), BF16)
    back, held = combine(kernel, operands + [first, aux, done], specs + [FULL, FULL, ANY], [out, out], "last")
    return back, held


def local(
    x_input,
    z_input,
    bc_input,
    conv_weight_x,
    conv_weight_bc,
    step_size,
    log_decay,
    skip_gain,
    norm_gain,
    out_weight,
):
    length, width = x_input.shape
    heads = step_size.shape[1]
    ways = lax.axis_size("head")
    pairs = lax.axis_size("seq") // 2
    mine = lax.axis_index("head")
    half = width // 2
    seq = lax.axis_index("seq")
    info = jnp.stack([seq & 1, mine ^ 3, mine ^ 2, mine ^ 1, mine, seq >> 1, seq, 1 - (seq & 1), seq & 1]).astype(jnp.int32)

    x_far, z_far, w_far = far(x_input, z_input, out_weight)
    (bc_far,) = far(bc_input)
    halo = rotate(tail_rows(x_far, bc_far), 1)
    bc = bc_input.reshape(length, -1)

    (cum, cum_s, log_s, f_dev, f_blk, rates), ones, x_sent = decays(
        info, log_decay, step_size, skip_gain, x_input, half
    )
    taps = far(conv_weight_x, conv_weight_bc)
    shared = (bc, halo, *taps)
    x0, bc0, send, x_kept = conv_states(0, info, x_sent, *shared, f_dev[0], ones, rates[0], x_far)
    got = swap(send, "seq", 1)
    (weight_mate,) = far(swap(lax.optimization_barrier((out_weight, send))[0], "head", 1))
    x1, bc1, keep, z_near = conv_states(1, info, x_kept, *shared, f_dev[1], ones, rates[1], z_far)
    rates_kept = rates[1]

    uvs = []
    groups = list(zip((x0, x1), (z_near, z_near), (bc0, bc1), cum, cum_s, log_s, f_blk, rates))

    def scan_next(token):
        if len(uvs) < 2 * B_PARTS:
            order, part = divmod(len(uvs), B_PARTS)
            uvs.append(scan_part(order, part, info, token, *groups[order]))
        return uvs[-1]

    full = ((N, half), F32)
    message = ((N + EXTRA, half), BF16)
    done = scan_next(keep)
    out = ((N, half), BF16)
    if pairs > 1 and half % (pairs * N) == 0:
        piece = half // pairs
        part = ((N + EXTRA, piece), BF16)
        first, aux, *parts = combine(
            pair_split_kernel,
            (info, got, keep, rates_kept, done),
            [SCALAR, FULL, FULL, FULL, ANY],
            [full, ((8, half), F32)] + [part] * pairs,
            "pair",
            [pltpu.VMEM(*message)],
        )
        parts = list(parts[:1]) + [rotate(parts[r], 2 * r) for r in range(1, pairs)]
        done = scan_next(parts[0])
        parts = combine(
            owner_kernel,
            [info] + parts + [done],
            [SCALAR] + [FULL] * pairs + [ANY],
            [((N, piece), BF16)] * pairs,
            "owner",
            [pltpu.VMEM((pairs, N + EXTRA, piece), BF16), pltpu.VMEM((pairs, N, piece), BF16)],
        )
        ready = parts[0]
        parts = list(parts[:1]) + [rotate(parts[r], 2 * r) for r in range(1, pairs)]
        done = scan_next(ready)
        back, held = combine(
            last_split_kernel,
            [info, first, aux, done] + parts,
            [SCALAR, FULL, FULL, ANY] + [FULL] * pairs,
            [out, out],
            "last",
            [pltpu.VMEM(*out)],
        )
    else:
        back, held = log_steps(info, got, keep, rates_kept, done, pairs, scan_next)
    other = swap(back, "seq", 1)
    while len(uvs) < 2 * B_PARTS:
        scan_next(back)

    count = length // ways
    gain = norm_gain[None, :]

    columns = out_weight.shape[1]
    chunk = columns // 8
    weights = (w_far, weight_mate)
    (kept,) = norm_rows(1, (0, 2, 1, 3), info, count, held, bc1, held, gain, uvs[B_PARTS:])
    shared = (bc0, other, gain, uvs[:B_PARTS], kept)
    far_mate, near_mate = norm_rows(0, (0, 2), info, count, kept, *shared, apart=True)
    owns, w0, w1 = norm_rows(0, (1, 3), info, count, far_mate, *shared, 2 * count, False, weights, chunk)
    far_mate = swap(far_mate, "head", 1)
    sent = project_ahead(owns, far_mate, w0, w1)
    first = swap(sent, "head", 2)
    operands = (owns, join(far_mate, swap(near_mate, "head", 1), sent), *weights)
    calls = []
    for lo, hi in ((1, 2), (2, 4), (4, 6), (6, 8)):
        sent, near = project_both(*operands, lo * chunk, (hi - lo) * chunk, chunk)
        calls.append((near, lo, [swap(part, "head", 2) for part in sent]))
    result = project_near(*operands, first)
    for near, lo, arrived in calls[:-1]:
        result = add_chunks(near, 0, arrived, result, lo * chunk)
    near, lo, arrived = calls[-1]
    for k, part in enumerate(arrived):
        result = add_chunks(near, k * chunk, [part], result, (lo + k) * chunk)
    return result


def solution(mesh):
    in_specs = (
        P("seq", "head"),
        P("seq", "head"),
        P("seq", "head", None),
        P(None, "head"),
        P(None, "head", None),
        P("seq", "head"),
        P("seq", "head"),
        P("head"),
        P("head"),
        P("head", None),
    )
    out_specs = P(("seq", "head"), None)
    return jax.shard_map(local, mesh=mesh, in_specs=in_specs, out_specs=out_specs, check_vma=False)
```

```python
import functools

import jax
import jax.numpy as jnp
from jax import lax
from jax.experimental import pallas as pl
from jax.experimental.pallas import tpu as pltpu
from jax.sharding import PartitionSpec as P

P_SIZE = 64
N = 128
KCONV = 4
EPS = 1e-05
LOG2E = 1.4426950408889634

TOK_A = 256
ROWS_A = 32
TOK_B = 128
STEP_B = 256
EXTRA = 16
SLAB = 256
ROWS_C = 128
TILE = 256
SLOTS = 4
LEAD = 16
B_PARTS = 2
HIGHEST = lax.Precision.HIGHEST
F32 = jnp.float32
BF16 = jnp.bfloat16


def params(mib):
    return pltpu.CompilerParams(vmem_limit_bytes=mib * 1024 * 1024)


CHEAP = pl.CostEstimate(flops=1, bytes_accessed=1, transcendentals=0)
SCALAR = pl.BlockSpec(memory_space=pltpu.SMEM)
FULL = pl.BlockSpec(memory_space=pltpu.VMEM)
FAR = pl.BlockSpec(memory_space=pltpu.HBM)
ANY = pl.BlockSpec(memory_space=pl.ANY)

ODD, ROWS, PAIR, SEQ, GROUP = 0, 1, 5, 6, 7


def dot(a, b, dims=((1,), (0,)), precision=None):
    return lax.dot_general(a, b, (dims, ((), ())), precision=precision, preferred_element_type=F32)


def half_silu(half):
    return half + half * jnp.tanh(half)


def far(*arrays):
    return [pltpu.with_memory_space_constraint(a, pltpu.HBM) for a in arrays]


def whole(shape):
    return pl.BlockSpec(shape, lambda *_: (0,) * len(shape))


def group_copies(x_far, x, group, sems):
    length, width = x.shape
    rows = length // 4
    lanes = pl.ds(pl.multiple_of(group * width, width), width)
    pieces = [pl.ds(k * rows, rows) for k in range(4)]
    return [pltpu.make_async_copy(x_far.at[at, lanes], x.at[at], sems.at[k]) for k, at in enumerate(pieces)]


def decay_kernel(info, ld_t, step_t, skip, *refs):
    cum, cum_s, log_s, f_dev, f_blk, rates = [refs[2 * k : 2 * k + 2] for k in range(6)]
    ones = refs[12]
    heads, length = ld_t.shape
    blocks = length // TOK_B
    per = heads // 2
    width = ones.shape[1]
    swapped = info[GROUP] == 1
    row = lax.broadcasted_iota(jnp.int32, (TOK_B, TOK_B), 0)
    col = lax.broadcasted_iota(jnp.int32, (TOK_B, TOK_B), 1)
    lower = (row >= col).astype(F32)
    upper = (row <= col).astype(F32)
    eye = (row == col).astype(BF16)

    def ordered(value):
        return jnp.where(swapped, jnp.concatenate([value[per:], value[:per]], 0), value)

    def put(ref, rows, value):
        high = value.astype(BF16)
        low = (value - high.astype(F32)).astype(BF16)
        for g in range(2):
            own = slice(g * per, (g + 1) * per)
            both = jnp.concatenate([high[own], low[own]], 0)
            ref[g][rows, :] = dot(eye, both, ((1,), (1,))).astype(BF16)

    first = lax.broadcasted_iota(jnp.int32, (per, width), 0) * P_SIZE
    lane = lax.broadcasted_iota(jnp.int32, (per, width), 1)
    member = ((lane >= first) & (lane < first + P_SIZE)).astype(F32)
    ones[0:per, :] = member.astype(BF16)
    ones[per:, :] = member.astype(BF16)
    cums, totals, row_totals = [], [], []
    for b in range(blocks):
        rows = slice(b * TOK_B, (b + 1) * TOK_B)
        logs = ordered(ld_t[:, rows]) * LOG2E
        c = dot(lower, logs, ((1,), (1,)), HIGHEST)
        for g in range(2):
            cum[g][rows, :] = c[:, g * per : (g + 1) * per]
        row_totals.append(c[TOK_B - 1 : TOK_B, :])
        c = dot(logs, upper, precision=HIGHEST)
        cums.append(c)
        totals.append(c[:, TOK_B - 1 : TOK_B])
    before, row_before = [jnp.zeros_like(totals[0])], [jnp.zeros_like(row_totals[0])]
    for b in range(blocks):
        before.append(before[-1] + totals[b])
        row_before.append(row_before[-1] + row_totals[b])
    total = before[-1]
    logs = jnp.concatenate(row_totals + row_before[:-1] + row_before[-1:] * 8, 0)
    gains = jnp.broadcast_to(skip[...], (8, heads))
    gains = jnp.where(swapped, jnp.concatenate([gains[:, per:], gains[:, :per]], 1), gains)
    values = jnp.concatenate([jnp.exp2(logs), gains], 0)
    for g in range(2):
        rates[g][...] = dot(values[:, g * per : (g + 1) * per], member, precision=HIGHEST)
    for b in range(blocks):
        rows = slice(b * TOK_B, (b + 1) * TOK_B)
        s = ordered(step_t[:, rows])
        log_step = jnp.log2(s)
        shifted = cums[b] - log_step
        fade = jnp.exp2(totals[b] - cums[b]) * s
        for g in range(2):
            own = slice(g * per, (g + 1) * per)
            log_s[g][:, rows] = log_step[own, :]
            cum_s[g][:, rows] = shifted[own, :]
            f_blk[g][:, rows] = fade[own, :]
        put(f_dev, rows, jnp.exp2(total - (cums[b] + before[b])) * s)


def decays(info, log_decay, step, skip, width):
    length, heads = log_decay.shape
    blocks = length // TOK_B
    per = heads // 2
    across = jax.ShapeDtypeStruct((per, length), F32)
    pair = jax.ShapeDtypeStruct((length, 2 * per), BF16)
    column = jax.ShapeDtypeStruct((length, per), F32)
    rates = jax.ShapeDtypeStruct((2 * blocks + 16, width), F32)
    shapes = [shape for shape in (column, across, across, pair, across, rates) for _ in range(2)]
    shapes += [
        jax.ShapeDtypeStruct((2 * per, width), BF16),
    ]
    *refs, ones = pl.pallas_call(
        decay_kernel,
        in_specs=[SCALAR] + [FULL] * 3,
        out_specs=[FULL] * len(shapes),
        out_shape=shapes,
        compiler_params=params(16),
        cost_estimate=CHEAP,
        name="decays",
    )(info, *far(log_decay.T, step.T, skip[None, :]))
    return [tuple(refs[2 * k : 2 * k + 2]) for k in range(6)], ones


def tail_kernel(x, bc, out):
    width, bc_width = x.shape[1], bc.shape[2]
    out[:, 0:width] = x[...]
    for g in range(bc.shape[1]):
        out[:, width + g * bc_width : width + (g + 1) * bc_width] = bc[:, g, :]


def tail_rows(x, bc):
    length, width = x.shape
    groups, bc_width = bc.shape[1:]
    at = length // LEAD - 1
    shape = (LEAD, width + groups * bc_width)
    return pl.pallas_call(
        tail_kernel,
        grid=(1,),
        in_specs=[
            pl.BlockSpec((LEAD, width), lambda i: (at, 0)),
            pl.BlockSpec((LEAD, groups, bc_width), lambda i: (at, 0, 0)),
        ],
        out_specs=whole(shape),
        out_shape=jax.ShapeDtypeStruct(shape, BF16),
        compiler_params=params(8),
        cost_estimate=CHEAP,
        name="tail_rows",
    )(x, bc)


def put_message(ref, state, decay):
    high = decay.astype(BF16)
    low = (decay - high.astype(F32)).astype(BF16)
    rest = jnp.zeros((EXTRA - 2, state.shape[1]), BF16)
    ref[0:N, :] = state.astype(BF16)
    ref[N:, :] = jnp.concatenate([high, low, rest], 0)


def take_message(ref):
    extra = ref[N:, :].astype(F32)
    return ref[0:N, :].astype(F32), extra[0:1] + extra[1:2]


def conv_kernel(order, info, x, bc, halo, wx, wbc, f_dev, ones, rates, *refs):
    next_far, refs = refs[0], refs[1:]
    x_out, bc_out, final = refs[:3]
    xf, state, down = refs[-3:]
    x_far, x, own_sem = (x, refs[5], refs[6]) if order == 0 else (None, x, None)
    length, width = x_out.shape
    rows = TOK_A
    group = info[GROUP + order]
    first_lane = pl.multiple_of(group * width, width)
    taken, sem = refs[3:5]
    first_bc = pl.multiple_of(group * 2 * N, 2 * N)
    if order == 0:
        copies = group_copies(next_far, taken, info[GROUP + 1], sem)
        for copy in group_copies(x_far, x, group, own_sem):
            copy.start()
    else:
        part = length // 4
        pieces = [pl.ds(k * part, part) for k in range(4)]
        copies = [pltpu.make_async_copy(next_far.at[at], taken.at[at], sem.at[k]) for k, at in enumerate(pieces)]
    for copy in copies:
        copy.start()
    state[...] = jnp.zeros_like(state)
    row = lax.broadcasted_iota(jnp.int32, down.shape, 0)
    col = lax.broadcasted_iota(jnp.int32, down.shape, 1)
    down[...] = (row == col + 1).astype(BF16)

    def conv(i, src, moved, first, behind, weights, emit):
        at_start = jnp.where(info[SEQ] == 0, jnp.zeros_like(first), first)
        lead = jnp.where(i == 0, at_start, behind).astype(F32)
        w0, w1, w2, w3 = [w * 0.5 for w in weights]
        back = LEAD - 8
        lead_r1 = pltpu.roll(lead, 1, 0)
        last_p = (w1 * lead + w0 * lead_r1)[back:]
        top = lax.broadcasted_iota(jnp.int32, (8, lead.shape[1]), 0) == 0
        head = jnp.where(top, jnp.broadcast_to(lead[LEAD - 1 :], top.shape), moved[0:8])
        for r in range(0, rows, ROWS_A):
            cur = src[r : r + ROWS_A].astype(F32)
            r1 = moved[r : r + ROWS_A] if r else jnp.concatenate([head, moved[8:ROWS_A]], 0)
            p = w1 * cur + w0 * r1
            p2 = pltpu.roll(jnp.concatenate([last_p, p], 0), 2, 0)[8:]
            emit(r, half_silu((w3 * cur + w2 * r1) + p2))
            last_p = p[ROWS_A - 8 :]

    def step(i, _):
        at = pl.ds(pl.multiple_of(i * rows, rows), rows)
        if order == 0:
            source = x_far.at[at, pl.ds(first_lane, width)]
            here = pltpu.make_async_copy(source, x.at[at], own_sem.at[i])
        behind = pl.ds(pl.multiple_of(jnp.maximum(i * rows - LEAD, 0), LEAD), LEAD)

        def out(r):
            return pl.ds(pl.multiple_of(i * rows + r, ROWS_A), ROWS_A)

        for lanes in range(0, 2 * N, SLAB):
            ds = slice(lanes, lanes + SLAB)
            src = pl.ds(pl.multiple_of(first_bc + lanes, SLAB), SLAB)
            halo_src = pl.ds(pl.multiple_of(2 * width + first_bc + lanes, SLAB), SLAB)

            def emit_bc(r, value):
                bc_out[out(r), ds] = value.astype(BF16)

            weights = [jnp.where(group == 0, wbc[k, 0:1, ds], wbc[k, 1:2, ds]) for k in range(KCONV)]
            conv(i, bc[at, src], dot(down[...], bc[at, src]), halo[:, halo_src], bc[behind, src], weights, emit_bc)

        if order == 0:
            here.wait()
        for lanes in range(0, width, SLAB):
            ds = slice(lanes, lanes + SLAB)
            src = pl.ds(pl.multiple_of(first_lane + lanes, SLAB), SLAB)
            scale = dot(f_dev[at, :], ones[:, ds])

            def emit(r, value):
                x_out[out(r), ds] = value.astype(BF16)
                xf[r : r + ROWS_A, ds] = (value * scale[r : r + ROWS_A]).astype(BF16)

            weights = [wx[k : k + 1, ds] for k in range(KCONV)]
            conv(i, x[at, ds], dot(down[...], x[at, ds]), halo[:, src], x[behind, ds], weights, emit)

        state[...] += dot(bc_out[at, 0:N], xf[...], ((0,), (0,)))
        return 0

    lax.fori_loop(0, length // rows, step, 0)
    if order == 0:
        row = rates.shape[0] - 16
        put_message(final, state[...], rates[row : row + 1, :])
    else:
        final[...] = state[...]
    for copy in copies:
        copy.wait()


def conv_states(order, info, x, bc, halo, wx, wbc, f_dev, ones, rates, ahead):
    length, width = bc.shape[0], ones.shape[1]
    column = lambda i, info: (0, info[GROUP + order])
    own = [] if order else [pltpu.VMEM((length, width), BF16), pltpu.SemaphoreType.DMA((4,))]
    final = ((N + EXTRA, width), BF16) if order == 0 else ((N, width), F32)
    taken = (length, width) if order == 0 else ahead.shape
    return pl.pallas_call(
        functools.partial(conv_kernel, order),
        grid_spec=pltpu.PrefetchScalarGridSpec(
            num_scalar_prefetch=1,
            grid=(1,),
            in_specs=[FULL if order else FAR] + [FULL] * 2 + [pl.BlockSpec((KCONV, width), column)] + [FULL] * 4 + [FAR],
            out_specs=[FULL] * 4,
            scratch_shapes=[
                pltpu.SemaphoreType.DMA((4,)),
                *own,
                pltpu.VMEM((TOK_A, width), BF16),
                pltpu.VMEM((N, width), F32),
                pltpu.VMEM((TOK_A, TOK_A), BF16),
            ],
        ),
        out_shape=[
            pltpu.VMEM((length, width), BF16),
            pltpu.VMEM((length, 2 * N), BF16),
            jax.ShapeDtypeStruct(*final),
            pltpu.VMEM(taken, BF16),
        ],
        compiler_params=params(16),
        cost_estimate=CHEAP,
        name="conv_states",
    )(info, x, bc, halo, wx, wbc, f_dev, ones, rates, ahead)


def pair_kernel(info, got, keep, rates, _, msg, own, first, aux):
    half = keep.shape[1]
    is_odd = info[ODD] == 1
    arrived, their = take_message(got)
    row = rates.shape[0] - 16
    mine = rates[row : row + 1, :]
    early = jnp.where(is_odd, arrived, keep[...])
    late = jnp.where(is_odd, keep[...], arrived)
    even_decay = jnp.where(is_odd, their, mine)
    odd_decay = jnp.where(is_odd, mine, their)
    state = odd_decay * early + late
    own[...] = state
    first[...] = early
    aux[0:8, :] = jnp.broadcast_to(even_decay, (8, half))
    aux[8:16, :] = jnp.broadcast_to(even_decay * odd_decay, (8, half))
    put_message(msg, state, even_decay * odd_decay)


def wave_kernel(got, own, aux, behind_in, _, msg, behind):
    before, decay = take_message(got)
    if behind_in is not None:
        before_decay = behind_in[N : N + 1, :]
        before = behind_in[0:N, :] + before_decay * before
        decay = before_decay * decay
    pair_decay = aux[8:9, :]
    behind[0:N, :] = before
    behind[N:, :] = jnp.broadcast_to(decay, (8, before.shape[1]))
    put_message(msg, own[...] + pair_decay * before, pair_decay * decay)


def last_kernel(info, got, behind_in, first, aux, _, back, held):
    is_odd = info[ODD] == 1
    before, _unused = take_message(got)
    if behind_in is not None:
        before = behind_in[0:N, :] + behind_in[N : N + 1, :] * before
    entering_odd = aux[0:1, :] * before + first[...]
    back[...] = jnp.where(is_odd, before, entering_odd).astype(BF16)
    held[...] = jnp.where(is_odd, entering_odd, before).astype(BF16)


def pair_split_kernel(info, got, keep, rates, _, first, aux, *refs):
    outs, wide = refs[:-1], refs[-1]
    half = keep.shape[1]
    pairs = len(outs)
    piece = half // pairs
    is_odd = info[ODD] == 1
    arrived, their = take_message(got)
    row = rates.shape[0] - 16
    mine = rates[row : row + 1, :]
    early = jnp.where(is_odd, arrived, keep[...])
    late = jnp.where(is_odd, keep[...], arrived)
    even_decay = jnp.where(is_odd, their, mine)
    odd_decay = jnp.where(is_odd, mine, their)
    first[...] = early
    aux[...] = jnp.broadcast_to(even_decay, (8, half))
    put_message(wide, odd_decay * early + late, even_decay * odd_decay)
    for r in range(pairs):
        owner = lax.rem(info[PAIR] + r, pairs)
        outs[r][...] = wide[:, pl.ds(pl.multiple_of(owner * piece, piece), piece)]


def owner_kernel(info, *refs):
    pairs = (len(refs) - 3) // 2
    ins, outs = refs[:pairs], refs[pairs + 1 : 2 * pairs + 1]
    states, prefixes = refs[-2:]
    for r in range(pairs):
        states[lax.rem(info[PAIR] + pairs - r, pairs)] = ins[r][...]
    before = jnp.zeros(prefixes.shape[1:], F32)
    for q in range(pairs):
        prefixes[q] = before.astype(BF16)
        if q < pairs - 1:
            state, decay = take_message(states.at[q])
            before = decay * before + state
    for r in range(pairs):
        outs[r][...] = prefixes[lax.rem(info[PAIR] + r, pairs)]


def last_split_kernel(info, first, aux, _, *refs):
    pairs = len(refs) - 3
    back, held, wide = refs[-3:]
    piece = back.shape[1] // pairs
    for r in range(pairs):
        owner = lax.rem(info[PAIR] + pairs - r, pairs)
        wide[:, pl.ds(pl.multiple_of(owner * piece, piece), piece)] = refs[r][...]
    is_odd = info[ODD] == 1
    before = wide[...].astype(F32)
    entering_odd = aux[0:1, :] * before + first[...]
    back[...] = jnp.where(is_odd, before, entering_odd).astype(BF16)
    held[...] = jnp.where(is_odd, entering_odd, before).astype(BF16)


def combine(kernel, operands, specs, outs, name, scratch=()):
    return pl.pallas_call(
        kernel,
        in_specs=specs,
        out_specs=[FULL] * len(outs),
        out_shape=[jax.ShapeDtypeStruct(s, t) for s, t in outs],
        scratch_shapes=list(scratch),
        compiler_params=params(16),
        cost_estimate=CHEAP,
        name=name,
    )(*operands)


def scan_kernel(order, part, info, x, z, bc, cum, cum_s, log_s, f_blk, rates, _, uv_out, state):
    length = x.shape[0]
    width = state.shape[1]
    per_slab = SLAB // P_SIZE
    inner = STEP_B // TOK_B
    blocks = length // TOK_B
    first_head = part * width // P_SIZE
    first_lane = info[GROUP + order] * x.shape[1] + part * width
    state[...] = jnp.zeros_like(state)

    row = lax.broadcasted_iota(jnp.int32, (TOK_B, TOK_B), 0)
    col = lax.broadcasted_iota(jnp.int32, (TOK_B, TOK_B), 1)
    keep = row >= col
    first = lax.broadcasted_iota(jnp.int32, (TOK_B, 2 * P_SIZE), 1) < P_SIZE
    zero = jnp.zeros((TOK_B, 2 * P_SIZE), BF16)

    def turn(step, _):
        for k in range(inner):
            block(step * inner + k)
        return 0

    def block(b):
        at = pl.ds(pl.multiple_of(b * TOK_B, TOK_B), TOK_B)
        b_mat = bc[at, 0:N]
        c_mat = bc[at, N : 2 * N]
        b_across = b_mat.T
        scores = jnp.where(keep, dot(c_mat, b_mat, ((1,), (1,))), 0.0)
        for s in range(width // SLAB):
            lanes = slice(s * SLAB, (s + 1) * SLAB)
            xb = x[at, part * width + s * SLAB : part * width + (s + 1) * SLAB]
            wide = slice(part * width + s * SLAB, part * width + (s + 1) * SLAB)
            fade_row = rates[pl.ds(b, 1), wide]
            lead_row = rates[pl.ds(blocks + b, 1), wide]
            skip = rates[2 * blocks + 8 : 2 * blocks + 9, wide]
            old = state[:, lanes]
            carried = dot(c_mat, old.astype(BF16))
            within, grown, rises = [], [], []
            for q in range(per_slab // 2):
                tables, fades, columns = [], [], []
                for h in (2 * q, 2 * q + 1):
                    head = first_head + s * per_slab + h
                    own = slice(head, head + 1)
                    column = jnp.broadcast_to(cum[at, own], (TOK_B, TOK_B))
                    gap = jnp.minimum(column - cum_s[own, at], log_s[own, at])
                    tables.append((scores * jnp.exp2(gap)).astype(BF16))
                    fades.append(b_across * f_blk[own, at].astype(BF16))
                    columns.append(column)
                xp = xb[:, q * 2 * P_SIZE : (q + 1) * 2 * P_SIZE]
                stacked = jnp.concatenate([jnp.where(first, xp, zero), jnp.where(first, zero, xp)], 0)
                both = jnp.concatenate([jnp.concatenate(tables, 1), jnp.concatenate(fades, 1)], 0)
                product = dot(both, stacked)
                within.append(product[0:TOK_B])
                grown.append(product[TOK_B:])
                rises.append(jnp.exp2(jnp.where(first, columns[0], columns[1])))
            rise = jnp.concatenate(rises, 1)
            xs = xb.astype(F32)
            y = jnp.concatenate(within, 1) + carried * rise + skip * xs
            gate = half_silu((z[at, pl.ds(pl.multiple_of(first_lane + s * SLAB, SLAB), SLAB)] * 0.5).astype(F32))
            uv_out[at, lanes] = (y * gate).astype(BF16)
            uv_out[at, width + s * SLAB : width + (s + 1) * SLAB] = (gate * rise * lead_row).astype(BF16)
            state[:, lanes] = old * fade_row + jnp.concatenate(grown, 1)

    lax.fori_loop(0, length // STEP_B, turn, 0)


def scan_part(order, part, info, token, x, z, bc, cum, cum_s, log_s, f_blk, rates):
    length, full = x.shape
    width = full // B_PARTS
    return pl.pallas_call(
        functools.partial(scan_kernel, order, part),
        in_specs=[SCALAR] + [FULL] * 8 + [ANY],
        out_specs=FULL,
        out_shape=pltpu.VMEM((length, 2 * width), BF16),
        scratch_shapes=[pltpu.VMEM((N, width), F32)],
        compiler_params=params(12),
        cost_estimate=CHEAP,
        name="scan_part",
    )(info, x, z, bc, cum, cum_s, log_s, f_blk, rates, token)


def norm_kernel(order, places, skip, fetched, info, bc, state, gain, _, *refs):
    uvs, refs = refs[:B_PARTS], refs[B_PARTS:]
    if order == 0:
        kept, refs = refs[0], refs[1:]
    weights, outs, tiles, sem = refs[:fetched], refs[fetched : -1 - fetched], refs[len(refs) - 1 - fetched : -1], refs[-1]
    copies = [
        pltpu.make_async_copy(weight.at[:, pl.ds(0, tile.shape[1])], tile, sem.at[k])
        for k, (weight, tile) in enumerate(zip(weights, tiles))
    ]
    for copy in copies:
        copy.start()
    count = outs[0].shape[0] * len(outs) // len(places)
    per = state.shape[1]
    part = per // B_PARTS

    def lanes(group, p=0, size=per):
        return pl.ds(pl.multiple_of(info[GROUP + group] * per + p * part, part), size)

    def rows(out, first, base, source):
        to = pl.ds(pl.multiple_of(first, ROWS_C), ROWS_C)
        at = pl.ds(pl.multiple_of(base, ROWS_C), ROWS_C)
        c_mat = bc[at, N : 2 * N]
        pieces = []
        squares = None
        for p, uv in enumerate(uvs):
            inc = state[:, p * part : (p + 1) * part]
            gated = uv[at, 0:part].astype(F32) + uv[at, part:].astype(F32) * dot(c_mat, inc)
            square = jnp.sum(gated * gated, axis=-1, keepdims=True)
            squares = square if squares is None else squares + square
            pieces.append(gated)
        scale = lax.rsqrt(squares * (1.0 / per) + EPS)
        for p, gated in enumerate(pieces):
            value = (gated * scale * gain[:, lanes(order, p, part)]).astype(BF16)
            if order == 0:
                out[to, lanes(0, p, part)] = value
            else:
                out[to, p * part : (p + 1) * part] = value
        if order == 0:
            out[to, lanes(1)] = kept[pl.ds(pl.multiple_of(source, ROWS_C), ROWS_C), :]

    for k, place in enumerate(places):

        def step(j, _):
            out, first = (outs[k], 0) if len(outs) > 1 else (outs[0], k * count)
            source = skip + k * count + j * ROWS_C
            rows(out, first + j * ROWS_C, info[ROWS + place] * count + j * ROWS_C, source)
            return 0

        lax.fori_loop(0, count // ROWS_C, step, 0)
    for copy in copies:
        copy.wait()


def norm_rows(order, places, info, count, token, bc, state, gain, uvs, kept=None, skip=0, apart=False, weights=(), columns=0):
    width = state.shape[1] if order else gain.shape[1]
    tile = jax.ShapeDtypeStruct((gain.shape[1], columns), BF16)
    arrays = len(places) if apart else 1
    rows = jax.ShapeDtypeStruct((len(places) * count // arrays, width), BF16)
    joined = [] if kept is None else [kept]
    return pl.pallas_call(
        functools.partial(norm_kernel, order, places, skip, len(weights)),
        in_specs=[SCALAR] + [FULL] * 3 + [ANY] + [FULL] * (len(uvs) + len(joined)) + [FAR] * len(weights),
        out_specs=[FULL] * (arrays + len(weights)),
        out_shape=[rows] * arrays + [tile] * len(weights),
        scratch_shapes=[pltpu.SemaphoreType.DMA((2,))],
        compiler_params=params(16),
        cost_estimate=CHEAP,
        name="norm_rows",
    )(info, bc, state, gain, token, *uvs, *joined, *weights)


def stream(base, w0_far, w1_far, w0, w1, sem):
    j = pl.program_id(0)
    tiles = pl.num_programs(0)

    def fetch(t):
        slot = lax.rem(t, SLOTS)
        lanes = pl.ds(pl.multiple_of((base + t) * TILE, TILE), TILE)
        return (
            pltpu.make_async_copy(w0_far.at[:, lanes], w0.at[slot], sem.at[0, slot]),
            pltpu.make_async_copy(w1_far.at[:, lanes], w1.at[slot], sem.at[1, slot]),
        )

    def start(t):
        @pl.when(t < tiles)
        def _():
            for copy in fetch(t):
                copy.start()

    @pl.when(j == 0)
    def _():
        for t in range(SLOTS - 1):
            start(t)

    start(j + SLOTS - 1)
    for copy in fetch(j):
        copy.wait()
    return lax.rem(j, SLOTS)


def buffers(depth):
    return [
        pltpu.VMEM((SLOTS, depth, TILE), BF16),
        pltpu.VMEM((SLOTS, depth, TILE), BF16),
        pltpu.SemaphoreType.DMA((2, SLOTS)),
    ]


def ahead_kernel(owns, mate, w0, w1, out):
    out[...] = (dot(owns[0 : out.shape[0], :], w0[...]) + dot(mate[...], w1[...])).astype(BF16)


def project_ahead(owns, mate, w0, w1):
    return pl.pallas_call(
        ahead_kernel,
        in_specs=[FULL] * 4,
        out_specs=FULL,
        out_shape=jax.ShapeDtypeStruct((owns.shape[0] // 2, w0.shape[1]), BF16),
        compiler_params=params(16),
        cost_estimate=CHEAP,
        name="project_ahead",
    )(owns, mate, w0, w1)


def join_kernel(first, second, _, out):
    rows = first.shape[0]
    out[0:rows, :] = first[...]
    out[rows:, :] = second[...]


def join(first, second, token):
    rows, depth = first.shape
    return pl.pallas_call(
        join_kernel,
        in_specs=[FULL, FULL, ANY],
        out_specs=FULL,
        out_shape=jax.ShapeDtypeStruct((2 * rows, depth), BF16),
        compiler_params=params(8),
        cost_estimate=CHEAP,
        name="join",
    )(first, second, token)


def both_kernel(base, cut, owns, mates, w0_far, w1_far, *refs):
    fars, near, w0, w1, sem = refs[:-4], *refs[-4:]
    rows = near.shape[0]
    slot = stream(base, w0_far, w1_far, w0, w1, sem)
    total = dot(owns[...], w0[slot]) + dot(mates[...], w1[slot])
    near[...] = total[rows:]
    for k, far_out in enumerate(fars):

        @pl.when(pl.program_id(0) // cut == k)
        def _():
            far_out[...] = total[0:rows].astype(BF16)


def project_both(owns, mates, w0, w1, first, count, chunk):
    rows, depth = owns.shape[0] // 2, owns.shape[1]
    cut = chunk // TILE
    chunks = count // chunk

    def placed(k):
        return pl.BlockSpec((rows, TILE), lambda j: (0, jnp.clip(j - k * cut, 0, cut - 1)))

    *fars, near = pl.pallas_call(
        functools.partial(both_kernel, first // TILE, cut),
        grid=(count // TILE,),
        in_specs=[FULL] * 2 + [FAR] * 2,
        out_specs=[placed(k) for k in range(chunks)] + [pl.BlockSpec((rows, TILE), lambda j: (0, j))],
        out_shape=[jax.ShapeDtypeStruct((rows, chunk), BF16)] * chunks + [jax.ShapeDtypeStruct((rows, count), F32)],
        scratch_shapes=buffers(depth),
        compiler_params=params(24),
        cost_estimate=CHEAP,
        name="project_both",
    )(owns, mates, w0, w1)
    return fars, near


def near_kernel(owns, mates, w0_far, w1_far, arrived, out, w0, w1, sem):
    slot = stream(0, w0_far, w1_far, w0, w1, sem)
    rows = out.shape[0]
    total = dot(owns[rows:, :], w0[slot]) + dot(mates[rows:, :], w1[slot])
    out[...] = (total + arrived[...].astype(F32)).astype(BF16)


def project_near(owns, mates, w0, w1, arrived):
    rows, depth = owns.shape[0] // 2, owns.shape[1]
    placed = pl.BlockSpec((rows, TILE), lambda j: (0, j))
    return pl.pallas_call(
        near_kernel,
        grid=(arrived.shape[1] // TILE,),
        in_specs=[FULL, FULL, FAR, FAR, placed],
        out_specs=placed,
        out_shape=jax.ShapeDtypeStruct((rows, w0.shape[1]), BF16),
        scratch_shapes=buffers(depth),
        compiler_params=params(20),
        cost_estimate=CHEAP,
        name="project_near",
    )(owns, mates, w0, w1, arrived)


def add_kernel(near, *refs):
    arrived, out = refs[:-2], refs[-1]
    chunk = arrived[0].shape[1]
    for k, part in enumerate(arrived):
        lanes = slice(k * chunk, (k + 1) * chunk)
        out[:, lanes] = (near[:, lanes] + part[...].astype(F32)).astype(BF16)


def add_chunks(near, first, arrived, result, at):
    rows, chunk = arrived[0].shape
    count = chunk * len(arrived)
    return pl.pallas_call(
        add_kernel,
        grid=(1,),
        in_specs=[pl.BlockSpec((rows, count), lambda j: (0, first // count))] + [FULL] * len(arrived) + [ANY],
        out_specs=pl.BlockSpec((rows, count), lambda j: (0, at // count)),
        out_shape=jax.ShapeDtypeStruct(result.shape, BF16),
        input_output_aliases={1 + len(arrived): 0},
        compiler_params=params(8),
        cost_estimate=CHEAP,
        name="add_chunks",
    )(near, *arrived, result)


def shift(block, distance):
    size = lax.axis_size("seq")
    return lax.ppermute(block, "seq", [(i, i + distance) for i in range(size - distance)])


def swap(block, axis, bit):
    return lax.ppermute(block, axis, [(i, i ^ bit) for i in range(lax.axis_size(axis))])


def rotate(block, distance):
    size = lax.axis_size("seq")
    return lax.ppermute(block, "seq", [(i, (i + distance) % size) for i in range(size)])


def log_steps(info, got, keep, rates_kept, done, pairs, scan_next):
    half = keep.shape[1]
    message = ((N + EXTRA, half), BF16)
    full = ((N, half), F32)
    msg, own, first, aux = combine(
        pair_kernel,
        (info, got, keep, rates_kept, done),
        [SCALAR, FULL, FULL, FULL, ANY],
        [message, full, full, ((16, half), F32)],
        "pair",
    )
    behind = None
    covered = 0
    while True:
        got = shift(msg, 2 * (covered + 1))
        done = scan_next(msg)
        covered = 2 * covered + 1
        if covered >= pairs - 1:
            break
        operands, specs = [got, own, aux], [FULL, FULL, FULL]
        if behind is None:
            kernel = lambda g, o, a, t, m, b: wave_kernel(g, o, a, None, t, m, b)
        else:
            kernel = wave_kernel
            operands.append(behind)
            specs.append(FULL)
        msg, behind = combine(kernel, operands + [done], specs + [ANY], [message, ((N + 8, half), F32)], "wave")
    operands, specs = [info, got], [SCALAR, FULL]
    if behind is None:
        kernel = lambda o, g, f, a, t, b, h: last_kernel(o, g, None, f, a, t, b, h)
    else:
        kernel = last_kernel
        operands.append(behind)
        specs.append(FULL)
    out = ((N, half), BF16)
    back, held = combine(kernel, operands + [first, aux, done], specs + [FULL, FULL, ANY], [out, out], "last")
    return back, held


def local(
    x_input,
    z_input,
    bc_input,
    conv_weight_x,
    conv_weight_bc,
    step_size,
    log_decay,
    skip_gain,
    norm_gain,
    out_weight,
):
    length, width = x_input.shape
    heads = step_size.shape[1]
    ways = lax.axis_size("head")
    pairs = lax.axis_size("seq") // 2
    mine = lax.axis_index("head")
    half = width // 2
    seq = lax.axis_index("seq")
    info = jnp.stack([seq & 1, mine ^ 3, mine ^ 2, mine ^ 1, mine, seq >> 1, seq, 1 - (seq & 1), seq & 1]).astype(jnp.int32)

    x_far, z_far, w_far = far(x_input, z_input, out_weight)
    (bc_far,) = far(bc_input)
    halo = rotate(tail_rows(x_far, bc_far), 1)
    bc = bc_input.reshape(length, -1)
    (weight_mate,) = far(swap(out_weight, "head", 1))

    (cum, cum_s, log_s, f_dev, f_blk, rates), ones = decays(info, log_decay, step_size, skip_gain, half)
    taps = far(conv_weight_x, conv_weight_bc)
    shared = (bc, halo, *taps)
    x0, bc0, send, x_kept = conv_states(0, info, x_far, *shared, f_dev[0], ones, rates[0], x_far)
    got = swap(send, "seq", 1)
    x1, bc1, keep, z_near = conv_states(1, info, x_kept, *shared, f_dev[1], ones, rates[1], z_far)
    rates_kept = rates[1]

    uvs = []
    groups = list(zip((x0, x1), (z_near, z_near), (bc0, bc1), cum, cum_s, log_s, f_blk, rates))

    def scan_next(token):
        if len(uvs) < 2 * B_PARTS:
            order, part = divmod(len(uvs), B_PARTS)
            uvs.append(scan_part(order, part, info, token, *groups[order]))
        return uvs[-1]

    full = ((N, half), F32)
    message = ((N + EXTRA, half), BF16)
    done = scan_next(keep)
    out = ((N, half), BF16)
    if pairs > 1 and half % (pairs * N) == 0:
        piece = half // pairs
        part = ((N + EXTRA, piece), BF16)
        first, aux, *parts = combine(
            pair_split_kernel,
            (info, got, keep, rates_kept, done),
            [SCALAR, FULL, FULL, FULL, ANY],
            [full, ((8, half), F32)] + [part] * pairs,
            "pair",
            [pltpu.VMEM(*message)],
        )
        parts = list(parts[:1]) + [rotate(parts[r], 2 * r) for r in range(1, pairs)]
        done = scan_next(parts[0])
        parts = combine(
            owner_kernel,
            [info] + parts + [done],
            [SCALAR] + [FULL] * pairs + [ANY],
            [((N, piece), BF16)] * pairs,
            "owner",
            [pltpu.VMEM((pairs, N + EXTRA, piece), BF16), pltpu.VMEM((pairs, N, piece), BF16)],
        )
        ready = parts[0]
        parts = list(parts[:1]) + [rotate(parts[r], 2 * r) for r in range(1, pairs)]
        done = scan_next(ready)
        back, held = combine(
            last_split_kernel,
            [info, first, aux, done] + parts,
            [SCALAR, FULL, FULL, ANY] + [FULL] * pairs,
            [out, out],
            "last",
            [pltpu.VMEM(*out)],
        )
    else:
        back, held = log_steps(info, got, keep, rates_kept, done, pairs, scan_next)
    other = swap(back, "seq", 1)
    while len(uvs) < 2 * B_PARTS:
        scan_next(back)

    count = length // ways
    gain = norm_gain[None, :]

    columns = out_weight.shape[1]
    chunk = columns // 8
    weights = (w_far, weight_mate)
    kept, w0, w1 = norm_rows(
        1, (0, 2, 1, 3), info, count, held, bc1, held, gain, uvs[B_PARTS:], weights=weights, columns=chunk
    )
    shared = (bc0, other, gain, uvs[:B_PARTS], kept)
    far_mate, near_mate = norm_rows(0, (0, 2), info, count, kept, *shared, apart=True)
    (owns,) = norm_rows(0, (1, 3), info, count, far_mate, *shared, 2 * count)
    far_mate = swap(far_mate, "head", 1)
    sent = project_ahead(owns, far_mate, w0, w1)
    first = swap(sent, "head", 2)
    operands = (owns, join(far_mate, swap(near_mate, "head", 1), sent), *weights)
    calls = []
    for lo, hi in ((1, 2), (2, 4), (4, 6), (6, 8)):
        sent, near = project_both(*operands, lo * chunk, (hi - lo) * chunk, chunk)
        calls.append((near, lo, [swap(part, "head", 2) for part in sent]))
    result = project_near(*operands, first)
    for near, lo, arrived in calls[:-1]:
        result = add_chunks(near, 0, arrived, result, lo * chunk)
    near, lo, arrived = calls[-1]
    for k, part in enumerate(arrived):
        result = add_chunks(near, k * chunk, [part], result, (lo + k) * chunk)
    return result


def solution(mesh):
    in_specs = (
        P("seq", "head"),
        P("seq", "head"),
        P("seq", "head", None),
        P(None, "head"),
        P(None, "head", None),
        P("seq", "head"),
        P("seq", "head"),
        P("head"),
        P("head"),
        P("head", None),
    )
    out_specs = P(("seq", "head"), None)
    return jax.shard_map(local, mesh=mesh, in_specs=in_specs, out_specs=out_specs, check_vma=False)
```

```python
import functools

import jax
import jax.numpy as jnp
from jax import lax
from jax.experimental import pallas as pl
from jax.experimental.pallas import tpu as pltpu
from jax.sharding import PartitionSpec as P

P_SIZE = 64
N = 128
KCONV = 4
EPS = 1e-05
LOG2E = 1.4426950408889634

TOK_A = 256
ROWS_A = 32
TOK_B = 128
STEP_B = 256
EXTRA = 16
SLAB = 256
ROWS_C = 128
TILE = 256
SLOTS = 4
LEAD = 16
B_PARTS = 2
HIGHEST = lax.Precision.HIGHEST
F32 = jnp.float32
BF16 = jnp.bfloat16


def params(mib):
    return pltpu.CompilerParams(vmem_limit_bytes=mib * 1024 * 1024)


CHEAP = pl.CostEstimate(flops=1, bytes_accessed=1, transcendentals=0)
SCALAR = pl.BlockSpec(memory_space=pltpu.SMEM)
FULL = pl.BlockSpec(memory_space=pltpu.VMEM)
FAR = pl.BlockSpec(memory_space=pltpu.HBM)
ANY = pl.BlockSpec(memory_space=pl.ANY)

ODD, ROWS, PAIR, SEQ, GROUP = 0, 1, 5, 6, 7


def dot(a, b, dims=((1,), (0,)), precision=None):
    return lax.dot_general(a, b, (dims, ((), ())), precision=precision, preferred_element_type=F32)


def half_silu(half):
    return half + half * jnp.tanh(half)


def far(*arrays):
    return [pltpu.with_memory_space_constraint(a, pltpu.HBM) for a in arrays]


def whole(shape):
    return pl.BlockSpec(shape, lambda *_: (0,) * len(shape))


def group_copies(x_far, x, group, sems):
    length, width = x.shape
    rows = length // 4
    lanes = pl.ds(pl.multiple_of(group * width, width), width)
    pieces = [pl.ds(k * rows, rows) for k in range(4)]
    return [pltpu.make_async_copy(x_far.at[at, lanes], x.at[at], sems.at[k]) for k, at in enumerate(pieces)]


def decay_kernel(info, ld_t, step_t, skip, *refs):
    cum, cum_s, log_s, f_dev, f_blk, rates = [refs[2 * k : 2 * k + 2] for k in range(6)]
    ones = refs[12]
    heads, length = ld_t.shape
    blocks = length // TOK_B
    per = heads // 2
    width = ones.shape[1]
    swapped = info[GROUP] == 1
    row = lax.broadcasted_iota(jnp.int32, (TOK_B, TOK_B), 0)
    col = lax.broadcasted_iota(jnp.int32, (TOK_B, TOK_B), 1)
    lower = (row >= col).astype(F32)
    upper = (row <= col).astype(F32)
    eye = (row == col).astype(BF16)

    def ordered(value):
        return jnp.where(swapped, jnp.concatenate([value[per:], value[:per]], 0), value)

    def put(ref, rows, value):
        high = value.astype(BF16)
        low = (value - high.astype(F32)).astype(BF16)
        for g in range(2):
            own = slice(g * per, (g + 1) * per)
            both = jnp.concatenate([high[own], low[own]], 0)
            ref[g][rows, :] = dot(eye, both, ((1,), (1,))).astype(BF16)

    first = lax.broadcasted_iota(jnp.int32, (per, width), 0) * P_SIZE
    lane = lax.broadcasted_iota(jnp.int32, (per, width), 1)
    member = ((lane >= first) & (lane < first + P_SIZE)).astype(F32)
    ones[0:per, :] = member.astype(BF16)
    ones[per:, :] = member.astype(BF16)
    cums, totals, row_totals = [], [], []
    for b in range(blocks):
        rows = slice(b * TOK_B, (b + 1) * TOK_B)
        logs = ordered(ld_t[:, rows]) * LOG2E
        c = dot(lower, logs, ((1,), (1,)), HIGHEST)
        for g in range(2):
            cum[g][rows, :] = c[:, g * per : (g + 1) * per]
        row_totals.append(c[TOK_B - 1 : TOK_B, :])
        c = dot(logs, upper, precision=HIGHEST)
        cums.append(c)
        totals.append(c[:, TOK_B - 1 : TOK_B])
    before, row_before = [jnp.zeros_like(totals[0])], [jnp.zeros_like(row_totals[0])]
    for b in range(blocks):
        before.append(before[-1] + totals[b])
        row_before.append(row_before[-1] + row_totals[b])
    total = before[-1]
    logs = jnp.concatenate(row_totals + row_before[:-1] + row_before[-1:] * 8, 0)
    gains = jnp.broadcast_to(skip[...], (8, heads))
    gains = jnp.where(swapped, jnp.concatenate([gains[:, per:], gains[:, :per]], 1), gains)
    values = jnp.concatenate([jnp.exp2(logs), gains], 0)
    for g in range(2):
        rates[g][...] = dot(values[:, g * per : (g + 1) * per], member, precision=HIGHEST)
    for b in range(blocks):
        rows = slice(b * TOK_B, (b + 1) * TOK_B)
        s = ordered(step_t[:, rows])
        log_step = jnp.log2(s)
        shifted = cums[b] - log_step
        fade = jnp.exp2(totals[b] - cums[b]) * s
        for g in range(2):
            own = slice(g * per, (g + 1) * per)
            log_s[g][:, rows] = log_step[own, :]
            cum_s[g][:, rows] = shifted[own, :]
            f_blk[g][:, rows] = fade[own, :]
        put(f_dev, rows, jnp.exp2(total - (cums[b] + before[b])) * s)


def decays(info, log_decay, step, skip, width):
    length, heads = log_decay.shape
    blocks = length // TOK_B
    per = heads // 2
    across = jax.ShapeDtypeStruct((per, length), F32)
    pair = jax.ShapeDtypeStruct((length, 2 * per), BF16)
    column = jax.ShapeDtypeStruct((length, per), F32)
    rates = jax.ShapeDtypeStruct((2 * blocks + 16, width), F32)
    shapes = [shape for shape in (column, across, across, pair, across, rates) for _ in range(2)]
    shapes += [
        jax.ShapeDtypeStruct((2 * per, width), BF16),
    ]
    *refs, ones = pl.pallas_call(
        decay_kernel,
        in_specs=[SCALAR] + [FULL] * 3,
        out_specs=[FULL] * len(shapes),
        out_shape=shapes,
        compiler_params=params(16),
        cost_estimate=CHEAP,
        name="decays",
    )(info, *far(log_decay.T, step.T, skip[None, :]))
    return [tuple(refs[2 * k : 2 * k + 2]) for k in range(6)], ones


def tail_kernel(x, bc, out):
    width, bc_width = x.shape[1], bc.shape[2]
    out[:, 0:width] = x[...]
    for g in range(bc.shape[1]):
        out[:, width + g * bc_width : width + (g + 1) * bc_width] = bc[:, g, :]


def tail_rows(x, bc):
    length, width = x.shape
    groups, bc_width = bc.shape[1:]
    at = length // LEAD - 1
    shape = (LEAD, width + groups * bc_width)
    return pl.pallas_call(
        tail_kernel,
        grid=(1,),
        in_specs=[
            pl.BlockSpec((LEAD, width), lambda i: (at, 0)),
            pl.BlockSpec((LEAD, groups, bc_width), lambda i: (at, 0, 0)),
        ],
        out_specs=whole(shape),
        out_shape=jax.ShapeDtypeStruct(shape, BF16),
        compiler_params=params(8),
        cost_estimate=CHEAP,
        name="tail_rows",
    )(x, bc)


def put_message(ref, state, decay):
    high = decay.astype(BF16)
    low = (decay - high.astype(F32)).astype(BF16)
    rest = jnp.zeros((EXTRA - 2, state.shape[1]), BF16)
    ref[0:N, :] = state.astype(BF16)
    ref[N:, :] = jnp.concatenate([high, low, rest], 0)


def take_message(ref):
    extra = ref[N:, :].astype(F32)
    return ref[0:N, :].astype(F32), extra[0:1] + extra[1:2]


def conv_kernel(order, info, x, bc, halo, wx, wbc, f_dev, ones, rates, *refs):
    next_far, refs = refs[0], refs[1:]
    x_out, bc_out, final = refs[:3]
    xf, state, down = refs[-3:]
    x_far, x, own_sem = (x, refs[5], refs[6]) if order == 0 else (None, x, None)
    length, width = x_out.shape
    rows = TOK_A
    group = info[GROUP + order]
    first_lane = pl.multiple_of(group * width, width)
    taken, sem = refs[3:5]
    first_bc = pl.multiple_of(group * 2 * N, 2 * N)
    if order == 0:
        copies = group_copies(next_far, taken, info[GROUP + 1], sem)
        for copy in group_copies(x_far, x, group, own_sem):
            copy.start()
    else:
        part = length // 4
        pieces = [pl.ds(k * part, part) for k in range(4)]
        copies = [pltpu.make_async_copy(next_far.at[at], taken.at[at], sem.at[k]) for k, at in enumerate(pieces)]
    for copy in copies:
        copy.start()
    state[...] = jnp.zeros_like(state)
    row = lax.broadcasted_iota(jnp.int32, down.shape, 0)
    col = lax.broadcasted_iota(jnp.int32, down.shape, 1)
    down[...] = (row == col + 1).astype(BF16)

    def conv(i, src, moved, first, behind, weights, emit):
        at_start = jnp.where(info[SEQ] == 0, jnp.zeros_like(first), first)
        lead = jnp.where(i == 0, at_start, behind).astype(F32)
        w0, w1, w2, w3 = [w * 0.5 for w in weights]
        back = LEAD - 8
        lead_r1 = pltpu.roll(lead, 1, 0)
        last_p = (w1 * lead + w0 * lead_r1)[back:]
        top = lax.broadcasted_iota(jnp.int32, (8, lead.shape[1]), 0) == 0
        head = jnp.where(top, jnp.broadcast_to(lead[LEAD - 1 :], top.shape), moved[0:8])
        for r in range(0, rows, ROWS_A):
            cur = src[r : r + ROWS_A].astype(F32)
            r1 = moved[r : r + ROWS_A] if r else jnp.concatenate([head, moved[8:ROWS_A]], 0)
            p = w1 * cur + w0 * r1
            p2 = pltpu.roll(jnp.concatenate([last_p, p], 0), 2, 0)[8:]
            emit(r, half_silu((w3 * cur + w2 * r1) + p2))
            last_p = p[ROWS_A - 8 :]

    def step(i, _):
        at = pl.ds(pl.multiple_of(i * rows, rows), rows)
        if order == 0:
            source = x_far.at[at, pl.ds(first_lane, width)]
            here = pltpu.make_async_copy(source, x.at[at], own_sem.at[i])
        behind = pl.ds(pl.multiple_of(jnp.maximum(i * rows - LEAD, 0), LEAD), LEAD)

        def out(r):
            return pl.ds(pl.multiple_of(i * rows + r, ROWS_A), ROWS_A)

        for lanes in range(0, 2 * N, SLAB):
            ds = slice(lanes, lanes + SLAB)
            src = pl.ds(pl.multiple_of(first_bc + lanes, SLAB), SLAB)
            halo_src = pl.ds(pl.multiple_of(2 * width + first_bc + lanes, SLAB), SLAB)

            def emit_bc(r, value):
                bc_out[out(r), ds] = value.astype(BF16)

            weights = [jnp.where(group == 0, wbc[k, 0:1, ds], wbc[k, 1:2, ds]) for k in range(KCONV)]
            conv(i, bc[at, src], dot(down[...], bc[at, src]), halo[:, halo_src], bc[behind, src], weights, emit_bc)

        if order == 0:
            here.wait()
        for lanes in range(0, width, SLAB):
            ds = slice(lanes, lanes + SLAB)
            src = pl.ds(pl.multiple_of(first_lane + lanes, SLAB), SLAB)
            scale = dot(f_dev[at, :], ones[:, ds])

            def emit(r, value):
                x_out[out(r), ds] = value.astype(BF16)
                xf[r : r + ROWS_A, ds] = (value * scale[r : r + ROWS_A]).astype(BF16)

            weights = [wx[k : k + 1, ds] for k in range(KCONV)]
            conv(i, x[at, ds], dot(down[...], x[at, ds]), halo[:, src], x[behind, ds], weights, emit)

        state[...] += dot(bc_out[at, 0:N], xf[...], ((0,), (0,)))
        return 0

    lax.fori_loop(0, length // rows, step, 0)
    if order == 0:
        row = rates.shape[0] - 16
        put_message(final, state[...], rates[row : row + 1, :])
    else:
        final[...] = state[...]
    for copy in copies:
        copy.wait()


def conv_states(order, info, x, bc, halo, wx, wbc, f_dev, ones, rates, ahead):
    length, width = bc.shape[0], ones.shape[1]
    column = lambda i, info: (0, info[GROUP + order])
    own = [] if order else [pltpu.VMEM((length, width), BF16), pltpu.SemaphoreType.DMA((4,))]
    final = ((N + EXTRA, width), BF16) if order == 0 else ((N, width), F32)
    taken = (length, width) if order == 0 else ahead.shape
    return pl.pallas_call(
        functools.partial(conv_kernel, order),
        grid_spec=pltpu.PrefetchScalarGridSpec(
            num_scalar_prefetch=1,
            grid=(1,),
            in_specs=[FULL if order else FAR] + [FULL] * 2 + [pl.BlockSpec((KCONV, width), column)] + [FULL] * 4 + [FAR],
            out_specs=[FULL] * 4,
            scratch_shapes=[
                pltpu.SemaphoreType.DMA((4,)),
                *own,
                pltpu.VMEM((TOK_A, width), BF16),
                pltpu.VMEM((N, width), F32),
                pltpu.VMEM((TOK_A, TOK_A), BF16),
            ],
        ),
        out_shape=[
            pltpu.VMEM((length, width), BF16),
            pltpu.VMEM((length, 2 * N), BF16),
            jax.ShapeDtypeStruct(*final),
            pltpu.VMEM(taken, BF16),
        ],
        compiler_params=params(16),
        cost_estimate=CHEAP,
        name="conv_states",
    )(info, x, bc, halo, wx, wbc, f_dev, ones, rates, ahead)


def pair_kernel(info, got, keep, rates, _, msg, own, first, aux):
    half = keep.shape[1]
    is_odd = info[ODD] == 1
    arrived, their = take_message(got)
    row = rates.shape[0] - 16
    mine = rates[row : row + 1, :]
    early = jnp.where(is_odd, arrived, keep[...])
    late = jnp.where(is_odd, keep[...], arrived)
    even_decay = jnp.where(is_odd, their, mine)
    odd_decay = jnp.where(is_odd, mine, their)
    state = odd_decay * early + late
    own[...] = state
    first[...] = early
    aux[0:8, :] = jnp.broadcast_to(even_decay, (8, half))
    aux[8:16, :] = jnp.broadcast_to(even_decay * odd_decay, (8, half))
    put_message(msg, state, even_decay * odd_decay)


def wave_kernel(got, own, aux, behind_in, _, msg, behind):
    before, decay = take_message(got)
    if behind_in is not None:
        before_decay = behind_in[N : N + 1, :]
        before = behind_in[0:N, :] + before_decay * before
        decay = before_decay * decay
    pair_decay = aux[8:9, :]
    behind[0:N, :] = before
    behind[N:, :] = jnp.broadcast_to(decay, (8, before.shape[1]))
    put_message(msg, own[...] + pair_decay * before, pair_decay * decay)


def last_kernel(info, got, behind_in, first, aux, _, back, held):
    is_odd = info[ODD] == 1
    before, _unused = take_message(got)
    if behind_in is not None:
        before = behind_in[0:N, :] + behind_in[N : N + 1, :] * before
    entering_odd = aux[0:1, :] * before + first[...]
    back[...] = jnp.where(is_odd, before, entering_odd).astype(BF16)
    held[...] = jnp.where(is_odd, entering_odd, before).astype(BF16)


def pair_split_kernel(info, got, keep, rates, _, first, aux, *refs):
    outs, wide = refs[:-1], refs[-1]
    half = keep.shape[1]
    pairs = len(outs)
    piece = half // pairs
    is_odd = info[ODD] == 1
    arrived, their = take_message(got)
    row = rates.shape[0] - 16
    mine = rates[row : row + 1, :]
    early = jnp.where(is_odd, arrived, keep[...])
    late = jnp.where(is_odd, keep[...], arrived)
    even_decay = jnp.where(is_odd, their, mine)
    odd_decay = jnp.where(is_odd, mine, their)
    first[...] = early
    aux[...] = jnp.broadcast_to(even_decay, (8, half))
    put_message(wide, odd_decay * early + late, even_decay * odd_decay)
    for r in range(pairs):
        owner = lax.rem(info[PAIR] + r, pairs)
        outs[r][...] = wide[:, pl.ds(pl.multiple_of(owner * piece, piece), piece)]


def owner_kernel(info, *refs):
    pairs = (len(refs) - 3) // 2
    ins, outs = refs[:pairs], refs[pairs + 1 : 2 * pairs + 1]
    states, prefixes = refs[-2:]
    for r in range(pairs):
        states[lax.rem(info[PAIR] + pairs - r, pairs)] = ins[r][...]
    before = jnp.zeros(prefixes.shape[1:], F32)
    for q in range(pairs):
        prefixes[q] = before.astype(BF16)
        if q < pairs - 1:
            state, decay = take_message(states.at[q])
            before = decay * before + state
    for r in range(pairs):
        outs[r][...] = prefixes[lax.rem(info[PAIR] + r, pairs)]


def last_split_kernel(info, first, aux, _, *refs):
    pairs = len(refs) - 3
    back, held, wide = refs[-3:]
    piece = back.shape[1] // pairs
    for r in range(pairs):
        owner = lax.rem(info[PAIR] + pairs - r, pairs)
        wide[:, pl.ds(pl.multiple_of(owner * piece, piece), piece)] = refs[r][...]
    is_odd = info[ODD] == 1
    before = wide[...].astype(F32)
    entering_odd = aux[0:1, :] * before + first[...]
    back[...] = jnp.where(is_odd, before, entering_odd).astype(BF16)
    held[...] = jnp.where(is_odd, entering_odd, before).astype(BF16)


def combine(kernel, operands, specs, outs, name, scratch=()):
    return pl.pallas_call(
        kernel,
        in_specs=specs,
        out_specs=[FULL] * len(outs),
        out_shape=[jax.ShapeDtypeStruct(s, t) for s, t in outs],
        scratch_shapes=list(scratch),
        compiler_params=params(16),
        cost_estimate=CHEAP,
        name=name,
    )(*operands)


def scan_kernel(order, part, info, x, z, bc, cum, cum_s, log_s, f_blk, rates, _, uv_out, state):
    length = x.shape[0]
    width = state.shape[1]
    per_slab = SLAB // P_SIZE
    inner = STEP_B // TOK_B
    blocks = length // TOK_B
    first_head = part * width // P_SIZE
    first_lane = info[GROUP + order] * x.shape[1] + part * width
    state[...] = jnp.zeros_like(state)

    row = lax.broadcasted_iota(jnp.int32, (TOK_B, TOK_B), 0)
    col = lax.broadcasted_iota(jnp.int32, (TOK_B, TOK_B), 1)
    keep = row >= col
    first = lax.broadcasted_iota(jnp.int32, (TOK_B, 2 * P_SIZE), 1) < P_SIZE
    zero = jnp.zeros((TOK_B, 2 * P_SIZE), BF16)

    def turn(step, _):
        for k in range(inner):
            block(step * inner + k)
        return 0

    def block(b):
        at = pl.ds(pl.multiple_of(b * TOK_B, TOK_B), TOK_B)
        b_mat = bc[at, 0:N]
        c_mat = bc[at, N : 2 * N]
        b_across = b_mat.T
        scores = jnp.where(keep, dot(c_mat, b_mat, ((1,), (1,))), 0.0)
        for s in range(width // SLAB):
            lanes = slice(s * SLAB, (s + 1) * SLAB)
            xb = x[at, part * width + s * SLAB : part * width + (s + 1) * SLAB]
            wide = slice(part * width + s * SLAB, part * width + (s + 1) * SLAB)
            fade_row = rates[pl.ds(b, 1), wide]
            lead_row = rates[pl.ds(blocks + b, 1), wide]
            skip = rates[2 * blocks + 8 : 2 * blocks + 9, wide]
            old = state[:, lanes]
            carried = dot(c_mat, old.astype(BF16))
            within, grown, rises = [], [], []
            for q in range(per_slab // 2):
                tables, fades, columns = [], [], []
                for h in (2 * q, 2 * q + 1):
                    head = first_head + s * per_slab + h
                    own = slice(head, head + 1)
                    column = jnp.broadcast_to(cum[at, own], (TOK_B, TOK_B))
                    gap = jnp.minimum(column - cum_s[own, at], log_s[own, at])
                    tables.append((scores * jnp.exp2(gap)).astype(BF16))
                    fades.append(b_across * f_blk[own, at].astype(BF16))
                    columns.append(column)
                xp = xb[:, q * 2 * P_SIZE : (q + 1) * 2 * P_SIZE]
                stacked = jnp.concatenate([jnp.where(first, xp, zero), jnp.where(first, zero, xp)], 0)
                both = jnp.concatenate([jnp.concatenate(tables, 1), jnp.concatenate(fades, 1)], 0)
                product = dot(both, stacked)
                within.append(product[0:TOK_B])
                grown.append(product[TOK_B:])
                rises.append(jnp.exp2(jnp.where(first, columns[0], columns[1])))
            rise = jnp.concatenate(rises, 1)
            xs = xb.astype(F32)
            y = jnp.concatenate(within, 1) + carried * rise + skip * xs
            gate = half_silu((z[at, pl.ds(pl.multiple_of(first_lane + s * SLAB, SLAB), SLAB)] * 0.5).astype(F32))
            uv_out[at, lanes] = (y * gate).astype(BF16)
            uv_out[at, width + s * SLAB : width + (s + 1) * SLAB] = (gate * rise * lead_row).astype(BF16)
            state[:, lanes] = old * fade_row + jnp.concatenate(grown, 1)

    lax.fori_loop(0, length // STEP_B, turn, 0)


def scan_part(order, part, info, token, x, z, bc, cum, cum_s, log_s, f_blk, rates):
    length, full = x.shape
    width = full // B_PARTS
    return pl.pallas_call(
        functools.partial(scan_kernel, order, part),
        in_specs=[SCALAR] + [FULL] * 8 + [ANY],
        out_specs=FULL,
        out_shape=pltpu.VMEM((length, 2 * width), BF16),
        scratch_shapes=[pltpu.VMEM((N, width), F32)],
        compiler_params=params(12),
        cost_estimate=CHEAP,
        name="scan_part",
    )(info, x, z, bc, cum, cum_s, log_s, f_blk, rates, token)


def norm_kernel(order, places, fetched, info, bc, state, gain, _, *refs):
    uvs, refs = refs[:B_PARTS], refs[B_PARTS:]
    weights, outs, tiles, sem = refs[:fetched], refs[fetched : -1 - fetched], refs[len(refs) - 1 - fetched : -1], refs[-1]
    copies = [
        pltpu.make_async_copy(weight.at[:, pl.ds(0, tile.shape[1])], tile, sem.at[k])
        for k, (weight, tile) in enumerate(zip(weights, tiles))
    ]
    for copy in copies:
        copy.start()
    each = len(places) // len(outs)
    count = outs[0].shape[0] // each
    per = state.shape[1]
    part = per // B_PARTS

    def rows(out, first, base):
        to = pl.ds(pl.multiple_of(first, ROWS_C), ROWS_C)
        at = pl.ds(pl.multiple_of(base, ROWS_C), ROWS_C)
        c_mat = bc[at, N : 2 * N]
        pieces = []
        squares = None
        for p, uv in enumerate(uvs):
            inc = state[:, p * part : (p + 1) * part]
            gated = uv[at, 0:part].astype(F32) + uv[at, part:].astype(F32) * dot(c_mat, inc)
            square = jnp.sum(gated * gated, axis=-1, keepdims=True)
            squares = square if squares is None else squares + square
            pieces.append(gated)
        scale = lax.rsqrt(squares * (1.0 / per) + EPS)
        for p, gated in enumerate(pieces):
            lanes = pl.ds(pl.multiple_of(info[GROUP + order] * per + p * part, part), part)
            out[to, p * part : (p + 1) * part] = (gated * scale * gain[:, lanes]).astype(BF16)

    for k, place in enumerate(places):

        def step(j, _):
            rows(outs[k // each], (k % each) * count + j * ROWS_C, info[ROWS + place] * count + j * ROWS_C)
            return 0

        lax.fori_loop(0, count // ROWS_C, step, 0)
    for copy in copies:
        copy.wait()


def norm_rows(order, places, arrays, info, count, token, bc, state, gain, uvs, weights=(), columns=0):
    tile = jax.ShapeDtypeStruct((gain.shape[1], columns), BF16)
    rows = jax.ShapeDtypeStruct((len(places) * count // arrays, state.shape[1]), BF16)
    return pl.pallas_call(
        functools.partial(norm_kernel, order, places, len(weights)),
        in_specs=[SCALAR] + [FULL] * 3 + [ANY] + [FULL] * len(uvs) + [FAR] * len(weights),
        out_specs=[FULL] * (arrays + len(weights)),
        out_shape=[rows] * arrays + [tile] * len(weights),
        scratch_shapes=[pltpu.SemaphoreType.DMA((2,))],
        compiler_params=params(16),
        cost_estimate=CHEAP,
        name="norm_rows",
    )(info, bc, state, gain, token, *uvs, *weights)


def stream(base, w0_far, w1_far, w0, w1, sem):
    j = pl.program_id(0)
    tiles = pl.num_programs(0)

    def fetch(t):
        slot = lax.rem(t, SLOTS)
        lanes = pl.ds(pl.multiple_of((base + t) * TILE, TILE), TILE)
        return (
            pltpu.make_async_copy(w0_far.at[:, lanes], w0.at[slot], sem.at[0, slot]),
            pltpu.make_async_copy(w1_far.at[:, lanes], w1.at[slot], sem.at[1, slot]),
        )

    def start(t):
        @pl.when(t < tiles)
        def _():
            for copy in fetch(t):
                copy.start()

    @pl.when(j == 0)
    def _():
        for t in range(SLOTS - 1):
            start(t)

    start(j + SLOTS - 1)
    for copy in fetch(j):
        copy.wait()
    return lax.rem(j, SLOTS)


def buffers(depth):
    return [
        pltpu.VMEM((SLOTS, depth, TILE), BF16),
        pltpu.VMEM((SLOTS, depth, TILE), BF16),
        pltpu.SemaphoreType.DMA((2, SLOTS)),
    ]


def group_rows(info, order, depth):
    return pl.ds(pl.multiple_of(info[GROUP + order] * (depth // 2), depth // 2), depth // 2)


def ahead_kernel(info, own0, own1, mate0, mate1, w0, w1, out):
    rows = slice(0, out.shape[0])
    total = None
    for order, (own, mate) in enumerate(((own0, mate0), (own1, mate1))):
        at = group_rows(info, order, w0.shape[0])
        term = dot(own[rows, :], w0[at, :]) + dot(mate[rows, :], w1[at, :])
        total = term if total is None else total + term
    out[...] = total.astype(BF16)


def project_ahead(info, own0, own1, mate0, mate1, w0, w1):
    return pl.pallas_call(
        ahead_kernel,
        in_specs=[SCALAR] + [FULL] * 6,
        out_specs=FULL,
        out_shape=jax.ShapeDtypeStruct((own0.shape[0] // 2, w0.shape[1]), BF16),
        compiler_params=params(16),
        cost_estimate=CHEAP,
        name="project_ahead",
    )(info, own0, own1, mate0, mate1, w0, w1)


def join_kernel(first, second, _, out):
    rows = first.shape[0]
    out[0:rows, :] = first[...]
    out[rows:, :] = second[...]


def join(first, second, token):
    rows, depth = first.shape
    return pl.pallas_call(
        join_kernel,
        in_specs=[FULL, FULL, ANY],
        out_specs=FULL,
        out_shape=jax.ShapeDtypeStruct((2 * rows, depth), BF16),
        compiler_params=params(8),
        cost_estimate=CHEAP,
        name="join",
    )(first, second, token)


def both_kernel(base, cut, info, own0, own1, mate0, mate1, w0_far, w1_far, *refs):
    fars, near, w0, w1, sem = refs[:-4], *refs[-4:]
    rows = near.shape[0]
    slot = stream(base, w0_far, w1_far, w0, w1, sem)
    total = None
    for order, (own, mate) in enumerate(((own0, mate0), (own1, mate1))):
        at = group_rows(info, order, w0.shape[1])
        term = dot(own[...], w0[slot, at, :]) + dot(mate[...], w1[slot, at, :])
        total = term if total is None else total + term
    near[...] = total[rows:]
    for k, far_out in enumerate(fars):

        @pl.when(pl.program_id(0) // cut == k)
        def _():
            far_out[...] = total[0:rows].astype(BF16)


def project_both(info, own0, own1, mate0, mate1, w0, w1, first, count, chunk):
    rows, depth = own0.shape[0] // 2, w0.shape[0]
    cut = chunk // TILE
    chunks = count // chunk

    def placed(k):
        return pl.BlockSpec((rows, TILE), lambda j: (0, jnp.clip(j - k * cut, 0, cut - 1)))

    *fars, near = pl.pallas_call(
        functools.partial(both_kernel, first // TILE, cut),
        grid=(count // TILE,),
        in_specs=[SCALAR] + [FULL] * 4 + [FAR] * 2,
        out_specs=[placed(k) for k in range(chunks)] + [pl.BlockSpec((rows, TILE), lambda j: (0, j))],
        out_shape=[jax.ShapeDtypeStruct((rows, chunk), BF16)] * chunks + [jax.ShapeDtypeStruct((rows, count), F32)],
        scratch_shapes=buffers(depth),
        compiler_params=params(24),
        cost_estimate=CHEAP,
        name="project_both",
    )(info, own0, own1, mate0, mate1, w0, w1)
    return fars, near


def near_kernel(info, own0, own1, mate0, mate1, w0_far, w1_far, arrived, out, w0, w1, sem):
    slot = stream(0, w0_far, w1_far, w0, w1, sem)
    rows = slice(out.shape[0], 2 * out.shape[0])
    total = arrived[...].astype(F32)
    for order, (own, mate) in enumerate(((own0, mate0), (own1, mate1))):
        at = group_rows(info, order, w0.shape[1])
        total = total + dot(own[rows, :], w0[slot, at, :]) + dot(mate[rows, :], w1[slot, at, :])
    out[...] = total.astype(out.dtype)


def project_near(info, own0, own1, mate0, mate1, w0, w1, arrived):
    rows, depth = own0.shape[0] // 2, w0.shape[0]
    placed = pl.BlockSpec((rows, TILE), lambda j: (0, j))
    return pl.pallas_call(
        near_kernel,
        grid=(arrived.shape[1] // TILE,),
        in_specs=[SCALAR] + [FULL] * 4 + [FAR, FAR, placed],
        out_specs=placed,
        out_shape=jax.ShapeDtypeStruct((rows, w0.shape[1]), BF16),
        scratch_shapes=buffers(depth),
        compiler_params=params(20),
        cost_estimate=CHEAP,
        name="project_near",
    )(info, own0, own1, mate0, mate1, w0, w1, arrived)


def add_kernel(near, *refs):
    arrived, out = refs[:-2], refs[-1]
    chunk = arrived[0].shape[1]
    for k, part in enumerate(arrived):
        lanes = slice(k * chunk, (k + 1) * chunk)
        out[:, lanes] = (near[:, lanes] + part[...].astype(F32)).astype(BF16)


def add_chunks(near, first, arrived, result, at):
    rows, chunk = arrived[0].shape
    count = chunk * len(arrived)
    return pl.pallas_call(
        add_kernel,
        grid=(1,),
        in_specs=[pl.BlockSpec((rows, count), lambda j: (0, first // count))] + [FULL] * len(arrived) + [ANY],
        out_specs=pl.BlockSpec((rows, count), lambda j: (0, at // count)),
        out_shape=jax.ShapeDtypeStruct(result.shape, BF16),
        input_output_aliases={1 + len(arrived): 0},
        compiler_params=params(8),
        cost_estimate=CHEAP,
        name="add_chunks",
    )(near, *arrived, result)


def shift(block, distance):
    size = lax.axis_size("seq")
    return lax.ppermute(block, "seq", [(i, i + distance) for i in range(size - distance)])


def swap(block, axis, bit):
    return lax.ppermute(block, axis, [(i, i ^ bit) for i in range(lax.axis_size(axis))])


def rotate(block, distance):
    size = lax.axis_size("seq")
    return lax.ppermute(block, "seq", [(i, (i + distance) % size) for i in range(size)])


def log_steps(info, got, keep, rates_kept, done, pairs, scan_next):
    half = keep.shape[1]
    message = ((N + EXTRA, half), BF16)
    full = ((N, half), F32)
    msg, own, first, aux = combine(
        pair_kernel,
        (info, got, keep, rates_kept, done),
        [SCALAR, FULL, FULL, FULL, ANY],
        [message, full, full, ((16, half), F32)],
        "pair",
    )
    behind = None
    covered = 0
    while True:
        got = shift(msg, 2 * (covered + 1))
        done = scan_next(msg)
        covered = 2 * covered + 1
        if covered >= pairs - 1:
            break
        operands, specs = [got, own, aux], [FULL, FULL, FULL]
        if behind is None:
            kernel = lambda g, o, a, t, m, b: wave_kernel(g, o, a, None, t, m, b)
        else:
            kernel = wave_kernel
            operands.append(behind)
            specs.append(FULL)
        msg, behind = combine(kernel, operands + [done], specs + [ANY], [message, ((N + 8, half), F32)], "wave")
    operands, specs = [info, got], [SCALAR, FULL]
    if behind is None:
        kernel = lambda o, g, f, a, t, b, h: last_kernel(o, g, None, f, a, t, b, h)
    else:
        kernel = last_kernel
        operands.append(behind)
        specs.append(FULL)
    out = ((N, half), BF16)
    back, held = combine(kernel, operands + [first, aux, done], specs + [FULL, FULL, ANY], [out, out], "last")
    return back, held


def local(
    x_input,
    z_input,
    bc_input,
    conv_weight_x,
    conv_weight_bc,
    step_size,
    log_decay,
    skip_gain,
    norm_gain,
    out_weight,
):
    length, width = x_input.shape
    heads = step_size.shape[1]
    ways = lax.axis_size("head")
    pairs = lax.axis_size("seq") // 2
    mine = lax.axis_index("head")
    half = width // 2
    seq = lax.axis_index("seq")
    info = jnp.stack([seq & 1, mine ^ 3, mine ^ 2, mine ^ 1, mine, seq >> 1, seq, 1 - (seq & 1), seq & 1]).astype(jnp.int32)

    x_far, z_far, w_far = far(x_input, z_input, out_weight)
    (bc_far,) = far(bc_input)
    halo = rotate(tail_rows(x_far, bc_far), 1)
    bc = bc_input.reshape(length, -1)
    (weight_mate,) = far(swap(out_weight, "head", 1))

    (cum, cum_s, log_s, f_dev, f_blk, rates), ones = decays(info, log_decay, step_size, skip_gain, half)
    taps = far(conv_weight_x, conv_weight_bc)
    shared = (bc, halo, *taps)
    x0, bc0, send, x_kept = conv_states(0, info, x_far, *shared, f_dev[0], ones, rates[0], x_far)
    got = swap(send, "seq", 1)
    x1, bc1, keep, z_near = conv_states(1, info, x_kept, *shared, f_dev[1], ones, rates[1], z_far)
    rates_kept = rates[1]

    uvs = []
    groups = list(zip((x0, x1), (z_near, z_near), (bc0, bc1), cum, cum_s, log_s, f_blk, rates))

    def scan_next(token):
        if len(uvs) < 2 * B_PARTS:
            order, part = divmod(len(uvs), B_PARTS)
            uvs.append(scan_part(order, part, info, token, *groups[order]))
        return uvs[-1]

    full = ((N, half), F32)
    message = ((N + EXTRA, half), BF16)
    done = scan_next(keep)
    out = ((N, half), BF16)
    if pairs > 1 and half % (pairs * N) == 0:
        piece = half // pairs
        part = ((N + EXTRA, piece), BF16)
        first, aux, *parts = combine(
            pair_split_kernel,
            (info, got, keep, rates_kept, done),
            [SCALAR, FULL, FULL, FULL, ANY],
            [full, ((8, half), F32)] + [part] * pairs,
            "pair",
            [pltpu.VMEM(*message)],
        )
        parts = list(parts[:1]) + [rotate(parts[r], 2 * r) for r in range(1, pairs)]
        done = scan_next(parts[0])
        parts = combine(
            owner_kernel,
            [info] + parts + [done],
            [SCALAR] + [FULL] * pairs + [ANY],
            [((N, piece), BF16)] * pairs,
            "owner",
            [pltpu.VMEM((pairs, N + EXTRA, piece), BF16), pltpu.VMEM((pairs, N, piece), BF16)],
        )
        ready = parts[0]
        parts = list(parts[:1]) + [rotate(parts[r], 2 * r) for r in range(1, pairs)]
        done = scan_next(ready)
        back, held = combine(
            last_split_kernel,
            [info, first, aux, done] + parts,
            [SCALAR, FULL, FULL, ANY] + [FULL] * pairs,
            [out, out],
            "last",
            [pltpu.VMEM(*out)],
        )
    else:
        back, held = log_steps(info, got, keep, rates_kept, done, pairs, scan_next)
    other = swap(back, "seq", 1)
    while len(uvs) < 2 * B_PARTS:
        scan_next(back)

    count = length // ways
    gain = norm_gain[None, :]

    columns = out_weight.shape[1]
    chunk = columns // 8
    weights = (w_far, weight_mate)
    kept = (info, count, held, bc1, held, gain, uvs[B_PARTS:])
    kept_mates, kept_owns, w0, w1 = norm_rows(1, (0, 2, 1, 3), 2, *kept, weights, chunk)
    kept_mates = swap(lax.optimization_barrier((kept_mates, other))[0], "head", 1)
    sent_group = (bc0, other, gain, uvs[:B_PARTS])
    far_mate, near_mate = norm_rows(0, (0, 2), 2, info, count, kept_owns, *sent_group)
    (owns,) = norm_rows(0, (1, 3), 1, info, count, far_mate, *sent_group)
    far_mate = swap(far_mate, "head", 1)
    sent = project_ahead(info, owns, kept_owns, far_mate, kept_mates, w0, w1)
    first = swap(sent, "head", 2)
    mates = join(far_mate, swap(near_mate, "head", 1), sent)
    operands = (info, owns, kept_owns, mates, kept_mates, *weights)
    calls = []
    for lo, hi in ((1, 2), (2, 4), (4, 6), (6, 8)):
        sent, near = project_both(*operands, lo * chunk, (hi - lo) * chunk, chunk)
        calls.append((near, lo, [swap(part, "head", 2) for part in sent]))
    result = project_near(*operands, first)
    for near, lo, arrived in calls[:-1]:
        result = add_chunks(near, 0, arrived, result, lo * chunk)
    near, lo, arrived = calls[-1]
    for k, part in enumerate(arrived):
        result = add_chunks(near, k * chunk, [part], result, (lo + k) * chunk)
    return result


def solution(mesh):
    in_specs = (
        P("seq", "head"),
        P("seq", "head"),
        P("seq", "head", None),
        P(None, "head"),
        P(None, "head", None),
        P("seq", "head"),
        P("seq", "head"),
        P("head"),
        P("head"),
        P("head", None),
    )
    out_specs = P(("seq", "head"), None)
    return jax.shard_map(local, mesh=mesh, in_specs=in_specs, out_specs=out_specs, check_vma=False)
```

```python
import functools

import jax
import jax.numpy as jnp
from jax import lax
from jax.experimental import pallas as pl
from jax.experimental.pallas import tpu as pltpu
from jax.sharding import PartitionSpec as P

P_SIZE = 64
N = 128
KCONV = 4
EPS = 1e-05
LOG2E = 1.4426950408889634

TOK_A = 256
ROWS_A = 32
TOK_B = 128
STEP_B = 256
EXTRA = 16
SLAB = 256
ROWS_C = 128
TILE = 256
SLOTS = 4
LEAD = 16
B_PARTS = 2
HIGHEST = lax.Precision.HIGHEST
F32 = jnp.float32
BF16 = jnp.bfloat16


def params(mib):
    return pltpu.CompilerParams(vmem_limit_bytes=mib * 1024 * 1024)


CHEAP = pl.CostEstimate(flops=1, bytes_accessed=1, transcendentals=0)
SCALAR = pl.BlockSpec(memory_space=pltpu.SMEM)
FULL = pl.BlockSpec(memory_space=pltpu.VMEM)
FAR = pl.BlockSpec(memory_space=pltpu.HBM)
ANY = pl.BlockSpec(memory_space=pl.ANY)

ODD, ROWS, PAIR, SEQ, GROUP = 0, 1, 5, 6, 7


def dot(a, b, dims=((1,), (0,)), precision=None):
    return lax.dot_general(a, b, (dims, ((), ())), precision=precision, preferred_element_type=F32)


def half_silu(half):
    return half + half * jnp.tanh(half)


def far(*arrays):
    return [pltpu.with_memory_space_constraint(a, pltpu.HBM) for a in arrays]


def whole(shape):
    return pl.BlockSpec(shape, lambda *_: (0,) * len(shape))


def group_copies(x_far, x, group, sems):
    length, width = x.shape
    rows = length // 4
    lanes = pl.ds(pl.multiple_of(group * width, width), width)
    pieces = [pl.ds(k * rows, rows) for k in range(4)]
    return [pltpu.make_async_copy(x_far.at[at, lanes], x.at[at], sems.at[k]) for k, at in enumerate(pieces)]


def decay_kernel(info, ld_t, step_t, skip, x_far, *refs):
    cum, cum_s, log_s, f_dev, f_blk, rates = [refs[2 * k : 2 * k + 2] for k in range(6)]
    ones, x, sem = refs[12:]
    copies = group_copies(x_far, x, info[GROUP], sem)
    for copy in copies:
        copy.start()
    heads, length = ld_t.shape
    blocks = length // TOK_B
    per = heads // 2
    width = ones.shape[1]
    swapped = info[GROUP] == 1
    row = lax.broadcasted_iota(jnp.int32, (TOK_B, TOK_B), 0)
    col = lax.broadcasted_iota(jnp.int32, (TOK_B, TOK_B), 1)
    lower = (row >= col).astype(F32)
    upper = (row <= col).astype(F32)
    eye = (row == col).astype(BF16)

    def ordered(value):
        return jnp.where(swapped, jnp.concatenate([value[per:], value[:per]], 0), value)

    def put(ref, rows, value):
        high = value.astype(BF16)
        low = (value - high.astype(F32)).astype(BF16)
        for g in range(2):
            own = slice(g * per, (g + 1) * per)
            both = jnp.concatenate([high[own], low[own]], 0)
            ref[g][rows, :] = dot(eye, both, ((1,), (1,))).astype(BF16)

    first = lax.broadcasted_iota(jnp.int32, (per, width), 0) * P_SIZE
    lane = lax.broadcasted_iota(jnp.int32, (per, width), 1)
    member = ((lane >= first) & (lane < first + P_SIZE)).astype(F32)
    ones[0:per, :] = member.astype(BF16)
    ones[per:, :] = member.astype(BF16)
    cums, totals, row_totals = [], [], []
    for b in range(blocks):
        rows = slice(b * TOK_B, (b + 1) * TOK_B)
        logs = ordered(ld_t[:, rows]) * LOG2E
        c = dot(lower, logs, ((1,), (1,)), HIGHEST)
        for g in range(2):
            cum[g][rows, :] = c[:, g * per : (g + 1) * per]
        row_totals.append(c[TOK_B - 1 : TOK_B, :])
        c = dot(logs, upper, precision=HIGHEST)
        cums.append(c)
        totals.append(c[:, TOK_B - 1 : TOK_B])
    before, row_before = [jnp.zeros_like(totals[0])], [jnp.zeros_like(row_totals[0])]
    for b in range(blocks):
        before.append(before[-1] + totals[b])
        row_before.append(row_before[-1] + row_totals[b])
    total = before[-1]
    logs = jnp.concatenate(row_totals + row_before[:-1] + row_before[-1:] * 8, 0)
    gains = jnp.broadcast_to(skip[...], (8, heads))
    gains = jnp.where(swapped, jnp.concatenate([gains[:, per:], gains[:, :per]], 1), gains)
    values = jnp.concatenate([jnp.exp2(logs), gains], 0)
    for g in range(2):
        rates[g][...] = dot(values[:, g * per : (g + 1) * per], member, precision=HIGHEST)
    for b in range(blocks):
        rows = slice(b * TOK_B, (b + 1) * TOK_B)
        s = ordered(step_t[:, rows])
        log_step = jnp.log2(s)
        shifted = cums[b] - log_step
        fade = jnp.exp2(totals[b] - cums[b]) * s
        for g in range(2):
            own = slice(g * per, (g + 1) * per)
            log_s[g][:, rows] = log_step[own, :]
            cum_s[g][:, rows] = shifted[own, :]
            f_blk[g][:, rows] = fade[own, :]
        put(f_dev, rows, jnp.exp2(total - (cums[b] + before[b])) * s)
    for copy in copies:
        copy.wait()


def decays(info, log_decay, step, skip, x, width):
    length, heads = log_decay.shape
    blocks = length // TOK_B
    per = heads // 2
    across = jax.ShapeDtypeStruct((per, length), F32)
    pair = jax.ShapeDtypeStruct((length, 2 * per), BF16)
    column = jax.ShapeDtypeStruct((length, per), F32)
    rates = jax.ShapeDtypeStruct((2 * blocks + 16, width), F32)
    shapes = [shape for shape in (column, across, across, pair, across, rates) for _ in range(2)]
    shapes += [
        jax.ShapeDtypeStruct((2 * per, width), BF16),
        pltpu.VMEM((length, width), BF16),
    ]
    *refs, ones, x_near = pl.pallas_call(
        decay_kernel,
        in_specs=[SCALAR] + [FULL] * 3 + [FAR],
        out_specs=[FULL] * len(shapes),
        out_shape=shapes,
        scratch_shapes=[pltpu.SemaphoreType.DMA((4,))],
        compiler_params=params(16),
        cost_estimate=CHEAP,
        name="decays",
    )(info, *far(log_decay.T, step.T, skip[None, :], x))
    return [tuple(refs[2 * k : 2 * k + 2]) for k in range(6)], ones, x_near


def tail_kernel(x, bc, out):
    width, bc_width = x.shape[1], bc.shape[2]
    out[:, 0:width] = x[...]
    for g in range(bc.shape[1]):
        out[:, width + g * bc_width : width + (g + 1) * bc_width] = bc[:, g, :]


def tail_rows(x, bc):
    length, width = x.shape
    groups, bc_width = bc.shape[1:]
    at = length // LEAD - 1
    shape = (LEAD, width + groups * bc_width)
    return pl.pallas_call(
        tail_kernel,
        grid=(1,),
        in_specs=[
            pl.BlockSpec((LEAD, width), lambda i: (at, 0)),
            pl.BlockSpec((LEAD, groups, bc_width), lambda i: (at, 0, 0)),
        ],
        out_specs=whole(shape),
        out_shape=jax.ShapeDtypeStruct(shape, BF16),
        compiler_params=params(8),
        cost_estimate=CHEAP,
        name="tail_rows",
    )(x, bc)


def put_message(ref, state, decay):
    high = decay.astype(BF16)
    low = (decay - high.astype(F32)).astype(BF16)
    rest = jnp.zeros((EXTRA - 2, state.shape[1]), BF16)
    ref[0:N, :] = state.astype(BF16)
    ref[N:, :] = jnp.concatenate([high, low, rest], 0)


def take_message(ref):
    extra = ref[N:, :].astype(F32)
    return ref[0:N, :].astype(F32), extra[0:1] + extra[1:2]


def conv_kernel(order, info, x, bc, halo, wx, wbc, f_dev, ones, rates, *refs):
    next_far, refs = refs[0], refs[1:]
    x_out, bc_out, final = refs[:3]
    xf, state, down = refs[-3:]
    length, width = x_out.shape
    rows = TOK_A
    group = info[GROUP + order]
    first_lane = pl.multiple_of(group * width, width)
    taken, sem = refs[3:5]
    first_bc = pl.multiple_of(group * 2 * N, 2 * N)
    if order == 0:
        copies = group_copies(next_far, taken, info[GROUP + 1], sem)
    else:
        part = length // 4
        pieces = [pl.ds(k * part, part) for k in range(4)]
        copies = [pltpu.make_async_copy(next_far.at[at], taken.at[at], sem.at[k]) for k, at in enumerate(pieces)]
    for copy in copies:
        copy.start()
    state[...] = jnp.zeros_like(state)
    row = lax.broadcasted_iota(jnp.int32, down.shape, 0)
    col = lax.broadcasted_iota(jnp.int32, down.shape, 1)
    down[...] = (row == col + 1).astype(BF16)

    def conv(i, src, moved, first, behind, weights, emit):
        at_start = jnp.where(info[SEQ] == 0, jnp.zeros_like(first), first)
        lead = jnp.where(i == 0, at_start, behind).astype(F32)
        w0, w1, w2, w3 = [w * 0.5 for w in weights]
        back = LEAD - 8
        lead_r1 = pltpu.roll(lead, 1, 0)
        last_p = (w1 * lead + w0 * lead_r1)[back:]
        top = lax.broadcasted_iota(jnp.int32, (8, lead.shape[1]), 0) == 0
        head = jnp.where(top, jnp.broadcast_to(lead[LEAD - 1 :], top.shape), moved[0:8])
        for r in range(0, rows, ROWS_A):
            cur = src[r : r + ROWS_A].astype(F32)
            r1 = moved[r : r + ROWS_A] if r else jnp.concatenate([head, moved[8:ROWS_A]], 0)
            p = w1 * cur + w0 * r1
            p2 = pltpu.roll(jnp.concatenate([last_p, p], 0), 2, 0)[8:]
            emit(r, half_silu((w3 * cur + w2 * r1) + p2))
            last_p = p[ROWS_A - 8 :]

    def step(i, _):
        at = pl.ds(pl.multiple_of(i * rows, rows), rows)
        behind = pl.ds(pl.multiple_of(jnp.maximum(i * rows - LEAD, 0), LEAD), LEAD)

        def out(r):
            return pl.ds(pl.multiple_of(i * rows + r, ROWS_A), ROWS_A)

        for lanes in range(0, 2 * N, SLAB):
            ds = slice(lanes, lanes + SLAB)
            src = pl.ds(pl.multiple_of(first_bc + lanes, SLAB), SLAB)
            halo_src = pl.ds(pl.multiple_of(2 * width + first_bc + lanes, SLAB), SLAB)

            def emit_bc(r, value):
                bc_out[out(r), ds] = value.astype(BF16)

            weights = [jnp.where(group == 0, wbc[k, 0:1, ds], wbc[k, 1:2, ds]) for k in range(KCONV)]
            conv(i, bc[at, src], dot(down[...], bc[at, src]), halo[:, halo_src], bc[behind, src], weights, emit_bc)

        for lanes in range(0, width, SLAB):
            ds = slice(lanes, lanes + SLAB)
            src = pl.ds(pl.multiple_of(first_lane + lanes, SLAB), SLAB)
            scale = dot(f_dev[at, :], ones[:, ds])

            def emit(r, value):
                x_out[out(r), ds] = value.astype(BF16)
                xf[r : r + ROWS_A, ds] = (value * scale[r : r + ROWS_A]).astype(BF16)

            weights = [wx[k : k + 1, ds] for k in range(KCONV)]
            conv(i, x[at, ds], dot(down[...], x[at, ds]), halo[:, src], x[behind, ds], weights, emit)

        state[...] += dot(bc_out[at, 0:N], xf[...], ((0,), (0,)))
        return 0

    lax.fori_loop(0, length // rows, step, 0)
    if order == 0:
        row = rates.shape[0] - 16
        put_message(final, state[...], rates[row : row + 1, :])
    else:
        final[...] = state[...]
    for copy in copies:
        copy.wait()


def conv_states(order, info, x, bc, halo, wx, wbc, f_dev, ones, rates, ahead):
    length, width = x.shape
    column = lambda i, info: (0, info[GROUP + order])
    final = ((N + EXTRA, width), BF16) if order == 0 else ((N, width), F32)
    taken = (length, width) if order == 0 else ahead.shape
    return pl.pallas_call(
        functools.partial(conv_kernel, order),
        grid_spec=pltpu.PrefetchScalarGridSpec(
            num_scalar_prefetch=1,
            grid=(1,),
            in_specs=[FULL] * 3 + [pl.BlockSpec((KCONV, width), column)] + [FULL] * 4 + [FAR],
            out_specs=[FULL] * 4,
            scratch_shapes=[
                pltpu.SemaphoreType.DMA((4,)),
                pltpu.VMEM((TOK_A, width), BF16),
                pltpu.VMEM((N, width), F32),
                pltpu.VMEM((TOK_A, TOK_A), BF16),
            ],
        ),
        out_shape=[
            pltpu.VMEM((length, width), BF16),
            pltpu.VMEM((length, 2 * N), BF16),
            jax.ShapeDtypeStruct(*final),
            pltpu.VMEM(taken, BF16),
        ],
        compiler_params=params(16),
        cost_estimate=CHEAP,
        name="conv_states",
    )(info, x, bc, halo, wx, wbc, f_dev, ones, rates, ahead)


def pair_kernel(info, got, keep, rates, _, msg, own, first, aux):
    half = keep.shape[1]
    is_odd = info[ODD] == 1
    arrived, their = take_message(got)
    row = rates.shape[0] - 16
    mine = rates[row : row + 1, :]
    early = jnp.where(is_odd, arrived, keep[...])
    late = jnp.where(is_odd, keep[...], arrived)
    even_decay = jnp.where(is_odd, their, mine)
    odd_decay = jnp.where(is_odd, mine, their)
    state = odd_decay * early + late
    own[...] = state
    first[...] = early
    aux[0:8, :] = jnp.broadcast_to(even_decay, (8, half))
    aux[8:16, :] = jnp.broadcast_to(even_decay * odd_decay, (8, half))
    put_message(msg, state, even_decay * odd_decay)


def wave_kernel(got, own, aux, behind_in, _, msg, behind):
    before, decay = take_message(got)
    if behind_in is not None:
        before_decay = behind_in[N : N + 1, :]
        before = behind_in[0:N, :] + before_decay * before
        decay = before_decay * decay
    pair_decay = aux[8:9, :]
    behind[0:N, :] = before
    behind[N:, :] = jnp.broadcast_to(decay, (8, before.shape[1]))
    put_message(msg, own[...] + pair_decay * before, pair_decay * decay)


def last_kernel(info, got, behind_in, first, aux, _, back, held):
    is_odd = info[ODD] == 1
    before, _unused = take_message(got)
    if behind_in is not None:
        before = behind_in[0:N, :] + behind_in[N : N + 1, :] * before
    entering_odd = aux[0:1, :] * before + first[...]
    back[...] = jnp.where(is_odd, before, entering_odd).astype(BF16)
    held[...] = jnp.where(is_odd, entering_odd, before).astype(BF16)


def pair_split_kernel(info, got, keep, rates, _, first, aux, *refs):
    outs, wide = refs[:-1], refs[-1]
    half = keep.shape[1]
    pairs = len(outs)
    piece = half // pairs
    is_odd = info[ODD] == 1
    arrived, their = take_message(got)
    row = rates.shape[0] - 16
    mine = rates[row : row + 1, :]
    early = jnp.where(is_odd, arrived, keep[...])
    late = jnp.where(is_odd, keep[...], arrived)
    even_decay = jnp.where(is_odd, their, mine)
    odd_decay = jnp.where(is_odd, mine, their)
    first[...] = early
    aux[...] = jnp.broadcast_to(even_decay, (8, half))
    put_message(wide, odd_decay * early + late, even_decay * odd_decay)
    for r in range(pairs):
        owner = lax.rem(info[PAIR] + r, pairs)
        outs[r][...] = wide[:, pl.ds(pl.multiple_of(owner * piece, piece), piece)]


def owner_kernel(info, *refs):
    pairs = (len(refs) - 3) // 2
    ins, outs = refs[:pairs], refs[pairs + 1 : 2 * pairs + 1]
    states, prefixes = refs[-2:]
    for r in range(pairs):
        states[lax.rem(info[PAIR] + pairs - r, pairs)] = ins[r][...]
    before = jnp.zeros(prefixes.shape[1:], F32)
    for q in range(pairs):
        prefixes[q] = before.astype(BF16)
        if q < pairs - 1:
            state, decay = take_message(states.at[q])
            before = decay * before + state
    for r in range(pairs):
        outs[r][...] = prefixes[lax.rem(info[PAIR] + r, pairs)]


def last_split_kernel(info, first, aux, _, *refs):
    pairs = len(refs) - 3
    back, held, wide = refs[-3:]
    piece = back.shape[1] // pairs
    for r in range(pairs):
        owner = lax.rem(info[PAIR] + pairs - r, pairs)
        wide[:, pl.ds(pl.multiple_of(owner * piece, piece), piece)] = refs[r][...]
    is_odd = info[ODD] == 1
    before = wide[...].astype(F32)
    entering_odd = aux[0:1, :] * before + first[...]
    back[...] = jnp.where(is_odd, before, entering_odd).astype(BF16)
    held[...] = jnp.where(is_odd, entering_odd, before).astype(BF16)


def combine(kernel, operands, specs, outs, name, scratch=()):
    return pl.pallas_call(
        kernel,
        in_specs=specs,
        out_specs=[FULL] * len(outs),
        out_shape=[jax.ShapeDtypeStruct(s, t) for s, t in outs],
        scratch_shapes=list(scratch),
        compiler_params=params(16),
        cost_estimate=CHEAP,
        name=name,
    )(*operands)


def scan_kernel(order, part, info, x, z, bc, cum, cum_s, log_s, f_blk, rates, _, uv_out, state):
    length = x.shape[0]
    width = state.shape[1]
    per_slab = SLAB // P_SIZE
    inner = STEP_B // TOK_B
    blocks = length // TOK_B
    first_head = part * width // P_SIZE
    first_lane = info[GROUP + order] * x.shape[1] + part * width
    state[...] = jnp.zeros_like(state)

    row = lax.broadcasted_iota(jnp.int32, (TOK_B, TOK_B), 0)
    col = lax.broadcasted_iota(jnp.int32, (TOK_B, TOK_B), 1)
    keep = row >= col
    first = lax.broadcasted_iota(jnp.int32, (TOK_B, 2 * P_SIZE), 1) < P_SIZE
    zero = jnp.zeros((TOK_B, 2 * P_SIZE), BF16)

    def turn(step, _):
        for k in range(inner):
            block(step * inner + k)
        return 0

    def block(b):
        at = pl.ds(pl.multiple_of(b * TOK_B, TOK_B), TOK_B)
        b_mat = bc[at, 0:N]
        c_mat = bc[at, N : 2 * N]
        b_across = b_mat.T
        scores = jnp.where(keep, dot(c_mat, b_mat, ((1,), (1,))), 0.0)
        for s in range(width // SLAB):
            lanes = slice(s * SLAB, (s + 1) * SLAB)
            xb = x[at, part * width + s * SLAB : part * width + (s + 1) * SLAB]
            wide = slice(part * width + s * SLAB, part * width + (s + 1) * SLAB)
            fade_row = rates[pl.ds(b, 1), wide]
            lead_row = rates[pl.ds(blocks + b, 1), wide]
            skip = rates[2 * blocks + 8 : 2 * blocks + 9, wide]
            old = state[:, lanes]
            carried = dot(c_mat, old.astype(BF16))
            within, grown, rises = [], [], []
            for q in range(per_slab // 2):
                tables, fades, columns = [], [], []
                for h in (2 * q, 2 * q + 1):
                    head = first_head + s * per_slab + h
                    own = slice(head, head + 1)
                    column = jnp.broadcast_to(cum[at, own], (TOK_B, TOK_B))
                    gap = jnp.minimum(column - cum_s[own, at], log_s[own, at])
                    tables.append((scores * jnp.exp2(gap)).astype(BF16))
                    fades.append(b_across * f_blk[own, at].astype(BF16))
                    columns.append(column)
                xp = xb[:, q * 2 * P_SIZE : (q + 1) * 2 * P_SIZE]
                stacked = jnp.concatenate([jnp.where(first, xp, zero), jnp.where(first, zero, xp)], 0)
                both = jnp.concatenate([jnp.concatenate(tables, 1), jnp.concatenate(fades, 1)], 0)
                product = dot(both, stacked)
                within.append(product[0:TOK_B])
                grown.append(product[TOK_B:])
                rises.append(jnp.exp2(jnp.where(first, columns[0], columns[1])))
            rise = jnp.concatenate(rises, 1)
            xs = xb.astype(F32)
            y = jnp.concatenate(within, 1) + carried * rise + skip * xs
            gate = half_silu((z[at, pl.ds(pl.multiple_of(first_lane + s * SLAB, SLAB), SLAB)] * 0.5).astype(F32))
            uv_out[at, lanes] = (y * gate).astype(BF16)
            uv_out[at, width + s * SLAB : width + (s + 1) * SLAB] = (gate * rise * lead_row).astype(BF16)
            state[:, lanes] = old * fade_row + jnp.concatenate(grown, 1)

    lax.fori_loop(0, length // STEP_B, turn, 0)


def scan_part(order, part, info, token, x, z, bc, cum, cum_s, log_s, f_blk, rates):
    length, full = x.shape
    width = full // B_PARTS
    return pl.pallas_call(
        functools.partial(scan_kernel, order, part),
        in_specs=[SCALAR] + [FULL] * 8 + [ANY],
        out_specs=FULL,
        out_shape=pltpu.VMEM((length, 2 * width), BF16),
        scratch_shapes=[pltpu.VMEM((N, width), F32)],
        compiler_params=params(12),
        cost_estimate=CHEAP,
        name="scan_part",
    )(info, x, z, bc, cum, cum_s, log_s, f_blk, rates, token)


def norm_kernel(order, places, skip, fetched, info, bc, state, gain, _, *refs):
    uvs, refs = refs[:B_PARTS], refs[B_PARTS:]
    if order == 0:
        kept, refs = refs[0], refs[1:]
    weights, outs, tiles, sem = refs[:fetched], refs[fetched : -1 - fetched], refs[len(refs) - 1 - fetched : -1], refs[-1]
    copies = [
        pltpu.make_async_copy(weight.at[:, pl.ds(0, tile.shape[1])], tile, sem.at[k])
        for k, (weight, tile) in enumerate(zip(weights, tiles))
    ]
    for copy in copies:
        copy.start()
    count = outs[0].shape[0] * len(outs) // len(places)
    per = state.shape[1]
    part = per // B_PARTS

    def lanes(group, p=0, size=per):
        return pl.ds(pl.multiple_of(info[GROUP + group] * per + p * part, part), size)

    def rows(out, first, base, source):
        to = pl.ds(pl.multiple_of(first, ROWS_C), ROWS_C)
        at = pl.ds(pl.multiple_of(base, ROWS_C), ROWS_C)
        c_mat = bc[at, N : 2 * N]
        pieces = []
        squares = None
        for p, uv in enumerate(uvs):
            inc = state[:, p * part : (p + 1) * part]
            gated = uv[at, 0:part].astype(F32) + uv[at, part:].astype(F32) * dot(c_mat, inc)
            square = jnp.sum(gated * gated, axis=-1, keepdims=True)
            squares = square if squares is None else squares + square
            pieces.append(gated)
        scale = lax.rsqrt(squares * (1.0 / per) + EPS)
        for p, gated in enumerate(pieces):
            value = (gated * scale * gain[:, lanes(order, p, part)]).astype(BF16)
            if order == 0:
                out[to, lanes(0, p, part)] = value
            else:
                out[to, p * part : (p + 1) * part] = value
        if order == 0:
            out[to, lanes(1)] = kept[pl.ds(pl.multiple_of(source, ROWS_C), ROWS_C), :]

    for k, place in enumerate(places):

        def step(j, _):
            out, first = (outs[k], 0) if len(outs) > 1 else (outs[0], k * count)
            source = skip + k * count + j * ROWS_C
            rows(out, first + j * ROWS_C, info[ROWS + place] * count + j * ROWS_C, source)
            return 0

        lax.fori_loop(0, count // ROWS_C, step, 0)
    for copy in copies:
        copy.wait()


def norm_rows(order, places, info, count, token, bc, state, gain, uvs, kept=None, skip=0, apart=False, weights=(), columns=0):
    width = state.shape[1] if order else gain.shape[1]
    tile = jax.ShapeDtypeStruct((gain.shape[1], columns), BF16)
    arrays = len(places) if apart else 1
    rows = jax.ShapeDtypeStruct((len(places) * count // arrays, width), BF16)
    joined = [] if kept is None else [kept]
    return pl.pallas_call(
        functools.partial(norm_kernel, order, places, skip, len(weights)),
        in_specs=[SCALAR] + [FULL] * 3 + [ANY] + [FULL] * (len(uvs) + len(joined)) + [FAR] * len(weights),
        out_specs=[FULL] * (arrays + len(weights)),
        out_shape=[rows] * arrays + [tile] * len(weights),
        scratch_shapes=[pltpu.SemaphoreType.DMA((2,))],
        compiler_params=params(16),
        cost_estimate=CHEAP,
        name="norm_rows",
    )(info, bc, state, gain, token, *uvs, *joined, *weights)


def stream(base, w0_far, w1_far, w0, w1, sem):
    j = pl.program_id(0)
    tiles = pl.num_programs(0)

    def fetch(t):
        slot = lax.rem(t, SLOTS)
        lanes = pl.ds(pl.multiple_of((base + t) * TILE, TILE), TILE)
        return (
            pltpu.make_async_copy(w0_far.at[:, lanes], w0.at[slot], sem.at[0, slot]),
            pltpu.make_async_copy(w1_far.at[:, lanes], w1.at[slot], sem.at[1, slot]),
        )

    def start(t):
        @pl.when(t < tiles)
        def _():
            for copy in fetch(t):
                copy.start()

    @pl.when(j == 0)
    def _():
        for t in range(SLOTS - 1):
            start(t)

    start(j + SLOTS - 1)
    for copy in fetch(j):
        copy.wait()
    return lax.rem(j, SLOTS)


def buffers(depth):
    return [
        pltpu.VMEM((SLOTS, depth, TILE), BF16),
        pltpu.VMEM((SLOTS, depth, TILE), BF16),
        pltpu.SemaphoreType.DMA((2, SLOTS)),
    ]


def ahead_kernel(owns, mate, w0, w1, out):
    out[...] = (dot(owns[0 : out.shape[0], :], w0[...]) + dot(mate[...], w1[...])).astype(BF16)


def project_ahead(owns, mate, w0, w1):
    return pl.pallas_call(
        ahead_kernel,
        in_specs=[FULL] * 4,
        out_specs=FULL,
        out_shape=jax.ShapeDtypeStruct((owns.shape[0] // 2, w0.shape[1]), BF16),
        compiler_params=params(16),
        cost_estimate=CHEAP,
        name="project_ahead",
    )(owns, mate, w0, w1)


def join_kernel(first, second, _, out):
    rows = first.shape[0]
    out[0:rows, :] = first[...]
    out[rows:, :] = second[...]


def join(first, second, token):
    rows, depth = first.shape
    return pl.pallas_call(
        join_kernel,
        in_specs=[FULL, FULL, ANY],
        out_specs=FULL,
        out_shape=jax.ShapeDtypeStruct((2 * rows, depth), BF16),
        compiler_params=params(8),
        cost_estimate=CHEAP,
        name="join",
    )(first, second, token)


def both_kernel(base, cut, owns, mates, w0_far, w1_far, *refs):
    fars, near, w0, w1, sem = refs[:-4], *refs[-4:]
    rows = near.shape[0]
    slot = stream(base, w0_far, w1_far, w0, w1, sem)
    total = dot(owns[...], w0[slot]) + dot(mates[...], w1[slot])
    near[...] = total[rows:]
    for k, far_out in enumerate(fars):

        @pl.when(pl.program_id(0) // cut == k)
        def _():
            far_out[...] = total[0:rows].astype(BF16)


def project_both(owns, mates, w0, w1, first, count, chunk):
    rows, depth = owns.shape[0] // 2, owns.shape[1]
    cut = chunk // TILE
    chunks = count // chunk

    def placed(k):
        return pl.BlockSpec((rows, TILE), lambda j: (0, jnp.clip(j - k * cut, 0, cut - 1)))

    *fars, near = pl.pallas_call(
        functools.partial(both_kernel, first // TILE, cut),
        grid=(count // TILE,),
        in_specs=[FULL] * 2 + [FAR] * 2,
        out_specs=[placed(k) for k in range(chunks)] + [pl.BlockSpec((rows, TILE), lambda j: (0, j))],
        out_shape=[jax.ShapeDtypeStruct((rows, chunk), BF16)] * chunks + [jax.ShapeDtypeStruct((rows, count), F32)],
        scratch_shapes=buffers(depth),
        compiler_params=params(24),
        cost_estimate=CHEAP,
        name="project_both",
    )(owns, mates, w0, w1)
    return fars, near


def near_kernel(owns, mates, w0_far, w1_far, arrived, out, w0, w1, sem):
    slot = stream(0, w0_far, w1_far, w0, w1, sem)
    rows = out.shape[0]
    total = dot(owns[rows:, :], w0[slot]) + dot(mates[rows:, :], w1[slot])
    out[...] = (total + arrived[...].astype(F32)).astype(BF16)


def project_near(owns, mates, w0, w1, arrived):
    rows, depth = owns.shape[0] // 2, owns.shape[1]
    placed = pl.BlockSpec((rows, TILE), lambda j: (0, j))
    return pl.pallas_call(
        near_kernel,
        grid=(arrived.shape[1] // TILE,),
        in_specs=[FULL, FULL, FAR, FAR, placed],
        out_specs=placed,
        out_shape=jax.ShapeDtypeStruct((rows, w0.shape[1]), BF16),
        scratch_shapes=buffers(depth),
        compiler_params=params(20),
        cost_estimate=CHEAP,
        name="project_near",
    )(owns, mates, w0, w1, arrived)


def add_kernel(near, *refs):
    arrived, out = refs[:-2], refs[-1]
    chunk = arrived[0].shape[1]
    for k, part in enumerate(arrived):
        lanes = slice(k * chunk, (k + 1) * chunk)
        out[:, lanes] = (near[:, lanes] + part[...].astype(F32)).astype(BF16)


def add_chunks(near, first, arrived, result, at):
    rows, chunk = arrived[0].shape
    count = chunk * len(arrived)
    return pl.pallas_call(
        add_kernel,
        grid=(1,),
        in_specs=[pl.BlockSpec((rows, count), lambda j: (0, first // count))] + [FULL] * len(arrived) + [ANY],
        out_specs=pl.BlockSpec((rows, count), lambda j: (0, at // count)),
        out_shape=jax.ShapeDtypeStruct(result.shape, BF16),
        input_output_aliases={1 + len(arrived): 0},
        compiler_params=params(8),
        cost_estimate=CHEAP,
        name="add_chunks",
    )(near, *arrived, result)


def shift(block, distance):
    size = lax.axis_size("seq")
    return lax.ppermute(block, "seq", [(i, i + distance) for i in range(size - distance)])


def swap(block, axis, bit):
    return lax.ppermute(block, axis, [(i, i ^ bit) for i in range(lax.axis_size(axis))])


def rotate(block, distance):
    size = lax.axis_size("seq")
    return lax.ppermute(block, "seq", [(i, (i + distance) % size) for i in range(size)])


def log_steps(info, got, keep, rates_kept, done, pairs, scan_next):
    half = keep.shape[1]
    message = ((N + EXTRA, half), BF16)
    full = ((N, half), F32)
    msg, own, first, aux = combine(
        pair_kernel,
        (info, got, keep, rates_kept, done),
        [SCALAR, FULL, FULL, FULL, ANY],
        [message, full, full, ((16, half), F32)],
        "pair",
    )
    behind = None
    covered = 0
    while True:
        got = shift(msg, 2 * (covered + 1))
        done = scan_next(msg)
        covered = 2 * covered + 1
        if covered >= pairs - 1:
            break
        operands, specs = [got, own, aux], [FULL, FULL, FULL]
        if behind is None:
            kernel = lambda g, o, a, t, m, b: wave_kernel(g, o, a, None, t, m, b)
        else:
            kernel = wave_kernel
            operands.append(behind)
            specs.append(FULL)
        msg, behind = combine(kernel, operands + [done], specs + [ANY], [message, ((N + 8, half), F32)], "wave")
    operands, specs = [info, got], [SCALAR, FULL]
    if behind is None:
        kernel = lambda o, g, f, a, t, b, h: last_kernel(o, g, None, f, a, t, b, h)
    else:
        kernel = last_kernel
        operands.append(behind)
        specs.append(FULL)
    out = ((N, half), BF16)
    back, held = combine(kernel, operands + [first, aux, done], specs + [FULL, FULL, ANY], [out, out], "last")
    return back, held


def local(
    x_input,
    z_input,
    bc_input,
    conv_weight_x,
    conv_weight_bc,
    step_size,
    log_decay,
    skip_gain,
    norm_gain,
    out_weight,
):
    length, width = x_input.shape
    heads = step_size.shape[1]
    ways = lax.axis_size("head")
    pairs = lax.axis_size("seq") // 2
    mine = lax.axis_index("head")
    half = width // 2
    seq = lax.axis_index("seq")
    info = jnp.stack([seq & 1, mine ^ 3, mine ^ 2, mine ^ 1, mine, seq >> 1, seq, 1 - (seq & 1), seq & 1]).astype(jnp.int32)

    x_far, z_far, w_far = far(x_input, z_input, out_weight)
    (bc_far,) = far(bc_input)
    halo = rotate(tail_rows(x_far, bc_far), 1)
    bc = bc_input.reshape(length, -1)
    (weight_mate,) = far(swap(out_weight, "head", 1))

    (cum, cum_s, log_s, f_dev, f_blk, rates), ones, x_sent = decays(
        info, log_decay, step_size, skip_gain, x_input, half
    )
    taps = far(conv_weight_x, conv_weight_bc)
    shared = (bc, halo, *taps)
    x0, bc0, send, x_kept = conv_states(0, info, x_sent, *shared, f_dev[0], ones, rates[0], x_far)
    got = swap(send, "seq", 1)
    x1, bc1, keep, z_near = conv_states(1, info, x_kept, *shared, f_dev[1], ones, rates[1], z_far)
    rates_kept = rates[1]

    uvs = []
    groups = list(zip((x0, x1), (z_near, z_near), (bc0, bc1), cum, cum_s, log_s, f_blk, rates))

    def scan_next(token):
        if len(uvs) < 2 * B_PARTS:
            order, part = divmod(len(uvs), B_PARTS)
            uvs.append(scan_part(order, part, info, token, *groups[order]))
        return uvs[-1]

    full = ((N, half), F32)
    message = ((N + EXTRA, half), BF16)
    done = scan_next(keep)
    out = ((N, half), BF16)
    if pairs > 1 and half % (pairs * N) == 0:
        piece = half // pairs
        part = ((N + EXTRA, piece), BF16)
        first, aux, *parts = combine(
            pair_split_kernel,
            (info, got, keep, rates_kept, done),
            [SCALAR, FULL, FULL, FULL, ANY],
            [full, ((8, half), F32)] + [part] * pairs,
            "pair",
            [pltpu.VMEM(*message)],
        )
        parts = list(parts[:1]) + [rotate(parts[r], 2 * r) for r in range(1, pairs)]
        done = scan_next(parts[0])
        parts = combine(
            owner_kernel,
            [info] + parts + [done],
            [SCALAR] + [FULL] * pairs + [ANY],
            [((N, piece), BF16)] * pairs,
            "owner",
            [pltpu.VMEM((pairs, N + EXTRA, piece), BF16), pltpu.VMEM((pairs, N, piece), BF16)],
        )
        ready = parts[0]
        parts = list(parts[:1]) + [rotate(parts[r], 2 * r) for r in range(1, pairs)]
        done = scan_next(ready)
        back, held = combine(
            last_split_kernel,
            [info, first, aux, done] + parts,
            [SCALAR, FULL, FULL, ANY] + [FULL] * pairs,
            [out, out],
            "last",
            [pltpu.VMEM(*out)],
        )
    else:
        back, held = log_steps(info, got, keep, rates_kept, done, pairs, scan_next)
    other = swap(back, "seq", 1)
    while len(uvs) < 2 * B_PARTS:
        scan_next(back)

    count = length // ways
    gain = norm_gain[None, :]

    columns = out_weight.shape[1]
    chunk = columns // 8
    weights = (w_far, weight_mate)
    kept, w0, w1 = norm_rows(
        1, (0, 2, 1, 3), info, count, held, bc1, held, gain, uvs[B_PARTS:], weights=weights, columns=chunk
    )
    shared = (bc0, other, gain, uvs[:B_PARTS], kept)
    far_mate, near_mate = norm_rows(0, (0, 2), info, count, kept, *shared, apart=True)
    (owns,) = norm_rows(0, (1, 3), info, count, far_mate, *shared, 2 * count)
    far_mate = swap(far_mate, "head", 1)
    sent = project_ahead(owns, far_mate, w0, w1)
    first = swap(sent, "head", 2)
    operands = (owns, join(far_mate, swap(near_mate, "head", 1), sent), *weights)
    calls = []
    for lo, hi in ((1, 2), (2, 4), (4, 6), (6, 8)):
        sent, near = project_both(*operands, lo * chunk, (hi - lo) * chunk, chunk)
        calls.append((near, lo, [swap(part, "head", 2) for part in sent]))
    result = project_near(*operands, first)
    for near, lo, arrived in calls[:-1]:
        result = add_chunks(near, 0, arrived, result, lo * chunk)
    near, lo, arrived = calls[-1]
    for k, part in enumerate(arrived):
        result = add_chunks(near, k * chunk, [part], result, (lo + k) * chunk)
    return result


def solution(mesh):
    in_specs = (
        P("seq", "head"),
        P("seq", "head"),
        P("seq", "head", None),
        P(None, "head"),
        P(None, "head", None),
        P("seq", "head"),
        P("seq", "head"),
        P("head"),
        P("head"),
        P("head", None),
    )
    out_specs = P(("seq", "head"), None)
    return jax.shard_map(local, mesh=mesh, in_specs=in_specs, out_specs=out_specs, check_vma=False)
```

```python
import functools

import jax
import jax.numpy as jnp
from jax import lax
from jax.experimental import pallas as pl
from jax.experimental.pallas import tpu as pltpu
from jax.sharding import PartitionSpec as P

P_SIZE = 64
N = 128
KCONV = 4
EPS = 1e-05
LOG2E = 1.4426950408889634

TOK_A = 256
ROWS_A = 32
TOK_B = 128
STEP_B = 256
EXTRA = 16
SLAB = 256
ROWS_C = 256
TILE = 256
SLOTS = 4
LEAD = 16
B_PARTS = 2
HIGHEST = lax.Precision.HIGHEST
F32 = jnp.float32
BF16 = jnp.bfloat16


def params(mib):
    return pltpu.CompilerParams(vmem_limit_bytes=mib * 1024 * 1024)


CHEAP = pl.CostEstimate(flops=1, bytes_accessed=1, transcendentals=0)
SCALAR = pl.BlockSpec(memory_space=pltpu.SMEM)
FULL = pl.BlockSpec(memory_space=pltpu.VMEM)
FAR = pl.BlockSpec(memory_space=pltpu.HBM)
ANY = pl.BlockSpec(memory_space=pl.ANY)

ODD, ROWS, PAIR, SEQ, GROUP = 0, 1, 5, 6, 7


def dot(a, b, dims=((1,), (0,)), precision=None):
    return lax.dot_general(a, b, (dims, ((), ())), precision=precision, preferred_element_type=F32)


def half_silu(half):
    return half + half * jnp.tanh(half)


def far(*arrays):
    return [pltpu.with_memory_space_constraint(a, pltpu.HBM) for a in arrays]


def whole(shape):
    return pl.BlockSpec(shape, lambda *_: (0,) * len(shape))


def group_copies(x_far, x, group, sems):
    length, width = x.shape
    rows = length // 4
    lanes = pl.ds(pl.multiple_of(group * width, width), width)
    pieces = [pl.ds(k * rows, rows) for k in range(4)]
    return [pltpu.make_async_copy(x_far.at[at, lanes], x.at[at], sems.at[k]) for k, at in enumerate(pieces)]


def decay_kernel(info, ld_t, step_t, skip, x_far, *refs):
    cum, cum_s, log_s, f_dev, f_blk, rates = [refs[2 * k : 2 * k + 2] for k in range(6)]
    ones, x, sem = refs[12:]
    copies = group_copies(x_far, x, info[GROUP], sem)
    for copy in copies:
        copy.start()
    heads, length = ld_t.shape
    blocks = length // TOK_B
    per = heads // 2
    width = ones.shape[1]
    swapped = info[GROUP] == 1
    row = lax.broadcasted_iota(jnp.int32, (TOK_B, TOK_B), 0)
    col = lax.broadcasted_iota(jnp.int32, (TOK_B, TOK_B), 1)
    lower = (row >= col).astype(F32)
    upper = (row <= col).astype(F32)
    eye = (row == col).astype(BF16)

    def ordered(value):
        return jnp.where(swapped, jnp.concatenate([value[per:], value[:per]], 0), value)

    def put(ref, rows, value):
        high = value.astype(BF16)
        low = (value - high.astype(F32)).astype(BF16)
        for g in range(2):
            own = slice(g * per, (g + 1) * per)
            both = jnp.concatenate([high[own], low[own]], 0)
            ref[g][rows, :] = dot(eye, both, ((1,), (1,))).astype(BF16)

    first = lax.broadcasted_iota(jnp.int32, (per, width), 0) * P_SIZE
    lane = lax.broadcasted_iota(jnp.int32, (per, width), 1)
    member = ((lane >= first) & (lane < first + P_SIZE)).astype(F32)
    ones[0:per, :] = member.astype(BF16)
    ones[per:, :] = member.astype(BF16)
    cums, totals, row_totals = [], [], []
    for b in range(blocks):
        rows = slice(b * TOK_B, (b + 1) * TOK_B)
        logs = ordered(ld_t[:, rows]) * LOG2E
        c = dot(lower, logs, ((1,), (1,)), HIGHEST)
        for g in range(2):
            cum[g][rows, :] = c[:, g * per : (g + 1) * per]
        row_totals.append(c[TOK_B - 1 : TOK_B, :])
        c = dot(logs, upper, precision=HIGHEST)
        cums.append(c)
        totals.append(c[:, TOK_B - 1 : TOK_B])
    before, row_before = [jnp.zeros_like(totals[0])], [jnp.zeros_like(row_totals[0])]
    for b in range(blocks):
        before.append(before[-1] + totals[b])
        row_before.append(row_before[-1] + row_totals[b])
    total = before[-1]
    logs = jnp.concatenate(row_totals + row_before[:-1] + row_before[-1:] * 8, 0)
    gains = jnp.broadcast_to(skip[...], (8, heads))
    gains = jnp.where(swapped, jnp.concatenate([gains[:, per:], gains[:, :per]], 1), gains)
    values = jnp.concatenate([jnp.exp2(logs), gains], 0)
    for g in range(2):
        rates[g][...] = dot(values[:, g * per : (g + 1) * per], member, precision=HIGHEST)
    for b in range(blocks):
        rows = slice(b * TOK_B, (b + 1) * TOK_B)
        s = ordered(step_t[:, rows])
        log_step = jnp.log2(s)
        shifted = cums[b] - log_step
        fade = jnp.exp2(totals[b] - cums[b]) * s
        for g in range(2):
            own = slice(g * per, (g + 1) * per)
            log_s[g][:, rows] = log_step[own, :]
            cum_s[g][:, rows] = shifted[own, :]
            f_blk[g][:, rows] = fade[own, :]
        put(f_dev, rows, jnp.exp2(total - (cums[b] + before[b])) * s)
    for copy in copies:
        copy.wait()


def decays(info, log_decay, step, skip, x, width):
    length, heads = log_decay.shape
    blocks = length // TOK_B
    per = heads // 2
    across = jax.ShapeDtypeStruct((per, length), F32)
    pair = jax.ShapeDtypeStruct((length, 2 * per), BF16)
    column = jax.ShapeDtypeStruct((length, per), F32)
    rates = jax.ShapeDtypeStruct((2 * blocks + 16, width), F32)
    shapes = [shape for shape in (column, across, across, pair, across, rates) for _ in range(2)]
    shapes += [
        jax.ShapeDtypeStruct((2 * per, width), BF16),
        pltpu.VMEM((length, width), BF16),
    ]
    *refs, ones, x_near = pl.pallas_call(
        decay_kernel,
        in_specs=[SCALAR] + [FULL] * 3 + [FAR],
        out_specs=[FULL] * len(shapes),
        out_shape=shapes,
        scratch_shapes=[pltpu.SemaphoreType.DMA((4,))],
        compiler_params=params(16),
        cost_estimate=CHEAP,
        name="decays",
    )(info, *far(log_decay.T, step.T, skip[None, :], x))
    return [tuple(refs[2 * k : 2 * k + 2]) for k in range(6)], ones, x_near


def tail_kernel(x, bc, out):
    width, bc_width = x.shape[1], bc.shape[2]
    out[:, 0:width] = x[...]
    for g in range(bc.shape[1]):
        out[:, width + g * bc_width : width + (g + 1) * bc_width] = bc[:, g, :]


def tail_rows(x, bc):
    length, width = x.shape
    groups, bc_width = bc.shape[1:]
    at = length // LEAD - 1
    shape = (LEAD, width + groups * bc_width)
    return pl.pallas_call(
        tail_kernel,
        grid=(1,),
        in_specs=[
            pl.BlockSpec((LEAD, width), lambda i: (at, 0)),
            pl.BlockSpec((LEAD, groups, bc_width), lambda i: (at, 0, 0)),
        ],
        out_specs=whole(shape),
        out_shape=jax.ShapeDtypeStruct(shape, BF16),
        compiler_params=params(8),
        cost_estimate=CHEAP,
        name="tail_rows",
    )(x, bc)


def put_message(ref, state, decay):
    high = decay.astype(BF16)
    low = (decay - high.astype(F32)).astype(BF16)
    rest = jnp.zeros((EXTRA - 2, state.shape[1]), BF16)
    ref[0:N, :] = state.astype(BF16)
    ref[N:, :] = jnp.concatenate([high, low, rest], 0)


def take_message(ref):
    extra = ref[N:, :].astype(F32)
    return ref[0:N, :].astype(F32), extra[0:1] + extra[1:2]


def conv_kernel(order, info, x, bc, halo, wx, wbc, f_dev, ones, rates, *refs):
    next_far, refs = refs[0], refs[1:]
    x_out, bc_out, final = refs[:3]
    xf, state, down = refs[-3:]
    length, width = x_out.shape
    rows = TOK_A
    group = info[GROUP + order]
    first_lane = pl.multiple_of(group * width, width)
    taken, sem = refs[3:5]
    first_bc = pl.multiple_of(group * 2 * N, 2 * N)
    if order == 0:
        copies = group_copies(next_far, taken, info[GROUP + 1], sem)
    else:
        part = length // 4
        pieces = [pl.ds(k * part, part) for k in range(4)]
        copies = [pltpu.make_async_copy(next_far.at[at], taken.at[at], sem.at[k]) for k, at in enumerate(pieces)]
    for copy in copies:
        copy.start()
    state[...] = jnp.zeros_like(state)
    row = lax.broadcasted_iota(jnp.int32, down.shape, 0)
    col = lax.broadcasted_iota(jnp.int32, down.shape, 1)
    down[...] = (row == col + 1).astype(BF16)

    def conv(i, src, moved, first, behind, weights, emit):
        at_start = jnp.where(info[SEQ] == 0, jnp.zeros_like(first), first)
        lead = jnp.where(i == 0, at_start, behind).astype(F32)
        w0, w1, w2, w3 = [w * 0.5 for w in weights]
        back = LEAD - 8
        lead_r1 = pltpu.roll(lead, 1, 0)
        last_p = (w1 * lead + w0 * lead_r1)[back:]
        top = lax.broadcasted_iota(jnp.int32, (8, lead.shape[1]), 0) == 0
        head = jnp.where(top, jnp.broadcast_to(lead[LEAD - 1 :], top.shape), moved[0:8])
        for r in range(0, rows, ROWS_A):
            cur = src[r : r + ROWS_A].astype(F32)
            r1 = moved[r : r + ROWS_A] if r else jnp.concatenate([head, moved[8:ROWS_A]], 0)
            p = w1 * cur + w0 * r1
            p2 = pltpu.roll(jnp.concatenate([last_p, p], 0), 2, 0)[8:]
            emit(r, half_silu((w3 * cur + w2 * r1) + p2))
            last_p = p[ROWS_A - 8 :]

    def step(i, _):
        at = pl.ds(pl.multiple_of(i * rows, rows), rows)
        behind = pl.ds(pl.multiple_of(jnp.maximum(i * rows - LEAD, 0), LEAD), LEAD)

        def out(r):
            return pl.ds(pl.multiple_of(i * rows + r, ROWS_A), ROWS_A)

        for lanes in range(0, 2 * N, SLAB):
            ds = slice(lanes, lanes + SLAB)
            src = pl.ds(pl.multiple_of(first_bc + lanes, SLAB), SLAB)
            halo_src = pl.ds(pl.multiple_of(2 * width + first_bc + lanes, SLAB), SLAB)

            def emit_bc(r, value):
                bc_out[out(r), ds] = value.astype(BF16)

            weights = [jnp.where(group == 0, wbc[k, 0:1, ds], wbc[k, 1:2, ds]) for k in range(KCONV)]
            conv(i, bc[at, src], dot(down[...], bc[at, src]), halo[:, halo_src], bc[behind, src], weights, emit_bc)

        for lanes in range(0, width, SLAB):
            ds = slice(lanes, lanes + SLAB)
            src = pl.ds(pl.multiple_of(first_lane + lanes, SLAB), SLAB)
            scale = dot(f_dev[at, :], ones[:, ds])

            def emit(r, value):
                x_out[out(r), ds] = value.astype(BF16)
                xf[r : r + ROWS_A, ds] = (value * scale[r : r + ROWS_A]).astype(BF16)

            weights = [wx[k : k + 1, ds] for k in range(KCONV)]
            conv(i, x[at, ds], dot(down[...], x[at, ds]), halo[:, src], x[behind, ds], weights, emit)

        state[...] += dot(bc_out[at, 0:N], xf[...], ((0,), (0,)))
        return 0

    lax.fori_loop(0, length // rows, step, 0)
    if order == 0:
        row = rates.shape[0] - 16
        put_message(final, state[...], rates[row : row + 1, :])
    else:
        final[...] = state[...]
    for copy in copies:
        copy.wait()


def conv_states(order, info, x, bc, halo, wx, wbc, f_dev, ones, rates, ahead):
    length, width = x.shape
    column = lambda i, info: (0, info[GROUP + order])
    final = ((N + EXTRA, width), BF16) if order == 0 else ((N, width), F32)
    taken = (length, width) if order == 0 else ahead.shape
    return pl.pallas_call(
        functools.partial(conv_kernel, order),
        grid_spec=pltpu.PrefetchScalarGridSpec(
            num_scalar_prefetch=1,
            grid=(1,),
            in_specs=[FULL] * 3 + [pl.BlockSpec((KCONV, width), column)] + [FULL] * 4 + [FAR],
            out_specs=[FULL] * 4,
            scratch_shapes=[
                pltpu.SemaphoreType.DMA((4,)),
                pltpu.VMEM((TOK_A, width), BF16),
                pltpu.VMEM((N, width), F32),
                pltpu.VMEM((TOK_A, TOK_A), BF16),
            ],
        ),
        out_shape=[
            pltpu.VMEM((length, width), BF16),
            pltpu.VMEM((length, 2 * N), BF16),
            jax.ShapeDtypeStruct(*final),
            pltpu.VMEM(taken, BF16),
        ],
        compiler_params=params(16),
        cost_estimate=CHEAP,
        name="conv_states",
    )(info, x, bc, halo, wx, wbc, f_dev, ones, rates, ahead)


def pair_kernel(info, got, keep, rates, _, msg, own, first, aux):
    half = keep.shape[1]
    is_odd = info[ODD] == 1
    arrived, their = take_message(got)
    row = rates.shape[0] - 16
    mine = rates[row : row + 1, :]
    early = jnp.where(is_odd, arrived, keep[...])
    late = jnp.where(is_odd, keep[...], arrived)
    even_decay = jnp.where(is_odd, their, mine)
    odd_decay = jnp.where(is_odd, mine, their)
    state = odd_decay * early + late
    own[...] = state
    first[...] = early
    aux[0:8, :] = jnp.broadcast_to(even_decay, (8, half))
    aux[8:16, :] = jnp.broadcast_to(even_decay * odd_decay, (8, half))
    put_message(msg, state, even_decay * odd_decay)


def wave_kernel(got, own, aux, behind_in, _, msg, behind):
    before, decay = take_message(got)
    if behind_in is not None:
        before_decay = behind_in[N : N + 1, :]
        before = behind_in[0:N, :] + before_decay * before
        decay = before_decay * decay
    pair_decay = aux[8:9, :]
    behind[0:N, :] = before
    behind[N:, :] = jnp.broadcast_to(decay, (8, before.shape[1]))
    put_message(msg, own[...] + pair_decay * before, pair_decay * decay)


def last_kernel(info, got, behind_in, first, aux, _, back, held):
    is_odd = info[ODD] == 1
    before, _unused = take_message(got)
    if behind_in is not None:
        before = behind_in[0:N, :] + behind_in[N : N + 1, :] * before
    entering_odd = aux[0:1, :] * before + first[...]
    back[...] = jnp.where(is_odd, before, entering_odd).astype(BF16)
    held[...] = jnp.where(is_odd, entering_odd, before).astype(BF16)


def pair_split_kernel(info, got, keep, rates, _, first, aux, *refs):
    outs, wide = refs[:-1], refs[-1]
    half = keep.shape[1]
    pairs = len(outs)
    piece = half // pairs
    is_odd = info[ODD] == 1
    arrived, their = take_message(got)
    row = rates.shape[0] - 16
    mine = rates[row : row + 1, :]
    early = jnp.where(is_odd, arrived, keep[...])
    late = jnp.where(is_odd, keep[...], arrived)
    even_decay = jnp.where(is_odd, their, mine)
    odd_decay = jnp.where(is_odd, mine, their)
    first[...] = early
    aux[...] = jnp.broadcast_to(even_decay, (8, half))
    put_message(wide, odd_decay * early + late, even_decay * odd_decay)
    for r in range(pairs):
        owner = lax.rem(info[PAIR] + r, pairs)
        outs[r][...] = wide[:, pl.ds(pl.multiple_of(owner * piece, piece), piece)]


def owner_kernel(info, *refs):
    pairs = (len(refs) - 3) // 2
    ins, outs = refs[:pairs], refs[pairs + 1 : 2 * pairs + 1]
    states, prefixes = refs[-2:]
    for r in range(pairs):
        states[lax.rem(info[PAIR] + pairs - r, pairs)] = ins[r][...]
    before = jnp.zeros(prefixes.shape[1:], F32)
    for q in range(pairs):
        prefixes[q] = before.astype(BF16)
        if q < pairs - 1:
            state, decay = take_message(states.at[q])
            before = decay * before + state
    for r in range(pairs):
        outs[r][...] = prefixes[lax.rem(info[PAIR] + r, pairs)]


def last_split_kernel(info, first, aux, _, *refs):
    pairs = len(refs) - 3
    back, held, wide = refs[-3:]
    piece = back.shape[1] // pairs
    for r in range(pairs):
        owner = lax.rem(info[PAIR] + pairs - r, pairs)
        wide[:, pl.ds(pl.multiple_of(owner * piece, piece), piece)] = refs[r][...]
    is_odd = info[ODD] == 1
    before = wide[...].astype(F32)
    entering_odd = aux[0:1, :] * before + first[...]
    back[...] = jnp.where(is_odd, before, entering_odd).astype(BF16)
    held[...] = jnp.where(is_odd, entering_odd, before).astype(BF16)


def combine(kernel, operands, specs, outs, name, scratch=()):
    return pl.pallas_call(
        kernel,
        in_specs=specs,
        out_specs=[FULL] * len(outs),
        out_shape=[jax.ShapeDtypeStruct(s, t) for s, t in outs],
        scratch_shapes=list(scratch),
        compiler_params=params(16),
        cost_estimate=CHEAP,
        name=name,
    )(*operands)


def scan_kernel(order, part, info, x, z, bc, cum, cum_s, log_s, f_blk, rates, _, uv_out, state):
    length = x.shape[0]
    width = state.shape[1]
    per_slab = SLAB // P_SIZE
    inner = STEP_B // TOK_B
    blocks = length // TOK_B
    first_head = part * width // P_SIZE
    first_lane = info[GROUP + order] * x.shape[1] + part * width
    state[...] = jnp.zeros_like(state)

    row = lax.broadcasted_iota(jnp.int32, (TOK_B, TOK_B), 0)
    col = lax.broadcasted_iota(jnp.int32, (TOK_B, TOK_B), 1)
    keep = row >= col
    first = lax.broadcasted_iota(jnp.int32, (TOK_B, 2 * P_SIZE), 1) < P_SIZE
    zero = jnp.zeros((TOK_B, 2 * P_SIZE), BF16)

    def turn(step, _):
        for k in range(inner):
            block(step * inner + k)
        return 0

    def block(b):
        at = pl.ds(pl.multiple_of(b * TOK_B, TOK_B), TOK_B)
        b_mat = bc[at, 0:N]
        c_mat = bc[at, N : 2 * N]
        b_across = b_mat.T
        scores = jnp.where(keep, dot(c_mat, b_mat, ((1,), (1,))), 0.0).astype(BF16)
        for s in range(width // SLAB):
            lanes = slice(s * SLAB, (s + 1) * SLAB)
            xb = x[at, part * width + s * SLAB : part * width + (s + 1) * SLAB]
            wide = slice(part * width + s * SLAB, part * width + (s + 1) * SLAB)
            fade_row = rates[pl.ds(b, 1), wide]
            lead_row = rates[pl.ds(blocks + b, 1), wide]
            skip = rates[2 * blocks + 8 : 2 * blocks + 9, wide]
            old = state[:, lanes]
            carried = dot(c_mat, old.astype(BF16))
            within, grown, rises = [], [], []
            for q in range(per_slab // 2):
                tables, fades, columns = [], [], []
                for h in (2 * q, 2 * q + 1):
                    head = first_head + s * per_slab + h
                    own = slice(head, head + 1)
                    column = jnp.broadcast_to(cum[at, own], (TOK_B, TOK_B))
                    gap = jnp.minimum(column - cum_s[own, at], log_s[own, at])
                    tables.append(scores * jnp.exp2(gap).astype(BF16))
                    fades.append(b_across * f_blk[own, at].astype(BF16))
                    columns.append(column)
                xp = xb[:, q * 2 * P_SIZE : (q + 1) * 2 * P_SIZE]
                stacked = jnp.concatenate([jnp.where(first, xp, zero), jnp.where(first, zero, xp)], 0)
                both = jnp.concatenate([jnp.concatenate(tables, 1), jnp.concatenate(fades, 1)], 0)
                product = dot(both, stacked)
                within.append(product[0:TOK_B])
                grown.append(product[TOK_B:])
                rises.append(jnp.exp2(jnp.where(first, columns[0], columns[1])))
            rise = jnp.concatenate(rises, 1)
            xs = xb.astype(F32)
            y = jnp.concatenate(within, 1) + carried * rise + skip * xs
            gate = half_silu((z[at, pl.ds(pl.multiple_of(first_lane + s * SLAB, SLAB), SLAB)] * 0.5).astype(F32))
            uv_out[at, lanes] = (y * gate).astype(BF16)
            uv_out[at, width + s * SLAB : width + (s + 1) * SLAB] = (gate * rise * lead_row).astype(BF16)
            state[:, lanes] = old * fade_row + jnp.concatenate(grown, 1)

    lax.fori_loop(0, length // STEP_B, turn, 0)


def scan_part(order, part, info, token, x, z, bc, cum, cum_s, log_s, f_blk, rates):
    length, full = x.shape
    width = full // B_PARTS
    return pl.pallas_call(
        functools.partial(scan_kernel, order, part),
        in_specs=[SCALAR] + [FULL] * 8 + [ANY],
        out_specs=FULL,
        out_shape=pltpu.VMEM((length, 2 * width), BF16),
        scratch_shapes=[pltpu.VMEM((N, width), F32)],
        compiler_params=params(12),
        cost_estimate=CHEAP,
        name="scan_part",
    )(info, x, z, bc, cum, cum_s, log_s, f_blk, rates, token)


def norm_kernel(order, places, skip, fetched, info, bc, state, gain, _, *refs):
    uvs, refs = refs[:B_PARTS], refs[B_PARTS:]
    if order == 0:
        kept, refs = refs[0], refs[1:]
    weights, outs, tiles, sem = refs[:fetched], refs[fetched : -1 - fetched], refs[len(refs) - 1 - fetched : -1], refs[-1]
    copies = [
        pltpu.make_async_copy(weight.at[:, pl.ds(0, tile.shape[1])], tile, sem.at[k])
        for k, (weight, tile) in enumerate(zip(weights, tiles))
    ]
    for copy in copies:
        copy.start()
    count = outs[0].shape[0] * len(outs) // len(places)
    per = state.shape[1]
    part = per // B_PARTS

    def lanes(group, p=0, size=per):
        return pl.ds(pl.multiple_of(info[GROUP + group] * per + p * part, part), size)

    def rows(out, first, base, source):
        to = pl.ds(pl.multiple_of(first, ROWS_C), ROWS_C)
        at = pl.ds(pl.multiple_of(base, ROWS_C), ROWS_C)
        c_mat = bc[at, N : 2 * N]
        pieces = []
        squares = None
        for p, uv in enumerate(uvs):
            inc = state[:, p * part : (p + 1) * part]
            gated = uv[at, 0:part].astype(F32) + uv[at, part:].astype(F32) * dot(c_mat, inc)
            square = jnp.sum(gated * gated, axis=-1, keepdims=True)
            squares = square if squares is None else squares + square
            pieces.append(gated)
        scale = lax.rsqrt(squares * (1.0 / per) + EPS)
        for p, gated in enumerate(pieces):
            value = (gated * scale * gain[:, lanes(order, p, part)]).astype(BF16)
            if order == 0:
                out[to, lanes(0, p, part)] = value
            else:
                out[to, p * part : (p + 1) * part] = value
        if order == 0:
            out[to, lanes(1)] = kept[pl.ds(pl.multiple_of(source, ROWS_C), ROWS_C), :]

    for k, place in enumerate(places):

        def step(j, _):
            out, first = (outs[k], 0) if len(outs) > 1 else (outs[0], k * count)
            source = skip + k * count + j * ROWS_C
            rows(out, first + j * ROWS_C, info[ROWS + place] * count + j * ROWS_C, source)
            return 0

        lax.fori_loop(0, count // ROWS_C, step, 0)
    for copy in copies:
        copy.wait()


def norm_rows(order, places, info, count, token, bc, state, gain, uvs, kept=None, skip=0, apart=False, weights=(), columns=0):
    width = state.shape[1] if order else gain.shape[1]
    tile = jax.ShapeDtypeStruct((gain.shape[1], columns), BF16)
    arrays = len(places) if apart else 1
    rows = jax.ShapeDtypeStruct((len(places) * count // arrays, width), BF16)
    joined = [] if kept is None else [kept]
    return pl.pallas_call(
        functools.partial(norm_kernel, order, places, skip, len(weights)),
        in_specs=[SCALAR] + [FULL] * 3 + [ANY] + [FULL] * (len(uvs) + len(joined)) + [FAR] * len(weights),
        out_specs=[FULL] * (arrays + len(weights)),
        out_shape=[rows] * arrays + [tile] * len(weights),
        scratch_shapes=[pltpu.SemaphoreType.DMA((2,))],
        compiler_params=params(16),
        cost_estimate=CHEAP,
        name="norm_rows",
    )(info, bc, state, gain, token, *uvs, *joined, *weights)


def stream(base, w0_far, w1_far, w0, w1, sem):
    j = pl.program_id(0)
    tiles = pl.num_programs(0)

    def fetch(t):
        slot = lax.rem(t, SLOTS)
        lanes = pl.ds(pl.multiple_of((base + t) * TILE, TILE), TILE)
        return (
            pltpu.make_async_copy(w0_far.at[:, lanes], w0.at[slot], sem.at[0, slot]),
            pltpu.make_async_copy(w1_far.at[:, lanes], w1.at[slot], sem.at[1, slot]),
        )

    def start(t):
        @pl.when(t < tiles)
        def _():
            for copy in fetch(t):
                copy.start()

    @pl.when(j == 0)
    def _():
        for t in range(SLOTS - 1):
            start(t)

    start(j + SLOTS - 1)
    for copy in fetch(j):
        copy.wait()
    return lax.rem(j, SLOTS)


def buffers(depth):
    return [
        pltpu.VMEM((SLOTS, depth, TILE), BF16),
        pltpu.VMEM((SLOTS, depth, TILE), BF16),
        pltpu.SemaphoreType.DMA((2, SLOTS)),
    ]


def ahead_kernel(owns, mate, w0, w1, out):
    out[...] = (dot(owns[0 : out.shape[0], :], w0[...]) + dot(mate[...], w1[...])).astype(BF16)


def project_ahead(owns, mate, w0, w1):
    return pl.pallas_call(
        ahead_kernel,
        in_specs=[FULL] * 4,
        out_specs=FULL,
        out_shape=jax.ShapeDtypeStruct((owns.shape[0] // 2, w0.shape[1]), BF16),
        compiler_params=params(16),
        cost_estimate=CHEAP,
        name="project_ahead",
    )(owns, mate, w0, w1)


def join_kernel(first, second, _, out):
    rows = first.shape[0]
    out[0:rows, :] = first[...]
    out[rows:, :] = second[...]


def join(first, second, token):
    rows, depth = first.shape
    return pl.pallas_call(
        join_kernel,
        in_specs=[FULL, FULL, ANY],
        out_specs=FULL,
        out_shape=jax.ShapeDtypeStruct((2 * rows, depth), BF16),
        compiler_params=params(8),
        cost_estimate=CHEAP,
        name="join",
    )(first, second, token)


def both_kernel(base, cut, owns, mates, w0_far, w1_far, *refs):
    fars, near, w0, w1, sem = refs[:-4], *refs[-4:]
    rows = near.shape[0]
    slot = stream(base, w0_far, w1_far, w0, w1, sem)
    total = dot(owns[...], w0[slot]) + dot(mates[...], w1[slot])
    near[...] = total[rows:]
    for k, far_out in enumerate(fars):

        @pl.when(pl.program_id(0) // cut == k)
        def _():
            far_out[...] = total[0:rows].astype(BF16)


def project_both(owns, mates, w0, w1, first, count, chunk):
    rows, depth = owns.shape[0] // 2, owns.shape[1]
    cut = chunk // TILE
    chunks = count // chunk

    def placed(k):
        return pl.BlockSpec((rows, TILE), lambda j: (0, jnp.clip(j - k * cut, 0, cut - 1)))

    *fars, near = pl.pallas_call(
        functools.partial(both_kernel, first // TILE, cut),
        grid=(count // TILE,),
        in_specs=[FULL] * 2 + [FAR] * 2,
        out_specs=[placed(k) for k in range(chunks)] + [pl.BlockSpec((rows, TILE), lambda j: (0, j))],
        out_shape=[jax.ShapeDtypeStruct((rows, chunk), BF16)] * chunks + [jax.ShapeDtypeStruct((rows, count), F32)],
        scratch_shapes=buffers(depth),
        compiler_params=params(24),
        cost_estimate=CHEAP,
        name="project_both",
    )(owns, mates, w0, w1)
    return fars, near


def near_kernel(owns, mates, w0_far, w1_far, arrived, out, w0, w1, sem):
    slot = stream(0, w0_far, w1_far, w0, w1, sem)
    rows = out.shape[0]
    total = dot(owns[rows:, :], w0[slot]) + dot(mates[rows:, :], w1[slot])
    out[...] = (total + arrived[...].astype(F32)).astype(BF16)


def project_near(owns, mates, w0, w1, arrived):
    rows, depth = owns.shape[0] // 2, owns.shape[1]
    placed = pl.BlockSpec((rows, TILE), lambda j: (0, j))
    return pl.pallas_call(
        near_kernel,
        grid=(arrived.shape[1] // TILE,),
        in_specs=[FULL, FULL, FAR, FAR, placed],
        out_specs=placed,
        out_shape=jax.ShapeDtypeStruct((rows, w0.shape[1]), BF16),
        scratch_shapes=buffers(depth),
        compiler_params=params(20),
        cost_estimate=CHEAP,
        name="project_near",
    )(owns, mates, w0, w1, arrived)


def add_kernel(near, *refs):
    arrived, out = refs[:-2], refs[-1]
    chunk = arrived[0].shape[1]
    for k, part in enumerate(arrived):
        lanes = slice(k * chunk, (k + 1) * chunk)
        out[:, lanes] = (near[:, lanes] + part[...].astype(F32)).astype(BF16)


def add_chunks(near, first, arrived, result, at):
    rows, chunk = arrived[0].shape
    count = chunk * len(arrived)
    return pl.pallas_call(
        add_kernel,
        grid=(1,),
        in_specs=[pl.BlockSpec((rows, count), lambda j: (0, first // count))] + [FULL] * len(arrived) + [ANY],
        out_specs=pl.BlockSpec((rows, count), lambda j: (0, at // count)),
        out_shape=jax.ShapeDtypeStruct(result.shape, BF16),
        input_output_aliases={1 + len(arrived): 0},
        compiler_params=params(8),
        cost_estimate=CHEAP,
        name="add_chunks",
    )(near, *arrived, result)


def shift(block, distance):
    size = lax.axis_size("seq")
    return lax.ppermute(block, "seq", [(i, i + distance) for i in range(size - distance)])


def swap(block, axis, bit):
    return lax.ppermute(block, axis, [(i, i ^ bit) for i in range(lax.axis_size(axis))])


def rotate(block, distance):
    size = lax.axis_size("seq")
    return lax.ppermute(block, "seq", [(i, (i + distance) % size) for i in range(size)])


def log_steps(info, got, keep, rates_kept, done, pairs, scan_next):
    half = keep.shape[1]
    message = ((N + EXTRA, half), BF16)
    full = ((N, half), F32)
    msg, own, first, aux = combine(
        pair_kernel,
        (info, got, keep, rates_kept, done),
        [SCALAR, FULL, FULL, FULL, ANY],
        [message, full, full, ((16, half), F32)],
        "pair",
    )
    behind = None
    covered = 0
    while True:
        got = shift(msg, 2 * (covered + 1))
        done = scan_next(msg)
        covered = 2 * covered + 1
        if covered >= pairs - 1:
            break
        operands, specs = [got, own, aux], [FULL, FULL, FULL]
        if behind is None:
            kernel = lambda g, o, a, t, m, b: wave_kernel(g, o, a, None, t, m, b)
        else:
            kernel = wave_kernel
            operands.append(behind)
            specs.append(FULL)
        msg, behind = combine(kernel, operands + [done], specs + [ANY], [message, ((N + 8, half), F32)], "wave")
    operands, specs = [info, got], [SCALAR, FULL]
    if behind is None:
        kernel = lambda o, g, f, a, t, b, h: last_kernel(o, g, None, f, a, t, b, h)
    else:
        kernel = last_kernel
        operands.append(behind)
        specs.append(FULL)
    out = ((N, half), BF16)
    back, held = combine(kernel, operands + [first, aux, done], specs + [FULL, FULL, ANY], [out, out], "last")
    return back, held


def local(
    x_input,
    z_input,
    bc_input,
    conv_weight_x,
    conv_weight_bc,
    step_size,
    log_decay,
    skip_gain,
    norm_gain,
    out_weight,
):
    length, width = x_input.shape
    heads = step_size.shape[1]
    ways = lax.axis_size("head")
    pairs = lax.axis_size("seq") // 2
    mine = lax.axis_index("head")
    half = width // 2
    seq = lax.axis_index("seq")
    info = jnp.stack([seq & 1, mine ^ 3, mine ^ 2, mine ^ 1, mine, seq >> 1, seq, 1 - (seq & 1), seq & 1]).astype(jnp.int32)

    x_far, z_far, w_far = far(x_input, z_input, out_weight)
    (bc_far,) = far(bc_input)
    halo = rotate(tail_rows(x_far, bc_far), 1)
    bc = bc_input.reshape(length, -1)
    (weight_mate,) = far(swap(out_weight, "head", 1))

    (cum, cum_s, log_s, f_dev, f_blk, rates), ones, x_sent = decays(
        info, log_decay, step_size, skip_gain, x_input, half
    )
    taps = far(conv_weight_x, conv_weight_bc)
    shared = (bc, halo, *taps)
    x0, bc0, send, x_kept = conv_states(0, info, x_sent, *shared, f_dev[0], ones, rates[0], x_far)
    got = swap(send, "seq", 1)
    x1, bc1, keep, z_near = conv_states(1, info, x_kept, *shared, f_dev[1], ones, rates[1], z_far)
    rates_kept = rates[1]

    uvs = []
    groups = list(zip((x0, x1), (z_near, z_near), (bc0, bc1), cum, cum_s, log_s, f_blk, rates))

    def scan_next(token):
        if len(uvs) < 2 * B_PARTS:
            order, part = divmod(len(uvs), B_PARTS)
            uvs.append(scan_part(order, part, info, token, *groups[order]))
        return uvs[-1]

    full = ((N, half), F32)
    message = ((N + EXTRA, half), BF16)
    done = scan_next(keep)
    out = ((N, half), BF16)
    if pairs > 1 and half % (pairs * N) == 0:
        piece = half // pairs
        part = ((N + EXTRA, piece), BF16)
        first, aux, *parts = combine(
            pair_split_kernel,
            (info, got, keep, rates_kept, done),
            [SCALAR, FULL, FULL, FULL, ANY],
            [full, ((8, half), F32)] + [part] * pairs,
            "pair",
            [pltpu.VMEM(*message)],
        )
        parts = list(parts[:1]) + [rotate(parts[r], 2 * r) for r in range(1, pairs)]
        done = scan_next(parts[0])
        parts = combine(
            owner_kernel,
            [info] + parts + [done],
            [SCALAR] + [FULL] * pairs + [ANY],
            [((N, piece), BF16)] * pairs,
            "owner",
            [pltpu.VMEM((pairs, N + EXTRA, piece), BF16), pltpu.VMEM((pairs, N, piece), BF16)],
        )
        ready = parts[0]
        parts = list(parts[:1]) + [rotate(parts[r], 2 * r) for r in range(1, pairs)]
        done = scan_next(ready)
        back, held = combine(
            last_split_kernel,
            [info, first, aux, done] + parts,
            [SCALAR, FULL, FULL, ANY] + [FULL] * pairs,
            [out, out],
            "last",
            [pltpu.VMEM(*out)],
        )
    else:
        back, held = log_steps(info, got, keep, rates_kept, done, pairs, scan_next)
    other = swap(back, "seq", 1)
    while len(uvs) < 2 * B_PARTS:
        scan_next(back)

    count = length // ways
    gain = norm_gain[None, :]

    columns = out_weight.shape[1]
    chunk = columns // 8
    weights = (w_far, weight_mate)
    kept, w0, w1 = norm_rows(
        1, (0, 2, 1, 3), info, count, held, bc1, held, gain, uvs[B_PARTS:], weights=weights, columns=chunk
    )
    shared = (bc0, other, gain, uvs[:B_PARTS], kept)
    far_mate, near_mate = norm_rows(0, (0, 2), info, count, kept, *shared, apart=True)
    (owns,) = norm_rows(0, (1, 3), info, count, far_mate, *shared, 2 * count)
    far_mate = swap(far_mate, "head", 1)
    sent = project_ahead(owns, far_mate, w0, w1)
    first = swap(sent, "head", 2)
    operands = (owns, join(far_mate, swap(near_mate, "head", 1), sent), *weights)
    calls = []
    for lo, hi in ((1, 2), (2, 4), (4, 6), (6, 8)):
        sent, near = project_both(*operands, lo * chunk, (hi - lo) * chunk, chunk)
        calls.append((near, lo, [swap(part, "head", 2) for part in sent]))
    result = project_near(*operands, first)
    for near, lo, arrived in calls[:-1]:
        result = add_chunks(near, 0, arrived, result, lo * chunk)
    near, lo, arrived = calls[-1]
    for k, part in enumerate(arrived):
        result = add_chunks(near, k * chunk, [part], result, (lo + k) * chunk)
    return result


def solution(mesh):
    in_specs = (
        P("seq", "head"),
        P("seq", "head"),
        P("seq", "head", None),
        P(None, "head"),
        P(None, "head", None),
        P("seq", "head"),
        P("seq", "head"),
        P("head"),
        P("head"),
        P("head", None),
    )
    out_specs = P(("seq", "head"), None)
    return jax.shard_map(local, mesh=mesh, in_specs=in_specs, out_specs=out_specs, check_vma=False)
```
